32 devices in a mesh: role: 2 (over y), dp: 16 (over z, x, core).
Axes of the slice: x: 2, y: 2, z: 4, core: 2. Of those that a mesh axis runs over, the one named last changes fastest.
Arguments:
- frames: bfloat16 [2, 128, 121, 2048], P('role', 'dp'), may hold values from -6 to 6
- game_ids: int32 [128], P('dp'), may hold values from 0 to 39, as said below
- taken_actions: int32 [128], P('dp'), may hold values from 0 to 17
- next_actions: int32 [128], P('dp'), may hold values from 0 to 17
- expert_flags: int32 [128], P('dp'), may hold values 0 or 1
- rewards: float32 [128], P('dp'), may hold values from -1 to 1
- done_flags: int32 [128], P('dp'), may hold values 0 or 1
- weight_in: float32 [1, 2048, 512], P(None, 'dp'), may hold values from -0.125 to 0.125
- weight_mid: float32 [1, 4608, 512], P(None, 'dp'), may hold values from -0.09375 to 0.09375
- weight_out: float32 [1, 512, 2048], P(None, 'dp'), may hold values from -0.25 to 0.25
- norm_gains: float32 [1, 6144], P(None, 'dp'), may hold values from 0.5 to 1.5
- head_table: float32 [2048, 36720], P('dp'), may hold values from -0.125 to 0.125
- moment_in: float32 [1, 2048, 512], P(None, 'dp'), may hold values from -0.046875 to 0.046875
- moment_mid: float32 [1, 4608, 512], P(None, 'dp'), may hold values from -0.046875 to 0.046875
- moment_out: float32 [1, 512, 2048], P(None, 'dp'), may hold values from -0.046875 to 0.046875
- moment_gains: float32 [1, 6144], P(None, 'dp'), may hold values from -0.15625 to 0.15625
- moment_head: float32 [2048, 36720], P('dp'), may hold values from -0.046875 to 0.046875
- average_in: float32 [1, 2048, 512], P(None, 'dp'), may hold values from -0.125 to 0.125
- average_mid: float32 [1, 4608, 512], P(None, 'dp'), may hold values from -0.09375 to 0.09375
- average_out: float32 [1, 512, 2048], P(None, 'dp'), may hold values from -0.25 to 0.25
- average_gains: float32 [1, 6144], P(None, 'dp'), may hold values from 0.5 to 1.5
- average_head: float32 [2048, 36720], P('dp'), may hold values from -0.125 to 0.125
Outputs:
- loss_total: float32 [], replicated
- new_weight_in: float32 [1, 2048, 512], P(None, 'dp', 'role')
- gradient_in: float32 [1, 2048, 512], P(None, 'dp', 'role')
- new_average_in: float32 [1, 2048, 512], P(None, 'dp', 'role')
- copy_weight_in: bfloat16 [1, 2048, 512], P(None, 'dp', 'role')
- new_weight_mid: float32 [1, 4608, 512], P(None, 'dp', 'role')
- new_moment_mid: float32 [1, 4608, 512], P(None, 'dp', 'role')
- new_average_mid: float32 [1, 4608, 512], P(None, 'dp', 'role')
- copy_weight_mid: bfloat16 [1, 4608, 512], P(None, 'dp', 'role')
- new_weight_out: float32 [1, 512, 2048], P(None, 'dp', 'role')
- new_moment_out: float32 [1, 512, 2048], P(None, 'dp', 'role')
- new_average_out: float32 [1, 512, 2048], P(None, 'dp', 'role')
- copy_weight_out: bfloat16 [1, 512, 2048], P(None, 'dp', 'role')
- new_norm_gains: float32 [1, 6144], P(None, 'dp')
- new_moment_gains: float32 [1, 6144], P(None, 'dp')
- new_average_gains: float32 [1, 6144], P(None, 'dp')
- copy_norm_gains: bfloat16 [1, 6144], P(None, 'dp')
- new_head_table: float32 [2048, 36720], P('dp', 'role')
- new_moment_head: float32 [2048, 36720], P('dp', 'role')
- new_average_head: float32 [2048, 36720], P('dp', 'role')
- copy_head_table: bfloat16 [2048, 36720], P('dp', 'role')
The draws below stay inside these ranges and needn't reach their ends.
Inputs may be any that keep to these rules, and one draw needn't show every extreme that they name: `game_ids`: 10 of the games, never game 0 nor game 40 - 1, are never drawn; which ones is drawn from the seed; the other games are equally likely.
All inputs are finite; a program needn't handle non-finite values. No bound on the sum of `expert_flags` or of `done_flags` on one device may be relied on, other than what follows from the above.
Results may differ from the reference program's by a relative error of at most 0.015.
Values may be sent and summed in bfloat16 or wider, within the bound.
A program may use at most 320 MiB of HBM per device.

```python
import jax
import jax.numpy as jnp
from jax import lax

D = 2048
MID = 512
GAMES = 40
ACTIONS = 18
ATOMS = 51
GROUPS = 32
SIDE = 11
LAYERS = 1
PIX = 121
TRANS = 128


def draw_game_ids(key, part):
    order_key = jax.random.fold_in(key, 11)
    pick_key = jax.random.fold_in(key, 23)
    middle = 1 + jax.random.permutation(order_key, GAMES - 2).astype(jnp.int32)
    present = jnp.concatenate([jnp.zeros((1,), jnp.int32), middle[GAMES // 4:], jnp.full((1,), GAMES - 1, jnp.int32)])
    chosen = jax.random.randint(pick_key, (TRANS,), 0, GAMES - GAMES // 4)
    return present[chosen].astype(jnp.int32)


def place_ends(drawn, stream_key, low, high):
    extent = drawn.shape
    index_at = [jax.random.randint(jax.random.fold_in(stream_key, axis), (), 0, extent[axis]) for axis in range(len(extent))]
    drawn = drawn.at[tuple(index_at)].set(low)
    longest = extent.index(max(extent))
    index_at[longest] = (index_at[longest] + 1) % extent[longest]
    return drawn.at[tuple(index_at)].set(high)


def shard_levels(stream_key, dims, cuts, low, largest):
    def one(axis_at, blocks):
        heights = jax.random.uniform(jax.random.fold_in(jax.random.fold_in(stream_key, 6), axis_at), (blocks,), jnp.float32, low / len(cuts), largest / len(cuts))
        return jnp.repeat(jnp.exp(heights), dims[axis_at] // blocks).reshape((-1,) + (1,) * (len(dims) - axis_at - 1))

    level = one(*cuts[0])
    for cut in cuts[1:]:
        level = level * one(*cut)
    return level


def gaussian(key, extent, scale, bound, shards=(), held_as=jnp.bfloat16):
    array = jax.random.normal(key, extent, jnp.float32) * scale
    if len(shards) > 0:
        array = shard_levels(key, extent, shards, -0.22, 0.18) * array
    return jnp.clip(array, min=-bound, max=bound).astype(held_as)


def setup_inputs(seed: int = 0) -> dict:
    key_list = jax.random.split(jax.random.key(seed), 23)
    frames = gaussian(key_list[0], (2, TRANS, PIX, D), 1.0, 6.0, ((0, 2), (1, 16)))
    game_ids = draw_game_ids(jax.random.fold_in(key_list[22], 71), 0)
    taken_actions = place_ends(jax.random.randint(key_list[2], (TRANS,), 0, ACTIONS), jax.random.fold_in(key_list[2], 1), 0, ACTIONS - 1).astype(jnp.int32)
    next_actions = place_ends(jax.random.randint(key_list[3], (TRANS,), 0, ACTIONS), jax.random.fold_in(key_list[3], 1), 0, ACTIONS - 1).astype(jnp.int32)
    expert_flags = place_ends((jax.random.randint(key_list[4], (TRANS,), 0, 2) < 1).astype(jnp.int32), jax.random.fold_in(key_list[4], 1), 0, 1)
    rewards = jnp.clip(jax.random.uniform(key_list[5], (TRANS,), jnp.float32, -1.0, 1.0) * shard_levels(key_list[5], (TRANS,), ((0, 16),), -0.4, 0.0), -1.0, 1.0)
    done_flags = place_ends((jax.random.randint(key_list[6], (TRANS,), 0, 8) < 1).astype(jnp.int32), jax.random.fold_in(key_list[6], 1), 0, 1)
    weight_in = gaussian(key_list[7], (LAYERS, D, MID), D ** -0.5, 0.125, ((1, 16),), jnp.float32)
    weight_mid = gaussian(key_list[8], (LAYERS, 9 * MID, MID), (9 * MID) ** -0.5, 0.09375, ((1, 16),), jnp.float32)
    weight_out = gaussian(key_list[9], (LAYERS, MID, D), MID ** -0.5, 0.25, ((1, 16),), jnp.float32)
    norm_gains = jnp.clip(1.0 + 0.1 * jax.random.normal(key_list[10], (LAYERS, 4 * MID + 2 * D), jnp.float32), 0.5, 1.5)
    head_table = gaussian(key_list[11], (D, GAMES * ACTIONS * ATOMS), D ** -0.5, 0.125, ((0, 16),), jnp.float32)
    moment_in = gaussian(key_list[12], (LAYERS, D, MID), 0.003, 0.046875, ((1, 16),), jnp.float32)
    moment_mid = gaussian(key_list[13], (LAYERS, 9 * MID, MID), 0.003, 0.046875, ((1, 16),), jnp.float32)
    moment_out = gaussian(key_list[14], (LAYERS, MID, D), 0.003, 0.046875, ((1, 16),), jnp.float32)
    moment_gains = gaussian(key_list[15], (LAYERS, 4 * MID + 2 * D), 0.01, 0.15625, ((1, 16),), jnp.float32)
    moment_head = gaussian(key_list[16], (D, GAMES * ACTIONS * ATOMS), 0.003, 0.046875, ((0, 16),), jnp.float32)
    average_in = gaussian(key_list[17], (LAYERS, D, MID), D ** -0.5, 0.125, ((1, 16),), jnp.float32)
    average_mid = gaussian(key_list[18], (LAYERS, 9 * MID, MID), (9 * MID) ** -0.5, 0.09375, ((1, 16),), jnp.float32)
    average_out = gaussian(key_list[19], (LAYERS, MID, D), MID ** -0.5, 0.25, ((1, 16),), jnp.float32)
    average_gains = jnp.clip(1.0 + 0.1 * jax.random.normal(key_list[20], (LAYERS, 4 * MID + 2 * D), jnp.float32), 0.5, 1.5)
    average_head = gaussian(key_list[21], (D, GAMES * ACTIONS * ATOMS), D ** -0.5, 0.125, ((0, 16),), jnp.float32)
    return {"frames": frames, "game_ids": game_ids, "taken_actions": taken_actions, "next_actions": next_actions, "expert_flags": expert_flags, "rewards": rewards, "done_flags": done_flags, "weight_in": weight_in, "weight_mid": weight_mid, "weight_out": weight_out, "norm_gains": norm_gains, "head_table": head_table, "moment_in": moment_in, "moment_mid": moment_mid, "moment_out": moment_out, "moment_gains": moment_gains, "moment_head": moment_head, "average_in": average_in, "average_mid": average_mid, "average_out": average_out, "average_gains": average_gains, "average_head": average_head}


support_low = -10.0
support_high = 10.0
discount = 0.99
penalty = 0.05
momentum_decay = 0.5
average_decay = 0.5
learn_rate = 4.0
gain_rate = 40.0
epsilon = 1e-05
HIGHEST = lax.Precision.HIGHEST

@jax.custom_vjp
def low(v):
    return lax.optimization_barrier(v.astype(jnp.bfloat16)).astype(jnp.float32)

@jax.custom_vjp
def low_back(v):
    return v

def low_keep(v):
    return (low(v), None)

def low_pass(kept, grad):
    return (grad,)

def back_keep(v):
    return (v, None)

def back_low(kept, grad):
    return (low(grad),)
low.defvjp(low_keep, low_pass)
low_back.defvjp(back_keep, back_low)

def split_gains(gains):
    return (gains[:MID], gains[MID:2 * MID], gains[2 * MID:3 * MID], gains[3 * MID:4 * MID], gains[4 * MID:4 * MID + D], gains[4 * MID + D:])

def group_norm(values, gain, shift):
    rows, pixels, width = values.shape
    grouped = values.reshape(rows, pixels, GROUPS, width // GROUPS)
    center = grouped - lax.optimization_barrier(jnp.mean(grouped, axis=(1, 3), keepdims=True))
    spread = lax.optimization_barrier(jnp.mean(center * center, axis=(1, 3), keepdims=True))
    normed = (center * lax.rsqrt(spread + epsilon)).reshape(values.shape)
    return normed * gain + shift

def patches_of(acts):
    rows, pixels, width = acts.shape
    grid = acts.reshape(rows, SIDE, SIDE, width)
    padded = jnp.pad(grid, ((0, 0), (1, 1), (1, 1), (0, 0)))
    pieces = [padded[:, down:down + SIDE, right:right + SIDE, :] for down in range(3) for right in range(3)]
    return jnp.concatenate(pieces, axis=-1).reshape(rows, pixels, 9 * width)

def block(stream, w_in, w_mid, w_out, gains):
    gain_one, shift_one, gain_two, shift_two, gain_three, shift_three = split_gains(gains)
    hidden_in = low_back(jnp.einsum('bpc,cm->bpm', low(stream), w_in, precision=HIGHEST))
    act_in = low(jax.nn.gelu(group_norm(hidden_in, gain_one, shift_one)))
    hidden_mid = low_back(jnp.einsum('bpc,cm->bpm', patches_of(act_in), w_mid, precision=HIGHEST))
    act_mid = low(jax.nn.gelu(group_norm(hidden_mid, gain_two, shift_two)))
    hidden_out = low_back(jnp.einsum('bpc,cm->bpm', act_mid, w_out, precision=HIGHEST))
    return jax.nn.gelu(stream + group_norm(hidden_out, gain_three, shift_three))

def network(params, stream, game_hot):
    w_in, w_mid, w_out, gains, head = params
    for layer in range(LAYERS):
        stream = block(stream, low(w_in[layer]), low(w_mid[layer]), low(w_out[layer]), low(gains[layer]))
    feat = low(lax.optimization_barrier(jnp.mean(stream, axis=1)))
    full = jnp.dot(feat, low(head), precision=HIGHEST)
    rows = full.shape[0]
    chosen = lax.optimization_barrier(jnp.sum(full.reshape(rows, GAMES, ACTIONS * ATOMS) * game_hot[:, :, None], axis=1))
    return low_back(chosen).reshape(rows, ACTIONS, ATOMS)

def transition_loss(logits, target_dist, action_hot, expert, support):
    log_prob = jax.nn.log_softmax(logits, axis=-1)
    values = lax.optimization_barrier(jnp.sum(jnp.exp(log_prob) * support, axis=-1))
    spread_sum = jax.nn.logsumexp(values, axis=-1)
    chosen_log = lax.optimization_barrier(jnp.sum(log_prob * action_hot[:, :, None], axis=1))
    cross = -lax.optimization_barrier(jnp.sum(target_dist * chosen_log, axis=-1))
    regular = spread_sum - lax.optimization_barrier(jnp.sum(values * action_hot, axis=-1))
    return cross + penalty * expert * regular

def project_target(next_prob, rewards, done_f, support):
    moved = jnp.clip(rewards[:, None] + discount * (1.0 - done_f)[:, None] * support[None, :], support_low, support_high)
    spacing = (support_high - support_low) / (ATOMS - 1)
    weight = jnp.maximum(0.0, 1.0 - jnp.abs(moved[:, :, None] - support[None, None, :]) / spacing)
    return lax.optimization_barrier(jnp.sum(next_prob[:, :, None] * weight, axis=1))

def renew(weight, grad, moment, average, rate):
    new_moment = momentum_decay * moment + grad
    new_weight = weight - rate * (grad + momentum_decay * new_moment)
    new_average = average_decay * average + (1.0 - average_decay) * new_weight
    return (new_weight, new_moment, new_average, new_weight.astype(jnp.bfloat16))

def reference(frames, game_ids, taken_actions, next_actions, expert_flags, rewards, done_flags, weight_in, weight_mid, weight_out, norm_gains, head_table, moment_in, moment_mid, moment_out, moment_gains, moment_head, average_in, average_mid, average_out, average_gains, average_head):
    support = support_low + (support_high - support_low) * jnp.arange(ATOMS, dtype=jnp.float32) / (ATOMS - 1)
    game_hot = jax.nn.one_hot(game_ids, GAMES, dtype=jnp.float32)
    action_hot = jax.nn.one_hot(taken_actions, ACTIONS, dtype=jnp.float32)
    next_hot = jax.nn.one_hot(next_actions, ACTIONS, dtype=jnp.float32)
    expert = expert_flags.astype(jnp.float32)
    averages = (average_in, average_mid, average_out, average_gains, average_head)
    target_logits = network(averages, frames[1].astype(jnp.float32), game_hot)
    next_prob = jax.nn.softmax(lax.optimization_barrier(jnp.sum(target_logits * next_hot[:, :, None], axis=1)), axis=-1)
    target_dist = project_target(next_prob, rewards, done_flags.astype(jnp.float32), support)
    counts = jnp.maximum(lax.optimization_barrier(jnp.sum(game_hot, axis=0)), 1.0)
    current = frames[0].astype(jnp.float32)

    def objective(params):
        logits = network(params, current, game_hot)
        row_loss = transition_loss(logits, target_dist, action_hot, expert, support)
        sums = jnp.dot(row_loss, game_hot, precision=HIGHEST)
        return jnp.sum(sums / counts)
    params = (weight_in, weight_mid, weight_out, norm_gains, head_table)
    loss_total, loss_back = jax.vjp(objective, params)
    grads, = loss_back(jnp.full((), 1.0 / GAMES, jnp.float32))
    in_w, in_m, in_a, in_c = renew(weight_in, grads[0], moment_in, average_in, learn_rate)
    mid_w, mid_m, mid_a, mid_c = renew(weight_mid, grads[1], moment_mid, average_mid, learn_rate)
    out_w, out_m, out_a, out_c = renew(weight_out, grads[2], moment_out, average_out, learn_rate)
    gain_w, gain_m, gain_a, gain_c = renew(norm_gains, grads[3], moment_gains, average_gains, gain_rate)
    head_w, head_m, head_a, head_c = renew(head_table, grads[4], moment_head, average_head, learn_rate)
    return (loss_total, in_w, grads[0], in_a, in_c, mid_w, mid_m, mid_a, mid_c, out_w, out_m, out_a, out_c, gain_w, gain_m, gain_a, gain_c, head_w, head_m, head_a, head_c)
```

```python
import functools

import jax
import jax.numpy as jnp
import numpy as np
from jax import lax
from jax.experimental import pallas as pl
from jax.experimental.pallas import tpu as pltpu
from jax.sharding import PartitionSpec as P

D = 2048
MID = 512
GAMES = 40
ACTIONS = 18
ATOMS = 51
GROUPS = 32
SIDE = 11
LAYERS = 1


support_low = -10.0
support_high = 10.0
discount = 0.99
penalty = 0.05
momentum_decay = 0.5
average_decay = 0.5
learn_rate = 4.0
gain_rate = 40.0
epsilon = 1e-05
HIGHEST = lax.Precision.HIGHEST


def passed_along(block, axis, distance):
    devices = range(lax.axis_size(axis))
    route = [(i - distance, i) for i in devices if i - distance in devices]
    return lax.ppermute(block, axis, route)


def split_gains(gains):
    return (
        gains[:MID],
        gains[MID : 2 * MID],
        gains[2 * MID : 3 * MID],
        gains[3 * MID : 4 * MID],
        gains[4 * MID : 4 * MID + D],
        gains[4 * MID + D :],
    )


def group_norm(values, gain, shift):
    rows, pixels, width = values.shape
    grouped = values.reshape(rows, pixels, GROUPS, width // GROUPS)
    center = grouped - jnp.mean(grouped, axis=(1, 3), keepdims=True)
    spread = jnp.mean(center * center, axis=(1, 3), keepdims=True)
    normed = (center * lax.rsqrt(spread + epsilon)).reshape(values.shape)
    return normed * gain + shift


def patches_of(acts):
    rows, pixels, width = acts.shape
    grid = acts.reshape(rows, SIDE, SIDE, width)
    padded = jnp.pad(grid, ((0, 0), (1, 1), (1, 1), (0, 0)))
    pieces = [
        padded[:, down : down + SIDE, right : right + SIDE, :]
        for down in range(3)
        for right in range(3)
    ]
    return jnp.concatenate(pieces, axis=-1).reshape(rows, pixels, 9 * width)


def transition_loss(logits, target_dist, action_hot, expert, support):
    log_prob = jax.nn.log_softmax(logits, axis=-1)
    values = jnp.sum(jnp.exp(log_prob) * support, axis=-1)
    spread_sum = jax.nn.logsumexp(values, axis=-1)
    chosen_log = jnp.sum(log_prob * action_hot[:, :, None], axis=1)
    cross = -jnp.sum(target_dist * chosen_log, axis=-1)
    regular = spread_sum - jnp.sum(values * action_hot, axis=-1)
    return cross + penalty * expert * regular


def project_target(next_prob, rewards, done_f, support):
    moved = jnp.clip(
        rewards[:, None] + discount * (1.0 - done_f)[:, None] * support[None, :],
        support_low,
        support_high,
    )
    spacing = (support_high - support_low) / (ATOMS - 1)
    weight = jnp.maximum(0.0, 1.0 - jnp.abs(moved[:, :, None] - support[None, None, :]) / spacing)
    return jnp.sum(next_prob[:, :, None] * weight, axis=1)


def renew(weight, grad, moment, average, rate):
    new_moment = momentum_decay * moment + grad
    new_weight = weight - rate * (grad + momentum_decay * new_moment)
    new_average = average_decay * average + (1.0 - average_decay) * new_weight
    return (new_weight, new_moment, new_average, new_weight.astype(jnp.bfloat16))


def lower_half(values):
    return values[..., : values.shape[-1] // 2]


def upper_half(values):
    return values[..., values.shape[-1] // 2 :]


def own_half(values, role_index):
    half = values.shape[-1] // 2
    return lax.dynamic_slice_in_dim(values, role_index * half, half, values.ndim - 1)


def norm_act(hidden, gain, shift):
    return jax.nn.gelu(group_norm(hidden, gain, shift))


def outer_act(hidden, gain, shift, stream):
    return jax.nn.gelu(stream + group_norm(hidden, gain, shift))


def block_forward(stream, weights):
    w_in, w_mid, w_out, gains = weights
    gain_one, shift_one, gain_two, shift_two, gain_three, shift_three = split_gains(gains)
    stream_low = stream.astype(jnp.bfloat16)
    hidden_in = jnp.einsum("bpc,cm->bpm", stream_low, w_in, preferred_element_type=jnp.float32)
    act_in = norm_act(hidden_in, gain_one, shift_one).astype(jnp.bfloat16)
    hidden_mid = jnp.einsum(
        "bpc,cm->bpm", patches_of(act_in), w_mid, preferred_element_type=jnp.float32
    )
    act_mid = norm_act(hidden_mid, gain_two, shift_two).astype(jnp.bfloat16)
    hidden_out = jnp.einsum("bpc,cm->bpm", act_mid, w_out, preferred_element_type=jnp.float32)
    result = outer_act(hidden_out, gain_three, shift_three, stream)
    return (result, (stream, stream_low, hidden_in, act_in, hidden_mid, act_mid, hidden_out))


def block_backward(grad_result, weights, kept, settle):
    w_in, w_mid, w_out, gains = weights
    stream, stream_low, hidden_in, act_in, hidden_mid, act_mid, hidden_out = kept
    gain_one, shift_one, gain_two, shift_two, gain_three, shift_three = split_gains(gains)
    _, back_three = jax.vjp(outer_act, hidden_out, gain_three, shift_three, stream)
    d_three, dg_three, db_three, d_resid = back_three(grad_result)
    d_three = d_three.astype(jnp.bfloat16)
    grad_out = settle(
        jnp.einsum("bpm,bpc->mc", act_mid, d_three, preferred_element_type=jnp.float32)
    )
    d_act_mid = jnp.einsum("bpc,mc->bpm", d_three, w_out, preferred_element_type=jnp.float32)
    _, back_two = jax.vjp(norm_act, hidden_mid, gain_two, shift_two)
    d_two, dg_two, db_two = back_two(d_act_mid)
    d_two = d_two.astype(jnp.bfloat16)
    grad_mid = settle(
        jnp.einsum("bpk,bpm->km", patches_of(act_in), d_two, preferred_element_type=jnp.float32)
    )
    d_cols = jnp.einsum("bpm,km->bpk", d_two, w_mid, preferred_element_type=jnp.float32)
    _, back_cols = jax.vjp(patches_of, act_in.astype(jnp.float32))
    (d_act_in,) = back_cols(d_cols)
    _, back_one = jax.vjp(norm_act, hidden_in, gain_one, shift_one)
    d_one, dg_one, db_one = back_one(d_act_in)
    d_one = d_one.astype(jnp.bfloat16)
    grad_in = jnp.einsum("bpc,bpm->cm", stream_low, d_one, preferred_element_type=jnp.float32)
    d_stream = d_resid + jnp.einsum("bpm,cm->bpc", d_one, w_in, preferred_element_type=jnp.float32)
    grad_gains = jnp.concatenate([dg_one, db_one, dg_two, db_two, dg_three, db_three])
    grad_in, grad_gains = settle((grad_in, grad_gains))
    return (d_stream, (grad_in, grad_mid, grad_out, grad_gains))


def on_device(
    frames,
    game_ids,
    taken_actions,
    next_actions,
    expert_flags,
    rewards,
    done_flags,
    weight_in,
    weight_mid,
    weight_out,
    norm_gains,
    head_table,
    moment_in,
    moment_mid,
    moment_out,
    moment_gains,
    moment_head,
    average_in,
    average_mid,
    average_out,
    average_gains,
    average_head,
):
    role_index = lax.axis_index("role")
    online = role_index == 0
    use_in = jnp.where(online, weight_in, average_in).astype(jnp.bfloat16)
    use_mid = jnp.where(online, weight_mid, average_mid).astype(jnp.bfloat16)
    use_out = jnp.where(online, weight_out, average_out).astype(jnp.bfloat16)
    use_gains = jnp.where(online, norm_gains, average_gains).astype(jnp.bfloat16)
    use_head = jnp.where(online, head_table, average_head).astype(jnp.bfloat16)
    support = support_low + (support_high - support_low) * jnp.arange(ATOMS, dtype=jnp.float32) / (
        ATOMS - 1
    )
    own_hot = (game_ids[:, None] == lax.broadcasted_iota(jnp.int32, (1, GAMES), 1)).astype(
        jnp.float32
    )
    counts = jnp.sum(own_hot, axis=0)
    stream = frames[0].astype(jnp.float32)
    layer = 0
    pieces = (
        lax.all_gather(use_in[layer], "dp", axis=0, tiled=True),
        lax.all_gather(use_mid[layer], "dp", axis=0, tiled=True),
        lax.all_gather(use_out[layer], "dp", axis=0, tiled=True),
        lax.all_gather(use_gains[layer], "dp", axis=0, tiled=True),
    )
    weights = (pieces[0], pieces[1], pieces[2], pieces[3].astype(jnp.float32))
    stream, saved = block_forward(stream, weights)
    gathered = [weights]
    kept = [saved]
    trans = stream.shape[0]
    pixels = stream.shape[1]
    wide_k = ACTIONS * ATOMS
    head_rows = head_table.shape[0]
    feat_low = jnp.mean(stream, axis=1).astype(jnp.bfloat16)
    feat_all, game_all = (
        lax.all_gather(feat_low, "dp", axis=0, tiled=True),
        lax.all_gather(game_ids.astype(jnp.bfloat16)[:, None], "dp", axis=0, tiled=True),
    )
    game_iota = lax.broadcasted_iota(jnp.int32, (1, GAMES), 1).astype(jnp.float32)
    all_hot = (game_all.astype(jnp.float32) == game_iota).astype(jnp.bfloat16)
    feat_rows = lax.dynamic_slice_in_dim(feat_all, lax.axis_index("dp") * head_rows, head_rows, 1)
    head_low = use_head.reshape(head_rows * GAMES, wide_k)

    def widen(count):
        spread_rows = (feat_rows[:, :, None] * all_hot[:, None, :]).reshape(
            count, head_rows * GAMES
        )
        return (spread_rows, all_hot)

    spread_rows, hot_piece = widen(trans * lax.axis_size("dp"))
    flat_logits = lax.psum_scatter(
        jnp.dot(spread_rows, head_low, preferred_element_type=jnp.float32),
        "dp",
        scatter_dimension=0,
        tiled=True,
    )
    logits = flat_logits.reshape(trans, ACTIONS, ATOMS)
    next_hot = (next_actions[:, None] == lax.broadcasted_iota(jnp.int32, (1, ACTIONS), 1)).astype(
        jnp.float32
    )
    next_prob = jax.nn.softmax(jnp.sum(logits * next_hot[:, :, None], axis=1), axis=-1)
    projected = project_target(next_prob, rewards, done_flags.astype(jnp.float32), support)
    target_dist = passed_along(projected, "role", -1)
    action_hot = (
        taken_actions[:, None] == lax.broadcasted_iota(jnp.int32, (1, ACTIONS), 1)
    ).astype(jnp.float32)
    expert = expert_flags.astype(jnp.float32)

    def local_loss(values):
        return transition_loss(values, target_dist, action_hot, expert, support)

    row_loss, loss_back = jax.vjp(local_loss, logits)
    sums = jnp.dot(row_loss, own_hot, precision=HIGHEST)
    total_counts, total_sums = lax.psum((counts, sums), "dp")
    floor_counts = jnp.maximum(total_counts, 1.0)
    loss_total = jnp.sum(total_sums / floor_counts)
    row_weight = jnp.dot(own_hot, 1.0 / (GAMES * floor_counts), precision=HIGHEST)
    (d_logits,) = loss_back(row_weight)
    d_low = d_logits.reshape(trans, wide_k).astype(jnp.bfloat16)
    piece = lax.all_gather(d_low, "dp", axis=0, tiled=True)
    count = piece.shape[0]
    spread_rows, hot_piece = widen(count)
    grad_head = lax.dot_general(
        spread_rows, piece, (((0,), (0,)), ((), ())), preferred_element_type=jnp.float32
    )
    back_wide = jnp.dot(piece, head_low.T, preferred_element_type=jnp.float32)
    back_rows = jnp.sum(
        back_wide.reshape(count, head_rows, GAMES) * hot_piece[:, None, :].astype(jnp.float32),
        axis=2,
    )
    grad_rows = back_rows
    grad_head, grad_rows = (grad_head, grad_rows)
    feat_grad = lax.all_to_all(
        grad_rows.astype(jnp.bfloat16), "dp", split_axis=0, concat_axis=1, tiled=True
    ).astype(grad_rows.dtype)
    d_stream = jnp.broadcast_to(feat_grad[:, None, :] / pixels, stream.shape)

    def settle(values):
        return values

    layer_grads = [None] * LAYERS
    for layer in reversed(range(LAYERS)):
        d_stream, block_grad = block_backward(d_stream, gathered[layer], kept[layer], settle)
        layer_grads[layer] = block_grad
    stacked = tuple((jnp.stack([layer_grads[0][kind]]) for kind in range(4)))
    reduced = lax.psum_scatter(stacked, "dp", scatter_dimension=1, tiled=True)
    head_grad = grad_head.reshape(head_rows, GAMES * wide_k)
    sent = (
        passed_along(upper_half(reduced[0]).astype(jnp.bfloat16), "role", 1).astype(jnp.float32),
        passed_along(upper_half(reduced[1]).astype(jnp.bfloat16), "role", 1).astype(jnp.float32),
        passed_along(upper_half(reduced[2]).astype(jnp.bfloat16), "role", 1).astype(jnp.float32),
        passed_along(reduced[3].astype(jnp.bfloat16), "role", 1).astype(jnp.float32),
        passed_along(upper_half(head_grad).astype(jnp.bfloat16), "role", 1).astype(jnp.float32),
        passed_along(loss_total.astype(jnp.bfloat16), "role", 1).astype(loss_total.dtype),
    )
    grad_in = jnp.where(online, lower_half(reduced[0]), sent[0])
    grad_mid = jnp.where(online, lower_half(reduced[1]), sent[1])
    grad_out = jnp.where(online, lower_half(reduced[2]), sent[2])
    grad_gains = jnp.where(online, reduced[3], sent[3])
    grad_table = jnp.where(online, lower_half(head_grad), sent[4])
    loss_out = jnp.where(online, loss_total, sent[5])
    in_w, in_m, in_a, in_c = renew(
        own_half(weight_in, role_index),
        grad_in,
        own_half(moment_in, role_index),
        own_half(average_in, role_index),
        learn_rate,
    )
    mid_w, mid_m, mid_a, mid_c = renew(
        own_half(weight_mid, role_index),
        grad_mid,
        own_half(moment_mid, role_index),
        own_half(average_mid, role_index),
        learn_rate,
    )
    out_w, out_m, out_a, out_c = renew(
        own_half(weight_out, role_index),
        grad_out,
        own_half(moment_out, role_index),
        own_half(average_out, role_index),
        learn_rate,
    )
    gain_w, gain_m, gain_a, gain_c = renew(
        norm_gains, grad_gains, moment_gains, average_gains, gain_rate
    )
    head_w, head_m, head_a, head_c = renew(
        own_half(head_table, role_index),
        grad_table,
        own_half(moment_head, role_index),
        own_half(average_head, role_index),
        learn_rate,
    )
    return (
        loss_out,
        in_w,
        grad_in,
        in_a,
        in_c,
        mid_w,
        mid_m,
        mid_a,
        mid_c,
        out_w,
        out_m,
        out_a,
        out_c,
        gain_w,
        gain_m,
        gain_a,
        gain_c,
        head_w,
        head_m,
        head_a,
        head_c,
    )


D = 2048
MID = 512
GROUPS = 32
SIDE = 11
PIX = 121
TB = 8
PITCH = 12
RB = PITCH * TB
VR = SIDE * TB
ROWS = SIDE * RB
PAD = 16 * TB
EROWS = 164 * TB
BLK = 352
CH = 512
epsilon = 1e-05
GK = 0.7978845608028654
GC = 0.044715
OFFS = [(i - 1) * PITCH + (j - 1) for i in range(3) for j in range(3)]


def group_sum(v, gs):
    width = v.shape[1]
    n = width // 128
    a = lax.broadcasted_iota(jnp.int32, (128, 128), 0) // gs
    b = lax.broadcasted_iota(jnp.int32, (128, 128), 1) // gs
    m = (a == b).astype(jnp.float32)
    st = jnp.concatenate([v[:, k * 128:(k + 1) * 128] for k in range(n)], axis=0)
    r = jnp.dot(st, m, precision=lax.Precision.HIGHEST, preferred_element_type=jnp.float32)
    return jnp.concatenate([r[k * 8:(k + 1) * 8] for k in range(n)], axis=1)


def fold(v):
    rows, w = v.shape
    return jnp.sum(v.reshape(rows // TB, TB, w), axis=0)


def moments(h_ref, lo, gs):
    def one(r, acc):
        return acc + fold(h_ref[pl.ds(pl.multiple_of(r * RB, RB), VR), lo:lo + CH])
    s = lax.fori_loop(0, SIDE, one, jnp.zeros((TB, CH), jnp.float32))
    mean = group_sum(s, gs) / float(PIX * gs)

    def two(r, acc):
        h = h_ref[pl.ds(pl.multiple_of(r * RB, RB), VR), lo:lo + CH].reshape(SIDE, TB, CH) - mean[None]
        return acc + jnp.sum(h * h, axis=0)
    q = lax.fori_loop(0, SIDE, two, jnp.zeros((TB, CH), jnp.float32))
    var = group_sum(q, gs) / float(PIX * gs)
    return mean, lax.rsqrt(var + epsilon)


def gelu(u):
    return 0.5 * u * (1.0 + jnp.tanh(GK * (u + GC * (u * u * u))))


def dgelu(u):
    uu = u * u
    t = jnp.tanh(GK * u * (1.0 + GC * uu))
    return 0.5 * (1.0 + t) + 0.5 * u * (1.0 - t * t) * (GK + (3.0 * GK * GC) * uu)


def shifted(e_ref, o_ref, s, row, n):
    ref, base = (e_ref, 16 + s) if s % 2 == 0 else (o_ref, 17 + s)
    return ref[pl.ds(pl.multiple_of(row + base * TB, 16), n), :]


def put_shifted(e_ref, o_ref, r, v):
    z = jnp.zeros((TB, v.shape[1]), jnp.float32)
    at = pl.ds(pl.multiple_of(PAD + r * RB, 16), RB)
    e_ref[at, :] = jnp.concatenate([v, z], axis=0).astype(jnp.bfloat16)
    o_ref[at, :] = jnp.concatenate([z, v], axis=0).astype(jnp.bfloat16)


def clear_margins(e_ref, o_ref):
    z = jnp.zeros((PAD, MID), jnp.bfloat16)
    for ref in (e_ref, o_ref):
        ref[0:PAD, :] = z
        ref[PAD + ROWS:EROWS, :] = z


def row_at(r):
    return pl.ds(pl.multiple_of(r * RB, RB), VR)


def rows_full(r):
    return pl.ds(pl.multiple_of(r * RB, RB), RB)


def fwd_kernel(fr_ref, win_ref, wmid_ref, wout_ref, g_ref, x_ref, h1_ref, h2_ref, h3_ref, a1_ref, a2_ref, st_ref,
               feat_ref, e_ref, o_ref):
    def place_row(r, c):
        v = fr_ref[pl.ds(r * SIDE, SIDE)].astype(jnp.float32).reshape(VR, D)
        z = jnp.zeros((TB, D), jnp.float32)
        x_ref[rows_full(r), :] = jnp.concatenate([v, z], axis=0).astype(jnp.bfloat16)
        return c
    lax.fori_loop(0, SIDE, place_row, 0)
    clear_margins(e_ref, o_ref)

    def mm1(i, c):
        rs = pl.ds(pl.multiple_of(i * BLK, BLK), BLK)
        h1_ref[rs, :] = jnp.dot(x_ref[rs, :], win_ref[...], preferred_element_type=jnp.float32)
        return c
    lax.fori_loop(0, ROWS // BLK, mm1, 0)
    mean, rstd = moments(h1_ref, 0, MID // GROUPS)
    st_ref[0:8, 0:MID] = mean
    st_ref[8:16, 0:MID] = rstd
    sc = rstd * g_ref[:, 0:MID]
    sh = g_ref[:, MID:2 * MID] - mean * sc

    def act1(r, c):
        h = h1_ref[row_at(r), :].reshape(SIDE, TB, MID)
        a = gelu(h * sc[None] + sh[None]).reshape(VR, MID)
        put_shifted(e_ref, o_ref, r, a)
        return c
    lax.fori_loop(0, SIDE, act1, 0)
    a1_ref[...] = e_ref[PAD:PAD + ROWS, :]

    def mm2(i, c):
        row = i * BLK
        acc = None
        for n, s in enumerate(OFFS):
            p = jnp.dot(shifted(e_ref, o_ref, s, row, BLK), wmid_ref[n * MID:(n + 1) * MID, :],
                        preferred_element_type=jnp.float32)
            acc = p if acc is None else acc + p
        h2_ref[pl.ds(pl.multiple_of(row, BLK), BLK), :] = acc
        return c
    lax.fori_loop(0, ROWS // BLK, mm2, 0)
    mean, rstd = moments(h2_ref, 0, MID // GROUPS)
    st_ref[0:8, MID:2 * MID] = mean
    st_ref[8:16, MID:2 * MID] = rstd
    sc2 = rstd * g_ref[:, 2 * MID:3 * MID]
    sh2 = g_ref[:, 3 * MID:4 * MID] - mean * sc2

    def act2(r, c):
        h = h2_ref[rows_full(r), :].reshape(PITCH, TB, MID)
        a2_ref[rows_full(r), :] = gelu(h * sc2[None] + sh2[None]).reshape(RB, MID).astype(jnp.bfloat16)
        return c
    lax.fori_loop(0, SIDE, act2, 0)

    def mm3(i, c):
        rs = pl.ds(pl.multiple_of(i * BLK, BLK), BLK)
        h3_ref[rs, :] = jnp.dot(a2_ref[rs, :], wout_ref[...], preferred_element_type=jnp.float32)
        return c
    lax.fori_loop(0, ROWS // BLK, mm3, 0)
    for k in range(D // CH):
        lo = k * CH
        mean, rstd = moments(h3_ref, lo, D // GROUPS)
        st_ref[0:8, 2 * MID + lo:2 * MID + lo + CH] = mean
        st_ref[8:16, 2 * MID + lo:2 * MID + lo + CH] = rstd
        sc3 = rstd * g_ref[:, 4 * MID + lo:4 * MID + lo + CH]
        sh3 = g_ref[:, 4 * MID + D + lo:4 * MID + D + lo + CH] - mean * sc3

        def act3(r, acc):
            h = h3_ref[row_at(r), lo:lo + CH].reshape(SIDE, TB, CH)
            s = x_ref[rows_full(r), lo:lo + CH].astype(jnp.float32)[0:VR].reshape(SIDE, TB, CH)
            return acc + jnp.sum(gelu(s + (h * sc3[None] + sh3[None])), axis=0)
        acc = lax.fori_loop(0, SIDE, act3, jnp.zeros((TB, CH), jnp.float32))
        feat_ref[:, lo:lo + CH] = (acc / float(PIX)).astype(jnp.bfloat16).astype(jnp.float32)


def VS():
    return pl.BlockSpec(memory_space=pltpu.VMEM)


def forward(frames, w_in, w_mid, w_out, gains):
    f32, b16 = jnp.float32, jnp.bfloat16
    S = jax.ShapeDtypeStruct
    return pl.pallas_call(
        fwd_kernel,
        out_shape=(S((ROWS, D), b16), S((ROWS, MID), f32), S((ROWS, MID), f32), S((ROWS, D), f32), S((ROWS, MID), b16),
                   S((ROWS, MID), b16), S((16, 2 * MID + D), f32), S((TB, D), f32)),
        in_specs=[VS()] * 5,
        out_specs=(VS(),) * 8,
        scratch_shapes=[pltpu.VMEM((EROWS, MID), b16), pltpu.VMEM((EROWS, MID), b16)],
        compiler_params=pltpu.CompilerParams(vmem_limit_bytes=60 * 1024 * 1024),
        name="block_forward",
    )(frames, w_in, w_mid, w_out, gains)


def norm_back(h_ref, dy_ref, lo, mean, rstd, gain, gs, s1, s2, emit):
    n = 1.0 / float(PIX * gs)
    m1 = group_sum(gain * s1, gs) * n
    m2 = group_sum(gain * s2, gs) * n
    ca = rstd * gain
    cc = -rstd * rstd * m2
    cb = -rstd * m1 - mean * cc

    def one(r, c):
        h = h_ref[row_at(r), lo:lo + CH].reshape(SIDE, TB, CH)
        dy = dy_ref[row_at(r), lo:lo + CH].reshape(SIDE, TB, CH)
        emit(r, (ca[None] * dy + cc[None] * h + cb[None]).reshape(VR, CH))
        return c
    lax.fori_loop(0, SIDE, one, 0)


def bwd_kernel(dfeat_ref, x_ref, h1_ref, h2_ref, h3_ref, a1_ref, a2_ref, st_ref, wmid_ref, wout_ref, g_ref, gin_ref,
               gmid_ref, gout_ref, gg_ref, du_ref, dh3_ref, d2_ref, e_ref, o_ref, dh1_ref):
    T0 = (((0,), (0,)), ((), ()))
    T1 = (((1,), (1,)), ((), ()))
    clear_margins(e_ref, o_ref)
    z8 = jnp.zeros((TB, CH), jnp.float32)

    def put_gain(at, s):
        gg_ref[:, at:at + CH] = jnp.sum(s, axis=0, keepdims=True)

    for k in range(D // CH):
        lo = k * CH
        mean = st_ref[0:8, 2 * MID + lo:2 * MID + lo + CH]
        rstd = st_ref[8:16, 2 * MID + lo:2 * MID + lo + CH]
        gain = g_ref[:, 4 * MID + lo:4 * MID + lo + CH]
        shift = g_ref[:, 4 * MID + D + lo:4 * MID + D + lo + CH]
        dout = dfeat_ref[:, lo:lo + CH] / float(PIX)
        mr = mean * rstd

        def one(r, acc):
            s1, s2 = acc
            h = h3_ref[row_at(r), lo:lo + CH].reshape(SIDE, TB, CH)
            s = x_ref[rows_full(r), lo:lo + CH].astype(jnp.float32)[0:VR].reshape(SIDE, TB, CH)
            xh = h * rstd[None] - mr[None]
            du = dout[None] * dgelu(s + (xh * gain + shift))
            du_ref[row_at(r), :] = du.reshape(VR, CH)
            return s1 + jnp.sum(du, axis=0), s2 + jnp.sum(du * xh, axis=0)
        s1, s2 = lax.fori_loop(0, SIDE, one, (z8, z8))
        put_gain(4 * MID + lo, s2)
        put_gain(4 * MID + D + lo, s1)
        gs = D // GROUPS
        n = 1.0 / float(PIX * gs)
        m1 = group_sum(gain * s1, gs) * n
        m2 = group_sum(gain * s2, gs) * n
        ca = rstd * gain
        cc = -rstd * rstd * m2
        cb = -rstd * m1 - mean * cc

        def two(r, c):
            h = h3_ref[row_at(r), lo:lo + CH].reshape(SIDE, TB, CH)
            dy = du_ref[row_at(r), :].reshape(SIDE, TB, CH)
            v = (ca[None] * dy + cc[None] * h + cb[None]).reshape(VR, CH)
            dh3_ref[rows_full(r), lo:lo + CH] = jnp.concatenate([v, z8], axis=0).astype(jnp.bfloat16)
            return c
        lax.fori_loop(0, SIDE, two, 0)
        gout_ref[:, lo:lo + CH] = lax.dot_general(a2_ref[...], dh3_ref[:, lo:lo + CH], T0,
                                                  preferred_element_type=jnp.float32)

    def da2(i, c):
        rs = pl.ds(pl.multiple_of(i * BLK, BLK), BLK)
        d2_ref[rs, :] = lax.dot_general(dh3_ref[rs, :], wout_ref[...], T1, preferred_element_type=jnp.float32)
        return c
    lax.fori_loop(0, ROWS // BLK, da2, 0)

    def through(h_ref, at, goff, boff, emit):
        mean = st_ref[0:8, at:at + MID]
        rstd = st_ref[8:16, at:at + MID]
        gain = g_ref[:, goff:goff + MID]
        shift = g_ref[:, boff:boff + MID]
        mr = mean * rstd

        def one(r, acc):
            s1, s2 = acc
            h = h_ref[row_at(r), :].reshape(SIDE, TB, MID)
            da = d2_ref[row_at(r), :].reshape(SIDE, TB, MID)
            xh = h * rstd[None] - mr[None]
            dy = da * dgelu(xh * gain + shift)
            d2_ref[row_at(r), :] = dy.reshape(VR, MID)
            return s1 + jnp.sum(dy, axis=0), s2 + jnp.sum(dy * xh, axis=0)
        s1, s2 = lax.fori_loop(0, SIDE, one, (z8, z8))
        put_gain(goff, s2)
        put_gain(boff, s1)
        norm_back(h_ref, d2_ref, 0, mean, rstd, gain, MID // GROUPS, s1, s2, emit)

    through(h2_ref, MID, 2 * MID, 3 * MID, lambda r, v: put_shifted(e_ref, o_ref, r, v))
    for n, s in enumerate(OFFS):
        gmid_ref[n * MID:(n + 1) * MID, :] = lax.dot_general(
            a1_ref[...], shifted(e_ref, o_ref, -s, 0, ROWS), T0, preferred_element_type=jnp.float32)

    def da1(i, c):
        row = i * BLK
        acc = None
        for n, s in enumerate(OFFS):
            p = lax.dot_general(shifted(e_ref, o_ref, -s, row, BLK), wmid_ref[n * MID:(n + 1) * MID, :], T1,
                                preferred_element_type=jnp.float32)
            acc = p if acc is None else acc + p
        d2_ref[pl.ds(pl.multiple_of(row, BLK), BLK), :] = acc
        return c
    lax.fori_loop(0, ROWS // BLK, da1, 0)

    def put1(r, v):
        dh1_ref[rows_full(r), :] = jnp.concatenate([v, z8], axis=0).astype(jnp.bfloat16)
    through(h1_ref, 0, 0, MID, put1)

    for k in range(D // CH):
        gin_ref[k * CH:(k + 1) * CH, :] = lax.dot_general(x_ref[:, k * CH:(k + 1) * CH], dh1_ref[...], T0,
                                                          preferred_element_type=jnp.float32)


def backward(dfeat, saved, w_mid, w_out, gains):
    f32, b16 = jnp.float32, jnp.bfloat16
    S = jax.ShapeDtypeStruct
    x, h1, h2, h3, a1, a2, st, feat = saved
    V = pltpu.VMEM
    return pl.pallas_call(
        bwd_kernel,
        out_shape=(S((D, MID), f32), S((9 * MID, MID), f32), S((MID, D), f32), S((1, 4 * MID + 2 * D), f32)),
        in_specs=[VS()] * 11,
        out_specs=(VS(),) * 4,
        scratch_shapes=[V((ROWS, CH), f32), V((ROWS, D), b16), V((ROWS, MID), f32), V((EROWS, MID), b16),
                        V((EROWS, MID), b16), V((ROWS, MID), b16)],
        compiler_params=pltpu.CompilerParams(vmem_limit_bytes=62 * 1024 * 1024),
        name="block_backward",
    )(dfeat, x, h1, h2, h3, a1, a2, st, w_mid, w_out, gains)


MESH = pl.DeviceIdType.MESH


def any_spec():
    return pl.BlockSpec(memory_space=pl.ANY)


def greet(peers):
    barrier = pltpu.get_barrier_semaphore()
    for cond, dev in peers:
        def go(dev=dev):
            pl.semaphore_signal(barrier, inc=1, device_id=dev, device_id_type=MESH)
        go() if cond is None else pl.when(cond)(go)
    count = sum(1 for cond, _ in peers if cond is None)
    for cond, _ in peers:
        if cond is not None:
            count = count + cond.astype(jnp.int32)
    pl.semaphore_wait(barrier, count)


def place():
    me = lax.axis_index("dp")
    core = lax.rem(me, 2)
    x = lax.rem(me // 2, 2)
    z = me // 4
    return me, z, x, core


def gather_kernel(nz, na, *refs):
    ins, outs = refs[:na], refs[na:2 * na]
    own_sem, send, recv = refs[2 * na:]
    me, z, x, c = place()
    up, down = {"dp": me + 4}, {"dp": me - 4}
    xp = {"dp": me + 2 - 4 * x}
    cp = {"dp": me + 1 - 2 * c}
    has_up, has_down = z < nz - 1, z > 0
    greet([(has_up, up), (has_down, down), (None, xp), (None, cp)])

    def slot_of(zz, xx, cc):
        return zz * 4 + xx * 2 + cc

    started = []

    def send_to(cond, a, src, slot, dev, k):
        d = pltpu.make_async_remote_copy(src_ref=src, dst_ref=outs[a].at[slot], send_sem=send.at[a, k],
                                         recv_sem=recv.at[a, slot], device_id=dev, device_id_type=MESH)
        if cond is None:
            d.start()
        else:
            pl.when(cond)(d.start)
        started.append((cond, d))

    def wait_for(cond, a, slot):
        d = pltpu.make_async_remote_copy(src_ref=outs[a].at[slot], dst_ref=outs[a].at[slot], send_sem=send.at[a, 0],
                                         recv_sem=recv.at[a, slot], device_id=cp, device_id_type=MESH)
        if cond is None:
            d.wait_recv()
        else:
            pl.when(cond)(d.wait_recv)

    locals_ = []
    for a in range(na):
        send_to(has_up, a, ins[a], me, up, 0)
        send_to(has_down, a, ins[a], me, down, 1)
        send_to(None, a, ins[a], me, xp, 2)
        send_to(None, a, ins[a], me, cp, 3)
        l = pltpu.make_async_copy(ins[a], outs[a].at[me], own_sem.at[a])
        l.start()
        locals_.append(l)
    for d in range(1, nz):
        for a in range(na):
            k = 4 + (d - 1) * 6
            zb, za = z - d, z + d
            ok_b, ok_a = zb >= 0, za < nz
            sb, sa = me - 4 * d, me + 4 * d
            wait_for(ok_b, a, sb)
            send_to(jnp.logical_and(ok_b, has_up), a, outs[a].at[sb], sb, up, k)
            send_to(ok_b, a, outs[a].at[sb], sb, xp, k + 1)
            send_to(ok_b, a, outs[a].at[sb], sb, cp, k + 2)
            wait_for(ok_a, a, sa)
            send_to(jnp.logical_and(ok_a, has_down), a, outs[a].at[sa], sa, down, k + 3)
            send_to(ok_a, a, outs[a].at[sa], sa, xp, k + 4)
            send_to(ok_a, a, outs[a].at[sa], sa, cp, k + 5)
    k = 4 + (nz - 1) * 6
    for d in range(nz):
        for a in range(na):
            for sgn in ((1,) if d == 0 else (-1, 1)):
                zz = z + sgn * d
                ok = None if d == 0 else jnp.logical_and(zz >= 0, zz < nz)
                s = slot_of(zz, 1 - x, c)
                wait_for(ok, a, s)
                send_to(ok, a, outs[a].at[s], s, cp, k + 2 * d + (1 if sgn > 0 else 0))
    for d in range(nz):
        for a in range(na):
            for xx in (x, 1 - x):
                for sgn in ((1,) if d == 0 else (-1, 1)):
                    zz = z + sgn * d
                    ok = None if d == 0 else jnp.logical_and(zz >= 0, zz < nz)
                    wait_for(ok, a, slot_of(zz, xx, 1 - c))
    for l in locals_:
        l.wait()
    for cond, d in started:
        if cond is None:
            d.wait_send()
        else:
            pl.when(cond)(d.wait_send)


def gather(arrays, n, cid):
    na = len(arrays)
    nz = n // 4
    return pl.pallas_call(
        functools.partial(gather_kernel, nz, na),
        out_shape=tuple(jax.ShapeDtypeStruct((n,) + a.shape, a.dtype) for a in arrays),
        in_specs=[any_spec()] * na,
        out_specs=(any_spec(),) * na,
        scratch_shapes=[pltpu.SemaphoreType.DMA((na,)), pltpu.SemaphoreType.DMA((na, 4 + 6 * (nz - 1) + 2 * nz)),
                        pltpu.SemaphoreType.DMA((na, n))],
        compiler_params=pltpu.CompilerParams(collective_id=cid, has_side_effects=True),
        name="weights_gather",
    )(*arrays)


def scatter_kernel(nz, na, *refs):
    g, outs = refs[:na], refs[na:2 * na]
    r1, r2, ru, rd, fs, fr = (refs[(2 + j) * na:(3 + j) * na] for j in range(6))
    s1, q1, s2, q2, su, qu, sd, qd, sf, qf = refs[8 * na:]
    me, z, x, c = place()
    role = lax.axis_index("role")
    up, down = {"dp": me + 4}, {"dp": me - 4}
    xp = {"dp": me + 2 - 4 * x}
    cp = {"dp": me + 1 - 2 * c}
    has_up, has_down = z < nz - 1, z > 0
    greet([(has_up, up), (has_down, down), (None, xp), (None, cp), (None, {"role": 1 - role})])

    def rc(src, dst, ss, rs, dev):
        return pltpu.make_async_remote_copy(src_ref=src, dst_ref=dst, send_sem=ss, recv_sem=rs, device_id=dev,
                                            device_id_type=MESH)

    def slot(zz, xx, cc):
        return zz * 4 + xx * 2 + cc

    order = list(range(nz))

    def c1(a, zz, k):
        xx = 1 - x if k == 0 else x
        return rc(g[a].at[slot(zz, xx, 1 - c)], r1[a].at[k * nz + zz], s1.at[a, k * nz + zz], q1.at[a, k * nz + zz], cp)

    def c2(a, zz):
        return rc(g[a].at[slot(zz, 1 - x, c)], r2[a].at[zz], s2.at[a, zz], q2.at[a, zz], xp)

    def cu(a, t):
        return rc(g[a].at[slot(t, x, c)], ru[a].at[t], su.at[a, t], qu.at[a, t], up)

    def cd(a, t):
        return rc(g[a].at[slot(t, x, c)], rd[a].at[t], sd.at[a, t], qd.at[a, t], down)

    def cf(a, to):
        return rc(fs[a], fr[a], sf.at[a], qf.at[a], {"role": to})

    @pl.when(role == 0)
    def _():
        for a in range(na):
            for zz in order:
                c1(a, zz, 0).start()
            for zz in order:
                c1(a, zz, 1).start()
        for a in range(na):
            for zz in order:
                c1(a, zz, 0).wait_recv()
                s = slot(zz, 1 - x, c)
                g[a][s] = g[a][s] + r1[a][zz]
                c2(a, zz).start()
            for zz in order:
                c1(a, zz, 1).wait_recv()
                s = slot(zz, x, c)
                g[a][s] = g[a][s] + r1[a][nz + zz]
        for a in range(na):
            for zz in order:
                c2(a, zz).wait_recv()
                s = slot(zz, x, c)
                g[a][s] = g[a][s] + r2[a][zz]
            for t in range(nz - 1, 0, -1):
                @pl.when(z < t)
                def _():
                    @pl.when(z > 0)
                    def _():
                        cu(a, t).wait_recv()
                        s = slot(t, x, c)
                        g[a][s] = g[a][s] + ru[a][t]
                    cu(a, t).start()
                b = nz - 1 - t

                @pl.when(z > b)
                def _():
                    @pl.when(z < nz - 1)
                    def _():
                        cd(a, b).wait_recv()
                        s = slot(b, x, c)
                        g[a][s] = g[a][s] + rd[a][b]
                    cd(a, b).start()
        for a in range(na):
            @pl.when(z > 0)
            def _():
                cu(a, z).wait_recv()
                g[a][me] = g[a][me] + ru[a][z]

            @pl.when(z < nz - 1)
            def _():
                cd(a, z).wait_recv()
                g[a][me] = g[a][me] + rd[a][z]
            cols = outs[a].shape[1]
            total = g[a][me]
            outs[a][...] = total[:, :cols]
            fs[a][...] = total[:, total.shape[1] - cols:].astype(fs[a].dtype)
            cf(a, 1).start()
        for a in range(na):
            for zz in order:
                c1(a, zz, 0).wait_send()
                c1(a, zz, 1).wait_send()
                c2(a, zz).wait_send()
                pl.when(z < zz)(cu(a, zz).wait_send)
                pl.when(z > zz)(cd(a, zz).wait_send)
            cf(a, 1).wait_send()

    @pl.when(role == 1)
    def _():
        for a in range(na):
            cf(a, 0).wait_recv()
            outs[a][...] = fr[a][...].astype(jnp.float32)


def scatter(arrays, n, cid):
    na = len(arrays)
    nz = n // 4
    V = pltpu.VMEM
    sh = [a.shape[1:] for a in arrays]
    half = [(s[0], s[1] // 2 if s[1] > 128 else s[1]) for s in sh]
    low = [jnp.bfloat16 if s[1] > 128 else jnp.float32 for s in sh]
    dt = jnp.float32
    dma = pltpu.SemaphoreType.DMA
    return pl.pallas_call(
        functools.partial(scatter_kernel, nz, na),
        out_shape=tuple(jax.ShapeDtypeStruct(s, dt) for s in half),
        in_specs=[pl.BlockSpec(memory_space=pltpu.VMEM)] * na,
        out_specs=(pl.BlockSpec(memory_space=pltpu.VMEM),) * na,
        scratch_shapes=[V((2 * nz,) + s, dt) for s in sh] + [V((nz,) + s, dt) for s in sh] * 3 +
        [V(s, t) for s, t in zip(half, low)] * 2 +
        [dma((na, 2 * nz)), dma((na, 2 * nz))] + [dma((na, nz))] * 6 + [dma((na,))] * 2,
        compiler_params=pltpu.CompilerParams(collective_id=cid, has_side_effects=True,
                                             vmem_limit_bytes=62 * 1024 * 1024),
        name="gradient_sums",
    )(*arrays)


D = 2048
GAMES = 40
ACTIONS = 18
ATOMS = 51
WIDE = ACTIONS * ATOMS
LW = 1024
WIN = 1024
COLS = GAMES * WIDE
HALF = COLS // 2
PADC = 36864
TB = 8
support_low = -10.0
support_high = 10.0
discount = 0.99
penalty = 0.05


def window_of(g):
    return (WIDE * g) // 16 * 16


def ids_offset(ids):
    return lax.bitwise_and(WIDE * ids, 15)


def shift_rows(v, off, right):
    width = v.shape[1]
    for b in range(1, 4):
        n = 1 << b
        bit = lax.bitwise_and(off, n) != 0
        bit = jnp.concatenate([bit.astype(jnp.float32)] * (width // 128), axis=1) > 0.5
        v = jnp.where(bit, pltpu.roll(v, n if right else width - n, 1), v)
    return v


def head_kernel(n, feat_ref, gall_ref, scal_ref, head_ref, dfeat_ref, frow_ref, dlog_ref, loss_ref,
                fsend, frecv, part, r1, r2, tgt_s, tgt_r, down_s, dsend, drecv,
                s_f, q_f, s_1, q_1, s_2, q_2, s_t, q_t, s_l, q_l, s_c, q_c, s_d, q_d, s_r, q_r):
    me, z, x, c = place()
    role = lax.axis_index("role")
    half = n // 2
    peers = [lax.rem(me + k, n) for k in range(1, n)]
    cp = me + 1 - 2 * c
    greet([(None, {"dp": p}) for p in peers] + [(None, {"role": 1 - role})])

    def rc(src, dst, ss, rs, dev):
        return pltpu.make_async_remote_copy(src_ref=src, dst_ref=dst, send_sem=ss, recv_sem=rs, device_id=dev,
                                            device_id_type=MESH)

    for j in range(n):
        fsend[j] = feat_ref[:, j * 128:(j + 1) * 128]
    for k, p in enumerate(peers):
        rc(fsend.at[p], frecv.at[me], s_f.at[k], q_f.at[me], {"dp": p}).start()
    frecv[me] = fsend[me]
    for k, p in enumerate(peers):
        rc(fsend.at[p], frecv.at[p], s_f.at[k], q_f.at[p], {"dp": p}).wait_recv()
    feats = frecv[...].reshape(n * TB, 128)
    ids = gall_ref[...].reshape(n * TB, 128).astype(jnp.int32)

    acc = None
    for g in range(GAMES):
        lhs = jnp.where(ids == g, feats, 0.0).astype(jnp.bfloat16)
        a = window_of(g)
        p = lax.dot_general(lhs, head_ref[a:a + WIN, :], (((1,), (1,)), ((), ())),
                            preferred_element_type=jnp.float32)
        acc = p if acc is None else acc + p
    off = ids_offset(ids)
    part[...] = shift_rows(acc, off, False).reshape(half, 2, TB, LW)

    d1 = rc(part.at[:, 1 - c], r1, s_1, q_1, {"dp": cp})
    d1.start()
    d1.wait()
    pair = me // 2
    r1[...] = r1[...] + part[:, c]
    pps = [lax.rem(pair + k, half) for k in range(1, half)]
    for k, p in enumerate(pps):
        rc(r1.at[p], r2.at[pair], s_2.at[k], q_2.at[pair], {"dp": 2 * p + c}).start()
    r2[pair] = r1[pair]
    for k, p in enumerate(pps):
        rc(r1.at[p], r2.at[p], s_2.at[k], q_2.at[p], {"dp": 2 * p + c}).wait_recv()
    logits = jnp.sum(r2[...], axis=0)

    lane = lax.broadcasted_iota(jnp.int32, (TB, 128), 1)
    live = lane < ATOMS
    zi = support_low + (support_high - support_low) * lane.astype(jnp.float32) / (ATOMS - 1)
    zi = jnp.where(live, zi, 0.0)
    taken, nxt, expert, reward, done, gid = (scal_ref[k] for k in range(6))
    pieces = []
    for a in range(ACTIONS):
        v = logits if a == 0 else pltpu.roll(logits, LW - ATOMS * a, 1)
        pieces.append(v[:, :128])

    @pl.when(role == 1)
    def _():
        sel = jnp.zeros((TB, 128), jnp.float32)
        for a in range(ACTIONS):
            sel = sel + jnp.where(nxt == float(a), pieces[a], 0.0)
        sel = jnp.where(live, sel, -1e30)
        e = jnp.exp(sel - jnp.max(sel, axis=1, keepdims=True))
        e = jnp.where(live, e, 0.0)
        prob = e / jnp.sum(e, axis=1, keepdims=True)
        spacing = (support_high - support_low) / (ATOMS - 1)
        m = jnp.zeros((TB, 128), jnp.float32)
        for j in range(ATOMS):
            zj = float(np.float32(support_low) + np.float32(support_high - support_low) * np.float32(j) /
                       np.float32(ATOMS - 1))
            tz = jnp.clip(reward + discount * (1.0 - done) * zj, support_low, support_high)
            wt = jnp.maximum(0.0, 1.0 - jnp.abs(tz - zi) / spacing)
            m = m + prob[:, j:j + 1] * wt
        tgt_s[...] = jnp.where(live, m, 0.0)
        d = rc(tgt_s, tgt_r, s_t, q_t, {"role": 0})
        d.start()
        d.wait_send()
        rc(frow_ref, frow_ref, s_r.at[0], q_r.at[0], {"role": 0}).wait_recv()
        rc(dlog_ref, dlog_ref, s_r.at[1], q_r.at[1], {"role": 0}).wait_recv()
        dfeat_ref[...] = jnp.zeros_like(dfeat_ref)

    @pl.when(role == 0)
    def _():
        frow_ref[...] = feats.astype(jnp.bfloat16)
        gt = jnp.transpose(gall_ref[...].reshape(n * TB, 128))[0:TB]
        count = jnp.sum((gt == gid).astype(jnp.float32), axis=1, keepdims=True)
        weight = 1.0 / jnp.maximum(count, 1.0)
        x3 = jnp.where(live[None], jnp.stack(pieces), -1e30)
        act = lax.broadcasted_iota(jnp.int32, (ACTIONS, TB, 128), 0).astype(jnp.float32)
        hot = (act == taken[None]).astype(jnp.float32)
        mx = jnp.max(x3, axis=2, keepdims=True)
        e = jnp.where(live[None], jnp.exp(x3 - mx), 0.0)
        s = jnp.sum(e, axis=2, keepdims=True)
        logp = jnp.where(live[None], x3 - mx - jnp.log(s), 0.0)
        prob = e / s
        q = jnp.sum(prob * zi[None], axis=2, keepdims=True)
        qb = jnp.broadcast_to(q, (ACTIONS, TB, 128))
        qm = jnp.max(qb, axis=0)
        qe = jnp.exp(qb - qm[None])
        qs = jnp.sum(qe, axis=0)
        lse = qm + jnp.log(qs)
        pol = qe / qs[None]
        chosen = jnp.sum(logp * hot, axis=0)
        qt = jnp.sum(qb * hot, axis=0)
        rc(tgt_s, tgt_r, s_t, q_t, {"role": 1}).wait_recv()
        m = tgt_r[...]
        cross = -jnp.sum(m * chosen, axis=1, keepdims=True)
        row_loss = cross + penalty * expert * (lse - qt)
        msum = jnp.sum(m, axis=1, keepdims=True)
        dl = hot * (prob * msum[None] - m[None]) + (penalty * expert)[None] * (pol - hot) * prob * (zi[None] - qb)
        dl = jnp.where(live[None], dl * (weight * (1.0 / GAMES))[None], 0.0)
        flat = jnp.zeros((TB, LW), jnp.float32)
        pad = jnp.zeros((TB, LW - 128), jnp.float32)
        for a in range(ACTIONS):
            v = jnp.concatenate([dl[a], pad], axis=1)
            flat = flat + (v if a == 0 else pltpu.roll(v, ATOMS * a, 1))
        l0 = row_loss * weight
        p0 = l0.astype(jnp.bfloat16).astype(jnp.float32)
        p1 = (l0 - p0).astype(jnp.bfloat16).astype(jnp.float32)
        p2 = l0 - p0 - p1
        last = flat[:, LW - 128:]
        last = jnp.where(lane == 125, p0, jnp.where(lane == 126, p1, jnp.where(lane == 127, p2, last)))
        flat = jnp.concatenate([flat[:, :LW - 128], last], axis=1)
        down_s[...] = jnp.concatenate([flat[:, :LW // 2], flat[:, LW // 2:]], axis=0).astype(jnp.bfloat16)
        for k, p in enumerate(pps):
            rc(down_s, dlog_ref.at[me], s_l.at[k], q_l.at[me], {"dp": 2 * p + c}).start()
        rc(down_s, dlog_ref.at[me], s_c.at[0], q_c.at[me], {"dp": cp}).start()
        dlog_ref[me] = down_s[...]
        for k, p in enumerate(pps):
            o = 2 * p + c
            rc(down_s, dlog_ref.at[o], s_l.at[k], q_l.at[o], {"dp": cp}).wait_recv()
            rc(dlog_ref.at[o], dlog_ref.at[o], s_c.at[k + 1], q_c.at[o], {"dp": cp}).start()
        for p in [pair] + pps:
            o = 2 * p + 1 - c
            rc(dlog_ref.at[o], dlog_ref.at[o], s_c.at[0], q_c.at[o], {"dp": cp}).wait_recv()
        to0 = rc(frow_ref, frow_ref, s_r.at[0], q_r.at[0], {"role": 1})
        to1 = rc(dlog_ref, dlog_ref, s_r.at[1], q_r.at[1], {"role": 1})
        to0.start()
        to1.start()
        rolled = shift_rows(widen(dlog_ref[...]), off, True)
        acc = None
        for g in range(GAMES):
            lhs = jnp.where(jnp.concatenate([ids == g] * (WIN // 128), axis=1), rolled, 0.0).astype(jnp.bfloat16)
            a = window_of(g)
            p = jnp.dot(lhs, head_ref[a:a + WIN, :], preferred_element_type=jnp.float32)
            acc = p if acc is None else acc + p
        dsend[...] = acc.reshape(n, TB, 128)
        for k, p in enumerate(peers):
            rc(dsend.at[p], drecv.at[me], s_d.at[k], q_d.at[me], {"dp": p}).start()
        drecv[me] = dsend[me]
        for k, p in enumerate(peers):
            rc(dsend.at[p], drecv.at[p], s_d.at[k], q_d.at[p], {"dp": p}).wait_recv()
        for j in range(n):
            dfeat_ref[:, j * 128:(j + 1) * 128] = drecv[j]
        for k, p in enumerate(pps):
            rc(down_s, dlog_ref.at[me], s_l.at[k], q_l.at[me], {"dp": 2 * p + c}).wait_send()
        rc(down_s, dlog_ref.at[me], s_c.at[0], q_c.at[me], {"dp": cp}).wait_send()
        for k, p in enumerate(pps):
            o = 2 * p + c
            rc(dlog_ref.at[o], dlog_ref.at[o], s_c.at[k + 1], q_c.at[o], {"dp": cp}).wait_send()
        for k, p in enumerate(peers):
            rc(dsend.at[p], drecv.at[me], s_d.at[k], q_d.at[me], {"dp": p}).wait_send()
        to0.wait_send()
        to1.wait_send()

    for k, p in enumerate(peers):
        rc(fsend.at[p], frecv.at[me], s_f.at[k], q_f.at[me], {"dp": p}).wait_send()
    for k, p in enumerate(pps):
        rc(r1.at[p], r2.at[pair], s_2.at[k], q_2.at[pair], {"dp": 2 * p + c}).wait_send()
    tail = dlog_ref[:, :, 384:512].astype(jnp.float32)[:, TB:2 * TB].reshape(n * TB, 128)
    lanes = lax.broadcasted_iota(jnp.int32, (n * TB, 128), 1)
    total = jnp.sum(jnp.where(lanes >= 125, tail, 0.0))
    loss_ref[...] = jnp.full((TB, 128), total, jnp.float32)


def widen(dl):
    n = dl.shape[0]
    v = dl.astype(jnp.float32)
    v = jnp.concatenate([v[:, 0:TB], v[:, TB:2 * TB]], axis=2).reshape(n * TB, LW)
    lanes = lax.broadcasted_iota(jnp.int32, (n * TB, 128), 1)
    last = jnp.where(lanes < WIDE - LW + 128, v[:, LW - 128:], 0.0)
    return jnp.concatenate([v[:, :LW - 128], last], axis=1)


def head_stage(feat, games_all, scal, head_low, n, cid):
    f32, b16 = jnp.float32, jnp.bfloat16
    S = jax.ShapeDtypeStruct
    V, dma = pltpu.VMEM, pltpu.SemaphoreType.DMA
    vs = pl.BlockSpec(memory_space=pltpu.VMEM)
    h = n // 2
    return pl.pallas_call(
        functools.partial(head_kernel, n),
        out_shape=(S((TB, D), f32), S((n * TB, 128), b16), S((n, 16, 512), b16), S((TB, 128), f32)),
        in_specs=[vs] * 4,
        out_specs=(vs,) * 4,
        scratch_shapes=[V((n, TB, 128), f32), V((n, TB, 128), f32), V((h, 2, TB, LW), f32), V((h, TB, LW), f32),
                        V((h, TB, LW), f32), V((TB, 128), f32), V((TB, 128), f32), V((16, 512), b16),
                        V((n, TB, 128), f32), V((n, TB, 128), f32),
                        dma((n,)), dma((n,)), dma, dma, dma((h,)), dma((h,)), dma, dma, dma((h,)), dma((n,)),
                        dma((h,)), dma((n,)), dma((n,)), dma((n,)), dma((2,)), dma((2,))],
        compiler_params=pltpu.CompilerParams(collective_id=cid, has_side_effects=True,
                                             vmem_limit_bytes=56 * 1024 * 1024),
        name="head_stage",
    )(feat, games_all, scal, head_low)


CR = 4096


def cast_kernel(role_ref, h_ref, a_ref, o_ref):
    rows = pl.program_id(0) * CR + lax.broadcasted_iota(jnp.int32, (256, 128), 0)

    def fill(ref):
        def one(r, c):
            rs = pl.ds(pl.multiple_of(r * 256, 256), 256)
            o_ref[rs, :] = jnp.where(rows + r * 256 < COLS, ref[rs, :], 0.0).astype(jnp.bfloat16)
            return c
        lax.fori_loop(0, CR // 256, one, 0)
    pl.when(role_ref[0] == 0)(lambda: fill(h_ref))
    pl.when(role_ref[0] != 0)(lambda: fill(a_ref))


def head_cast(role, head, avg):
    lanes = head.shape[1]
    return pl.pallas_call(
        cast_kernel,
        grid_spec=pltpu.PrefetchScalarGridSpec(
            num_scalar_prefetch=1, grid=(PADC // CR,),
            in_specs=[pl.BlockSpec((CR, lanes), lambda j, r: (j * (1 - r[0]), 0)),
                      pl.BlockSpec((CR, lanes), lambda j, r: (j * r[0], 0))],
            out_specs=pl.BlockSpec((CR, lanes), lambda j, r: (j, 0))),
        out_shape=jax.ShapeDtypeStruct((PADC, lanes), jnp.bfloat16),
        compiler_params=pltpu.CompilerParams(vmem_limit_bytes=32 * 1024 * 1024),
        name="head_cast",
    )(role, head, avg)


UR = 2048
NB = -(-HALF // UR)
LASTR = HALF - (NB - 1) * UR


def games_of_block(k):
    lo = [window_of(i) for i in range(GAMES // 2)]
    return [i for i in range(GAMES // 2) if k * UR <= lo[i] < (k + 1) * UR]


def update_kernel(role_ref, gall_ref, frow_ref, dlog_ref, h_hbm, m_hbm, a_hbm, ow, om, oa, oc, gr, dlt, buf, sems):
    j = pl.program_id(0)
    role = role_ref[0]
    hbm = (h_hbm, m_hbm, a_hbm)

    def copies(k, slot, rows, go):
        for t in range(3):
            c = pltpu.make_async_copy(hbm[t].at[pl.ds(pl.multiple_of(role * HALF + k * UR, 8), rows)],
                                      buf.at[slot, t, pl.ds(0, rows)], sems.at[slot, t])
            c.start() if go else c.wait()

    def each(k, slot, go):
        pl.when(k < NB - 1)(lambda: copies(k, slot, UR, go))
        pl.when(k == NB - 1)(lambda: copies(k, slot, LASTR, go))

    slot = lax.rem(j, 2)

    @pl.when(j == 0)
    def _():
        each(j, slot, True)
    each(j + 1, 1 - slot, True)

    @pl.when(j == 0)
    def _():
        gr[...] = jnp.zeros_like(gr)
        ids = gall_ref[...].reshape(-1, 128).astype(jnp.int32) - role * (GAMES // 2)
        v = shift_rows(widen(dlog_ref[...]), ids_offset(ids), True)
        for k in range(WIN // 128):
            dlt[k * 128:(k + 1) * 128, :] = jnp.transpose(v[:, k * 128:(k + 1) * 128]).astype(jnp.bfloat16)
    for k in range(NB):
        todo = games_of_block(k)
        if todo:
            @pl.when(j == k)
            def _(todo=todo):
                own = gall_ref[...].reshape(-1, 128).astype(jnp.int32) - role * (GAMES // 2)
                for i in todo:
                    rhs = jnp.where(own == i, frow_ref[...].astype(jnp.float32), 0.0).astype(jnp.bfloat16)
                    a = window_of(i)
                    gr[a:a + WIN, :] = gr[a:a + WIN, :] + jnp.dot(dlt[...], rhs, preferred_element_type=jnp.float32)
    each(j, slot, False)

    def one(r, c):
        rs = pl.ds(pl.multiple_of(r * 128, 128), 128)
        g = gr[pl.ds(pl.multiple_of(j * UR + r * 128, 128), 128), :]
        m = 0.5 * buf[slot, 1, rs, :] + g
        w = buf[slot, 0, rs, :] - 4.0 * (g + 0.5 * m)
        om[rs, :] = m
        ow[rs, :] = w
        oa[rs, :] = 0.5 * buf[slot, 2, rs, :] + 0.5 * w
        oc[rs, :] = w.astype(jnp.bfloat16)
        return c
    lax.fori_loop(0, UR // 128, one, 0)


def head_update(role, games_all, frow, dlog, head, moment, avg):
    lanes = head.shape[1]
    n = games_all.shape[0]
    f32 = jnp.float32
    S = jax.ShapeDtypeStruct
    out = pl.BlockSpec((UR, lanes), lambda j, r: (j, 0))

    def whole(*s):
        return pl.BlockSpec(s, lambda j, r: (0,) * len(s))
    hb = pl.BlockSpec(memory_space=pl.ANY)
    return pl.pallas_call(
        update_kernel,
        grid_spec=pltpu.PrefetchScalarGridSpec(
            num_scalar_prefetch=1, grid=(NB,),
            in_specs=[whole(n, TB, 128), whole(n * TB, 128), whole(n, 16, 512), hb, hb, hb],
            out_specs=(out,) * 4,
            scratch_shapes=[pltpu.VMEM((NB * UR + WIN, lanes), f32), pltpu.VMEM((WIN, n * TB), jnp.bfloat16),
                            pltpu.VMEM((2, 3, UR, lanes), f32), pltpu.SemaphoreType.DMA((2, 3))]),
        out_shape=(S((HALF, lanes), f32),) * 3 + (S((HALF, lanes), jnp.bfloat16),),
        compiler_params=pltpu.CompilerParams(vmem_limit_bytes=56 * 1024 * 1024),
        name="head_update",
    )(role, games_all, frow, dlog, head, moment, avg)


def fast_device(
    frames,
    game_ids,
    taken_actions,
    next_actions,
    expert_flags,
    rewards,
    done_flags,
    weight_in,
    weight_mid,
    weight_out,
    norm_gains,
    head_table,
    moment_in,
    moment_mid,
    moment_out,
    moment_gains,
    moment_head,
    average_in,
    average_mid,
    average_out,
    average_gains,
    average_head,
):
    n = lax.axis_size("dp")
    role_index = lax.axis_index("role")
    online = role_index == 0
    role = jnp.reshape(role_index, (1,)).astype(jnp.int32)
    use_in = jnp.where(online, weight_in, average_in)[0].astype(jnp.bfloat16)
    use_mid = jnp.where(online, weight_mid, average_mid)[0].astype(jnp.bfloat16)
    use_out = jnp.where(online, weight_out, average_out)[0].astype(jnp.bfloat16)
    use_gains = jnp.where(online, norm_gains, average_gains).astype(jnp.bfloat16)
    gains3 = use_gains.astype(jnp.float32).reshape(-1, 128)

    def lanes(v):
        return jnp.broadcast_to(v.astype(jnp.float32)[:, None], (TB, 128))

    ids = lanes(game_ids)
    scal = jnp.stack(
        [lanes(taken_actions), lanes(next_actions), lanes(expert_flags), lanes(rewards), lanes(done_flags), ids]
    )
    head_low = head_cast(role, head_table.T, average_head.T)
    all_in, all_mid, all_out, all_gains, all_ids = gather([use_in, use_mid, use_out, gains3, ids], n, 1)
    w_mid = all_mid.reshape(9 * MID, MID)
    w_out = all_out.reshape(MID, D)
    gains = all_gains.reshape(1, 4 * MID + 2 * D)
    saved = forward(jnp.transpose(frames[0], (1, 0, 2)), all_in.reshape(D, MID), w_mid, w_out, gains)
    dfeat, feat_rows, dlog, loss = head_stage(saved[-1], all_ids, scal, head_low, n, 2)
    g_in, g_mid, g_out, g_gains = backward(dfeat, saved, w_mid, w_out, gains)
    grad_out, grad_mid, grad_in, grad_gains = scatter(
        [
            g_out.reshape(n, MID // n, D),
            g_mid.reshape(n, 9 * MID // n, MID),
            g_in.reshape(n, D // n, MID),
            g_gains.reshape(n, -1, 128),
        ],
        n,
        3,
    )
    head_w, head_m, head_a, head_c = head_update(
        role, all_ids, feat_rows, dlog, head_table.T, moment_head.T, average_head.T
    )

    def own(v):
        return own_half(v, role_index)

    in_w, in_m, in_a, in_c = renew(own(weight_in), grad_in[None], own(moment_in), own(average_in), learn_rate)
    mid_w, mid_m, mid_a, mid_c = renew(
        own(weight_mid), grad_mid[None], own(moment_mid), own(average_mid), learn_rate
    )
    out_w, out_m, out_a, out_c = renew(
        own(weight_out), grad_out[None], own(moment_out), own(average_out), learn_rate
    )
    gain_w, gain_m, gain_a, gain_c = renew(
        norm_gains, grad_gains.reshape(norm_gains.shape), moment_gains, average_gains, gain_rate
    )
    return (
        loss[0, 0],
        in_w,
        grad_in[None],
        in_a,
        in_c,
        mid_w,
        mid_m,
        mid_a,
        mid_c,
        out_w,
        out_m,
        out_a,
        out_c,
        gain_w,
        gain_m,
        gain_a,
        gain_c,
        head_w.T,
        head_m.T,
        head_a.T,
        head_c.T,
    )


def solution(mesh):
    return jax.shard_map(
        fast_device if mesh.shape["dp"] == 16 else on_device,
        mesh=mesh,
        in_specs=(
            P("role", "dp", None, None),
            P("dp"),
            P("dp"),
            P("dp"),
            P("dp"),
            P("dp"),
            P("dp"),
            P(None, "dp", None),
            P(None, "dp", None),
            P(None, "dp", None),
            P(None, "dp"),
            P("dp", None),
            P(None, "dp", None),
            P(None, "dp", None),
            P(None, "dp", None),
            P(None, "dp"),
            P("dp", None),
            P(None, "dp", None),
            P(None, "dp", None),
            P(None, "dp", None),
            P(None, "dp"),
            P("dp", None),
        ),
        out_specs=(
            P(),
            P(None, "dp", "role"),
            P(None, "dp", "role"),
            P(None, "dp", "role"),
            P(None, "dp", "role"),
            P(None, "dp", "role"),
            P(None, "dp", "role"),
            P(None, "dp", "role"),
            P(None, "dp", "role"),
            P(None, "dp", "role"),
            P(None, "dp", "role"),
            P(None, "dp", "role"),
            P(None, "dp", "role"),
            P(None, "dp"),
            P(None, "dp"),
            P(None, "dp"),
            P(None, "dp"),
            P("dp", "role"),
            P("dp", "role"),
            P("dp", "role"),
            P("dp", "role"),
        ),
        check_vma=False,
    )
```

```python
import functools

import jax
import jax.numpy as jnp
import numpy as np
from jax import lax
from jax.experimental import pallas as pl
from jax.experimental.pallas import tpu as pltpu
from jax.sharding import PartitionSpec as P

D = 2048
MID = 512
GAMES = 40
ACTIONS = 18
ATOMS = 51
GROUPS = 32
SIDE = 11
LAYERS = 1


support_low = -10.0
support_high = 10.0
discount = 0.99
penalty = 0.05
momentum_decay = 0.5
average_decay = 0.5
learn_rate = 4.0
gain_rate = 40.0
epsilon = 1e-05
HIGHEST = lax.Precision.HIGHEST


def passed_along(block, axis, distance):
    devices = range(lax.axis_size(axis))
    route = [(i - distance, i) for i in devices if i - distance in devices]
    return lax.ppermute(block, axis, route)


def split_gains(gains):
    return (
        gains[:MID],
        gains[MID : 2 * MID],
        gains[2 * MID : 3 * MID],
        gains[3 * MID : 4 * MID],
        gains[4 * MID : 4 * MID + D],
        gains[4 * MID + D :],
    )


def group_norm(values, gain, shift):
    rows, pixels, width = values.shape
    grouped = values.reshape(rows, pixels, GROUPS, width // GROUPS)
    center = grouped - jnp.mean(grouped, axis=(1, 3), keepdims=True)
    spread = jnp.mean(center * center, axis=(1, 3), keepdims=True)
    normed = (center * lax.rsqrt(spread + epsilon)).reshape(values.shape)
    return normed * gain + shift


def patches_of(acts):
    rows, pixels, width = acts.shape
    grid = acts.reshape(rows, SIDE, SIDE, width)
    padded = jnp.pad(grid, ((0, 0), (1, 1), (1, 1), (0, 0)))
    pieces = [
        padded[:, down : down + SIDE, right : right + SIDE, :]
        for down in range(3)
        for right in range(3)
    ]
    return jnp.concatenate(pieces, axis=-1).reshape(rows, pixels, 9 * width)


def transition_loss(logits, target_dist, action_hot, expert, support):
    log_prob = jax.nn.log_softmax(logits, axis=-1)
    values = jnp.sum(jnp.exp(log_prob) * support, axis=-1)
    spread_sum = jax.nn.logsumexp(values, axis=-1)
    chosen_log = jnp.sum(log_prob * action_hot[:, :, None], axis=1)
    cross = -jnp.sum(target_dist * chosen_log, axis=-1)
    regular = spread_sum - jnp.sum(values * action_hot, axis=-1)
    return cross + penalty * expert * regular


def project_target(next_prob, rewards, done_f, support):
    moved = jnp.clip(
        rewards[:, None] + discount * (1.0 - done_f)[:, None] * support[None, :],
        support_low,
        support_high,
    )
    spacing = (support_high - support_low) / (ATOMS - 1)
    weight = jnp.maximum(0.0, 1.0 - jnp.abs(moved[:, :, None] - support[None, None, :]) / spacing)
    return jnp.sum(next_prob[:, :, None] * weight, axis=1)


def renew(weight, grad, moment, average, rate):
    new_moment = momentum_decay * moment + grad
    new_weight = weight - rate * (grad + momentum_decay * new_moment)
    new_average = average_decay * average + (1.0 - average_decay) * new_weight
    return (new_weight, new_moment, new_average, new_weight.astype(jnp.bfloat16))


def lower_half(values):
    return values[..., : values.shape[-1] // 2]


def upper_half(values):
    return values[..., values.shape[-1] // 2 :]


def own_half(values, role_index):
    half = values.shape[-1] // 2
    return lax.dynamic_slice_in_dim(values, role_index * half, half, values.ndim - 1)


def norm_act(hidden, gain, shift):
    return jax.nn.gelu(group_norm(hidden, gain, shift))


def outer_act(hidden, gain, shift, stream):
    return jax.nn.gelu(stream + group_norm(hidden, gain, shift))


def block_forward(stream, weights):
    w_in, w_mid, w_out, gains = weights
    gain_one, shift_one, gain_two, shift_two, gain_three, shift_three = split_gains(gains)
    stream_low = stream.astype(jnp.bfloat16)
    hidden_in = jnp.einsum("bpc,cm->bpm", stream_low, w_in, preferred_element_type=jnp.float32)
    act_in = norm_act(hidden_in, gain_one, shift_one).astype(jnp.bfloat16)
    hidden_mid = jnp.einsum(
        "bpc,cm->bpm", patches_of(act_in), w_mid, preferred_element_type=jnp.float32
    )
    act_mid = norm_act(hidden_mid, gain_two, shift_two).astype(jnp.bfloat16)
    hidden_out = jnp.einsum("bpc,cm->bpm", act_mid, w_out, preferred_element_type=jnp.float32)
    result = outer_act(hidden_out, gain_three, shift_three, stream)
    return (result, (stream, stream_low, hidden_in, act_in, hidden_mid, act_mid, hidden_out))


def block_backward(grad_result, weights, kept, settle):
    w_in, w_mid, w_out, gains = weights
    stream, stream_low, hidden_in, act_in, hidden_mid, act_mid, hidden_out = kept
    gain_one, shift_one, gain_two, shift_two, gain_three, shift_three = split_gains(gains)
    _, back_three = jax.vjp(outer_act, hidden_out, gain_three, shift_three, stream)
    d_three, dg_three, db_three, d_resid = back_three(grad_result)
    d_three = d_three.astype(jnp.bfloat16)
    grad_out = settle(
        jnp.einsum("bpm,bpc->mc", act_mid, d_three, preferred_element_type=jnp.float32)
    )
    d_act_mid = jnp.einsum("bpc,mc->bpm", d_three, w_out, preferred_element_type=jnp.float32)
    _, back_two = jax.vjp(norm_act, hidden_mid, gain_two, shift_two)
    d_two, dg_two, db_two = back_two(d_act_mid)
    d_two = d_two.astype(jnp.bfloat16)
    grad_mid = settle(
        jnp.einsum("bpk,bpm->km", patches_of(act_in), d_two, preferred_element_type=jnp.float32)
    )
    d_cols = jnp.einsum("bpm,km->bpk", d_two, w_mid, preferred_element_type=jnp.float32)
    _, back_cols = jax.vjp(patches_of, act_in.astype(jnp.float32))
    (d_act_in,) = back_cols(d_cols)
    _, back_one = jax.vjp(norm_act, hidden_in, gain_one, shift_one)
    d_one, dg_one, db_one = back_one(d_act_in)
    d_one = d_one.astype(jnp.bfloat16)
    grad_in = jnp.einsum("bpc,bpm->cm", stream_low, d_one, preferred_element_type=jnp.float32)
    d_stream = d_resid + jnp.einsum("bpm,cm->bpc", d_one, w_in, preferred_element_type=jnp.float32)
    grad_gains = jnp.concatenate([dg_one, db_one, dg_two, db_two, dg_three, db_three])
    grad_in, grad_gains = settle((grad_in, grad_gains))
    return (d_stream, (grad_in, grad_mid, grad_out, grad_gains))


def on_device(
    frames,
    game_ids,
    taken_actions,
    next_actions,
    expert_flags,
    rewards,
    done_flags,
    weight_in,
    weight_mid,
    weight_out,
    norm_gains,
    head_table,
    moment_in,
    moment_mid,
    moment_out,
    moment_gains,
    moment_head,
    average_in,
    average_mid,
    average_out,
    average_gains,
    average_head,
):
    role_index = lax.axis_index("role")
    online = role_index == 0
    use_in = jnp.where(online, weight_in, average_in).astype(jnp.bfloat16)
    use_mid = jnp.where(online, weight_mid, average_mid).astype(jnp.bfloat16)
    use_out = jnp.where(online, weight_out, average_out).astype(jnp.bfloat16)
    use_gains = jnp.where(online, norm_gains, average_gains).astype(jnp.bfloat16)
    use_head = jnp.where(online, head_table, average_head).astype(jnp.bfloat16)
    support = support_low + (support_high - support_low) * jnp.arange(ATOMS, dtype=jnp.float32) / (
        ATOMS - 1
    )
    own_hot = (game_ids[:, None] == lax.broadcasted_iota(jnp.int32, (1, GAMES), 1)).astype(
        jnp.float32
    )
    counts = jnp.sum(own_hot, axis=0)
    stream = frames[0].astype(jnp.float32)
    layer = 0
    pieces = (
        lax.all_gather(use_in[layer], "dp", axis=0, tiled=True),
        lax.all_gather(use_mid[layer], "dp", axis=0, tiled=True),
        lax.all_gather(use_out[layer], "dp", axis=0, tiled=True),
        lax.all_gather(use_gains[layer], "dp", axis=0, tiled=True),
    )
    weights = (pieces[0], pieces[1], pieces[2], pieces[3].astype(jnp.float32))
    stream, saved = block_forward(stream, weights)
    gathered = [weights]
    kept = [saved]
    trans = stream.shape[0]
    pixels = stream.shape[1]
    wide_k = ACTIONS * ATOMS
    head_rows = head_table.shape[0]
    feat_low = jnp.mean(stream, axis=1).astype(jnp.bfloat16)
    feat_all, game_all = (
        lax.all_gather(feat_low, "dp", axis=0, tiled=True),
        lax.all_gather(game_ids.astype(jnp.bfloat16)[:, None], "dp", axis=0, tiled=True),
    )
    game_iota = lax.broadcasted_iota(jnp.int32, (1, GAMES), 1).astype(jnp.float32)
    all_hot = (game_all.astype(jnp.float32) == game_iota).astype(jnp.bfloat16)
    feat_rows = lax.dynamic_slice_in_dim(feat_all, lax.axis_index("dp") * head_rows, head_rows, 1)
    head_low = use_head.reshape(head_rows * GAMES, wide_k)

    def widen(count):
        spread_rows = (feat_rows[:, :, None] * all_hot[:, None, :]).reshape(
            count, head_rows * GAMES
        )
        return (spread_rows, all_hot)

    spread_rows, hot_piece = widen(trans * lax.axis_size("dp"))
    flat_logits = lax.psum_scatter(
        jnp.dot(spread_rows, head_low, preferred_element_type=jnp.float32),
        "dp",
        scatter_dimension=0,
        tiled=True,
    )
    logits = flat_logits.reshape(trans, ACTIONS, ATOMS)
    next_hot = (next_actions[:, None] == lax.broadcasted_iota(jnp.int32, (1, ACTIONS), 1)).astype(
        jnp.float32
    )
    next_prob = jax.nn.softmax(jnp.sum(logits * next_hot[:, :, None], axis=1), axis=-1)
    projected = project_target(next_prob, rewards, done_flags.astype(jnp.float32), support)
    target_dist = passed_along(projected, "role", -1)
    action_hot = (
        taken_actions[:, None] == lax.broadcasted_iota(jnp.int32, (1, ACTIONS), 1)
    ).astype(jnp.float32)
    expert = expert_flags.astype(jnp.float32)

    def local_loss(values):
        return transition_loss(values, target_dist, action_hot, expert, support)

    row_loss, loss_back = jax.vjp(local_loss, logits)
    sums = jnp.dot(row_loss, own_hot, precision=HIGHEST)
    total_counts, total_sums = lax.psum((counts, sums), "dp")
    floor_counts = jnp.maximum(total_counts, 1.0)
    loss_total = jnp.sum(total_sums / floor_counts)
    row_weight = jnp.dot(own_hot, 1.0 / (GAMES * floor_counts), precision=HIGHEST)
    (d_logits,) = loss_back(row_weight)
    d_low = d_logits.reshape(trans, wide_k).astype(jnp.bfloat16)
    piece = lax.all_gather(d_low, "dp", axis=0, tiled=True)
    count = piece.shape[0]
    spread_rows, hot_piece = widen(count)
    grad_head = lax.dot_general(
        spread_rows, piece, (((0,), (0,)), ((), ())), preferred_element_type=jnp.float32
    )
    back_wide = jnp.dot(piece, head_low.T, preferred_element_type=jnp.float32)
    back_rows = jnp.sum(
        back_wide.reshape(count, head_rows, GAMES) * hot_piece[:, None, :].astype(jnp.float32),
        axis=2,
    )
    grad_rows = back_rows
    grad_head, grad_rows = (grad_head, grad_rows)
    feat_grad = lax.all_to_all(
        grad_rows.astype(jnp.bfloat16), "dp", split_axis=0, concat_axis=1, tiled=True
    ).astype(grad_rows.dtype)
    d_stream = jnp.broadcast_to(feat_grad[:, None, :] / pixels, stream.shape)

    def settle(values):
        return values

    layer_grads = [None] * LAYERS
    for layer in reversed(range(LAYERS)):
        d_stream, block_grad = block_backward(d_stream, gathered[layer], kept[layer], settle)
        layer_grads[layer] = block_grad
    stacked = tuple((jnp.stack([layer_grads[0][kind]]) for kind in range(4)))
    reduced = lax.psum_scatter(stacked, "dp", scatter_dimension=1, tiled=True)
    head_grad = grad_head.reshape(head_rows, GAMES * wide_k)
    sent = (
        passed_along(upper_half(reduced[0]).astype(jnp.bfloat16), "role", 1).astype(jnp.float32),
        passed_along(upper_half(reduced[1]).astype(jnp.bfloat16), "role", 1).astype(jnp.float32),
        passed_along(upper_half(reduced[2]).astype(jnp.bfloat16), "role", 1).astype(jnp.float32),
        passed_along(reduced[3].astype(jnp.bfloat16), "role", 1).astype(jnp.float32),
        passed_along(upper_half(head_grad).astype(jnp.bfloat16), "role", 1).astype(jnp.float32),
        passed_along(loss_total.astype(jnp.bfloat16), "role", 1).astype(loss_total.dtype),
    )
    grad_in = jnp.where(online, lower_half(reduced[0]), sent[0])
    grad_mid = jnp.where(online, lower_half(reduced[1]), sent[1])
    grad_out = jnp.where(online, lower_half(reduced[2]), sent[2])
    grad_gains = jnp.where(online, reduced[3], sent[3])
    grad_table = jnp.where(online, lower_half(head_grad), sent[4])
    loss_out = jnp.where(online, loss_total, sent[5])
    in_w, in_m, in_a, in_c = renew(
        own_half(weight_in, role_index),
        grad_in,
        own_half(moment_in, role_index),
        own_half(average_in, role_index),
        learn_rate,
    )
    mid_w, mid_m, mid_a, mid_c = renew(
        own_half(weight_mid, role_index),
        grad_mid,
        own_half(moment_mid, role_index),
        own_half(average_mid, role_index),
        learn_rate,
    )
    out_w, out_m, out_a, out_c = renew(
        own_half(weight_out, role_index),
        grad_out,
        own_half(moment_out, role_index),
        own_half(average_out, role_index),
        learn_rate,
    )
    gain_w, gain_m, gain_a, gain_c = renew(
        norm_gains, grad_gains, moment_gains, average_gains, gain_rate
    )
    head_w, head_m, head_a, head_c = renew(
        own_half(head_table, role_index),
        grad_table,
        own_half(moment_head, role_index),
        own_half(average_head, role_index),
        learn_rate,
    )
    return (
        loss_out,
        in_w,
        grad_in,
        in_a,
        in_c,
        mid_w,
        mid_m,
        mid_a,
        mid_c,
        out_w,
        out_m,
        out_a,
        out_c,
        gain_w,
        gain_m,
        gain_a,
        gain_c,
        head_w,
        head_m,
        head_a,
        head_c,
    )


MESH = pl.DeviceIdType.MESH


def any_spec():
    return pl.BlockSpec(memory_space=pl.ANY)


def greet(peers):
    barrier = pltpu.get_barrier_semaphore()
    for cond, dev in peers:
        def go(dev=dev):
            pl.semaphore_signal(barrier, inc=1, device_id=dev, device_id_type=MESH)
        go() if cond is None else pl.when(cond)(go)
    count = sum(1 for cond, _ in peers if cond is None)
    for cond, _ in peers:
        if cond is not None:
            count = count + cond.astype(jnp.int32)
    pl.semaphore_wait(barrier, count)


def place():
    me = lax.axis_index("dp")
    core = lax.rem(me, 2)
    x = lax.rem(me // 2, 2)
    z = me // 4
    return me, z, x, core


D = 2048
MID = 512
GROUPS = 32
SIDE = 11
PIX = 121
TB = 8
PITCH = 12
RB = PITCH * TB
VR = SIDE * TB
ROWS = SIDE * RB
PAD = 16 * TB
EROWS = 164 * TB
BLK = 352
CH = 512
epsilon = 1e-05
GK = 0.7978845608028654
GC = 0.044715
OFFS = [(i - 1) * PITCH + (j - 1) for i in range(3) for j in range(3)]


def group_sum(v, gs):
    width = v.shape[1]
    n = width // 128
    a = lax.broadcasted_iota(jnp.int32, (128, 128), 0) // gs
    b = lax.broadcasted_iota(jnp.int32, (128, 128), 1) // gs
    m = (a == b).astype(jnp.float32)
    st = jnp.concatenate([v[:, k * 128:(k + 1) * 128] for k in range(n)], axis=0)
    r = jnp.dot(st, m, precision=lax.Precision.HIGHEST, preferred_element_type=jnp.float32)
    return jnp.concatenate([r[k * 8:(k + 1) * 8] for k in range(n)], axis=1)


def fold(v):
    rows, w = v.shape
    return jnp.sum(v.reshape(rows // TB, TB, w), axis=0)


def moments(h_ref, lo, gs):
    def one(r, acc):
        return acc + fold(h_ref[pl.ds(pl.multiple_of(r * RB, RB), VR), lo:lo + CH])
    s = lax.fori_loop(0, SIDE, one, jnp.zeros((TB, CH), jnp.float32))
    mean = group_sum(s, gs) / float(PIX * gs)

    def two(r, acc):
        h = h_ref[pl.ds(pl.multiple_of(r * RB, RB), VR), lo:lo + CH].reshape(SIDE, TB, CH) - mean[None]
        return acc + jnp.sum(h * h, axis=0)
    q = lax.fori_loop(0, SIDE, two, jnp.zeros((TB, CH), jnp.float32))
    var = group_sum(q, gs) / float(PIX * gs)
    return mean, lax.rsqrt(var + epsilon)


def gelu(u):
    return 0.5 * u * (1.0 + jnp.tanh(GK * (u + GC * (u * u * u))))


def dgelu(u):
    uu = u * u
    t = jnp.tanh(GK * u * (1.0 + GC * uu))
    return 0.5 * (1.0 + t) + 0.5 * u * (1.0 - t * t) * (GK + (3.0 * GK * GC) * uu)


def shifted(e_ref, o_ref, s, row, n):
    ref, base = (e_ref, 16 + s) if s % 2 == 0 else (o_ref, 17 + s)
    return ref[pl.ds(pl.multiple_of(row + base * TB, 16), n), :]


def put_shifted(e_ref, o_ref, r, v):
    z = jnp.zeros((TB, v.shape[1]), jnp.float32)
    at = pl.ds(pl.multiple_of(PAD + r * RB, 16), RB)
    e_ref[at, :] = jnp.concatenate([v, z], axis=0).astype(jnp.bfloat16)
    o_ref[at, :] = jnp.concatenate([z, v], axis=0).astype(jnp.bfloat16)


def clear_margins(e_ref, o_ref):
    z = jnp.zeros((PAD, MID), jnp.bfloat16)
    for ref in (e_ref, o_ref):
        ref[0:PAD, :] = z
        ref[PAD + ROWS:EROWS, :] = z


def row_at(r):
    return pl.ds(pl.multiple_of(r * RB, RB), VR)


def rows_full(r):
    return pl.ds(pl.multiple_of(r * RB, RB), RB)


def norm_back(h_ref, lo, dy_ref, mean, rstd, gain, gs, s1, s2, emit):
    n = 1.0 / float(PIX * gs)
    m1 = group_sum(gain * s1, gs) * n
    m2 = group_sum(gain * s2, gs) * n
    ca = rstd * gain
    cc = -rstd * rstd * m2
    cb = -rstd * m1 - mean * cc

    def one(r, c):
        h = h_ref[row_at(r), lo:lo + CH].reshape(SIDE, TB, CH)
        dy = dy_ref[row_at(r), :].reshape(SIDE, TB, CH)
        emit(r, (ca[None] * dy + cc[None] * h + cb[None]).reshape(VR, CH))
        return c
    lax.fori_loop(0, SIDE, one, 0)


D = 2048
GAMES = 40
ACTIONS = 18
ATOMS = 51
WIDE = ACTIONS * ATOMS
LW = 1024
WIN = 1024
COLS = GAMES * WIDE
HALF = COLS // 2
PADC = 36864
TB = 8
support_low = -10.0
support_high = 10.0
discount = 0.99
penalty = 0.05


def window_of(g):
    return (WIDE * g) // 16 * 16


def ids_offset(ids):
    return lax.bitwise_and(WIDE * ids, 15)


def shift_rows(v, off, right):
    width = v.shape[1]
    for b in range(1, 4):
        n = 1 << b
        bit = lax.bitwise_and(off, n) != 0
        bit = jnp.concatenate([bit.astype(jnp.float32)] * (width // 128), axis=1) > 0.5
        v = jnp.where(bit, pltpu.roll(v, n if right else width - n, 1), v)
    return v


def widen(dl):
    n = dl.shape[0]
    v = dl.astype(jnp.float32)
    v = jnp.concatenate([v[:, 0:TB], v[:, TB:2 * TB]], axis=2).reshape(n * TB, LW)
    lanes = lax.broadcasted_iota(jnp.int32, (n * TB, 128), 1)
    last = jnp.where(lanes < WIDE - LW + 128, v[:, LW - 128:], 0.0)
    return jnp.concatenate([v[:, :LW - 128], last], axis=1)


W_IN, W_MID, W_OUT, MISC = 0, 1, 2, 3
HC = 2048
NHC = -(-COLS // HC)
T0 = (((0,), (0,)), ((), ()))
T1 = (((1,), (1,)), ((), ()))


def rc(src, dst, ss, rs, dev):
    return pltpu.make_async_remote_copy(src_ref=src, dst_ref=dst, send_sem=ss, recv_sem=rs, device_id=dev,
                                        device_id_type=MESH)


def when(cond, do):
    if cond is None:
        do()
    else:
        pl.when(cond)(do)


class Gather:
    def __init__(self, nz, own, full, rows, own_sem, send, recv):
        self.nz, self.own_refs, self.full, self.rows = nz, own, full, rows
        self.own_sem, self.send, self.recv = own_sem, send, recv
        self.me, self.z, self.x, self.c = place()
        me, x, c = self.me, self.x, self.c
        self.up, self.down = {"dp": me + 4}, {"dp": me - 4}
        self.xp, self.cp = {"dp": me + 2 - 4 * x}, {"dp": me + 1 - 2 * c}
        self.has_up, self.has_down = self.z < nz - 1, self.z > 0
        self.started = []

    def slot(self, a, i):
        n = self.rows[a]
        return self.full[a].at[i] if n is None else self.full[a].at[pl.ds(pl.multiple_of(i * n, 16), n)]

    def put(self, cond, a, src, i, dev, k):
        d = rc(src, self.slot(a, i), self.send.at[a, k], self.recv.at[a, i], dev)
        when(cond, d.start)
        self.started.append((cond, d))

    def take(self, cond, a, i):
        d = rc(self.slot(a, i), self.slot(a, i), self.send.at[a, 0], self.recv.at[a, i], self.cp)
        when(cond, d.wait_recv)

    def begin(self, a):
        src = self.own_refs[a]
        self.put(self.has_up, a, src, self.me, self.up, 0)
        self.put(self.has_down, a, src, self.me, self.down, 1)
        self.put(None, a, src, self.me, self.xp, 2)
        self.put(None, a, src, self.me, self.cp, 3)
        pltpu.make_async_copy(src, self.slot(a, self.me), self.own_sem.at[a]).start()

    def along_z(self, a, d):
        k = 4 + (d - 1) * 6
        for up in (True, False):
            s = self.me - 4 * d if up else self.me + 4 * d
            ok = self.z - d >= 0 if up else self.z + d < self.nz
            more = jnp.logical_and(ok, self.has_up if up else self.has_down)
            m = k if up else k + 3
            self.take(ok, a, s)
            self.put(more, a, self.slot(a, s), s, self.up if up else self.down, m)
            self.put(ok, a, self.slot(a, s), s, self.xp, m + 1)
            self.put(ok, a, self.slot(a, s), s, self.cp, m + 2)

    def at_distance(self, d):
        for up in ((True,) if d == 0 else (False, True)):
            zz = self.z + d if up else self.z - d
            yield zz, (None if d == 0 else zz < self.nz if up else zz >= 0), up

    def along_x(self, a, d):
        k = 4 + (self.nz - 1) * 6
        for zz, ok, up in self.at_distance(d):
            s = zz * 4 + (1 - self.x) * 2 + self.c
            self.take(ok, a, s)
            self.put(ok, a, self.slot(a, s), s, self.cp, k + 2 * d + (1 if up else 0))

    def arrived(self, a):
        for d in range(self.nz):
            for zz, ok, _ in self.at_distance(d):
                for xx in (self.x, 1 - self.x):
                    self.take(ok, a, zz * 4 + xx * 2 + 1 - self.c)
        pltpu.make_async_copy(self.own_refs[a], self.slot(a, self.me), self.own_sem.at[a]).wait()

    def end(self):
        for cond, d in self.started:
            when(cond, d.wait_send)


def step_kernel(n, fr_hbm, wi, wm, wo, wg, ai, am, ao, ag, scal_ref, ht_hbm, ha_hbm,
                gin_hbm, gmid_hbm, gout_hbm, gg_out, gall_ref, frow_ref, dlog_ref, loss_ref,
                own_in, own_mid, own_out, own_misc, win_ref, wmid_ref, wout_ref, misc_ref, g_ref, gg_ref,
                x_ref, h1_ref, h2_ref, h3_ref, a2_ref, st_ref, feat_ref, dfeat_ref, e_ref, o_ref,
                d2_ref, dh3_ref, low_ref, far_ref, fbuf, hbuf, stage, head_ref,
                fsend, frecv, part, r1, r2, tgt_s, tgt_r, down_s, dsend, drecv,
                own_sem, g_send, g_recv, f_sem, h_sem, st_sem, ss, rs_,
                s_f, q_f, s_1, q_1, s_2, q_2, s_t, q_t, s_l, q_l, s_c, q_c, s_d, q_d, s_r, q_r):
    me, z, x, c = place()
    role = lax.axis_index("role")
    half = n // 2
    peers = [lax.rem(me + k, n) for k in range(1, n)]
    cp = me + 1 - 2 * c
    du_ref = d2_ref

    def pick(w, a, dst):
        def fill(src):
            dst[...] = src[...].astype(jnp.bfloat16)
        pl.when(role == 0)(lambda: fill(w))
        pl.when(role != 0)(lambda: fill(a))

    def fetch_frames(r):
        return pltpu.make_async_copy(fr_hbm.at[pl.ds(r * SIDE, SIDE)], fbuf.at[r % 2], f_sem.at[r % 2])

    def fetch_head(k, go):
        m = HC if k < NHC - 1 else COLS - (NHC - 1) * HC

        def one(src):
            d = pltpu.make_async_copy(src.at[pl.ds(k * HC, m)], hbuf.at[k % 2, pl.ds(0, m)], h_sem.at[k % 2])
            d.start() if go else d.wait()
        if go:
            pl.when(role == 0)(lambda: one(ht_hbm))
            pl.when(role != 0)(lambda: one(ha_hbm))
        else:
            one(ht_hbm)
    fetch_frames(0).start()
    fetch_head(0, True)
    pick(wi, ai, own_in)
    pick(wm, am, own_mid)
    pick(wo, ao, own_out)

    def pick_gains(src):
        v = src[...].astype(jnp.bfloat16).astype(jnp.float32)
        for k in range(3):
            own_misc[k:k + 1, :] = v[:, k * 128:(k + 1) * 128]
    own_misc[0:TB, :] = jnp.zeros((TB, 128), jnp.float32)
    pl.when(role == 0)(lambda: pick_gains(wg))
    pl.when(role != 0)(lambda: pick_gains(ag))
    own_misc[TB:2 * TB, :] = scal_ref[5]
    greet([(None, {"dp": p}) for p in peers] + [(None, {"role": 1 - role})])

    gath = Gather(n // 4, (own_in, own_mid, own_out, own_misc), (win_ref, wmid_ref, wout_ref, misc_ref),
               (D // n, 9 * MID // n, MID // n, None), own_sem, g_send, g_recv)
    casts = iter(range(NHC))

    def cast_head(times):
        for _ in range(times):
            k = next(casts, None)
            if k is None:
                return
            if k + 1 < NHC:
                fetch_head(k + 1, True)
            fetch_head(k, False)
            m = HC if k < NHC - 1 else COLS - (NHC - 1) * HC
            u = 128 if m % 128 == 0 else 112

            def one(i, carry, k=k, u=u):
                rs = pl.ds(pl.multiple_of(i * u, 16), u)
                head_ref[pl.ds(pl.multiple_of(k * HC + i * u, 16), u), :] = hbuf[k % 2, rs, :].astype(jnp.bfloat16)
                return carry
            lax.fori_loop(0, m // u, one, 0)

    for a in (MISC, W_IN, W_MID):
        gath.begin(a)
    for r in range(SIDE):
        if r + 1 < SIDE:
            fetch_frames(r + 1).start()
        fetch_frames(r).wait()
        v = fbuf[r % 2].astype(jnp.float32).reshape(VR, D)
        x_ref[r * RB:(r + 1) * RB, :] = jnp.concatenate([v, jnp.zeros((TB, D), jnp.float32)], axis=0).astype(jnp.bfloat16)
    clear_margins(e_ref, o_ref)
    head_ref[COLS:PADC, :] = jnp.zeros((PADC - COLS, 128), jnp.bfloat16)
    far = n // 4 - 1
    gath.begin(W_OUT)
    for d in range(1, far + 1):
        gath.along_z(W_IN, d)
        gath.along_z(MISC, d)
        cast_head(2)
        if d > 1:
            gath.along_z(W_MID, d - 1)
            cast_head(1)
            gath.along_z(W_OUT, d - 1)
            cast_head(1)
    for d in range(far + 1):
        gath.along_x(MISC, d)
        gath.along_x(W_IN, d)
        cast_head(1)
    gath.along_z(W_MID, far)
    cast_head(1)
    gath.along_z(W_OUT, far)
    cast_head(1)
    gath.arrived(MISC)
    gath.arrived(W_IN)
    for i in range(n):
        gall_ref[i] = misc_ref[i, TB:2 * TB, :]
        for k in range(3):
            at = (i * 3 + k) * 128
            g_ref[:, at:at + 128] = misc_ref[i, k:k + 1, :]

    def mm1(i, carry):
        rs = pl.ds(pl.multiple_of(i * BLK, BLK), BLK)
        h1_ref[rs, :] = jnp.dot(x_ref[rs, :], win_ref[...], preferred_element_type=jnp.float32)
        return carry
    lax.fori_loop(0, ROWS // BLK, mm1, 0)
    for d in range(2):
        gath.along_x(W_MID, d)
        gath.along_x(W_OUT, d)
    mean, rstd = moments(h1_ref, 0, MID // GROUPS)
    st_ref[0:8, 0:MID] = mean
    st_ref[8:16, 0:MID] = rstd
    sc = rstd * g_ref[:, 0:MID]
    sh = g_ref[:, MID:2 * MID] - mean * sc

    def act1(r, carry):
        h = h1_ref[row_at(r), :].reshape(SIDE, TB, MID)
        a = gelu(h * sc[None] + sh[None]).reshape(VR, MID)
        put_shifted(e_ref, o_ref, r, a)
        return carry
    lax.fori_loop(0, SIDE, act1, 0)
    HW = MID // 2
    inner = pl.ds(PAD, ROWS)

    def far_a1(to):
        return rc(e_ref.at[inner], far_ref, ss.at[0], rs_.at[0], {"role": to})

    def far_d2(to, k):
        cs = pl.ds(k * HW, HW)
        return rc(e_ref.at[inner, cs], low_ref.at[:, cs], ss.at[1 + k], rs_.at[1 + k], {"role": to})
    pl.when(role == 0)(lambda: far_a1(1).start())
    cast_head(NHC)
    for d in range(2, far + 1):
        gath.along_x(W_MID, d)
        gath.along_x(W_OUT, d)
    gath.arrived(W_MID)

    def mm2(i, carry):
        row = i * BLK
        acc = None
        for m, s in enumerate(OFFS):
            p = jnp.dot(shifted(e_ref, o_ref, s, row, BLK), wmid_ref[m * MID:(m + 1) * MID, :],
                        preferred_element_type=jnp.float32)
            acc = p if acc is None else acc + p
        h2_ref[pl.ds(pl.multiple_of(row, BLK), BLK), :] = acc
        return carry
    lax.fori_loop(0, ROWS // BLK, mm2, 0)
    mean, rstd = moments(h2_ref, 0, MID // GROUPS)
    st_ref[0:8, MID:2 * MID] = mean
    st_ref[8:16, MID:2 * MID] = rstd
    sc2 = rstd * g_ref[:, 2 * MID:3 * MID]
    sh2 = g_ref[:, 3 * MID:4 * MID] - mean * sc2

    def act2(r, carry):
        h = h2_ref[rows_full(r), :].reshape(PITCH, TB, MID)
        a2_ref[rows_full(r), :] = gelu(h * sc2[None] + sh2[None]).reshape(RB, MID).astype(jnp.bfloat16)
        return carry
    lax.fori_loop(0, SIDE, act2, 0)
    gath.arrived(W_OUT)

    def mm3(i, carry):
        rs = pl.ds(pl.multiple_of(i * BLK, BLK), BLK)
        h3_ref[rs, :] = jnp.dot(a2_ref[rs, :], wout_ref[...], preferred_element_type=jnp.float32)
        return carry
    lax.fori_loop(0, ROWS // BLK, mm3, 0)
    for k in range(D // CH):
        lo = k * CH
        mean, rstd = moments(h3_ref, lo, D // GROUPS)
        st_ref[0:8, 2 * MID + lo:2 * MID + lo + CH] = mean
        st_ref[8:16, 2 * MID + lo:2 * MID + lo + CH] = rstd
        sc3 = rstd * g_ref[:, 4 * MID + lo:4 * MID + lo + CH]
        sh3 = g_ref[:, 4 * MID + D + lo:4 * MID + D + lo + CH] - mean * sc3

        def act3(r, acc):
            h = h3_ref[row_at(r), lo:lo + CH].reshape(SIDE, TB, CH)
            s = x_ref[rows_full(r), lo:lo + CH].astype(jnp.float32)[0:VR].reshape(SIDE, TB, CH)
            return acc + jnp.sum(gelu(s + (h * sc3[None] + sh3[None])), axis=0)
        acc = lax.fori_loop(0, SIDE, act3, jnp.zeros((TB, CH), jnp.float32))
        feat_ref[:, lo:lo + CH] = (acc / float(PIX)).astype(jnp.bfloat16).astype(jnp.float32)

    for j in range(n):
        fsend[j] = feat_ref[:, j * 128:(j + 1) * 128]
    for k, p in enumerate(peers):
        rc(fsend.at[p], frecv.at[me], s_f.at[k], q_f.at[me], {"dp": p}).start()
    frecv[me] = fsend[me]
    for k, p in enumerate(peers):
        rc(fsend.at[p], frecv.at[p], s_f.at[k], q_f.at[p], {"dp": p}).wait_recv()
    feats = frecv[...].reshape(n * TB, 128)
    ids = gall_ref[...].reshape(n * TB, 128).astype(jnp.int32)

    acc = None
    for g in range(GAMES):
        lhs = jnp.where(ids == g, feats, 0.0).astype(jnp.bfloat16)
        a = window_of(g)
        p = lax.dot_general(lhs, head_ref[a:a + WIN, :], (((1,), (1,)), ((), ())),
                            preferred_element_type=jnp.float32)
        acc = p if acc is None else acc + p
    off = ids_offset(ids)
    part[...] = shift_rows(acc, off, False).reshape(half, 2, TB, LW)

    d1 = rc(part.at[:, 1 - c], r1, s_1, q_1, {"dp": cp})
    d1.start()
    d1.wait()
    pair = me // 2
    r1[...] = r1[...] + part[:, c]
    pps = [lax.rem(pair + k, half) for k in range(1, half)]
    for k, p in enumerate(pps):
        rc(r1.at[p], r2.at[pair], s_2.at[k], q_2.at[pair], {"dp": 2 * p + c}).start()
    r2[pair] = r1[pair]
    for k, p in enumerate(pps):
        rc(r1.at[p], r2.at[p], s_2.at[k], q_2.at[p], {"dp": 2 * p + c}).wait_recv()
    logits = jnp.sum(r2[...], axis=0)

    lane = lax.broadcasted_iota(jnp.int32, (TB, 128), 1)
    live = lane < ATOMS
    zi = support_low + (support_high - support_low) * lane.astype(jnp.float32) / (ATOMS - 1)
    zi = jnp.where(live, zi, 0.0)
    taken, nxt, expert, reward, done, gid = (scal_ref[k] for k in range(6))
    pieces = []
    for a in range(ACTIONS):
        v = logits if a == 0 else pltpu.roll(logits, LW - ATOMS * a, 1)
        pieces.append(v[:, :128])

    @pl.when(role == 1)
    def _():
        sel = jnp.zeros((TB, 128), jnp.float32)
        for a in range(ACTIONS):
            sel = sel + jnp.where(nxt == float(a), pieces[a], 0.0)
        sel = jnp.where(live, sel, -1e30)
        e = jnp.exp(sel - jnp.max(sel, axis=1, keepdims=True))
        e = jnp.where(live, e, 0.0)
        prob = e / jnp.sum(e, axis=1, keepdims=True)
        spacing = (support_high - support_low) / (ATOMS - 1)
        m = jnp.zeros((TB, 128), jnp.float32)
        for j in range(ATOMS):
            zj = float(np.float32(support_low) + np.float32(support_high - support_low) * np.float32(j) /
                       np.float32(ATOMS - 1))
            tz = jnp.clip(reward + discount * (1.0 - done) * zj, support_low, support_high)
            wt = jnp.maximum(0.0, 1.0 - jnp.abs(tz - zi) / spacing)
            m = m + prob[:, j:j + 1] * wt
        tgt_s[...] = jnp.where(live, m, 0.0)
        d = rc(tgt_s, tgt_r, s_t, q_t, {"role": 0})
        d.start()
        d.wait_send()
        rc(frow_ref, frow_ref, s_r.at[0], q_r.at[0], {"role": 0}).wait_recv()
        rc(dlog_ref, dlog_ref, s_r.at[1], q_r.at[1], {"role": 0}).wait_recv()
        dfeat_ref[...] = jnp.zeros_like(dfeat_ref)

    @pl.when(role == 0)
    def _():
        frow_ref[...] = feats.astype(jnp.bfloat16)
        gt = jnp.transpose(gall_ref[...].reshape(n * TB, 128))[0:TB]
        count = jnp.sum((gt == gid).astype(jnp.float32), axis=1, keepdims=True)
        weight = 1.0 / jnp.maximum(count, 1.0)
        x3 = jnp.where(live[None], jnp.stack(pieces), -1e30)
        act = lax.broadcasted_iota(jnp.int32, (ACTIONS, TB, 128), 0).astype(jnp.float32)
        hot = (act == taken[None]).astype(jnp.float32)
        mx = jnp.max(x3, axis=2, keepdims=True)
        e = jnp.where(live[None], jnp.exp(x3 - mx), 0.0)
        s = jnp.sum(e, axis=2, keepdims=True)
        logp = jnp.where(live[None], x3 - mx - jnp.log(s), 0.0)
        prob = e / s
        q = jnp.sum(prob * zi[None], axis=2, keepdims=True)
        qb = jnp.broadcast_to(q, (ACTIONS, TB, 128))
        qm = jnp.max(qb, axis=0)
        qe = jnp.exp(qb - qm[None])
        qs = jnp.sum(qe, axis=0)
        lse = qm + jnp.log(qs)
        pol = qe / qs[None]
        chosen = jnp.sum(logp * hot, axis=0)
        qt = jnp.sum(qb * hot, axis=0)
        rc(tgt_s, tgt_r, s_t, q_t, {"role": 1}).wait_recv()
        m = tgt_r[...]
        cross = -jnp.sum(m * chosen, axis=1, keepdims=True)
        row_loss = cross + penalty * expert * (lse - qt)
        msum = jnp.sum(m, axis=1, keepdims=True)
        dl = hot * (prob * msum[None] - m[None]) + (penalty * expert)[None] * (pol - hot) * prob * (zi[None] - qb)
        dl = jnp.where(live[None], dl * (weight * (1.0 / GAMES))[None], 0.0)
        flat = jnp.zeros((TB, LW), jnp.float32)
        pad = jnp.zeros((TB, LW - 128), jnp.float32)
        for a in range(ACTIONS):
            v = jnp.concatenate([dl[a], pad], axis=1)
            flat = flat + (v if a == 0 else pltpu.roll(v, ATOMS * a, 1))
        l0 = row_loss * weight
        p0 = l0.astype(jnp.bfloat16).astype(jnp.float32)
        p1 = (l0 - p0).astype(jnp.bfloat16).astype(jnp.float32)
        p2 = l0 - p0 - p1
        last = flat[:, LW - 128:]
        last = jnp.where(lane == 125, p0, jnp.where(lane == 126, p1, jnp.where(lane == 127, p2, last)))
        flat = jnp.concatenate([flat[:, :LW - 128], last], axis=1)
        down_s[...] = jnp.concatenate([flat[:, :LW // 2], flat[:, LW // 2:]], axis=0).astype(jnp.bfloat16)
        for k, p in enumerate(pps):
            rc(down_s, dlog_ref.at[me], s_l.at[k], q_l.at[me], {"dp": 2 * p + c}).start()
        rc(down_s, dlog_ref.at[me], s_c.at[0], q_c.at[me], {"dp": cp}).start()
        dlog_ref[me] = down_s[...]
        for k, p in enumerate(pps):
            o = 2 * p + c
            rc(down_s, dlog_ref.at[o], s_l.at[k], q_l.at[o], {"dp": cp}).wait_recv()
            rc(dlog_ref.at[o], dlog_ref.at[o], s_c.at[k + 1], q_c.at[o], {"dp": cp}).start()
        for p in [pair] + pps:
            o = 2 * p + 1 - c
            rc(dlog_ref.at[o], dlog_ref.at[o], s_c.at[0], q_c.at[o], {"dp": cp}).wait_recv()
        to0 = rc(frow_ref, frow_ref, s_r.at[0], q_r.at[0], {"role": 1})
        to1 = rc(dlog_ref, dlog_ref, s_r.at[1], q_r.at[1], {"role": 1})
        to0.start()
        to1.start()
        rolled = shift_rows(widen(dlog_ref[...]), off, True)
        acc = None
        for g in range(GAMES):
            lhs = jnp.where(jnp.concatenate([ids == g] * (WIN // 128), axis=1), rolled, 0.0).astype(jnp.bfloat16)
            a = window_of(g)
            p = jnp.dot(lhs, head_ref[a:a + WIN, :], preferred_element_type=jnp.float32)
            acc = p if acc is None else acc + p
        dsend[...] = acc.reshape(n, TB, 128)
        for k, p in enumerate(peers):
            rc(dsend.at[p], drecv.at[me], s_d.at[k], q_d.at[me], {"dp": p}).start()
        drecv[me] = dsend[me]
        for k, p in enumerate(peers):
            rc(dsend.at[p], drecv.at[p], s_d.at[k], q_d.at[p], {"dp": p}).wait_recv()
        for j in range(n):
            dfeat_ref[:, j * 128:(j + 1) * 128] = drecv[j]
        for k, p in enumerate(pps):
            rc(down_s, dlog_ref.at[me], s_l.at[k], q_l.at[me], {"dp": 2 * p + c}).wait_send()
        rc(down_s, dlog_ref.at[me], s_c.at[0], q_c.at[me], {"dp": cp}).wait_send()
        for k, p in enumerate(pps):
            o = 2 * p + c
            rc(dlog_ref.at[o], dlog_ref.at[o], s_c.at[k + 1], q_c.at[o], {"dp": cp}).wait_send()
        for k, p in enumerate(peers):
            rc(dsend.at[p], drecv.at[me], s_d.at[k], q_d.at[me], {"dp": p}).wait_send()
        to0.wait_send()
        to1.wait_send()

    for k, p in enumerate(peers):
        rc(fsend.at[p], frecv.at[me], s_f.at[k], q_f.at[me], {"dp": p}).wait_send()
    for k, p in enumerate(pps):
        rc(r1.at[p], r2.at[pair], s_2.at[k], q_2.at[pair], {"dp": 2 * p + c}).wait_send()
    tail = dlog_ref[:, :, 384:512].astype(jnp.float32)[:, TB:2 * TB].reshape(n * TB, 128)
    lanes = lax.broadcasted_iota(jnp.int32, (n * TB, 128), 1)
    total = jnp.sum(jnp.where(lanes >= 125, tail, 0.0))
    loss_ref[...] = jnp.full((TB, 128), total, jnp.float32)

    z8 = jnp.zeros((TB, CH), jnp.float32)

    def put_gain(at, s):
        gg_ref[:, at:at + CH] = jnp.sum(s, axis=0, keepdims=True)
    sent = []

    def put_grad(dst, value):
        k = len(sent) % 2
        if len(sent) >= 2:
            sent[-2].wait()
        cols = value.shape[1]
        stage[k, :, 0:cols] = value
        d = pltpu.make_async_copy(stage.at[k, :, pl.ds(0, cols)], dst, st_sem.at[k])
        d.start()
        sent.append(d)

    def flush():
        for d in sent[-2:]:
            d.wait()
        sent.clear()

    def last_norm():
        for k in range(D // CH):
            lo = k * CH
            mean = st_ref[0:8, 2 * MID + lo:2 * MID + lo + CH]
            rstd = st_ref[8:16, 2 * MID + lo:2 * MID + lo + CH]
            gain = g_ref[:, 4 * MID + lo:4 * MID + lo + CH]
            shift = g_ref[:, 4 * MID + D + lo:4 * MID + D + lo + CH]
            dout = dfeat_ref[:, lo:lo + CH] / float(PIX)
            mr = mean * rstd

            def one(r, acc):
                s1, s2 = acc
                h = h3_ref[row_at(r), lo:lo + CH].reshape(SIDE, TB, CH)
                s = x_ref[rows_full(r), lo:lo + CH].astype(jnp.float32)[0:VR].reshape(SIDE, TB, CH)
                xh = h * rstd[None] - mr[None]
                du = dout[None] * dgelu(s + (xh * gain + shift))
                du_ref[row_at(r), :] = du.reshape(VR, CH)
                return s1 + jnp.sum(du, axis=0), s2 + jnp.sum(du * xh, axis=0)
            s1, s2 = lax.fori_loop(0, SIDE, one, (z8, z8))
            put_gain(4 * MID + lo, s2)
            put_gain(4 * MID + D + lo, s1)

            def put3(r, v):
                dh3_ref[rows_full(r), lo:lo + CH] = jnp.concatenate([v, z8], axis=0).astype(jnp.bfloat16)
            norm_back(h3_ref, lo, du_ref, mean, rstd, gain, D // GROUPS, s1, s2, put3)

    def through(h_ref, at, goff, boff, emit):
        mean = st_ref[0:8, at:at + MID]
        rstd = st_ref[8:16, at:at + MID]
        gain = g_ref[:, goff:goff + MID]
        shift = g_ref[:, boff:boff + MID]
        mr = mean * rstd

        def one(r, acc):
            s1, s2 = acc
            h = h_ref[row_at(r), :].reshape(SIDE, TB, MID)
            da = d2_ref[row_at(r), :].reshape(SIDE, TB, MID)
            xh = h * rstd[None] - mr[None]
            dy = da * dgelu(xh * gain + shift)
            d2_ref[row_at(r), :] = dy.reshape(VR, MID)
            return s1 + jnp.sum(dy, axis=0), s2 + jnp.sum(dy * xh, axis=0)
        s1, s2 = lax.fori_loop(0, SIDE, one, (z8, z8))
        put_gain(goff, s2)
        put_gain(boff, s1)
        norm_back(h_ref, 0, d2_ref, mean, rstd, gain, MID // GROUPS, s1, s2, emit)

    @pl.when(role == 0)
    def _():
        last_norm()

        def da2(i, c):
            rs = pl.ds(pl.multiple_of(i * BLK, BLK), BLK)
            d2_ref[rs, :] = lax.dot_general(dh3_ref[rs, :], wout_ref[...], T1, preferred_element_type=jnp.float32)
            return c
        lax.fori_loop(0, ROWS // BLK, da2, 0)
        far_a1(1).wait_send()
        through(h2_ref, MID, 2 * MID, 3 * MID, lambda r, v: put_shifted(e_ref, o_ref, r, v))
        far_d2(1, 0).start()
        far_d2(1, 1).start()

        def da1(i, c):
            row = i * BLK
            acc = None
            for m, s in enumerate(OFFS):
                p = lax.dot_general(shifted(e_ref, o_ref, -s, row, BLK), wmid_ref[m * MID:(m + 1) * MID, :], T1,
                                    preferred_element_type=jnp.float32)
                acc = p if acc is None else acc + p
            d2_ref[pl.ds(pl.multiple_of(row, BLK), BLK), :] = acc
            return c
        lax.fori_loop(0, ROWS // BLK, da1, 0)

        def put1(r, v):
            low_ref[rows_full(r), :] = jnp.concatenate([v, z8], axis=0).astype(jnp.bfloat16)
        through(h1_ref, 0, 0, MID, put1)
        for k in range(D // CH):
            lo = k * CH
            put_grad(gout_hbm.at[:, pl.ds(lo, CH)], lax.dot_general(
                a2_ref[...], dh3_ref[:, lo:lo + CH], T0, preferred_element_type=jnp.float32))
            put_grad(gin_hbm.at[pl.ds(lo, CH)], lax.dot_general(
                x_ref[:, lo:lo + CH], low_ref[...], T0, preferred_element_type=jnp.float32))
        flush()
        far_d2(1, 0).wait_send()
        far_d2(1, 1).wait_send()

    @pl.when(role == 1)
    def _():
        far_a1(0).wait_recv()
        for k in range(2):
            cs = slice(k * HW, (k + 1) * HW)
            far_d2(0, k).wait_recv()
            zh = jnp.zeros((TB, HW), jnp.float32)

            def rebuild(r, c):
                v = low_ref[rows_full(r), cs].astype(jnp.float32)
                at = pl.ds(pl.multiple_of(PAD + r * RB, 16), RB)
                e_ref[at, cs] = low_ref[rows_full(r), cs]
                o_ref[at, cs] = jnp.concatenate([zh, v[0:VR]], axis=0).astype(jnp.bfloat16)
                return c
            lax.fori_loop(0, SIDE, rebuild, 0)
            for m, s in enumerate(OFFS):
                ref, base = (e_ref, 16 - s) if s % 2 == 0 else (o_ref, 17 - s)
                put_grad(gmid_hbm.at[pl.ds(m * MID, MID), pl.ds(k * HW, HW)], lax.dot_general(
                    far_ref[...], ref[base * TB:base * TB + ROWS, cs], T0, preferred_element_type=jnp.float32))
        flush()

    for i in range(n):
        for k in range(3):
            at = (i * 3 + k) * 128
            gg_out[i, k:k + 1, :] = gg_ref[:, at:at + 128]
    gath.end()


def block_step(frames, weights, averages, scal, head, avg_head, n, cid):
    f32, b16 = jnp.float32, jnp.bfloat16
    S = jax.ShapeDtypeStruct
    V, dma = pltpu.VMEM, pltpu.SemaphoreType.DMA
    vs, hs = pl.BlockSpec(memory_space=pltpu.VMEM), pl.BlockSpec(memory_space=pl.ANY)
    h = n // 2
    nz = n // 4
    sends = 4 + 6 * (nz - 1) + 2 * nz
    return pl.pallas_call(
        functools.partial(step_kernel, n),
        out_shape=(S((D, MID), f32), S((9 * MID, MID), f32), S((MID, D), f32), S((n, 3, 128), f32),
                   S((n, TB, 128), f32), S((n * TB, 128), b16), S((n, 16, 512), b16), S((TB, 128), f32)),
        in_specs=[hs] + [vs] * 9 + [hs] * 2,
        out_specs=(hs,) * 3 + (vs,) * 5,
        scratch_shapes=[
            V((D // n, MID), b16), V((9 * MID // n, MID), b16), V((MID // n, D), b16), V((16, 128), f32),
            V((D, MID), b16), V((9 * MID, MID), b16), V((MID, D), b16), V((n, 16, 128), f32),
            V((1, 4 * MID + 2 * D), f32), V((1, 4 * MID + 2 * D), f32),
            V((ROWS, D), b16), V((ROWS, MID), f32), V((ROWS, MID), f32), V((ROWS, D), f32), V((ROWS, MID), b16),
            V((16, 2 * MID + D), f32), V((TB, D), f32), V((TB, D), f32), V((EROWS, MID), b16), V((EROWS, MID), b16),
            V((ROWS, MID), f32), V((ROWS, D), b16), V((ROWS, MID), b16), V((ROWS, MID), b16),
            V((2, SIDE, TB, D), b16), V((2, HC, 128), f32), V((2, MID, CH), f32), V((PADC, 128), b16),
            V((n, TB, 128), f32), V((n, TB, 128), f32), V((h, 2, TB, LW), f32), V((h, TB, LW), f32),
            V((h, TB, LW), f32), V((TB, 128), f32), V((TB, 128), f32), V((16, 512), b16),
            V((n, TB, 128), f32), V((n, TB, 128), f32),
            dma((4,)), dma((4, sends)), dma((4, n)), dma((2,)), dma((2,)), dma((2,)), dma((3,)), dma((3,)),
            dma((n,)), dma((n,)), dma, dma, dma((h,)), dma((h,)), dma, dma, dma((h,)), dma((n,)),
            dma((h,)), dma((n,)), dma((n,)), dma((n,)), dma((2,)), dma((2,))],
        compiler_params=pltpu.CompilerParams(collective_id=cid, has_side_effects=True,
                                             vmem_limit_bytes=64 * 1024 * 1024),
        name="block_step",
    )(frames, *weights, *averages, scal, head, avg_head)


KEEP, SEND, BOTH = 0, 1, 2
OUT, MIDDLE, IN, GAINS = 0, 1, 2, 3
ONLINE = ((GAINS, 0, 128, BOTH), (OUT, 1024, 1024, SEND), (OUT, 0, 1024, KEEP), (IN, 256, 256, SEND), (IN, 0, 256, KEEP))
TARGET = ((MIDDLE, 0, 128, SEND), (MIDDLE, 128, 128, SEND), (MIDDLE, 256, 128, KEEP), (MIDDLE, 384, 128, KEEP))
UB = 1024
NU = -(-HALF // UB)
LASTU = HALF - (NU - 1) * UB


def sums_kernel(nz, g_out, g_mid, g_in, g_gains, gall_ref, frow_ref, dlog_ref, h_hbm, m_hbm, a_hbm,
                t_out, t_mid, t_in, t_gains, w_hbm, n_hbm, v_hbm, c_hbm, *refs):
    g = (g_out, g_mid, g_in, g_gains)
    outs = (t_out, t_mid, t_in, t_gains)
    na = 4
    r1, r2, ru, rd, fs, fr = (refs[j * na:(j + 1) * na] for j in range(6))
    dlt, grow, ibuf, obuf, cbuf = refs[6 * na:6 * na + 5]
    s1, q1, s2, q2, su, qu, sd, qd, sf, qf, si, so = refs[6 * na + 5:]
    me, z, x, c = place()
    role = lax.axis_index("role")
    up, down = {"dp": me + 4}, {"dp": me - 4}
    xp = {"dp": me + 2 - 4 * x}
    cp = {"dp": me + 1 - 2 * c}
    has_up, has_down = z < nz - 1, z > 0
    greet([(has_up, up), (has_down, down), (None, xp), (None, cp), (None, {"role": 1 - role})])

    def rc(src, dst, ss, rs, dev):
        return pltpu.make_async_remote_copy(src_ref=src, dst_ref=dst, send_sem=ss, recv_sem=rs, device_id=dev,
                                            device_id_type=MESH)

    def slot(zz, xx, cc):
        return zz * 4 + xx * 2 + cc

    order = list(range(nz))

    hbm_in, hbm_out = (h_hbm, m_hbm, a_hbm), (w_hbm, n_hbm, v_hbm)

    def rows_of(k):
        return UB if k < NU - 1 else LASTU

    def fetch(k):
        n = rows_of(k)
        return [pltpu.make_async_copy(hbm_in[t].at[pl.ds(pl.multiple_of(role * HALF + k * UB, 8), n)],
                                      ibuf.at[k % 2, t, pl.ds(0, n)], si.at[k % 2, t]) for t in range(3)]

    def store(k):
        n = rows_of(k)
        cs = [pltpu.make_async_copy(obuf.at[k % 2, t, pl.ds(0, n)], hbm_out[t].at[pl.ds(k * UB, n)], so.at[k % 2, t])
              for t in range(3)]
        return cs + [pltpu.make_async_copy(cbuf.at[k % 2, pl.ds(0, n)], c_hbm.at[pl.ds(k * UB, n)], so.at[k % 2, 3])]

    def prepare():
        for d in fetch(0):
            d.start()
        ids = gall_ref[...].reshape(-1, 128).astype(jnp.int32) - role * (GAMES // 2)
        v = shift_rows(widen(dlog_ref[...]), ids_offset(ids), True)
        zero = jnp.zeros((UB, dlt.shape[1]), jnp.bfloat16)
        dlt[0:UB, :] = zero
        dlt[UB + WIN:2 * UB + WIN, :] = zero
        for k in range(WIN // 128):
            dlt[UB + k * 128:UB + (k + 1) * 128, :] = jnp.transpose(v[:, k * 128:(k + 1) * 128]).astype(jnp.bfloat16)

    def step(k):
        b = k % 2
        if k + 1 < NU:
            for d in fetch(k + 1):
                d.start()
        own = gall_ref[...].reshape(-1, 128).astype(jnp.int32) - role * (GAMES // 2)
        lo = k * UB
        todo = [i for i in range(GAMES // 2) if window_of(i) < lo + UB and window_of(i) + WIN > lo]
        for m, i in enumerate(todo):
            rhs = jnp.where(own == i, frow_ref[...].astype(jnp.float32), 0.0).astype(jnp.bfloat16)
            at = UB + lo - window_of(i)

            def some(r, carry, rhs=rhs, at=at, m=m):
                rs = pl.ds(pl.multiple_of(r * 256, 256), 256)
                v = jnp.dot(dlt[pl.ds(pl.multiple_of(at + r * 256, 16), 256), :], rhs,
                            preferred_element_type=jnp.float32)
                grow[rs, :] = v if m == 0 else grow[rs, :] + v
                return carry
            lax.fori_loop(0, UB // 256, some, 0)
        for d in fetch(k):
            d.wait()
        if k >= 2:
            for d in store(k - 2):
                d.wait()

        def one(r, carry):
            rs = pl.ds(pl.multiple_of(r * 128, 128), 128)
            gv = grow[rs, :]
            m = 0.5 * ibuf[b, 1, rs, :] + gv
            w = ibuf[b, 0, rs, :] - 4.0 * (gv + 0.5 * m)
            obuf[b, 0, rs, :] = w
            obuf[b, 1, rs, :] = m
            obuf[b, 2, rs, :] = 0.5 * ibuf[b, 2, rs, :] + 0.5 * w
            cbuf[b, rs, :] = w.astype(jnp.bfloat16)
            return carry
        lax.fori_loop(0, UB // 128, one, 0)
        for d in store(k):
            d.start()

    def run(units, mine):
        steps = iter(range(NU))

        def tick():
            k = next(steps, None)
            if k is not None:
                step(k)

        def cut(ref, i, u):
            return ref.at[i, :, pl.ds(u[1], u[2])]

        def add(u, i, ref, j):
            a, cs = u[0], slice(u[1], u[1] + u[2])
            g[a][i, :, cs] = g[a][i, :, cs] + ref[a][j, :, cs]

        def c1(n, zz, k):
            u = units[n]
            xx = 1 - x if k == 0 else x
            return rc(cut(g[u[0]], slot(zz, xx, 1 - c), u), cut(r1[u[0]], k * nz + zz, u), s1.at[n, k * nz + zz],
                      q1.at[n, k * nz + zz], cp)

        def c2(n, zz):
            u = units[n]
            return rc(cut(g[u[0]], slot(zz, 1 - x, c), u), cut(r2[u[0]], zz, u), s2.at[n, zz], q2.at[n, zz], xp)

        def cu(n, t):
            u = units[n]
            return rc(cut(g[u[0]], slot(t, x, c), u), cut(ru[u[0]], t, u), su.at[n, t], qu.at[n, t], up)

        def cd(n, t):
            u = units[n]
            return rc(cut(g[u[0]], slot(t, x, c), u), cut(rd[u[0]], t, u), sd.at[n, t], qd.at[n, t], down)

        nu = len(units)
        for n in range(nu):
            for k in range(2):
                for zz in order:
                    c1(n, zz, k).start()
        prepare()
        for n, u in enumerate(units):
            for zz in order:
                c1(n, zz, 0).wait_recv()
                add(u, slot(zz, 1 - x, c), r1, zz)
                c2(n, zz).start()
        for n, u in enumerate(units):
            for zz in order:
                c1(n, zz, 1).wait_recv()
                add(u, slot(zz, x, c), r1, nz + zz)

        def finish(n):
            u = units[n]
            a, cs = u[0], slice(u[1], u[1] + u[2])

            @pl.when(z > 0)
            def _():
                cu(n, z).wait_recv()
                add(u, me, ru, z)

            @pl.when(z < nz - 1)
            def _():
                cd(n, z).wait_recv()
                add(u, me, rd, z)
            total = g[a][me, :, cs]
            half = outs[a].shape[1]
            at = u[1] % half
            if u[3] != SEND:
                outs[a][:, at:at + u[2]] = total
            if u[3] != KEEP:
                fs[a][:, at:at + u[2]] = total.astype(fs[a].dtype)
                final(a, at, u[2], 1 - mine, n).start()

        for n, u in enumerate(units):
            for zz in order:
                tick()
                c2(n, zz).wait_recv()
                add(u, slot(zz, x, c), r2, zz)
            for t in range(nz - 1, 0, -1):
                @pl.when(z < t)
                def _():
                    @pl.when(z > 0)
                    def _():
                        cu(n, t).wait_recv()
                        add(u, slot(t, x, c), ru, t)
                    cu(n, t).start()
                b = nz - 1 - t

                @pl.when(z > b)
                def _():
                    @pl.when(z < nz - 1)
                    def _():
                        cd(n, b).wait_recv()
                        add(u, slot(b, x, c), rd, b)
                    cd(n, b).start()
            if n > 0:
                finish(n - 1)
        finish(nu - 1)
        for _ in range(NU):
            tick()
        for k in (NU - 2, NU - 1):
            for d in store(k):
                d.wait()
        for n, u in enumerate(units):
            for zz in order:
                c1(n, zz, 0).wait_send()
                c1(n, zz, 1).wait_send()
                c2(n, zz).wait_send()
                pl.when(z < zz)(cu(n, zz).wait_send)
                pl.when(z > zz)(cd(n, zz).wait_send)
            if u[3] != KEEP:
                a = u[0]
                final(a, u[1] % outs[a].shape[1], u[2], 1 - mine, n).wait_send()

    def final(a, at, w, to, n):
        return rc(fs[a].at[:, pl.ds(at, w)], fr[a].at[:, pl.ds(at, w)], sf.at[n], qf.at[n], {"role": to})

    def receive(units, other):
        for n, u in enumerate(units):
            if u[3] != KEEP:
                a = u[0]
                at = u[1] % outs[a].shape[1]
                final(a, at, u[2], other, n).wait_recv()
                outs[a][:, at:at + u[2]] = fr[a][:, at:at + u[2]].astype(jnp.float32)

    @pl.when(role == 0)
    def _():
        run(ONLINE, 0)
        receive(TARGET, 1)

    @pl.when(role == 1)
    def _():
        run(TARGET, 1)
        receive(ONLINE, 0)


def sums(arrays, games_all, frow, dlog, head, moment, avg, n, cid):
    nz = n // 4
    V, dma = pltpu.VMEM, pltpu.SemaphoreType.DMA
    f32, b16 = jnp.float32, jnp.bfloat16
    S = jax.ShapeDtypeStruct
    lanes = head.shape[1]
    sh = [a.shape[1:] for a in arrays]
    half = [(s[0], s[1] // 2 if s[1] > 128 else s[1]) for s in sh]
    low = [b16 if s[1] > 128 else f32 for s in sh]
    nu = max(len(ONLINE), len(TARGET))
    vs, hs = pl.BlockSpec(memory_space=pltpu.VMEM), pl.BlockSpec(memory_space=pl.ANY)
    return pl.pallas_call(
        functools.partial(sums_kernel, nz),
        out_shape=tuple(S(s, f32) for s in half) + (S((HALF, lanes), f32),) * 3 + (S((HALF, lanes), b16),),
        in_specs=[vs] * 7 + [hs] * 3,
        out_specs=(vs,) * 4 + (hs,) * 4,
        scratch_shapes=[V((2 * nz,) + s, f32) for s in sh] + [V((nz,) + s, f32) for s in sh] * 3 +
        [V(s, t) for s, t in zip(half, low)] * 2 +
        [V((2 * UB + WIN, n * TB), b16), V((UB, lanes), f32), V((2, 3, UB, lanes), f32), V((2, 3, UB, lanes), f32),
         V((2, UB, lanes), b16)] +
        [dma((nu, 2 * nz))] * 2 + [dma((nu, nz))] * 6 + [dma((nu,))] * 2 + [dma((2, 3)), dma((2, 4))],
        compiler_params=pltpu.CompilerParams(collective_id=cid, has_side_effects=True,
                                             vmem_limit_bytes=62 * 1024 * 1024),
        name="gradient_sums",
    )(*arrays, games_all, frow, dlog, head, moment, avg)


def fast_device(
    frames,
    game_ids,
    taken_actions,
    next_actions,
    expert_flags,
    rewards,
    done_flags,
    weight_in,
    weight_mid,
    weight_out,
    norm_gains,
    head_table,
    moment_in,
    moment_mid,
    moment_out,
    moment_gains,
    moment_head,
    average_in,
    average_mid,
    average_out,
    average_gains,
    average_head,
):
    n = lax.axis_size("dp")
    role_index = lax.axis_index("role")
    def lanes(v):
        return jnp.broadcast_to(v.astype(jnp.float32)[:, None], (TB, 128))

    ids = lanes(game_ids)
    scal = jnp.stack(
        [lanes(taken_actions), lanes(next_actions), lanes(expert_flags), lanes(rewards), lanes(done_flags), ids]
    )
    g_in, g_mid, g_out, g_gains, all_ids, feat_rows, dlog, loss = block_step(
        jnp.transpose(frames[0], (1, 0, 2)),
        (weight_in[0], weight_mid[0], weight_out[0], norm_gains),
        (average_in[0], average_mid[0], average_out[0], average_gains),
        scal,
        head_table.T,
        average_head.T,
        n,
        1,
    )
    grad_out, grad_mid, grad_in, grad_gains, head_w, head_m, head_a, head_c = sums(
        [
            g_out.reshape(n, MID // n, D),
            g_mid.reshape(n, 9 * MID // n, MID),
            g_in.reshape(n, D // n, MID),
            g_gains,
        ],
        all_ids,
        feat_rows,
        dlog,
        head_table.T,
        moment_head.T,
        average_head.T,
        n,
        2,
    )

    def own(v):
        return own_half(v, role_index)

    in_w, in_m, in_a, in_c = renew(own(weight_in), grad_in[None], own(moment_in), own(average_in), learn_rate)
    mid_w, mid_m, mid_a, mid_c = renew(
        own(weight_mid), grad_mid[None], own(moment_mid), own(average_mid), learn_rate
    )
    out_w, out_m, out_a, out_c = renew(
        own(weight_out), grad_out[None], own(moment_out), own(average_out), learn_rate
    )
    gain_w, gain_m, gain_a, gain_c = renew(
        norm_gains, grad_gains.reshape(norm_gains.shape), moment_gains, average_gains, gain_rate
    )
    return (
        loss[0, 0],
        in_w,
        grad_in[None],
        in_a,
        in_c,
        mid_w,
        mid_m,
        mid_a,
        mid_c,
        out_w,
        out_m,
        out_a,
        out_c,
        gain_w,
        gain_m,
        gain_a,
        gain_c,
        head_w.T,
        head_m.T,
        head_a.T,
        head_c.T,
    )


def solution(mesh):
    return jax.shard_map(
        fast_device if mesh.shape["dp"] == 16 else on_device,
        mesh=mesh,
        in_specs=(
            P("role", "dp", None, None),
            P("dp"),
            P("dp"),
            P("dp"),
            P("dp"),
            P("dp"),
            P("dp"),
            P(None, "dp", None),
            P(None, "dp", None),
            P(None, "dp", None),
            P(None, "dp"),
            P("dp", None),
            P(None, "dp", None),
            P(None, "dp", None),
            P(None, "dp", None),
            P(None, "dp"),
            P("dp", None),
            P(None, "dp", None),
            P(None, "dp", None),
            P(None, "dp", None),
            P(None, "dp"),
            P("dp", None),
        ),
        out_specs=(
            P(),
            P(None, "dp", "role"),
            P(None, "dp", "role"),
            P(None, "dp", "role"),
            P(None, "dp", "role"),
            P(None, "dp", "role"),
            P(None, "dp", "role"),
            P(None, "dp", "role"),
            P(None, "dp", "role"),
            P(None, "dp", "role"),
            P(None, "dp", "role"),
            P(None, "dp", "role"),
            P(None, "dp", "role"),
            P(None, "dp"),
            P(None, "dp"),
            P(None, "dp"),
            P(None, "dp"),
            P("dp", "role"),
            P("dp", "role"),
            P("dp", "role"),
            P("dp", "role"),
        ),
        check_vma=False,
    )
```

```python
import functools

import jax
import jax.numpy as jnp
import numpy as np
from jax import lax
from jax.experimental import pallas as pl
from jax.experimental.pallas import tpu as pltpu
from jax.sharding import PartitionSpec as P

D = 2048
MID = 512
GAMES = 40
ACTIONS = 18
ATOMS = 51
GROUPS = 32
SIDE = 11
LAYERS = 1


support_low = -10.0
support_high = 10.0
discount = 0.99
penalty = 0.05
momentum_decay = 0.5
average_decay = 0.5
learn_rate = 4.0
gain_rate = 40.0
epsilon = 1e-05
HIGHEST = lax.Precision.HIGHEST


def passed_along(block, axis, distance):
    devices = range(lax.axis_size(axis))
    route = [(i - distance, i) for i in devices if i - distance in devices]
    return lax.ppermute(block, axis, route)


def split_gains(gains):
    return (
        gains[:MID],
        gains[MID : 2 * MID],
        gains[2 * MID : 3 * MID],
        gains[3 * MID : 4 * MID],
        gains[4 * MID : 4 * MID + D],
        gains[4 * MID + D :],
    )


def group_norm(values, gain, shift):
    rows, pixels, width = values.shape
    grouped = values.reshape(rows, pixels, GROUPS, width // GROUPS)
    center = grouped - jnp.mean(grouped, axis=(1, 3), keepdims=True)
    spread = jnp.mean(center * center, axis=(1, 3), keepdims=True)
    normed = (center * lax.rsqrt(spread + epsilon)).reshape(values.shape)
    return normed * gain + shift


def patches_of(acts):
    rows, pixels, width = acts.shape
    grid = acts.reshape(rows, SIDE, SIDE, width)
    padded = jnp.pad(grid, ((0, 0), (1, 1), (1, 1), (0, 0)))
    pieces = [
        padded[:, down : down + SIDE, right : right + SIDE, :]
        for down in range(3)
        for right in range(3)
    ]
    return jnp.concatenate(pieces, axis=-1).reshape(rows, pixels, 9 * width)


def transition_loss(logits, target_dist, action_hot, expert, support):
    log_prob = jax.nn.log_softmax(logits, axis=-1)
    values = jnp.sum(jnp.exp(log_prob) * support, axis=-1)
    spread_sum = jax.nn.logsumexp(values, axis=-1)
    chosen_log = jnp.sum(log_prob * action_hot[:, :, None], axis=1)
    cross = -jnp.sum(target_dist * chosen_log, axis=-1)
    regular = spread_sum - jnp.sum(values * action_hot, axis=-1)
    return cross + penalty * expert * regular


def project_target(next_prob, rewards, done_f, support):
    moved = jnp.clip(
        rewards[:, None] + discount * (1.0 - done_f)[:, None] * support[None, :],
        support_low,
        support_high,
    )
    spacing = (support_high - support_low) / (ATOMS - 1)
    weight = jnp.maximum(0.0, 1.0 - jnp.abs(moved[:, :, None] - support[None, None, :]) / spacing)
    return jnp.sum(next_prob[:, :, None] * weight, axis=1)


def renew(weight, grad, moment, average, rate):
    new_moment = momentum_decay * moment + grad
    new_weight = weight - rate * (grad + momentum_decay * new_moment)
    new_average = average_decay * average + (1.0 - average_decay) * new_weight
    return (new_weight, new_moment, new_average, new_weight.astype(jnp.bfloat16))


def lower_half(values):
    return values[..., : values.shape[-1] // 2]


def upper_half(values):
    return values[..., values.shape[-1] // 2 :]


def own_half(values, role_index):
    half = values.shape[-1] // 2
    return lax.dynamic_slice_in_dim(values, role_index * half, half, values.ndim - 1)


def norm_act(hidden, gain, shift):
    return jax.nn.gelu(group_norm(hidden, gain, shift))


def outer_act(hidden, gain, shift, stream):
    return jax.nn.gelu(stream + group_norm(hidden, gain, shift))


def block_forward(stream, weights):
    w_in, w_mid, w_out, gains = weights
    gain_one, shift_one, gain_two, shift_two, gain_three, shift_three = split_gains(gains)
    stream_low = stream.astype(jnp.bfloat16)
    hidden_in = jnp.einsum("bpc,cm->bpm", stream_low, w_in, preferred_element_type=jnp.float32)
    act_in = norm_act(hidden_in, gain_one, shift_one).astype(jnp.bfloat16)
    hidden_mid = jnp.einsum(
        "bpc,cm->bpm", patches_of(act_in), w_mid, preferred_element_type=jnp.float32
    )
    act_mid = norm_act(hidden_mid, gain_two, shift_two).astype(jnp.bfloat16)
    hidden_out = jnp.einsum("bpc,cm->bpm", act_mid, w_out, preferred_element_type=jnp.float32)
    result = outer_act(hidden_out, gain_three, shift_three, stream)
    return (result, (stream, stream_low, hidden_in, act_in, hidden_mid, act_mid, hidden_out))


def block_backward(grad_result, weights, kept, settle):
    w_in, w_mid, w_out, gains = weights
    stream, stream_low, hidden_in, act_in, hidden_mid, act_mid, hidden_out = kept
    gain_one, shift_one, gain_two, shift_two, gain_three, shift_three = split_gains(gains)
    _, back_three = jax.vjp(outer_act, hidden_out, gain_three, shift_three, stream)
    d_three, dg_three, db_three, d_resid = back_three(grad_result)
    d_three = d_three.astype(jnp.bfloat16)
    grad_out = settle(
        jnp.einsum("bpm,bpc->mc", act_mid, d_three, preferred_element_type=jnp.float32)
    )
    d_act_mid = jnp.einsum("bpc,mc->bpm", d_three, w_out, preferred_element_type=jnp.float32)
    _, back_two = jax.vjp(norm_act, hidden_mid, gain_two, shift_two)
    d_two, dg_two, db_two = back_two(d_act_mid)
    d_two = d_two.astype(jnp.bfloat16)
    grad_mid = settle(
        jnp.einsum("bpk,bpm->km", patches_of(act_in), d_two, preferred_element_type=jnp.float32)
    )
    d_cols = jnp.einsum("bpm,km->bpk", d_two, w_mid, preferred_element_type=jnp.float32)
    _, back_cols = jax.vjp(patches_of, act_in.astype(jnp.float32))
    (d_act_in,) = back_cols(d_cols)
    _, back_one = jax.vjp(norm_act, hidden_in, gain_one, shift_one)
    d_one, dg_one, db_one = back_one(d_act_in)
    d_one = d_one.astype(jnp.bfloat16)
    grad_in = jnp.einsum("bpc,bpm->cm", stream_low, d_one, preferred_element_type=jnp.float32)
    d_stream = d_resid + jnp.einsum("bpm,cm->bpc", d_one, w_in, preferred_element_type=jnp.float32)
    grad_gains = jnp.concatenate([dg_one, db_one, dg_two, db_two, dg_three, db_three])
    grad_in, grad_gains = settle((grad_in, grad_gains))
    return (d_stream, (grad_in, grad_mid, grad_out, grad_gains))


def on_device(
    frames,
    game_ids,
    taken_actions,
    next_actions,
    expert_flags,
    rewards,
    done_flags,
    weight_in,
    weight_mid,
    weight_out,
    norm_gains,
    head_table,
    moment_in,
    moment_mid,
    moment_out,
    moment_gains,
    moment_head,
    average_in,
    average_mid,
    average_out,
    average_gains,
    average_head,
):
    role_index = lax.axis_index("role")
    online = role_index == 0
    use_in = jnp.where(online, weight_in, average_in).astype(jnp.bfloat16)
    use_mid = jnp.where(online, weight_mid, average_mid).astype(jnp.bfloat16)
    use_out = jnp.where(online, weight_out, average_out).astype(jnp.bfloat16)
    use_gains = jnp.where(online, norm_gains, average_gains).astype(jnp.bfloat16)
    use_head = jnp.where(online, head_table, average_head).astype(jnp.bfloat16)
    support = support_low + (support_high - support_low) * jnp.arange(ATOMS, dtype=jnp.float32) / (
        ATOMS - 1
    )
    own_hot = (game_ids[:, None] == lax.broadcasted_iota(jnp.int32, (1, GAMES), 1)).astype(
        jnp.float32
    )
    counts = jnp.sum(own_hot, axis=0)
    stream = frames[0].astype(jnp.float32)
    layer = 0
    pieces = (
        lax.all_gather(use_in[layer], "dp", axis=0, tiled=True),
        lax.all_gather(use_mid[layer], "dp", axis=0, tiled=True),
        lax.all_gather(use_out[layer], "dp", axis=0, tiled=True),
        lax.all_gather(use_gains[layer], "dp", axis=0, tiled=True),
    )
    weights = (pieces[0], pieces[1], pieces[2], pieces[3].astype(jnp.float32))
    stream, saved = block_forward(stream, weights)
    gathered = [weights]
    kept = [saved]
    trans = stream.shape[0]
    pixels = stream.shape[1]
    wide_k = ACTIONS * ATOMS
    head_rows = head_table.shape[0]
    feat_low = jnp.mean(stream, axis=1).astype(jnp.bfloat16)
    feat_all, game_all = (
        lax.all_gather(feat_low, "dp", axis=0, tiled=True),
        lax.all_gather(game_ids.astype(jnp.bfloat16)[:, None], "dp", axis=0, tiled=True),
    )
    game_iota = lax.broadcasted_iota(jnp.int32, (1, GAMES), 1).astype(jnp.float32)
    all_hot = (game_all.astype(jnp.float32) == game_iota).astype(jnp.bfloat16)
    feat_rows = lax.dynamic_slice_in_dim(feat_all, lax.axis_index("dp") * head_rows, head_rows, 1)
    head_low = use_head.reshape(head_rows * GAMES, wide_k)

    def widen(count):
        spread_rows = (feat_rows[:, :, None] * all_hot[:, None, :]).reshape(
            count, head_rows * GAMES
        )
        return (spread_rows, all_hot)

    spread_rows, hot_piece = widen(trans * lax.axis_size("dp"))
    flat_logits = lax.psum_scatter(
        jnp.dot(spread_rows, head_low, preferred_element_type=jnp.float32),
        "dp",
        scatter_dimension=0,
        tiled=True,
    )
    logits = flat_logits.reshape(trans, ACTIONS, ATOMS)
    next_hot = (next_actions[:, None] == lax.broadcasted_iota(jnp.int32, (1, ACTIONS), 1)).astype(
        jnp.float32
    )
    next_prob = jax.nn.softmax(jnp.sum(logits * next_hot[:, :, None], axis=1), axis=-1)
    projected = project_target(next_prob, rewards, done_flags.astype(jnp.float32), support)
    target_dist = passed_along(projected, "role", -1)
    action_hot = (
        taken_actions[:, None] == lax.broadcasted_iota(jnp.int32, (1, ACTIONS), 1)
    ).astype(jnp.float32)
    expert = expert_flags.astype(jnp.float32)

    def local_loss(values):
        return transition_loss(values, target_dist, action_hot, expert, support)

    row_loss, loss_back = jax.vjp(local_loss, logits)
    sums = jnp.dot(row_loss, own_hot, precision=HIGHEST)
    total_counts, total_sums = lax.psum((counts, sums), "dp")
    floor_counts = jnp.maximum(total_counts, 1.0)
    loss_total = jnp.sum(total_sums / floor_counts)
    row_weight = jnp.dot(own_hot, 1.0 / (GAMES * floor_counts), precision=HIGHEST)
    (d_logits,) = loss_back(row_weight)
    d_low = d_logits.reshape(trans, wide_k).astype(jnp.bfloat16)
    piece = lax.all_gather(d_low, "dp", axis=0, tiled=True)
    count = piece.shape[0]
    spread_rows, hot_piece = widen(count)
    grad_head = lax.dot_general(
        spread_rows, piece, (((0,), (0,)), ((), ())), preferred_element_type=jnp.float32
    )
    back_wide = jnp.dot(piece, head_low.T, preferred_element_type=jnp.float32)
    back_rows = jnp.sum(
        back_wide.reshape(count, head_rows, GAMES) * hot_piece[:, None, :].astype(jnp.float32),
        axis=2,
    )
    grad_rows = back_rows
    grad_head, grad_rows = (grad_head, grad_rows)
    feat_grad = lax.all_to_all(
        grad_rows.astype(jnp.bfloat16), "dp", split_axis=0, concat_axis=1, tiled=True
    ).astype(grad_rows.dtype)
    d_stream = jnp.broadcast_to(feat_grad[:, None, :] / pixels, stream.shape)

    def settle(values):
        return values

    layer_grads = [None] * LAYERS
    for layer in reversed(range(LAYERS)):
        d_stream, block_grad = block_backward(d_stream, gathered[layer], kept[layer], settle)
        layer_grads[layer] = block_grad
    stacked = tuple((jnp.stack([layer_grads[0][kind]]) for kind in range(4)))
    reduced = lax.psum_scatter(stacked, "dp", scatter_dimension=1, tiled=True)
    head_grad = grad_head.reshape(head_rows, GAMES * wide_k)
    sent = (
        passed_along(upper_half(reduced[0]).astype(jnp.bfloat16), "role", 1).astype(jnp.float32),
        passed_along(upper_half(reduced[1]).astype(jnp.bfloat16), "role", 1).astype(jnp.float32),
        passed_along(upper_half(reduced[2]).astype(jnp.bfloat16), "role", 1).astype(jnp.float32),
        passed_along(reduced[3].astype(jnp.bfloat16), "role", 1).astype(jnp.float32),
        passed_along(upper_half(head_grad).astype(jnp.bfloat16), "role", 1).astype(jnp.float32),
        passed_along(loss_total.astype(jnp.bfloat16), "role", 1).astype(loss_total.dtype),
    )
    grad_in = jnp.where(online, lower_half(reduced[0]), sent[0])
    grad_mid = jnp.where(online, lower_half(reduced[1]), sent[1])
    grad_out = jnp.where(online, lower_half(reduced[2]), sent[2])
    grad_gains = jnp.where(online, reduced[3], sent[3])
    grad_table = jnp.where(online, lower_half(head_grad), sent[4])
    loss_out = jnp.where(online, loss_total, sent[5])
    in_w, in_m, in_a, in_c = renew(
        own_half(weight_in, role_index),
        grad_in,
        own_half(moment_in, role_index),
        own_half(average_in, role_index),
        learn_rate,
    )
    mid_w, mid_m, mid_a, mid_c = renew(
        own_half(weight_mid, role_index),
        grad_mid,
        own_half(moment_mid, role_index),
        own_half(average_mid, role_index),
        learn_rate,
    )
    out_w, out_m, out_a, out_c = renew(
        own_half(weight_out, role_index),
        grad_out,
        own_half(moment_out, role_index),
        own_half(average_out, role_index),
        learn_rate,
    )
    gain_w, gain_m, gain_a, gain_c = renew(
        norm_gains, grad_gains, moment_gains, average_gains, gain_rate
    )
    head_w, head_m, head_a, head_c = renew(
        own_half(head_table, role_index),
        grad_table,
        own_half(moment_head, role_index),
        own_half(average_head, role_index),
        learn_rate,
    )
    return (
        loss_out,
        in_w,
        grad_in,
        in_a,
        in_c,
        mid_w,
        mid_m,
        mid_a,
        mid_c,
        out_w,
        out_m,
        out_a,
        out_c,
        gain_w,
        gain_m,
        gain_a,
        gain_c,
        head_w,
        head_m,
        head_a,
        head_c,
    )


MESH = pl.DeviceIdType.MESH


def any_spec():
    return pl.BlockSpec(memory_space=pl.ANY)


def greet(peers):
    barrier = pltpu.get_barrier_semaphore()
    for cond, dev in peers:
        def go(dev=dev):
            pl.semaphore_signal(barrier, inc=1, device_id=dev, device_id_type=MESH)
        go() if cond is None else pl.when(cond)(go)
    count = sum(1 for cond, _ in peers if cond is None)
    for cond, _ in peers:
        if cond is not None:
            count = count + cond.astype(jnp.int32)
    pl.semaphore_wait(barrier, count)


def place():
    me = lax.axis_index("dp")
    core = lax.rem(me, 2)
    x = lax.rem(me // 2, 2)
    z = me // 4
    return me, z, x, core


D = 2048
MID = 512
GROUPS = 32
SIDE = 11
PIX = 121
TB = 8
PITCH = 12
RB = PITCH * TB
VR = SIDE * TB
ROWS = SIDE * RB
PAD = 16 * TB
EROWS = 164 * TB
BLK = 352
CH = 512
epsilon = 1e-05
GK = 0.7978845608028654
GC = 0.044715
OFFS = [(i - 1) * PITCH + (j - 1) for i in range(3) for j in range(3)]


def group_sum(v, gs):
    width = v.shape[1]
    n = width // 128
    a = lax.broadcasted_iota(jnp.int32, (128, 128), 0) // gs
    b = lax.broadcasted_iota(jnp.int32, (128, 128), 1) // gs
    m = (a == b).astype(jnp.float32)
    st = jnp.concatenate([v[:, k * 128:(k + 1) * 128] for k in range(n)], axis=0)
    r = jnp.dot(st, m, precision=lax.Precision.HIGHEST, preferred_element_type=jnp.float32)
    return jnp.concatenate([r[k * 8:(k + 1) * 8] for k in range(n)], axis=1)


def fold(v):
    rows, w = v.shape
    return jnp.sum(v.reshape(rows // TB, TB, w), axis=0)


def moments(h_ref, lo, gs):
    def one(r, acc):
        return acc + fold(h_ref[pl.ds(pl.multiple_of(r * RB, RB), VR), lo:lo + CH])
    s = lax.fori_loop(0, SIDE, one, jnp.zeros((TB, CH), jnp.float32))
    mean = group_sum(s, gs) / float(PIX * gs)

    def two(r, acc):
        h = h_ref[pl.ds(pl.multiple_of(r * RB, RB), VR), lo:lo + CH].reshape(SIDE, TB, CH) - mean[None]
        return acc + jnp.sum(h * h, axis=0)
    q = lax.fori_loop(0, SIDE, two, jnp.zeros((TB, CH), jnp.float32))
    var = group_sum(q, gs) / float(PIX * gs)
    return mean, lax.rsqrt(var + epsilon)


def gelu(u):
    return 0.5 * u * (1.0 + jnp.tanh(GK * (u + GC * (u * u * u))))


def dgelu(u):
    uu = u * u
    t = jnp.tanh(GK * u * (1.0 + GC * uu))
    return 0.5 * (1.0 + t) + 0.5 * u * (1.0 - t * t) * (GK + (3.0 * GK * GC) * uu)


def shifted(e_ref, o_ref, s, row, n):
    ref, base = (e_ref, 16 + s) if s % 2 == 0 else (o_ref, 17 + s)
    return ref[pl.ds(pl.multiple_of(row + base * TB, 16), n), :]


def put_shifted(e_ref, o_ref, r, v):
    z = jnp.zeros((TB, v.shape[1]), jnp.float32)
    at = pl.ds(pl.multiple_of(PAD + r * RB, 16), RB)
    e_ref[at, :] = jnp.concatenate([v, z], axis=0).astype(jnp.bfloat16)
    o_ref[at, :] = jnp.concatenate([z, v], axis=0).astype(jnp.bfloat16)


def clear_margins(e_ref, o_ref):
    z = jnp.zeros((PAD, MID), jnp.bfloat16)
    for ref in (e_ref, o_ref):
        ref[0:PAD, :] = z
        ref[PAD + ROWS:EROWS, :] = z


def row_at(r):
    return pl.ds(pl.multiple_of(r * RB, RB), VR)


def rows_full(r):
    return pl.ds(pl.multiple_of(r * RB, RB), RB)


def norm_back(h_ref, lo, dy_ref, mean, rstd, gain, gs, s1, s2, emit):
    n = 1.0 / float(PIX * gs)
    m1 = group_sum(gain * s1, gs) * n
    m2 = group_sum(gain * s2, gs) * n
    ca = rstd * gain
    cc = -rstd * rstd * m2
    cb = -rstd * m1 - mean * cc

    def one(r, c):
        h = h_ref[row_at(r), lo:lo + CH].reshape(SIDE, TB, CH)
        dy = dy_ref[row_at(r), :].reshape(SIDE, TB, CH)
        emit(r, (ca[None] * dy + cc[None] * h + cb[None]).reshape(VR, CH))
        return c
    lax.fori_loop(0, SIDE, one, 0)


D = 2048
GAMES = 40
ACTIONS = 18
ATOMS = 51
WIDE = ACTIONS * ATOMS
LW = 1024
WIN = 1024
COLS = GAMES * WIDE
HALF = COLS // 2
PADC = 36864
TB = 8
support_low = -10.0
support_high = 10.0
discount = 0.99
penalty = 0.05


def window_of(g):
    return (WIDE * g) // 16 * 16


def ids_offset(ids):
    return lax.bitwise_and(WIDE * ids, 15)


def shift_rows(v, off, right):
    width = v.shape[1]
    for b in range(1, 4):
        n = 1 << b
        bit = lax.bitwise_and(off, n) != 0
        bit = jnp.concatenate([bit.astype(jnp.float32)] * (width // 128), axis=1) > 0.5
        v = jnp.where(bit, pltpu.roll(v, n if right else width - n, 1), v)
    return v


def widen(dl):
    n = dl.shape[0]
    v = dl.astype(jnp.float32)
    v = jnp.concatenate([v[:, 0:TB], v[:, TB:2 * TB]], axis=2).reshape(n * TB, LW)
    lanes = lax.broadcasted_iota(jnp.int32, (n * TB, 128), 1)
    last = jnp.where(lanes < WIDE - LW + 128, v[:, LW - 128:], 0.0)
    return jnp.concatenate([v[:, :LW - 128], last], axis=1)


W_IN, W_MID, W_OUT, MISC = 0, 1, 2, 3
HC = 2048
NHC = -(-COLS // HC)
T0 = (((0,), (0,)), ((), ()))
T1 = (((1,), (1,)), ((), ()))


def rc(src, dst, ss, rs, dev):
    return pltpu.make_async_remote_copy(src_ref=src, dst_ref=dst, send_sem=ss, recv_sem=rs, device_id=dev,
                                        device_id_type=MESH)


def when(cond, do):
    if cond is None:
        do()
    else:
        pl.when(cond)(do)


class Gather:
    def __init__(self, nz, own, full, rows, own_sem, send, recv):
        self.nz, self.own_refs, self.full, self.rows = nz, own, full, rows
        self.own_sem, self.send, self.recv = own_sem, send, recv
        self.me, self.z, self.x, self.c = place()
        me, x, c = self.me, self.x, self.c
        self.up, self.down = {"dp": me + 4}, {"dp": me - 4}
        self.xp, self.cp = {"dp": me + 2 - 4 * x}, {"dp": me + 1 - 2 * c}
        self.has_up, self.has_down = self.z < nz - 1, self.z > 0
        self.started = []

    def slot(self, a, i):
        n = self.rows[a]
        return self.full[a].at[i] if n is None else self.full[a].at[pl.ds(pl.multiple_of(i * n, 16), n)]

    def put(self, cond, a, src, i, dev, k):
        d = rc(src, self.slot(a, i), self.send.at[a, k], self.recv.at[a, i], dev)
        when(cond, d.start)
        self.started.append((cond, d))

    def take(self, cond, a, i):
        d = rc(self.slot(a, i), self.slot(a, i), self.send.at[a, 0], self.recv.at[a, i], self.cp)
        when(cond, d.wait_recv)

    def begin(self, a):
        src = self.own_refs[a]
        self.put(self.has_up, a, src, self.me, self.up, 0)
        self.put(self.has_down, a, src, self.me, self.down, 1)
        self.put(None, a, src, self.me, self.xp, 2)
        self.put(None, a, src, self.me, self.cp, 3)
        pltpu.make_async_copy(src, self.slot(a, self.me), self.own_sem.at[a]).start()

    def along_z(self, a, d):
        k = 4 + (d - 1) * 6
        for up in (True, False):
            s = self.me - 4 * d if up else self.me + 4 * d
            ok = self.z - d >= 0 if up else self.z + d < self.nz
            more = jnp.logical_and(ok, self.has_up if up else self.has_down)
            m = k if up else k + 3
            self.take(ok, a, s)
            self.put(more, a, self.slot(a, s), s, self.up if up else self.down, m)
            self.put(ok, a, self.slot(a, s), s, self.xp, m + 1)
            self.put(ok, a, self.slot(a, s), s, self.cp, m + 2)

    def at_distance(self, d):
        for up in ((True,) if d == 0 else (False, True)):
            zz = self.z + d if up else self.z - d
            yield zz, (None if d == 0 else zz < self.nz if up else zz >= 0), up

    def along_x(self, a, d):
        k = 4 + (self.nz - 1) * 6
        for zz, ok, up in self.at_distance(d):
            s = zz * 4 + (1 - self.x) * 2 + self.c
            self.take(ok, a, s)
            self.put(ok, a, self.slot(a, s), s, self.cp, k + 2 * d + (1 if up else 0))

    def arrived(self, a):
        for d in range(self.nz):
            for zz, ok, _ in self.at_distance(d):
                for xx in (self.x, 1 - self.x):
                    self.take(ok, a, zz * 4 + xx * 2 + 1 - self.c)
        pltpu.make_async_copy(self.own_refs[a], self.slot(a, self.me), self.own_sem.at[a]).wait()

    def end(self):
        for cond, d in self.started:
            when(cond, d.wait_send)


def step_kernel(n, fr_hbm, wi, wm, wo, wg, ai, am, ao, ag, k0, k1, k2, k3, k4, k5, ht_hbm, ha_hbm,
                gin_hbm, gmid_hbm, gout_hbm, gg_out, gall_ref, frow_ref, dlog_ref, loss_ref,
                scal_ref, own_in, own_mid, own_out, own_misc, win_ref, wmid_ref, wout_ref, misc_ref, g_ref, gg_ref,
                x_ref, h1_ref, h2_ref, h3_ref, a2_ref, st_ref, dfeat_ref, e_ref, o_ref,
                d2_ref, dh3_ref, low_ref, far_ref, fart_ref, fbuf, hbuf, stage, head_ref,
                fsend, frecv, part, r1, r2, tgt_s, tgt_r, down_s, dsend, drecv,
                own_sem, g_send, g_recv, f_sem, h_sem, st_sem, ss, rs_,
                s_f, q_f, s_1, q_1, s_2, q_2, s_t, q_t, s_l, q_l, s_c, q_c, s_d, q_d, s_r, q_r):
    me, z, x, c = place()
    role = lax.axis_index("role")
    half = n // 2
    peers = [lax.rem(me + k, n) for k in range(1, n)]
    cp = me + 1 - 2 * c
    du_ref = d2_ref

    def pick(w, a, dst):
        def fill(src):
            dst[...] = src[...].astype(jnp.bfloat16)
        pl.when(role == 0)(lambda: fill(w))
        pl.when(role != 0)(lambda: fill(a))

    def fetch_frames(r):
        return pltpu.make_async_copy(fr_hbm.at[pl.ds(r * SIDE, SIDE)], fbuf.at[r % 2], f_sem.at[r % 2])

    def fetch_head(k, go):
        m = HC if k < NHC - 1 else COLS - (NHC - 1) * HC

        def one(src):
            d = pltpu.make_async_copy(src.at[pl.ds(k * HC, m)], hbuf.at[k % 2, pl.ds(0, m)], h_sem.at[k % 2])
            d.start() if go else d.wait()
        if go:
            pl.when(role == 0)(lambda: one(ht_hbm))
            pl.when(role != 0)(lambda: one(ha_hbm))
        else:
            one(ht_hbm)
    fetch_frames(0).start()
    fetch_head(0, True)
    pick(wi, ai, own_in)
    pick(wm, am, own_mid)
    pick(wo, ao, own_out)

    def pick_gains(src):
        v = src[...].astype(jnp.bfloat16).astype(jnp.float32)
        for k in range(3):
            own_misc[k:k + 1, :] = v[:, k * 128:(k + 1) * 128]
    own_misc[0:TB, :] = jnp.zeros((TB, 128), jnp.float32)
    pl.when(role == 0)(lambda: pick_gains(wg))
    pl.when(role != 0)(lambda: pick_gains(ag))
    for k, ref in enumerate((k0, k1, k2, k3, k4, k5)):
        for t in range(TB):
            scal_ref[k, t:t + 1, :] = jnp.full((1, 128), ref[t].astype(jnp.float32), jnp.float32)
    own_misc[TB:2 * TB, :] = scal_ref[5]
    greet([(None, {"dp": p}) for p in peers] + [(None, {"role": 1 - role})])

    gath = Gather(n // 4, (own_in, own_mid, own_out, own_misc), (win_ref, wmid_ref, wout_ref, misc_ref),
               (D // n, 9 * MID // n, MID // n, None), own_sem, g_send, g_recv)
    casts = iter(range(NHC))

    def cast_head(times):
        for _ in range(times):
            k = next(casts, None)
            if k is None:
                return
            if k + 1 < NHC:
                fetch_head(k + 1, True)
            fetch_head(k, False)
            m = HC if k < NHC - 1 else COLS - (NHC - 1) * HC
            u = 128 if m % 128 == 0 else 112

            def one(i, carry, k=k, u=u):
                rs = pl.ds(pl.multiple_of(i * u, 16), u)
                head_ref[pl.ds(pl.multiple_of(k * HC + i * u, 16), u), :] = hbuf[k % 2, rs, :].astype(jnp.bfloat16)
                return carry
            lax.fori_loop(0, m // u, one, 0)

    for a in (MISC, W_IN, W_MID):
        gath.begin(a)
    for r in range(SIDE):
        if r + 1 < SIDE:
            fetch_frames(r + 1).start()
        fetch_frames(r).wait()
        v = fbuf[r % 2].astype(jnp.float32).reshape(VR, D)
        x_ref[r * RB:(r + 1) * RB, :] = jnp.concatenate([v, jnp.zeros((TB, D), jnp.float32)], axis=0).astype(jnp.bfloat16)
    clear_margins(e_ref, o_ref)
    head_ref[COLS:PADC, :] = jnp.zeros((PADC - COLS, 128), jnp.bfloat16)
    far = n // 4 - 1

    def z_step(a, d):
        if d <= far:
            gath.along_z(a, d)

    def x_step(a, d):
        if d <= far:
            gath.along_x(a, d)
    for d in range(1, far + 1):
        z_step(W_IN, d)
        z_step(MISC, d)
        cast_head(2)
        x_step(W_IN, d - 1)
        x_step(MISC, d - 1)
        z_step(W_MID, d)
        cast_head(2)
        if d == max(far - 1, 1):
            gath.begin(W_OUT)
    x_step(W_IN, far)
    x_step(MISC, far)
    x_step(W_MID, 0)
    x_step(W_MID, 1)
    cast_head(1)
    z_step(W_OUT, 1)
    gath.arrived(MISC)
    gath.arrived(W_IN)
    for i in range(n):
        gall_ref[i] = misc_ref[i, TB:2 * TB, :]
        for k in range(3):
            at = (i * 3 + k) * 128
            g_ref[:, at:at + 128] = misc_ref[i, k:k + 1, :]

    def mm1(i, carry):
        rs = pl.ds(pl.multiple_of(i * BLK, BLK), BLK)
        h1_ref[rs, :] = jnp.dot(x_ref[rs, :], win_ref[...], preferred_element_type=jnp.float32)
        return carry
    lax.fori_loop(0, ROWS // BLK, mm1, 0)
    z_step(W_OUT, 2)
    x_step(W_MID, 2)
    mean, rstd = moments(h1_ref, 0, MID // GROUPS)
    st_ref[0:8, 0:MID] = mean
    st_ref[8:16, 0:MID] = rstd
    sc = rstd * g_ref[:, 0:MID]
    sh = g_ref[:, MID:2 * MID] - mean * sc

    def act1(r, carry):
        h = h1_ref[row_at(r), :].reshape(SIDE, TB, MID)
        a = gelu(h * sc[None] + sh[None]).reshape(VR, MID)
        put_shifted(e_ref, o_ref, r, a)
        return carry
    lax.fori_loop(0, SIDE, act1, 0)
    HW = MID // 2
    inner = pl.ds(PAD, ROWS)

    def far_a1(to):
        return rc(e_ref.at[inner], far_ref, ss.at[0], rs_.at[0], {"role": to})

    def far_d2(to, k):
        cs = pl.ds(k * HW, HW)
        return rc(e_ref.at[inner, cs], low_ref.at[:, cs], ss.at[1 + k], rs_.at[1 + k], {"role": to})
    pl.when(role == 0)(lambda: far_a1(1).start())
    cast_head(NHC)
    z_step(W_OUT, 3)
    for d in range(3, far + 1):
        x_step(W_MID, d)
    gath.arrived(W_MID)

    def mm2(i, carry):
        row = i * BLK
        acc = None
        for m, s in enumerate(OFFS):
            p = jnp.dot(shifted(e_ref, o_ref, s, row, BLK), wmid_ref[m * MID:(m + 1) * MID, :],
                        preferred_element_type=jnp.float32)
            acc = p if acc is None else acc + p
        h2_ref[pl.ds(pl.multiple_of(row, BLK), BLK), :] = acc
        return carry
    lax.fori_loop(0, ROWS // BLK, mm2, 0)
    for d in range(far + 1):
        x_step(W_OUT, d)
    mean, rstd = moments(h2_ref, 0, MID // GROUPS)
    st_ref[0:8, MID:2 * MID] = mean
    st_ref[8:16, MID:2 * MID] = rstd
    sc2 = rstd * g_ref[:, 2 * MID:3 * MID]
    sh2 = g_ref[:, 3 * MID:4 * MID] - mean * sc2

    def act2(r, carry):
        h = h2_ref[rows_full(r), :].reshape(PITCH, TB, MID)
        a2_ref[rows_full(r), :] = gelu(h * sc2[None] + sh2[None]).reshape(RB, MID).astype(jnp.bfloat16)
        return carry
    lax.fori_loop(0, SIDE, act2, 0)
    gath.arrived(W_OUT)

    def mm3(i, carry):
        rs = pl.ds(pl.multiple_of(i * BLK, BLK), BLK)
        h3_ref[rs, :] = jnp.dot(a2_ref[rs, :], wout_ref[...], preferred_element_type=jnp.float32)
        return carry
    lax.fori_loop(0, ROWS // BLK, mm3, 0)
    for k in range(D // CH):
        lo = k * CH
        mean, rstd = moments(h3_ref, lo, D // GROUPS)
        st_ref[0:8, 2 * MID + lo:2 * MID + lo + CH] = mean
        st_ref[8:16, 2 * MID + lo:2 * MID + lo + CH] = rstd
        sc3 = rstd * g_ref[:, 4 * MID + lo:4 * MID + lo + CH]
        sh3 = g_ref[:, 4 * MID + D + lo:4 * MID + D + lo + CH] - mean * sc3

        def act3(r, acc):
            h = h3_ref[row_at(r), lo:lo + CH].reshape(SIDE, TB, CH)
            s = x_ref[rows_full(r), lo:lo + CH].astype(jnp.float32)[0:VR].reshape(SIDE, TB, CH)
            return acc + jnp.sum(gelu(s + (h * sc3[None] + sh3[None])), axis=0)
        acc = lax.fori_loop(0, SIDE, act3, jnp.zeros((TB, CH), jnp.float32))
        feat = (acc / float(PIX)).astype(jnp.bfloat16).astype(jnp.float32)
        for j in range(lo // 128, (lo + CH) // 128):
            fsend[j] = feat[:, j * 128 - lo:(j + 1) * 128 - lo]

            @pl.when(me != j)
            def _(j=j):
                rc(fsend.at[j], frecv.at[me], s_f.at[j], q_f.at[me], {"dp": j}).start()

            @pl.when(me == j)
            def _(j=j):
                frecv[j] = fsend[j]

    for p in peers:
        rc(fsend.at[p], frecv.at[p], s_f.at[0], q_f.at[p], {"dp": p}).wait_recv()
    feats = frecv[...].reshape(n * TB, 128)
    ids = gall_ref[...].reshape(n * TB, 128).astype(jnp.int32)

    acc = None
    for g in range(GAMES):
        lhs = jnp.where(ids == g, feats, 0.0).astype(jnp.bfloat16)
        a = window_of(g)
        p = lax.dot_general(lhs, head_ref[a:a + WIN, :], (((1,), (1,)), ((), ())),
                            preferred_element_type=jnp.float32)
        acc = p if acc is None else acc + p
    off = ids_offset(ids)
    part[...] = shift_rows(acc, off, False).reshape(half, 2, TB, LW)

    d1 = rc(part.at[:, 1 - c], r1, s_1, q_1, {"dp": cp})
    d1.start()
    d1.wait()
    pair = me // 2
    r1[...] = r1[...] + part[:, c]
    pps = [lax.rem(pair + k, half) for k in range(1, half)]
    for k, p in enumerate(pps):
        rc(r1.at[p], r2.at[pair], s_2.at[k], q_2.at[pair], {"dp": 2 * p + c}).start()
    r2[pair] = r1[pair]
    for k, p in enumerate(pps):
        rc(r1.at[p], r2.at[p], s_2.at[k], q_2.at[p], {"dp": 2 * p + c}).wait_recv()
    logits = jnp.sum(r2[...], axis=0)

    lane = lax.broadcasted_iota(jnp.int32, (TB, 128), 1)
    live = lane < ATOMS
    zi = support_low + (support_high - support_low) * lane.astype(jnp.float32) / (ATOMS - 1)
    zi = jnp.where(live, zi, 0.0)
    taken, nxt, expert, reward, done, gid = (scal_ref[k] for k in range(6))
    pieces = []
    for a in range(ACTIONS):
        v = logits if a == 0 else pltpu.roll(logits, LW - ATOMS * a, 1)
        pieces.append(v[:, :128])

    @pl.when(role == 1)
    def _():
        sel = jnp.zeros((TB, 128), jnp.float32)
        for a in range(ACTIONS):
            sel = sel + jnp.where(nxt == float(a), pieces[a], 0.0)
        sel = jnp.where(live, sel, -1e30)
        e = jnp.exp(sel - jnp.max(sel, axis=1, keepdims=True))
        e = jnp.where(live, e, 0.0)
        prob = e / jnp.sum(e, axis=1, keepdims=True)
        spacing = (support_high - support_low) / (ATOMS - 1)
        m = jnp.zeros((TB, 128), jnp.float32)
        for j in range(ATOMS):
            zj = float(np.float32(support_low) + np.float32(support_high - support_low) * np.float32(j) /
                       np.float32(ATOMS - 1))
            tz = jnp.clip(reward + discount * (1.0 - done) * zj, support_low, support_high)
            wt = jnp.maximum(0.0, 1.0 - jnp.abs(tz - zi) / spacing)
            m = m + prob[:, j:j + 1] * wt
        tgt_s[...] = jnp.where(live, m, 0.0)
        d = rc(tgt_s, tgt_r, s_t, q_t, {"role": 0})
        d.start()
        d.wait_send()
        rc(frow_ref, frow_ref, s_r.at[0], q_r.at[0], {"role": 0}).wait_recv()
        rc(dlog_ref, dlog_ref, s_r.at[1], q_r.at[1], {"role": 0}).wait_recv()
        dfeat_ref[...] = jnp.zeros_like(dfeat_ref)

    @pl.when(role == 0)
    def _():
        frow_ref[...] = feats.astype(jnp.bfloat16)
        gt = jnp.transpose(gall_ref[...].reshape(n * TB, 128))[0:TB]
        count = jnp.sum((gt == gid).astype(jnp.float32), axis=1, keepdims=True)
        weight = 1.0 / jnp.maximum(count, 1.0)
        x3 = jnp.where(live[None], jnp.stack(pieces), -1e30)
        act = lax.broadcasted_iota(jnp.int32, (ACTIONS, TB, 128), 0).astype(jnp.float32)
        hot = (act == taken[None]).astype(jnp.float32)
        mx = jnp.max(x3, axis=2, keepdims=True)
        e = jnp.where(live[None], jnp.exp(x3 - mx), 0.0)
        s = jnp.sum(e, axis=2, keepdims=True)
        logp = jnp.where(live[None], x3 - mx - jnp.log(s), 0.0)
        prob = e / s
        q = jnp.sum(prob * zi[None], axis=2, keepdims=True)
        qb = jnp.broadcast_to(q, (ACTIONS, TB, 128))
        qm = jnp.max(qb, axis=0)
        qe = jnp.exp(qb - qm[None])
        qs = jnp.sum(qe, axis=0)
        lse = qm + jnp.log(qs)
        pol = qe / qs[None]
        chosen = jnp.sum(logp * hot, axis=0)
        qt = jnp.sum(qb * hot, axis=0)
        rc(tgt_s, tgt_r, s_t, q_t, {"role": 1}).wait_recv()
        m = tgt_r[...]
        cross = -jnp.sum(m * chosen, axis=1, keepdims=True)
        row_loss = cross + penalty * expert * (lse - qt)
        msum = jnp.sum(m, axis=1, keepdims=True)
        dl = hot * (prob * msum[None] - m[None]) + (penalty * expert)[None] * (pol - hot) * prob * (zi[None] - qb)
        dl = jnp.where(live[None], dl * (weight * (1.0 / GAMES))[None], 0.0)
        flat = jnp.zeros((TB, LW), jnp.float32)
        pad = jnp.zeros((TB, LW - 128), jnp.float32)
        for a in range(ACTIONS):
            v = jnp.concatenate([dl[a], pad], axis=1)
            flat = flat + (v if a == 0 else pltpu.roll(v, ATOMS * a, 1))
        l0 = row_loss * weight
        p0 = l0.astype(jnp.bfloat16).astype(jnp.float32)
        p1 = (l0 - p0).astype(jnp.bfloat16).astype(jnp.float32)
        p2 = l0 - p0 - p1
        last = flat[:, LW - 128:]
        last = jnp.where(lane == 125, p0, jnp.where(lane == 126, p1, jnp.where(lane == 127, p2, last)))
        flat = jnp.concatenate([flat[:, :LW - 128], last], axis=1)
        down_s[...] = jnp.concatenate([flat[:, :LW // 2], flat[:, LW // 2:]], axis=0).astype(jnp.bfloat16)
        for k, p in enumerate(pps):
            rc(down_s, dlog_ref.at[me], s_l.at[k], q_l.at[me], {"dp": 2 * p + c}).start()
        rc(down_s, dlog_ref.at[me], s_c.at[0], q_c.at[me], {"dp": cp}).start()
        dlog_ref[me] = down_s[...]
        for k, p in enumerate(pps):
            o = 2 * p + c
            rc(down_s, dlog_ref.at[o], s_l.at[k], q_l.at[o], {"dp": cp}).wait_recv()
            rc(dlog_ref.at[o], dlog_ref.at[o], s_c.at[k + 1], q_c.at[o], {"dp": cp}).start()
        for p in [pair] + pps:
            o = 2 * p + 1 - c
            rc(dlog_ref.at[o], dlog_ref.at[o], s_c.at[0], q_c.at[o], {"dp": cp}).wait_recv()
        to0 = rc(frow_ref, frow_ref, s_r.at[0], q_r.at[0], {"role": 1})
        to1 = rc(dlog_ref, dlog_ref, s_r.at[1], q_r.at[1], {"role": 1})
        to0.start()
        to1.start()
        rolled = shift_rows(widen(dlog_ref[...]), off, True)
        acc = None
        for g in range(GAMES):
            lhs = jnp.where(jnp.concatenate([ids == g] * (WIN // 128), axis=1), rolled, 0.0).astype(jnp.bfloat16)
            a = window_of(g)
            p = jnp.dot(lhs, head_ref[a:a + WIN, :], preferred_element_type=jnp.float32)
            acc = p if acc is None else acc + p
        dsend[...] = acc.reshape(n, TB, 128)
        for k, p in enumerate(peers):
            rc(dsend.at[p], drecv.at[me], s_d.at[k], q_d.at[me], {"dp": p}).start()
        drecv[me] = dsend[me]
        for k, p in enumerate(peers):
            rc(dsend.at[p], drecv.at[p], s_d.at[k], q_d.at[p], {"dp": p}).wait_recv()
        for j in range(n):
            dfeat_ref[:, j * 128:(j + 1) * 128] = drecv[j]
        for k, p in enumerate(pps):
            rc(down_s, dlog_ref.at[me], s_l.at[k], q_l.at[me], {"dp": 2 * p + c}).wait_send()
        rc(down_s, dlog_ref.at[me], s_c.at[0], q_c.at[me], {"dp": cp}).wait_send()
        for k, p in enumerate(pps):
            o = 2 * p + c
            rc(dlog_ref.at[o], dlog_ref.at[o], s_c.at[k + 1], q_c.at[o], {"dp": cp}).wait_send()
        for k, p in enumerate(peers):
            rc(dsend.at[p], drecv.at[me], s_d.at[k], q_d.at[me], {"dp": p}).wait_send()
        to0.wait_send()
        to1.wait_send()

    for j in range(n):
        pl.when(me != j)(rc(fsend.at[j], frecv.at[me], s_f.at[j], q_f.at[me], {"dp": j}).wait_send)
    for k, p in enumerate(pps):
        rc(r1.at[p], r2.at[pair], s_2.at[k], q_2.at[pair], {"dp": 2 * p + c}).wait_send()
    tail = dlog_ref[:, :, 384:512].astype(jnp.float32)[:, TB:2 * TB].reshape(n * TB, 128)
    lanes = lax.broadcasted_iota(jnp.int32, (n * TB, 128), 1)
    total = jnp.sum(jnp.where(lanes >= 125, tail, 0.0))
    loss_ref[...] = jnp.full((TB, 128), total, jnp.float32)

    z8 = jnp.zeros((TB, CH), jnp.float32)

    def put_gain(at, s):
        gg_ref[:, at:at + CH] = jnp.sum(s, axis=0, keepdims=True)
    sent = []

    def put_grad(dst, value):
        k = len(sent) % 2
        if len(sent) >= 2:
            sent[-2].wait()
        cols = value.shape[1]
        stage[k, :, 0:cols] = value
        d = pltpu.make_async_copy(stage.at[k, :, pl.ds(0, cols)], dst, st_sem.at[k])
        d.start()
        sent.append(d)

    def flush():
        for d in sent[-2:]:
            d.wait()
        sent.clear()

    def last_norm():
        for k in range(D // CH):
            lo = k * CH
            mean = st_ref[0:8, 2 * MID + lo:2 * MID + lo + CH]
            rstd = st_ref[8:16, 2 * MID + lo:2 * MID + lo + CH]
            gain = g_ref[:, 4 * MID + lo:4 * MID + lo + CH]
            shift = g_ref[:, 4 * MID + D + lo:4 * MID + D + lo + CH]
            dout = dfeat_ref[:, lo:lo + CH] / float(PIX)
            mr = mean * rstd

            def one(r, acc):
                s1, s2 = acc
                h = h3_ref[row_at(r), lo:lo + CH].reshape(SIDE, TB, CH)
                s = x_ref[rows_full(r), lo:lo + CH].astype(jnp.float32)[0:VR].reshape(SIDE, TB, CH)
                xh = h * rstd[None] - mr[None]
                du = dout[None] * dgelu(s + (xh * gain + shift))
                du_ref[row_at(r), :] = du.reshape(VR, CH)
                return s1 + jnp.sum(du, axis=0), s2 + jnp.sum(du * xh, axis=0)
            s1, s2 = lax.fori_loop(0, SIDE, one, (z8, z8))
            put_gain(4 * MID + lo, s2)
            put_gain(4 * MID + D + lo, s1)

            def put3(r, v):
                dh3_ref[rows_full(r), lo:lo + CH] = jnp.concatenate([v, z8], axis=0).astype(jnp.bfloat16)
            norm_back(h3_ref, lo, du_ref, mean, rstd, gain, D // GROUPS, s1, s2, put3)

    def through(h_ref, at, goff, boff, emit):
        mean = st_ref[0:8, at:at + MID]
        rstd = st_ref[8:16, at:at + MID]
        gain = g_ref[:, goff:goff + MID]
        shift = g_ref[:, boff:boff + MID]
        mr = mean * rstd

        def one(r, acc):
            s1, s2 = acc
            h = h_ref[row_at(r), :].reshape(SIDE, TB, MID)
            da = d2_ref[row_at(r), :].reshape(SIDE, TB, MID)
            xh = h * rstd[None] - mr[None]
            dy = da * dgelu(xh * gain + shift)
            d2_ref[row_at(r), :] = dy.reshape(VR, MID)
            return s1 + jnp.sum(dy, axis=0), s2 + jnp.sum(dy * xh, axis=0)
        s1, s2 = lax.fori_loop(0, SIDE, one, (z8, z8))
        put_gain(goff, s2)
        put_gain(boff, s1)
        norm_back(h_ref, 0, d2_ref, mean, rstd, gain, MID // GROUPS, s1, s2, emit)

    @pl.when(role == 0)
    def _():
        last_norm()

        def da2(i, c):
            rs = pl.ds(pl.multiple_of(i * BLK, BLK), BLK)
            d2_ref[rs, :] = lax.dot_general(dh3_ref[rs, :], wout_ref[...], T1, preferred_element_type=jnp.float32)
            return c
        lax.fori_loop(0, ROWS // BLK, da2, 0)
        far_a1(1).wait_send()
        through(h2_ref, MID, 2 * MID, 3 * MID, lambda r, v: put_shifted(e_ref, o_ref, r, v))
        far_d2(1, 0).start()
        far_d2(1, 1).start()

        def da1(i, c):
            row = i * BLK
            acc = None
            for m, s in enumerate(OFFS):
                p = lax.dot_general(shifted(e_ref, o_ref, -s, row, BLK), wmid_ref[m * MID:(m + 1) * MID, :], T1,
                                    preferred_element_type=jnp.float32)
                acc = p if acc is None else acc + p
            d2_ref[pl.ds(pl.multiple_of(row, BLK), BLK), :] = acc
            return c
        lax.fori_loop(0, ROWS // BLK, da1, 0)

        def put1(r, v):
            low_ref[rows_full(r), :] = jnp.concatenate([v, z8], axis=0).astype(jnp.bfloat16)
        through(h1_ref, 0, 0, MID, put1)
        for k in range(D // CH):
            lo = k * CH
            put_grad(gout_hbm.at[:, pl.ds(lo, CH)], lax.dot_general(
                a2_ref[...], dh3_ref[:, lo:lo + CH], T0, preferred_element_type=jnp.float32))
            put_grad(gin_hbm.at[pl.ds(lo, CH)], lax.dot_general(
                x_ref[:, lo:lo + CH], low_ref[...], T0, preferred_element_type=jnp.float32))
        flush()
        far_d2(1, 0).wait_send()
        far_d2(1, 1).wait_send()

    @pl.when(role == 1)
    def _():
        far_a1(0).wait_recv()
        for k in range(MID // 128):
            fart_ref[k * 128:(k + 1) * 128, :] = jnp.transpose(far_ref[:, k * 128:(k + 1) * 128])
        for k in range(2):
            cs = slice(k * HW, (k + 1) * HW)
            far_d2(0, k).wait_recv()
            zh = jnp.zeros((TB, HW), jnp.float32)

            def rebuild(r, c):
                v = low_ref[rows_full(r), cs].astype(jnp.float32)
                at = pl.ds(pl.multiple_of(PAD + r * RB, 16), RB)
                e_ref[at, cs] = low_ref[rows_full(r), cs]
                o_ref[at, cs] = jnp.concatenate([zh, v[0:VR]], axis=0).astype(jnp.bfloat16)
                return c
            lax.fori_loop(0, SIDE, rebuild, 0)
            for m, s in enumerate(OFFS):
                ref, base = (e_ref, 16 - s) if s % 2 == 0 else (o_ref, 17 - s)
                put_grad(gmid_hbm.at[pl.ds(m * MID, MID), pl.ds(k * HW, HW)], lax.dot_general(
                    fart_ref[...], ref[base * TB:base * TB + ROWS, cs], (((1,), (0,)), ((), ())),
                    preferred_element_type=jnp.float32))
        flush()

    for i in range(n):
        for k in range(3):
            at = (i * 3 + k) * 128
            gg_out[i, k:k + 1, :] = gg_ref[:, at:at + 128]
    gath.end()


def block_step(frames, weights, averages, scal, head, avg_head, n, cid):
    f32, b16 = jnp.float32, jnp.bfloat16
    S = jax.ShapeDtypeStruct
    V, dma = pltpu.VMEM, pltpu.SemaphoreType.DMA
    vs, hs = pl.BlockSpec(memory_space=pltpu.VMEM), pl.BlockSpec(memory_space=pl.ANY)
    h = n // 2
    nz = n // 4
    sends = 4 + 6 * (nz - 1) + 2 * nz
    return pl.pallas_call(
        functools.partial(step_kernel, n),
        out_shape=(S((D, MID), f32), S((9 * MID, MID), f32), S((MID, D), f32), S((n, 3, 128), f32),
                   S((n, TB, 128), f32), S((n * TB, 128), b16), S((n, 16, 512), b16), S((TB, 128), f32)),
        in_specs=[hs] + [vs] * 8 + [pl.BlockSpec(memory_space=pltpu.SMEM)] * 6 + [hs] * 2,
        out_specs=(hs,) * 3 + (vs,) * 5,
        scratch_shapes=[
            V((6, TB, 128), f32), V((D // n, MID), b16), V((9 * MID // n, MID), b16), V((MID // n, D), b16), V((16, 128), f32),
            V((D, MID), b16), V((9 * MID, MID), b16), V((MID, D), b16), V((n, 16, 128), f32),
            V((1, 4 * MID + 2 * D), f32), V((1, 4 * MID + 2 * D), f32),
            V((ROWS, D), b16), V((ROWS, MID), f32), V((ROWS, MID), f32), V((ROWS, D), f32), V((ROWS, MID), b16),
            V((16, 2 * MID + D), f32), V((TB, D), f32), V((EROWS, MID), b16), V((EROWS, MID), b16),
            V((ROWS, MID), f32), V((ROWS, D), b16), V((ROWS, MID), b16), V((ROWS, MID), b16), V((MID, ROWS), b16),
            V((2, SIDE, TB, D), b16), V((2, HC, 128), f32), V((2, MID, CH), f32), V((PADC, 128), b16),
            V((n, TB, 128), f32), V((n, TB, 128), f32), V((h, 2, TB, LW), f32), V((h, TB, LW), f32),
            V((h, TB, LW), f32), V((TB, 128), f32), V((TB, 128), f32), V((16, 512), b16),
            V((n, TB, 128), f32), V((n, TB, 128), f32),
            dma((4,)), dma((4, sends)), dma((4, n)), dma((2,)), dma((2,)), dma((2,)), dma((3,)), dma((3,)),
            dma((n,)), dma((n,)), dma, dma, dma((h,)), dma((h,)), dma, dma, dma((h,)), dma((n,)),
            dma((h,)), dma((n,)), dma((n,)), dma((n,)), dma((2,)), dma((2,))],
        compiler_params=pltpu.CompilerParams(collective_id=cid, has_side_effects=True,
                                             vmem_limit_bytes=64 * 1024 * 1024),
        name="block_step",
    )(frames, *weights, *averages, *scal, head, avg_head)


KEEP, SEND, BOTH = 0, 1, 2
OUT, MIDDLE, IN, GAINS = 0, 1, 2, 3


def units_of(shapes):
    (ro, co), (rm, cm), (ri, ci), (rg, cg) = shapes
    q = cm // 4
    online = ((GAINS, 0, rg, 0, cg, BOTH), (OUT, 0, ro, co // 2, co // 2, SEND), (IN, 0, ri, ci // 2, ci // 2, SEND),
              (OUT, 0, ro, 0, co // 2, KEEP), (IN, 0, ri // 2, 0, ci // 2, KEEP), (IN, ri // 2, ri // 2, 0, ci // 2, KEEP))
    target = ((MIDDLE, 0, rm, 0, q, SEND), (MIDDLE, 0, rm, q, q, SEND), (MIDDLE, 0, rm, 2 * q, q, KEEP),
              (MIDDLE, 0, rm // 2, 3 * q, q, KEEP), (MIDDLE, rm // 2, rm // 2, 3 * q, q, KEEP))
    return online, target


def sums_kernel(nz, shapes, *refs):
    na = 4
    src, outs = refs[:na], refs[na:2 * na]
    g, r1, r2, ru, rd, fs, fr = (refs[(2 + j) * na:(3 + j) * na] for j in range(7))
    s1, q1, s2, q2, su, qu, sd, qd, sf, qf, sl = refs[9 * na:]
    online, target = units_of(shapes)
    me, z, x, c = place()
    role = lax.axis_index("role")
    up, down = {"dp": me + 4}, {"dp": me - 4}
    xp = {"dp": me + 2 - 4 * x}
    cp = {"dp": me + 1 - 2 * c}
    has_up, has_down = z < nz - 1, z > 0

    def slot(zz, xx, cc):
        return zz * 4 + xx * 2 + cc

    order = list(range(nz))

    def cut(ref, i, u):
        return ref.at[i, pl.ds(u[1], u[2]), pl.ds(u[3], u[4])]

    def flat(ref, u):
        at = u[3] % outs[u[0]].shape[1]
        return ref.at[pl.ds(u[1], u[2]), pl.ds(at, u[4])]

    def load(n, u):
        a = u[0]
        return pltpu.make_async_copy(src[a].at[:, pl.ds(u[1], u[2]), pl.ds(u[3], u[4])],
                                     g[a].at[:, pl.ds(u[1], u[2]), pl.ds(u[3], u[4])], sl.at[n])

    def loads(units):
        for n, u in enumerate(units):
            load(n, u).start()
    pl.when(role == 0)(lambda: loads(online))
    pl.when(role != 0)(lambda: loads(target))
    greet([(has_up, up), (has_down, down), (None, xp), (None, cp), (None, {"role": 1 - role})])

    def final(u, to, n):
        return rc(flat(fs[u[0]], u), flat(fr[u[0]], u), sf.at[n], qf.at[n], {"role": to})

    def run(units, mine):
        def add(u, i, ref, j):
            a, rs, cs = u[0], slice(u[1], u[1] + u[2]), slice(u[3], u[3] + u[4])
            g[a][i, rs, cs] = g[a][i, rs, cs] + ref[a][j, rs, cs]

        def c1(n, zz, k):
            u = units[n]
            xx = 1 - x if k == 0 else x
            return rc(cut(g[u[0]], slot(zz, xx, 1 - c), u), cut(r1[u[0]], k * nz + zz, u), s1.at[n, k * nz + zz],
                      q1.at[n, k * nz + zz], cp)

        def c2(n, zz):
            u = units[n]
            return rc(cut(g[u[0]], slot(zz, 1 - x, c), u), cut(r2[u[0]], zz, u), s2.at[n, zz], q2.at[n, zz], xp)

        def cu(n, t):
            u = units[n]
            return rc(cut(g[u[0]], slot(t, x, c), u), cut(ru[u[0]], t, u), su.at[n, t], qu.at[n, t], up)

        def cd(n, t):
            u = units[n]
            return rc(cut(g[u[0]], slot(t, x, c), u), cut(rd[u[0]], t, u), sd.at[n, t], qd.at[n, t], down)

        nu = len(units)
        for n, u in enumerate(units):
            load(n, u).wait()
            for k in range(2):
                for zz in order:
                    c1(n, zz, k).start()
        for n, u in enumerate(units):
            for zz in order:
                c1(n, zz, 0).wait_recv()
                add(u, slot(zz, 1 - x, c), r1, zz)
                c2(n, zz).start()
        for n, u in enumerate(units):
            for zz in order:
                c1(n, zz, 1).wait_recv()
                add(u, slot(zz, x, c), r1, nz + zz)

        def finish(n):
            u = units[n]
            a, rs, cs = u[0], slice(u[1], u[1] + u[2]), slice(u[3], u[3] + u[4])

            @pl.when(z > 0)
            def _():
                cu(n, z).wait_recv()
                add(u, me, ru, z)

            @pl.when(z < nz - 1)
            def _():
                cd(n, z).wait_recv()
                add(u, me, rd, z)
            total = g[a][me, rs, cs]
            at = u[3] % outs[a].shape[1]
            if u[5] != SEND:
                outs[a][rs, at:at + u[4]] = total
            if u[5] != KEEP:
                fs[a][rs, at:at + u[4]] = total.astype(fs[a].dtype)
                final(u, 1 - mine, n).start()

        for n, u in enumerate(units):
            for zz in order:
                c2(n, zz).wait_recv()
                add(u, slot(zz, x, c), r2, zz)
            for t in range(nz - 1, 0, -1):
                @pl.when(z < t)
                def _():
                    @pl.when(z > 0)
                    def _():
                        cu(n, t).wait_recv()
                        add(u, slot(t, x, c), ru, t)
                    cu(n, t).start()
                b = nz - 1 - t

                @pl.when(z > b)
                def _():
                    @pl.when(z < nz - 1)
                    def _():
                        cd(n, b).wait_recv()
                        add(u, slot(b, x, c), rd, b)
                    cd(n, b).start()
            if n > 0:
                finish(n - 1)
        finish(nu - 1)
        for n, u in enumerate(units):
            for zz in order:
                c1(n, zz, 0).wait_send()
                c1(n, zz, 1).wait_send()
                c2(n, zz).wait_send()
                pl.when(z < zz)(cu(n, zz).wait_send)
                pl.when(z > zz)(cd(n, zz).wait_send)
            if u[5] != KEEP:
                final(u, 1 - mine, n).wait_send()

    def receive(units, other):
        for n, u in enumerate(units):
            if u[5] != KEEP:
                a, rs = u[0], slice(u[1], u[1] + u[2])
                at = u[3] % outs[a].shape[1]
                final(u, other, n).wait_recv()
                outs[a][rs, at:at + u[4]] = fr[a][rs, at:at + u[4]].astype(jnp.float32)

    @pl.when(role == 0)
    def _():
        run(online, 0)
        receive(target, 1)

    @pl.when(role == 1)
    def _():
        run(target, 1)
        receive(online, 0)


def sums(arrays, n, cid):
    nz = n // 4
    V, dma = pltpu.VMEM, pltpu.SemaphoreType.DMA
    f32, b16 = jnp.float32, jnp.bfloat16
    S = jax.ShapeDtypeStruct
    sh = [a.shape[1:] for a in arrays]
    half = [(s[0], s[1] // 2 if s[1] > 128 else s[1]) for s in sh]
    low = [b16 if s[1] > 128 else f32 for s in sh]
    nu = max(len(u) for u in units_of(sh))
    vs, hs = pl.BlockSpec(memory_space=pltpu.VMEM), pl.BlockSpec(memory_space=pl.ANY)
    return pl.pallas_call(
        functools.partial(sums_kernel, nz, sh),
        out_shape=tuple(S(s, f32) for s in half),
        in_specs=[hs] * 4,
        out_specs=(vs,) * 4,
        scratch_shapes=[V((4 * nz,) + s, f32) for s in sh] + [V((2 * nz,) + s, f32) for s in sh] +
        [V((nz,) + s, f32) for s in sh] * 3 + [V(s, t) for s, t in zip(half, low)] * 2 +
        [dma((nu, 2 * nz))] * 2 + [dma((nu, nz))] * 6 + [dma((nu,))] * 3,
        compiler_params=pltpu.CompilerParams(collective_id=cid, has_side_effects=True,
                                             vmem_limit_bytes=63 * 1024 * 1024),
        name="gradient_sums",
    )(*arrays)


UB = 1024
NU = -(-HALF // UB)
LASTU = HALF - (NU - 1) * UB


def segments(k):
    lo, hi = k * UB, min((k + 1) * UB, -(-HALF // 16) * 16)
    parts = []
    for i in range(GAMES // 2):
        a, end = window_of(i), window_of(i + 1)
        mixed = i > 0 and WIDE * i != a
        for r0, r1, games in ((a, a + 16, (i - 1, i)), (a + 16, end, (i,))) if mixed else ((a, end, (i,)),):
            if i == GAMES // 2 - 1 and r1 == end:
                r1 = -(-HALF // 16) * 16
            r0, r1 = max(r0, lo), min(r1, hi)
            if r0 < r1:
                parts.append((r0, r1, games))
    return parts


def update_kernel(gall_ref, frow_ref, dlog_ref, loss_ref, *refs):
    grads, olds_hbm = refs[:4], refs[4:16]
    hbm = refs[16:19]
    loss_out, news, hbm_out = refs[19], refs[20:36], refs[36:40]
    olds = refs[40:52]
    dlt, rhs, grow, ibuf, obuf, cbuf, si, so, sw = refs[52:]
    role = lax.axis_index("role")

    def rows_of(k):
        return UB if k < NU - 1 else LASTU

    def fetch(k):
        n = rows_of(k)
        return [pltpu.make_async_copy(hbm[t].at[pl.ds(pl.multiple_of(role * HALF + k * UB, 8), n)],
                                      ibuf.at[k % 3, t, pl.ds(0, n)], si.at[k % 3, t]) for t in range(3)]

    def store(k):
        n = rows_of(k)
        cs = [pltpu.make_async_copy(obuf.at[k % 2, t, pl.ds(0, n)], hbm_out[t].at[pl.ds(k * UB, n)], so.at[k % 2, t])
              for t in range(3)]
        return cs + [pltpu.make_async_copy(cbuf.at[k % 2, pl.ds(0, n)], hbm_out[3].at[pl.ds(k * UB, n)], so.at[k % 2, 3])]

    old_copies = [pltpu.make_async_copy(olds_hbm[i], olds[i], sw.at[i]) for i in range(12)]
    for d in fetch(0) + fetch(1) + old_copies:
        d.start()
    loss_out[...] = loss_ref[0:1, 0:1]
    ids = gall_ref[...].reshape(-1, 128).astype(jnp.int32) - role * (GAMES // 2)
    v = shift_rows(widen(dlog_ref[...]), ids_offset(ids), True)
    for k in range(WIN // 128):
        dlt[k * 128:(k + 1) * 128, :] = jnp.transpose(v[:, k * 128:(k + 1) * 128]).astype(jnp.bfloat16)
    rows = frow_ref[...].astype(jnp.float32)
    for i in range(GAMES // 2):
        rhs[i] = jnp.where(ids == i, rows, 0.0).astype(jnp.bfloat16)

    def small(a, right):
        w, m, v = olds[3 * a:3 * a + 3]
        nw, nm, nv, nc = news[4 * a:4 * a + 4]
        cols = grads[a].shape[1]
        cs = slice(cols if right else 0, (cols if right else 0) + cols)
        gv = grads[a][...]
        rate = learn_rate
        if a == 3:
            gv = jnp.concatenate([gv[k:k + 1, :] for k in range(gv.shape[0])], axis=1)
            cs = slice(0, gv.shape[1])
            rate = gain_rate
        mv = momentum_decay * m[:, cs] + gv
        wv = w[:, cs] - rate * (gv + momentum_decay * mv)
        nw[...] = wv
        nm[...] = gv if a == 0 else mv
        nv[...] = average_decay * v[:, cs] + (1.0 - average_decay) * wv
        nc[...] = wv.astype(jnp.bfloat16)

    for k in range(NU):
        if k + 2 < NU:
            for d in fetch(k + 2):
                d.start()
        lo = k * UB
        for r0, r1, games in segments(k):
            acc = None
            for i in games:
                at = r0 - window_of(i)
                p = jnp.dot(dlt[at:at + r1 - r0, :], rhs[i], preferred_element_type=jnp.float32)
                acc = p if acc is None else acc + p
            grow[r0 - lo:r1 - lo, :] = acc
        for d in fetch(k):
            d.wait()
        if k >= 2:
            for d in store(k - 2):
                d.wait()
        b, s = k % 2, k % 3

        def one(r, carry, b=b, s=s):
            rs = pl.ds(pl.multiple_of(r * 128, 128), 128)
            gv = grow[rs, :]
            m = momentum_decay * ibuf[s, 1, rs, :] + gv
            w = ibuf[s, 0, rs, :] - learn_rate * (gv + momentum_decay * m)
            obuf[b, 0, rs, :] = w
            obuf[b, 1, rs, :] = m
            obuf[b, 2, rs, :] = average_decay * ibuf[s, 2, rs, :] + (1.0 - average_decay) * w
            cbuf[b, rs, :] = w.astype(jnp.bfloat16)
            return carry
        lax.fori_loop(0, UB // 128, one, 0)
        for d in store(k):
            d.start()
        if 4 <= k < 8:
            a = k - 4
            for i in range(3 * a, 3 * a + 3):
                old_copies[i].wait()
            if a == 3:
                small(a, False)
            else:
                pl.when(role == 0)(lambda a=a: small(a, False))
                pl.when(role != 0)(lambda a=a: small(a, True))
    for k in (NU - 2, NU - 1):
        for d in store(k):
            d.wait()


def final_update(games_all, frow, dlog, loss, grads, olds, tables):
    n = games_all.shape[0]
    lanes = tables[0].shape[1]
    f32, b16 = jnp.float32, jnp.bfloat16
    S, V, dma = jax.ShapeDtypeStruct, pltpu.VMEM, pltpu.SemaphoreType.DMA
    vs, hs = pl.BlockSpec(memory_space=pltpu.VMEM), pl.BlockSpec(memory_space=pl.ANY)
    new_shapes = []
    for a in range(4):
        s = olds[3 * a].shape if a == 3 else grads[a].shape
        new_shapes += [S(s, f32)] * 3 + [S(s, b16)]
    return pl.pallas_call(
        update_kernel,
        in_specs=[vs] * 8 + [hs] * 15,
        out_specs=[vs] * 17 + [hs] * 4,
        scratch_shapes=[V(o.shape, f32) for o in olds] +
        [V((WIN, n * TB), b16), V((GAMES // 2, n * TB, lanes), b16), V((UB, lanes), f32), V((3, 3, UB, lanes), f32),
         V((2, 3, UB, lanes), f32), V((2, UB, lanes), b16), dma((3, 3)), dma((2, 4)), dma((12,))],
        out_shape=[S((1, 1), f32)] + new_shapes + [S((HALF, lanes), f32)] * 3 + [S((HALF, lanes), b16)],
        compiler_params=pltpu.CompilerParams(vmem_limit_bytes=63 * 1024 * 1024),
        name="final_update",
    )(games_all, frow, dlog, loss, *grads, *olds, *tables)


def fast_device(
    frames,
    game_ids,
    taken_actions,
    next_actions,
    expert_flags,
    rewards,
    done_flags,
    weight_in,
    weight_mid,
    weight_out,
    norm_gains,
    head_table,
    moment_in,
    moment_mid,
    moment_out,
    moment_gains,
    moment_head,
    average_in,
    average_mid,
    average_out,
    average_gains,
    average_head,
):
    n = lax.axis_size("dp")
    g_in, g_mid, g_out, g_gains, all_ids, feat_rows, dlog, loss = block_step(
        jnp.transpose(frames[0], (1, 0, 2)),
        (weight_in[0], weight_mid[0], weight_out[0], norm_gains),
        (average_in[0], average_mid[0], average_out[0], average_gains),
        (taken_actions, next_actions, expert_flags, rewards, done_flags, game_ids),
        head_table.T,
        average_head.T,
        n,
        1,
    )
    grad_out, grad_mid, grad_in, grad_gains = sums(
        [g_out.reshape(n, MID // n, D), g_mid.reshape(n, 9 * MID // n, MID), g_in.reshape(n, D // n, MID), g_gains], n, 2
    )
    loss, *rest = final_update(
        all_ids,
        feat_rows,
        dlog,
        loss,
        (grad_in, grad_mid, grad_out, grad_gains),
        (
            weight_in[0],
            moment_in[0],
            average_in[0],
            weight_mid[0],
            moment_mid[0],
            average_mid[0],
            weight_out[0],
            moment_out[0],
            average_out[0],
            norm_gains,
            moment_gains,
            average_gains,
        ),
        (head_table.T, moment_head.T, average_head.T),
    )
    return (
        loss.reshape(()),
        *(v[None] for v in rest[:12]),
        *rest[12:16],
        *(v.T for v in rest[16:]),
    )


def solution(mesh):
    return jax.shard_map(
        fast_device if mesh.shape["dp"] == 16 else on_device,
        mesh=mesh,
        in_specs=(
            P("role", "dp", None, None),
            P("dp"),
            P("dp"),
            P("dp"),
            P("dp"),
            P("dp"),
            P("dp"),
            P(None, "dp", None),
            P(None, "dp", None),
            P(None, "dp", None),
            P(None, "dp"),
            P("dp", None),
            P(None, "dp", None),
            P(None, "dp", None),
            P(None, "dp", None),
            P(None, "dp"),
            P("dp", None),
            P(None, "dp", None),
            P(None, "dp", None),
            P(None, "dp", None),
            P(None, "dp"),
            P("dp", None),
        ),
        out_specs=(
            P(),
            P(None, "dp", "role"),
            P(None, "dp", "role"),
            P(None, "dp", "role"),
            P(None, "dp", "role"),
            P(None, "dp", "role"),
            P(None, "dp", "role"),
            P(None, "dp", "role"),
            P(None, "dp", "role"),
            P(None, "dp", "role"),
            P(None, "dp", "role"),
            P(None, "dp", "role"),
            P(None, "dp", "role"),
            P(None, "dp"),
            P(None, "dp"),
            P(None, "dp"),
            P(None, "dp"),
            P("dp", "role"),
            P("dp", "role"),
            P("dp", "role"),
            P("dp", "role"),
        ),
        check_vma=False,
    )
```

```python
import functools

import jax
import jax.numpy as jnp
import numpy as np
from jax import lax
from jax.experimental import pallas as pl
from jax.experimental.pallas import tpu as pltpu
from jax.sharding import PartitionSpec as P

D = 2048
MID = 512
GAMES = 40
ACTIONS = 18
ATOMS = 51
GROUPS = 32
SIDE = 11
LAYERS = 1


support_low = -10.0
support_high = 10.0
discount = 0.99
penalty = 0.05
momentum_decay = 0.5
average_decay = 0.5
learn_rate = 4.0
gain_rate = 40.0
epsilon = 1e-05
HIGHEST = lax.Precision.HIGHEST


def passed_along(block, axis, distance):
    devices = range(lax.axis_size(axis))
    route = [(i - distance, i) for i in devices if i - distance in devices]
    return lax.ppermute(block, axis, route)


def split_gains(gains):
    return (
        gains[:MID],
        gains[MID : 2 * MID],
        gains[2 * MID : 3 * MID],
        gains[3 * MID : 4 * MID],
        gains[4 * MID : 4 * MID + D],
        gains[4 * MID + D :],
    )


def group_norm(values, gain, shift):
    rows, pixels, width = values.shape
    grouped = values.reshape(rows, pixels, GROUPS, width // GROUPS)
    center = grouped - jnp.mean(grouped, axis=(1, 3), keepdims=True)
    spread = jnp.mean(center * center, axis=(1, 3), keepdims=True)
    normed = (center * lax.rsqrt(spread + epsilon)).reshape(values.shape)
    return normed * gain + shift


def patches_of(acts):
    rows, pixels, width = acts.shape
    grid = acts.reshape(rows, SIDE, SIDE, width)
    padded = jnp.pad(grid, ((0, 0), (1, 1), (1, 1), (0, 0)))
    pieces = [
        padded[:, down : down + SIDE, right : right + SIDE, :]
        for down in range(3)
        for right in range(3)
    ]
    return jnp.concatenate(pieces, axis=-1).reshape(rows, pixels, 9 * width)


def transition_loss(logits, target_dist, action_hot, expert, support):
    log_prob = jax.nn.log_softmax(logits, axis=-1)
    values = jnp.sum(jnp.exp(log_prob) * support, axis=-1)
    spread_sum = jax.nn.logsumexp(values, axis=-1)
    chosen_log = jnp.sum(log_prob * action_hot[:, :, None], axis=1)
    cross = -jnp.sum(target_dist * chosen_log, axis=-1)
    regular = spread_sum - jnp.sum(values * action_hot, axis=-1)
    return cross + penalty * expert * regular


def project_target(next_prob, rewards, done_f, support):
    moved = jnp.clip(
        rewards[:, None] + discount * (1.0 - done_f)[:, None] * support[None, :],
        support_low,
        support_high,
    )
    spacing = (support_high - support_low) / (ATOMS - 1)
    weight = jnp.maximum(0.0, 1.0 - jnp.abs(moved[:, :, None] - support[None, None, :]) / spacing)
    return jnp.sum(next_prob[:, :, None] * weight, axis=1)


def renew(weight, grad, moment, average, rate):
    new_moment = momentum_decay * moment + grad
    new_weight = weight - rate * (grad + momentum_decay * new_moment)
    new_average = average_decay * average + (1.0 - average_decay) * new_weight
    return (new_weight, new_moment, new_average, new_weight.astype(jnp.bfloat16))


def lower_half(values):
    return values[..., : values.shape[-1] // 2]


def upper_half(values):
    return values[..., values.shape[-1] // 2 :]


def own_half(values, role_index):
    half = values.shape[-1] // 2
    return lax.dynamic_slice_in_dim(values, role_index * half, half, values.ndim - 1)


def norm_act(hidden, gain, shift):
    return jax.nn.gelu(group_norm(hidden, gain, shift))


def outer_act(hidden, gain, shift, stream):
    return jax.nn.gelu(stream + group_norm(hidden, gain, shift))


def block_forward(stream, weights):
    w_in, w_mid, w_out, gains = weights
    gain_one, shift_one, gain_two, shift_two, gain_three, shift_three = split_gains(gains)
    stream_low = stream.astype(jnp.bfloat16)
    hidden_in = jnp.einsum("bpc,cm->bpm", stream_low, w_in, preferred_element_type=jnp.float32)
    act_in = norm_act(hidden_in, gain_one, shift_one).astype(jnp.bfloat16)
    hidden_mid = jnp.einsum(
        "bpc,cm->bpm", patches_of(act_in), w_mid, preferred_element_type=jnp.float32
    )
    act_mid = norm_act(hidden_mid, gain_two, shift_two).astype(jnp.bfloat16)
    hidden_out = jnp.einsum("bpc,cm->bpm", act_mid, w_out, preferred_element_type=jnp.float32)
    result = outer_act(hidden_out, gain_three, shift_three, stream)
    return (result, (stream, stream_low, hidden_in, act_in, hidden_mid, act_mid, hidden_out))


def block_backward(grad_result, weights, kept, settle):
    w_in, w_mid, w_out, gains = weights
    stream, stream_low, hidden_in, act_in, hidden_mid, act_mid, hidden_out = kept
    gain_one, shift_one, gain_two, shift_two, gain_three, shift_three = split_gains(gains)
    _, back_three = jax.vjp(outer_act, hidden_out, gain_three, shift_three, stream)
    d_three, dg_three, db_three, d_resid = back_three(grad_result)
    d_three = d_three.astype(jnp.bfloat16)
    grad_out = settle(
        jnp.einsum("bpm,bpc->mc", act_mid, d_three, preferred_element_type=jnp.float32)
    )
    d_act_mid = jnp.einsum("bpc,mc->bpm", d_three, w_out, preferred_element_type=jnp.float32)
    _, back_two = jax.vjp(norm_act, hidden_mid, gain_two, shift_two)
    d_two, dg_two, db_two = back_two(d_act_mid)
    d_two = d_two.astype(jnp.bfloat16)
    grad_mid = settle(
        jnp.einsum("bpk,bpm->km", patches_of(act_in), d_two, preferred_element_type=jnp.float32)
    )
    d_cols = jnp.einsum("bpm,km->bpk", d_two, w_mid, preferred_element_type=jnp.float32)
    _, back_cols = jax.vjp(patches_of, act_in.astype(jnp.float32))
    (d_act_in,) = back_cols(d_cols)
    _, back_one = jax.vjp(norm_act, hidden_in, gain_one, shift_one)
    d_one, dg_one, db_one = back_one(d_act_in)
    d_one = d_one.astype(jnp.bfloat16)
    grad_in = jnp.einsum("bpc,bpm->cm", stream_low, d_one, preferred_element_type=jnp.float32)
    d_stream = d_resid + jnp.einsum("bpm,cm->bpc", d_one, w_in, preferred_element_type=jnp.float32)
    grad_gains = jnp.concatenate([dg_one, db_one, dg_two, db_two, dg_three, db_three])
    grad_in, grad_gains = settle((grad_in, grad_gains))
    return (d_stream, (grad_in, grad_mid, grad_out, grad_gains))


def on_device(
    frames,
    game_ids,
    taken_actions,
    next_actions,
    expert_flags,
    rewards,
    done_flags,
    weight_in,
    weight_mid,
    weight_out,
    norm_gains,
    head_table,
    moment_in,
    moment_mid,
    moment_out,
    moment_gains,
    moment_head,
    average_in,
    average_mid,
    average_out,
    average_gains,
    average_head,
):
    role_index = lax.axis_index("role")
    online = role_index == 0
    use_in = jnp.where(online, weight_in, average_in).astype(jnp.bfloat16)
    use_mid = jnp.where(online, weight_mid, average_mid).astype(jnp.bfloat16)
    use_out = jnp.where(online, weight_out, average_out).astype(jnp.bfloat16)
    use_gains = jnp.where(online, norm_gains, average_gains).astype(jnp.bfloat16)
    use_head = jnp.where(online, head_table, average_head).astype(jnp.bfloat16)
    support = support_low + (support_high - support_low) * jnp.arange(ATOMS, dtype=jnp.float32) / (
        ATOMS - 1
    )
    own_hot = (game_ids[:, None] == lax.broadcasted_iota(jnp.int32, (1, GAMES), 1)).astype(
        jnp.float32
    )
    counts = jnp.sum(own_hot, axis=0)
    stream = frames[0].astype(jnp.float32)
    layer = 0
    pieces = (
        lax.all_gather(use_in[layer], "dp", axis=0, tiled=True),
        lax.all_gather(use_mid[layer], "dp", axis=0, tiled=True),
        lax.all_gather(use_out[layer], "dp", axis=0, tiled=True),
        lax.all_gather(use_gains[layer], "dp", axis=0, tiled=True),
    )
    weights = (pieces[0], pieces[1], pieces[2], pieces[3].astype(jnp.float32))
    stream, saved = block_forward(stream, weights)
    gathered = [weights]
    kept = [saved]
    trans = stream.shape[0]
    pixels = stream.shape[1]
    wide_k = ACTIONS * ATOMS
    head_rows = head_table.shape[0]
    feat_low = jnp.mean(stream, axis=1).astype(jnp.bfloat16)
    feat_all, game_all = (
        lax.all_gather(feat_low, "dp", axis=0, tiled=True),
        lax.all_gather(game_ids.astype(jnp.bfloat16)[:, None], "dp", axis=0, tiled=True),
    )
    game_iota = lax.broadcasted_iota(jnp.int32, (1, GAMES), 1).astype(jnp.float32)
    all_hot = (game_all.astype(jnp.float32) == game_iota).astype(jnp.bfloat16)
    feat_rows = lax.dynamic_slice_in_dim(feat_all, lax.axis_index("dp") * head_rows, head_rows, 1)
    head_low = use_head.reshape(head_rows * GAMES, wide_k)

    def widen(count):
        spread_rows = (feat_rows[:, :, None] * all_hot[:, None, :]).reshape(
            count, head_rows * GAMES
        )
        return (spread_rows, all_hot)

    spread_rows, hot_piece = widen(trans * lax.axis_size("dp"))
    flat_logits = lax.psum_scatter(
        jnp.dot(spread_rows, head_low, preferred_element_type=jnp.float32),
        "dp",
        scatter_dimension=0,
        tiled=True,
    )
    logits = flat_logits.reshape(trans, ACTIONS, ATOMS)
    next_hot = (next_actions[:, None] == lax.broadcasted_iota(jnp.int32, (1, ACTIONS), 1)).astype(
        jnp.float32
    )
    next_prob = jax.nn.softmax(jnp.sum(logits * next_hot[:, :, None], axis=1), axis=-1)
    projected = project_target(next_prob, rewards, done_flags.astype(jnp.float32), support)
    target_dist = passed_along(projected, "role", -1)
    action_hot = (
        taken_actions[:, None] == lax.broadcasted_iota(jnp.int32, (1, ACTIONS), 1)
    ).astype(jnp.float32)
    expert = expert_flags.astype(jnp.float32)

    def local_loss(values):
        return transition_loss(values, target_dist, action_hot, expert, support)

    row_loss, loss_back = jax.vjp(local_loss, logits)
    sums = jnp.dot(row_loss, own_hot, precision=HIGHEST)
    total_counts, total_sums = lax.psum((counts, sums), "dp")
    floor_counts = jnp.maximum(total_counts, 1.0)
    loss_total = jnp.sum(total_sums / floor_counts)
    row_weight = jnp.dot(own_hot, 1.0 / (GAMES * floor_counts), precision=HIGHEST)
    (d_logits,) = loss_back(row_weight)
    d_low = d_logits.reshape(trans, wide_k).astype(jnp.bfloat16)
    piece = lax.all_gather(d_low, "dp", axis=0, tiled=True)
    count = piece.shape[0]
    spread_rows, hot_piece = widen(count)
    grad_head = lax.dot_general(
        spread_rows, piece, (((0,), (0,)), ((), ())), preferred_element_type=jnp.float32
    )
    back_wide = jnp.dot(piece, head_low.T, preferred_element_type=jnp.float32)
    back_rows = jnp.sum(
        back_wide.reshape(count, head_rows, GAMES) * hot_piece[:, None, :].astype(jnp.float32),
        axis=2,
    )
    grad_rows = back_rows
    grad_head, grad_rows = (grad_head, grad_rows)
    feat_grad = lax.all_to_all(
        grad_rows.astype(jnp.bfloat16), "dp", split_axis=0, concat_axis=1, tiled=True
    ).astype(grad_rows.dtype)
    d_stream = jnp.broadcast_to(feat_grad[:, None, :] / pixels, stream.shape)

    def settle(values):
        return values

    layer_grads = [None] * LAYERS
    for layer in reversed(range(LAYERS)):
        d_stream, block_grad = block_backward(d_stream, gathered[layer], kept[layer], settle)
        layer_grads[layer] = block_grad
    stacked = tuple((jnp.stack([layer_grads[0][kind]]) for kind in range(4)))
    reduced = lax.psum_scatter(stacked, "dp", scatter_dimension=1, tiled=True)
    head_grad = grad_head.reshape(head_rows, GAMES * wide_k)
    sent = (
        passed_along(upper_half(reduced[0]).astype(jnp.bfloat16), "role", 1).astype(jnp.float32),
        passed_along(upper_half(reduced[1]).astype(jnp.bfloat16), "role", 1).astype(jnp.float32),
        passed_along(upper_half(reduced[2]).astype(jnp.bfloat16), "role", 1).astype(jnp.float32),
        passed_along(reduced[3].astype(jnp.bfloat16), "role", 1).astype(jnp.float32),
        passed_along(upper_half(head_grad).astype(jnp.bfloat16), "role", 1).astype(jnp.float32),
        passed_along(loss_total.astype(jnp.bfloat16), "role", 1).astype(loss_total.dtype),
    )
    grad_in = jnp.where(online, lower_half(reduced[0]), sent[0])
    grad_mid = jnp.where(online, lower_half(reduced[1]), sent[1])
    grad_out = jnp.where(online, lower_half(reduced[2]), sent[2])
    grad_gains = jnp.where(online, reduced[3], sent[3])
    grad_table = jnp.where(online, lower_half(head_grad), sent[4])
    loss_out = jnp.where(online, loss_total, sent[5])
    in_w, in_m, in_a, in_c = renew(
        own_half(weight_in, role_index),
        grad_in,
        own_half(moment_in, role_index),
        own_half(average_in, role_index),
        learn_rate,
    )
    mid_w, mid_m, mid_a, mid_c = renew(
        own_half(weight_mid, role_index),
        grad_mid,
        own_half(moment_mid, role_index),
        own_half(average_mid, role_index),
        learn_rate,
    )
    out_w, out_m, out_a, out_c = renew(
        own_half(weight_out, role_index),
        grad_out,
        own_half(moment_out, role_index),
        own_half(average_out, role_index),
        learn_rate,
    )
    gain_w, gain_m, gain_a, gain_c = renew(
        norm_gains, grad_gains, moment_gains, average_gains, gain_rate
    )
    head_w, head_m, head_a, head_c = renew(
        own_half(head_table, role_index),
        grad_table,
        own_half(moment_head, role_index),
        own_half(average_head, role_index),
        learn_rate,
    )
    return (
        loss_out,
        in_w,
        grad_in,
        in_a,
        in_c,
        mid_w,
        mid_m,
        mid_a,
        mid_c,
        out_w,
        out_m,
        out_a,
        out_c,
        gain_w,
        gain_m,
        gain_a,
        gain_c,
        head_w,
        head_m,
        head_a,
        head_c,
    )


MESH = pl.DeviceIdType.MESH


def any_spec():
    return pl.BlockSpec(memory_space=pl.ANY)


def greet(peers):
    barrier = pltpu.get_barrier_semaphore()
    for cond, dev in peers:
        def go(dev=dev):
            pl.semaphore_signal(barrier, inc=1, device_id=dev, device_id_type=MESH)
        go() if cond is None else pl.when(cond)(go)
    count = sum(1 for cond, _ in peers if cond is None)
    for cond, _ in peers:
        if cond is not None:
            count = count + cond.astype(jnp.int32)
    pl.semaphore_wait(barrier, count)


def place():
    me = lax.axis_index("dp")
    core = lax.rem(me, 2)
    x = lax.rem(me // 2, 2)
    z = me // 4
    return me, z, x, core


D = 2048
MID = 512
GROUPS = 32
SIDE = 11
PIX = 121
TB = 8
PITCH = 12
RB = PITCH * TB
VR = SIDE * TB
ROWS = SIDE * RB
PAD = 16 * TB
EROWS = 164 * TB
BLK = 352
CH = 512
epsilon = 1e-05
GK = 0.7978845608028654
GC = 0.044715
OFFS = [(i - 1) * PITCH + (j - 1) for i in range(3) for j in range(3)]


def group_sum(v, gs):
    width = v.shape[1]
    n = width // 128
    a = lax.broadcasted_iota(jnp.int32, (128, 128), 0) // gs
    b = lax.broadcasted_iota(jnp.int32, (128, 128), 1) // gs
    m = (a == b).astype(jnp.float32)
    st = jnp.concatenate([v[:, k * 128:(k + 1) * 128] for k in range(n)], axis=0)
    r = jnp.dot(st, m, precision=lax.Precision.HIGHEST, preferred_element_type=jnp.float32)
    return jnp.concatenate([r[k * 8:(k + 1) * 8] for k in range(n)], axis=1)


def fold(v):
    rows, w = v.shape
    return jnp.sum(v.reshape(rows // TB, TB, w), axis=0)


def moments(h_ref, lo, gs):
    def one(r, acc):
        return acc + fold(h_ref[pl.ds(pl.multiple_of(r * RB, RB), VR), lo:lo + CH])
    s = lax.fori_loop(0, SIDE, one, jnp.zeros((TB, CH), jnp.float32))
    mean = group_sum(s, gs) / float(PIX * gs)

    def two(r, acc):
        h = h_ref[pl.ds(pl.multiple_of(r * RB, RB), VR), lo:lo + CH].reshape(SIDE, TB, CH) - mean[None]
        return acc + jnp.sum(h * h, axis=0)
    q = lax.fori_loop(0, SIDE, two, jnp.zeros((TB, CH), jnp.float32))
    var = group_sum(q, gs) / float(PIX * gs)
    return mean, lax.rsqrt(var + epsilon)


def gelu(u):
    return 0.5 * u * (1.0 + jnp.tanh(GK * (u + GC * (u * u * u))))


def dgelu(u):
    uu = u * u
    t = jnp.tanh(GK * u * (1.0 + GC * uu))
    return 0.5 * (1.0 + t) + 0.5 * u * (1.0 - t * t) * (GK + (3.0 * GK * GC) * uu)


def shifted(e_ref, o_ref, s, row, n):
    ref, base = (e_ref, 16 + s) if s % 2 == 0 else (o_ref, 17 + s)
    return ref[pl.ds(pl.multiple_of(row + base * TB, 16), n), :]


def put_shifted(e_ref, o_ref, r, v):
    z = jnp.zeros((TB, v.shape[1]), jnp.float32)
    at = pl.ds(pl.multiple_of(PAD + r * RB, 16), RB)
    e_ref[at, :] = jnp.concatenate([v, z], axis=0).astype(jnp.bfloat16)
    o_ref[at, :] = jnp.concatenate([z, v], axis=0).astype(jnp.bfloat16)


def clear_margins(e_ref, o_ref):
    z = jnp.zeros((PAD, MID), jnp.bfloat16)
    for ref in (e_ref, o_ref):
        ref[0:PAD, :] = z
        ref[PAD + ROWS:EROWS, :] = z


def row_at(r):
    return pl.ds(pl.multiple_of(r * RB, RB), VR)


def rows_full(r):
    return pl.ds(pl.multiple_of(r * RB, RB), RB)


def norm_back(h_ref, lo, dy_ref, mean, rstd, gain, gs, s1, s2, emit):
    n = 1.0 / float(PIX * gs)
    m1 = group_sum(gain * s1, gs) * n
    m2 = group_sum(gain * s2, gs) * n
    ca = rstd * gain
    cc = -rstd * rstd * m2
    cb = -rstd * m1 - mean * cc

    def one(r, c):
        h = h_ref[row_at(r), lo:lo + CH].reshape(SIDE, TB, CH)
        dy = dy_ref[row_at(r), :].reshape(SIDE, TB, CH)
        emit(r, (ca[None] * dy + cc[None] * h + cb[None]).reshape(VR, CH))
        return c
    lax.fori_loop(0, SIDE, one, 0)


D = 2048
GAMES = 40
ACTIONS = 18
ATOMS = 51
WIDE = ACTIONS * ATOMS
LW = 1024
WIN = 1024
COLS = GAMES * WIDE
HALF = COLS // 2
PADC = 36864
TB = 8
support_low = -10.0
support_high = 10.0
discount = 0.99
penalty = 0.05


def window_of(g):
    return (WIDE * g) // 16 * 16


def ids_offset(ids):
    return lax.bitwise_and(WIDE * ids, 15)


def shift_rows(v, off, right):
    width = v.shape[1]
    for b in range(1, 4):
        n = 1 << b
        bit = lax.bitwise_and(off, n) != 0
        bit = jnp.concatenate([bit.astype(jnp.float32)] * (width // 128), axis=1) > 0.5
        v = jnp.where(bit, pltpu.roll(v, n if right else width - n, 1), v)
    return v


def widen(dl):
    n = dl.shape[0]
    v = dl.astype(jnp.float32)
    v = jnp.concatenate([v[:, 0:TB], v[:, TB:2 * TB]], axis=2).reshape(n * TB, LW)
    lanes = lax.broadcasted_iota(jnp.int32, (n * TB, 128), 1)
    last = jnp.where(lanes < WIDE - LW + 128, v[:, LW - 128:], 0.0)
    return jnp.concatenate([v[:, :LW - 128], last], axis=1)


W_IN, W_MID, W_OUT, MISC = 0, 1, 2, 3
HC = 2048
NHC = -(-COLS // HC)
T0 = (((0,), (0,)), ((), ()))
T1 = (((1,), (1,)), ((), ()))


def rc(src, dst, ss, rs, dev):
    return pltpu.make_async_remote_copy(src_ref=src, dst_ref=dst, send_sem=ss, recv_sem=rs, device_id=dev,
                                        device_id_type=MESH)


def when(cond, do):
    if cond is None:
        do()
    else:
        pl.when(cond)(do)


class Gather:
    def __init__(self, nz, own, full, rows, own_sem, send, recv):
        self.nz, self.own_refs, self.full, self.rows = nz, own, full, rows
        self.own_sem, self.send, self.recv = own_sem, send, recv
        self.me, self.z, self.x, self.c = place()
        me, x, c = self.me, self.x, self.c
        self.up, self.down = {"dp": me + 4}, {"dp": me - 4}
        self.xp, self.cp = {"dp": me + 2 - 4 * x}, {"dp": me + 1 - 2 * c}
        self.has_up, self.has_down = self.z < nz - 1, self.z > 0
        self.started = []

    def slot(self, a, i):
        n = self.rows[a]
        return self.full[a].at[i] if n is None else self.full[a].at[pl.ds(pl.multiple_of(i * n, 16), n)]

    def put(self, cond, a, src, i, dev, k):
        d = rc(src, self.slot(a, i), self.send.at[a, k], self.recv.at[a, i], dev)
        when(cond, d.start)
        self.started.append((cond, d))

    def take(self, cond, a, i):
        d = rc(self.slot(a, i), self.slot(a, i), self.send.at[a, 0], self.recv.at[a, i], self.cp)
        when(cond, d.wait_recv)

    def begin(self, a):
        src = self.own_refs[a]
        self.put(self.has_up, a, src, self.me, self.up, 0)
        self.put(self.has_down, a, src, self.me, self.down, 1)
        self.put(None, a, src, self.me, self.xp, 2)
        self.put(None, a, src, self.me, self.cp, 3)
        pltpu.make_async_copy(src, self.slot(a, self.me), self.own_sem.at[a]).start()

    def along_z(self, a, d):
        k = 4 + (d - 1) * 6
        for up in (True, False):
            s = self.me - 4 * d if up else self.me + 4 * d
            ok = self.z - d >= 0 if up else self.z + d < self.nz
            more = jnp.logical_and(ok, self.has_up if up else self.has_down)
            m = k if up else k + 3
            self.take(ok, a, s)
            self.put(more, a, self.slot(a, s), s, self.up if up else self.down, m)
            self.put(ok, a, self.slot(a, s), s, self.xp, m + 1)
            self.put(ok, a, self.slot(a, s), s, self.cp, m + 2)

    def at_distance(self, d):
        for up in ((True,) if d == 0 else (False, True)):
            zz = self.z + d if up else self.z - d
            yield zz, (None if d == 0 else zz < self.nz if up else zz >= 0), up

    def along_x(self, a, d):
        k = 4 + (self.nz - 1) * 6
        for zz, ok, up in self.at_distance(d):
            s = zz * 4 + (1 - self.x) * 2 + self.c
            self.take(ok, a, s)
            self.put(ok, a, self.slot(a, s), s, self.cp, k + 2 * d + (1 if up else 0))

    def arrived(self, a):
        for d in range(self.nz):
            for zz, ok, _ in self.at_distance(d):
                for xx in (self.x, 1 - self.x):
                    self.take(ok, a, zz * 4 + xx * 2 + 1 - self.c)
        pltpu.make_async_copy(self.own_refs[a], self.slot(a, self.me), self.own_sem.at[a]).wait()

    def end(self):
        for cond, d in self.started:
            when(cond, d.wait_send)


def put_gain(gg_ref, at, s):
    gg_ref[:, at:at + CH] = jnp.sum(s, axis=0, keepdims=True)


def through(h_ref, d2_ref, st_ref, g_ref, gg_ref, at, goff, boff, emit):
    z8 = jnp.zeros((TB, CH), jnp.float32)
    mean = st_ref[0:8, at:at + MID]
    rstd = st_ref[8:16, at:at + MID]
    gain = g_ref[:, goff:goff + MID]
    shift = g_ref[:, boff:boff + MID]
    mr = mean * rstd

    def one(r, acc):
        s1, s2 = acc
        h = h_ref[row_at(r), :].reshape(SIDE, TB, MID)
        da = d2_ref[row_at(r), :].reshape(SIDE, TB, MID)
        xh = h * rstd[None] - mr[None]
        dy = da * dgelu(xh * gain + shift)
        d2_ref[row_at(r), :] = dy.reshape(VR, MID)
        return s1 + jnp.sum(dy, axis=0), s2 + jnp.sum(dy * xh, axis=0)
    s1, s2 = lax.fori_loop(0, SIDE, one, (z8, z8))
    put_gain(gg_ref, goff, s2)
    put_gain(gg_ref, boff, s1)
    norm_back(h_ref, 0, d2_ref, mean, rstd, gain, MID // GROUPS, s1, s2, emit)


def step_kernel(n, fr_hbm, wi, wm, wo, wg, ai, am, ao, ag, k0, k1, k2, k3, k4, k5, ht_hbm, ha_hbm,
                x_hbm, h1_hbm, a2_hbm, dh3_hbm, e_hbm, o_hbm, wmid_hbm, fart_hbm,
                st_ref, g_ref, gg_ref, gall_ref, frow_ref, dlog_ref, loss_ref,
                scal_ref, own_in, own_mid, own_out, own_misc, win_ref, wmid_ref, wout_ref, misc_ref,
                x_ref, h1_ref, h2_ref, h3_ref, a2_ref, dfeat_ref, e_ref, o_ref,
                d2_ref, dh3_ref, far_ref, fart_ref, fbuf, hbuf, head_ref,
                fsend, frecv, part, r1, r2, tgt_s, tgt_r, down_s, dsend, drecv,
                own_sem, g_send, g_recv, f_sem, h_sem, k_sem, ss, rs_,
                s_f, q_f, s_1, q_1, s_2, q_2, s_t, q_t, s_l, q_l, s_c, q_c, s_d, q_d, s_r, q_r):
    me, z, x, c = place()
    role = lax.axis_index("role")
    half = n // 2
    peers = [lax.rem(me + k, n) for k in range(1, n)]
    cp = me + 1 - 2 * c
    du_ref = d2_ref

    def pick(w, a, dst):
        def fill(src):
            dst[...] = src[...].astype(jnp.bfloat16)
        pl.when(role == 0)(lambda: fill(w))
        pl.when(role != 0)(lambda: fill(a))

    def fetch_frames(r):
        return pltpu.make_async_copy(fr_hbm.at[pl.ds(r * SIDE, SIDE)], fbuf.at[r % 2], f_sem.at[r % 2])

    def fetch_head(k, go):
        m = HC if k < NHC - 1 else COLS - (NHC - 1) * HC

        def one(src):
            d = pltpu.make_async_copy(src.at[pl.ds(k * HC, m)], hbuf.at[k % 2, pl.ds(0, m)], h_sem.at[k % 2])
            d.start() if go else d.wait()
        if go:
            pl.when(role == 0)(lambda: one(ht_hbm))
            pl.when(role != 0)(lambda: one(ha_hbm))
        else:
            one(ht_hbm)
    fetch_frames(0).start()
    fetch_head(0, True)
    pick(wi, ai, own_in)
    pick(wm, am, own_mid)
    pick(wo, ao, own_out)

    def pick_gains(src):
        v = src[...].astype(jnp.bfloat16).astype(jnp.float32)
        for k in range(3):
            own_misc[k:k + 1, :] = v[:, k * 128:(k + 1) * 128]
    own_misc[0:TB, :] = jnp.zeros((TB, 128), jnp.float32)
    pl.when(role == 0)(lambda: pick_gains(wg))
    pl.when(role != 0)(lambda: pick_gains(ag))
    for k, ref in enumerate((k0, k1, k2, k3, k4, k5)):
        for t in range(TB):
            scal_ref[k, t:t + 1, :] = jnp.full((1, 128), ref[t].astype(jnp.float32), jnp.float32)
    own_misc[TB:2 * TB, :] = scal_ref[5]
    greet([(None, {"dp": p}) for p in peers] + [(None, {"role": 1 - role})])

    gath = Gather(n // 4, (own_in, own_mid, own_out, own_misc), (win_ref, wmid_ref, wout_ref, misc_ref),
               (D // n, 9 * MID // n, MID // n, None), own_sem, g_send, g_recv)
    casts = iter(range(NHC))

    def cast_head(times):
        for _ in range(times):
            k = next(casts, None)
            if k is None:
                return
            if k + 1 < NHC:
                fetch_head(k + 1, True)
            fetch_head(k, False)
            m = HC if k < NHC - 1 else COLS - (NHC - 1) * HC
            u = 128 if m % 128 == 0 else 112

            def one(i, carry, k=k, u=u):
                rs = pl.ds(pl.multiple_of(i * u, 16), u)
                head_ref[pl.ds(pl.multiple_of(k * HC + i * u, 16), u), :] = hbuf[k % 2, rs, :].astype(jnp.bfloat16)
                return carry
            lax.fori_loop(0, m // u, one, 0)

    for a in (MISC, W_IN, W_MID):
        gath.begin(a)
    for r in range(SIDE):
        if r + 1 < SIDE:
            fetch_frames(r + 1).start()
        fetch_frames(r).wait()
        v = fbuf[r % 2].astype(jnp.float32).reshape(VR, D)
        x_ref[r * RB:(r + 1) * RB, :] = jnp.concatenate([v, jnp.zeros((TB, D), jnp.float32)], axis=0).astype(jnp.bfloat16)
    clear_margins(e_ref, o_ref)
    head_ref[COLS:PADC, :] = jnp.zeros((PADC - COLS, 128), jnp.bfloat16)
    far = n // 4 - 1
    kept = [pltpu.make_async_copy(src, dst, k_sem.at[k]) for k, (src, dst) in enumerate((
        (x_ref, x_hbm), (h1_ref, h1_hbm), (a2_ref, a2_hbm), (dh3_ref, dh3_hbm), (e_ref, e_hbm), (o_ref, o_hbm),
        (wmid_ref, wmid_hbm)))]

    def keep(k):
        pl.when(role == 0)(kept[k].start)
    keep(0)

    def z_step(a, d):
        if d <= far:
            gath.along_z(a, d)

    def x_step(a, d):
        if d <= far:
            gath.along_x(a, d)
    for d in range(1, far + 1):
        z_step(W_IN, d)
        z_step(MISC, d)
        cast_head(2)
        x_step(W_IN, d - 1)
        x_step(MISC, d - 1)
        z_step(W_MID, d)
        cast_head(2)
        if d == max(far - 1, 1):
            gath.begin(W_OUT)
    x_step(W_IN, far)
    x_step(MISC, far)
    x_step(W_MID, 0)
    x_step(W_MID, 1)
    cast_head(1)
    z_step(W_OUT, 1)
    gath.arrived(MISC)
    gath.arrived(W_IN)
    for i in range(n):
        gall_ref[i] = misc_ref[i, TB:2 * TB, :]
        for k in range(3):
            at = (i * 3 + k) * 128
            g_ref[:, at:at + 128] = misc_ref[i, k:k + 1, :]

    def mm1(i, carry):
        rs = pl.ds(pl.multiple_of(i * BLK, BLK), BLK)
        h1_ref[rs, :] = jnp.dot(x_ref[rs, :], win_ref[...], preferred_element_type=jnp.float32)
        return carry
    lax.fori_loop(0, ROWS // BLK, mm1, 0)
    z_step(W_OUT, 2)
    x_step(W_MID, 2)
    keep(1)
    mean, rstd = moments(h1_ref, 0, MID // GROUPS)
    st_ref[0:8, 0:MID] = mean
    st_ref[8:16, 0:MID] = rstd
    sc = rstd * g_ref[:, 0:MID]
    sh = g_ref[:, MID:2 * MID] - mean * sc

    def act1(r, carry):
        h = h1_ref[row_at(r), :].reshape(SIDE, TB, MID)
        a = gelu(h * sc[None] + sh[None]).reshape(VR, MID)
        put_shifted(e_ref, o_ref, r, a)
        return carry
    lax.fori_loop(0, SIDE, act1, 0)
    inner = pl.ds(PAD, ROWS)

    def far_a1(to):
        return rc(e_ref.at[inner], far_ref, ss.at[0], rs_.at[0], {"role": to})

    pl.when(role == 0)(lambda: far_a1(1).start())
    cast_head(NHC)
    z_step(W_OUT, 3)
    for d in range(3, far + 1):
        x_step(W_MID, d)
    gath.arrived(W_MID)
    keep(6)

    def mm2(i, carry):
        row = i * BLK
        acc = None
        for m, s in enumerate(OFFS):
            p = jnp.dot(shifted(e_ref, o_ref, s, row, BLK), wmid_ref[m * MID:(m + 1) * MID, :],
                        preferred_element_type=jnp.float32)
            acc = p if acc is None else acc + p
        h2_ref[pl.ds(pl.multiple_of(row, BLK), BLK), :] = acc
        return carry
    lax.fori_loop(0, ROWS // BLK, mm2, 0)
    for d in range(far + 1):
        x_step(W_OUT, d)
    mean, rstd = moments(h2_ref, 0, MID // GROUPS)
    st_ref[0:8, MID:2 * MID] = mean
    st_ref[8:16, MID:2 * MID] = rstd
    sc2 = rstd * g_ref[:, 2 * MID:3 * MID]
    sh2 = g_ref[:, 3 * MID:4 * MID] - mean * sc2

    def act2(r, carry):
        h = h2_ref[rows_full(r), :].reshape(PITCH, TB, MID)
        a2_ref[rows_full(r), :] = gelu(h * sc2[None] + sh2[None]).reshape(RB, MID).astype(jnp.bfloat16)
        return carry
    lax.fori_loop(0, SIDE, act2, 0)
    keep(2)
    gath.arrived(W_OUT)

    def mm3(i, carry):
        rs = pl.ds(pl.multiple_of(i * BLK, BLK), BLK)
        h3_ref[rs, :] = jnp.dot(a2_ref[rs, :], wout_ref[...], preferred_element_type=jnp.float32)
        return carry
    lax.fori_loop(0, ROWS // BLK, mm3, 0)
    for k in range(D // CH):
        lo = k * CH
        mean, rstd = moments(h3_ref, lo, D // GROUPS)
        st_ref[0:8, 2 * MID + lo:2 * MID + lo + CH] = mean
        st_ref[8:16, 2 * MID + lo:2 * MID + lo + CH] = rstd
        sc3 = rstd * g_ref[:, 4 * MID + lo:4 * MID + lo + CH]
        sh3 = g_ref[:, 4 * MID + D + lo:4 * MID + D + lo + CH] - mean * sc3

        def act3(r, acc):
            h = h3_ref[row_at(r), lo:lo + CH].reshape(SIDE, TB, CH)
            s = x_ref[rows_full(r), lo:lo + CH].astype(jnp.float32)[0:VR].reshape(SIDE, TB, CH)
            return acc + jnp.sum(gelu(s + (h * sc3[None] + sh3[None])), axis=0)
        acc = lax.fori_loop(0, SIDE, act3, jnp.zeros((TB, CH), jnp.float32))
        feat = (acc / float(PIX)).astype(jnp.bfloat16).astype(jnp.float32)
        for j in range(lo // 128, (lo + CH) // 128):
            fsend[j] = feat[:, j * 128 - lo:(j + 1) * 128 - lo]

            @pl.when(me != j)
            def _(j=j):
                rc(fsend.at[j], frecv.at[me], s_f.at[j], q_f.at[me], {"dp": j}).start()

            @pl.when(me == j)
            def _(j=j):
                frecv[j] = fsend[j]

    for p in peers:
        rc(fsend.at[p], frecv.at[p], s_f.at[0], q_f.at[p], {"dp": p}).wait_recv()
    feats = frecv[...].reshape(n * TB, 128)
    ids = gall_ref[...].reshape(n * TB, 128).astype(jnp.int32)

    acc = None
    for g in range(GAMES):
        lhs = jnp.where(ids == g, feats, 0.0).astype(jnp.bfloat16)
        a = window_of(g)
        p = lax.dot_general(lhs, head_ref[a:a + WIN, :], (((1,), (1,)), ((), ())),
                            preferred_element_type=jnp.float32)
        acc = p if acc is None else acc + p
    off = ids_offset(ids)
    part[...] = shift_rows(acc, off, False).reshape(half, 2, TB, LW)

    d1 = rc(part.at[:, 1 - c], r1, s_1, q_1, {"dp": cp})
    d1.start()
    d1.wait()
    pair = me // 2
    r1[...] = r1[...] + part[:, c]
    pps = [lax.rem(pair + k, half) for k in range(1, half)]
    for k, p in enumerate(pps):
        rc(r1.at[p], r2.at[pair], s_2.at[k], q_2.at[pair], {"dp": 2 * p + c}).start()
    r2[pair] = r1[pair]
    for k, p in enumerate(pps):
        rc(r1.at[p], r2.at[p], s_2.at[k], q_2.at[p], {"dp": 2 * p + c}).wait_recv()
    logits = jnp.sum(r2[...], axis=0)

    lane = lax.broadcasted_iota(jnp.int32, (TB, 128), 1)
    live = lane < ATOMS
    zi = support_low + (support_high - support_low) * lane.astype(jnp.float32) / (ATOMS - 1)
    zi = jnp.where(live, zi, 0.0)
    taken, nxt, expert, reward, done, gid = (scal_ref[k] for k in range(6))
    pieces = []
    for a in range(ACTIONS):
        v = logits if a == 0 else pltpu.roll(logits, LW - ATOMS * a, 1)
        pieces.append(v[:, :128])

    @pl.when(role == 1)
    def _():
        sel = jnp.zeros((TB, 128), jnp.float32)
        for a in range(ACTIONS):
            sel = sel + jnp.where(nxt == float(a), pieces[a], 0.0)
        sel = jnp.where(live, sel, -1e30)
        e = jnp.exp(sel - jnp.max(sel, axis=1, keepdims=True))
        e = jnp.where(live, e, 0.0)
        prob = e / jnp.sum(e, axis=1, keepdims=True)
        spacing = (support_high - support_low) / (ATOMS - 1)
        m = jnp.zeros((TB, 128), jnp.float32)
        for j in range(ATOMS):
            zj = float(np.float32(support_low) + np.float32(support_high - support_low) * np.float32(j) /
                       np.float32(ATOMS - 1))
            tz = jnp.clip(reward + discount * (1.0 - done) * zj, support_low, support_high)
            wt = jnp.maximum(0.0, 1.0 - jnp.abs(tz - zi) / spacing)
            m = m + prob[:, j:j + 1] * wt
        tgt_s[...] = jnp.where(live, m, 0.0)
        d = rc(tgt_s, tgt_r, s_t, q_t, {"role": 0})
        d.start()
        d.wait_send()
        rc(frow_ref, frow_ref, s_r.at[0], q_r.at[0], {"role": 0}).wait_recv()
        rc(dlog_ref, dlog_ref, s_r.at[1], q_r.at[1], {"role": 0}).wait_recv()
        dfeat_ref[...] = jnp.zeros_like(dfeat_ref)

    @pl.when(role == 0)
    def _():
        frow_ref[...] = feats.astype(jnp.bfloat16)
        gt = jnp.transpose(gall_ref[...].reshape(n * TB, 128))[0:TB]
        count = jnp.sum((gt == gid).astype(jnp.float32), axis=1, keepdims=True)
        weight = 1.0 / jnp.maximum(count, 1.0)
        x3 = jnp.where(live[None], jnp.stack(pieces), -1e30)
        act = lax.broadcasted_iota(jnp.int32, (ACTIONS, TB, 128), 0).astype(jnp.float32)
        hot = (act == taken[None]).astype(jnp.float32)
        mx = jnp.max(x3, axis=2, keepdims=True)
        e = jnp.where(live[None], jnp.exp(x3 - mx), 0.0)
        s = jnp.sum(e, axis=2, keepdims=True)
        logp = jnp.where(live[None], x3 - mx - jnp.log(s), 0.0)
        prob = e / s
        q = jnp.sum(prob * zi[None], axis=2, keepdims=True)
        qb = jnp.broadcast_to(q, (ACTIONS, TB, 128))
        qm = jnp.max(qb, axis=0)
        qe = jnp.exp(qb - qm[None])
        qs = jnp.sum(qe, axis=0)
        lse = qm + jnp.log(qs)
        pol = qe / qs[None]
        chosen = jnp.sum(logp * hot, axis=0)
        qt = jnp.sum(qb * hot, axis=0)
        rc(tgt_s, tgt_r, s_t, q_t, {"role": 1}).wait_recv()
        m = tgt_r[...]
        cross = -jnp.sum(m * chosen, axis=1, keepdims=True)
        row_loss = cross + penalty * expert * (lse - qt)
        msum = jnp.sum(m, axis=1, keepdims=True)
        dl = hot * (prob * msum[None] - m[None]) + (penalty * expert)[None] * (pol - hot) * prob * (zi[None] - qb)
        dl = jnp.where(live[None], dl * (weight * (1.0 / GAMES))[None], 0.0)
        flat = jnp.zeros((TB, LW), jnp.float32)
        pad = jnp.zeros((TB, LW - 128), jnp.float32)
        for a in range(ACTIONS):
            v = jnp.concatenate([dl[a], pad], axis=1)
            flat = flat + (v if a == 0 else pltpu.roll(v, ATOMS * a, 1))
        l0 = row_loss * weight
        p0 = l0.astype(jnp.bfloat16).astype(jnp.float32)
        p1 = (l0 - p0).astype(jnp.bfloat16).astype(jnp.float32)
        p2 = l0 - p0 - p1
        last = flat[:, LW - 128:]
        last = jnp.where(lane == 125, p0, jnp.where(lane == 126, p1, jnp.where(lane == 127, p2, last)))
        flat = jnp.concatenate([flat[:, :LW - 128], last], axis=1)
        down_s[...] = jnp.concatenate([flat[:, :LW // 2], flat[:, LW // 2:]], axis=0).astype(jnp.bfloat16)
        for k, p in enumerate(pps):
            rc(down_s, dlog_ref.at[me], s_l.at[k], q_l.at[me], {"dp": 2 * p + c}).start()
        rc(down_s, dlog_ref.at[me], s_c.at[0], q_c.at[me], {"dp": cp}).start()
        dlog_ref[me] = down_s[...]
        for k, p in enumerate(pps):
            o = 2 * p + c
            rc(down_s, dlog_ref.at[o], s_l.at[k], q_l.at[o], {"dp": cp}).wait_recv()
            rc(dlog_ref.at[o], dlog_ref.at[o], s_c.at[k + 1], q_c.at[o], {"dp": cp}).start()
        for p in [pair] + pps:
            o = 2 * p + 1 - c
            rc(dlog_ref.at[o], dlog_ref.at[o], s_c.at[0], q_c.at[o], {"dp": cp}).wait_recv()
        to0 = rc(frow_ref, frow_ref, s_r.at[0], q_r.at[0], {"role": 1})
        to1 = rc(dlog_ref, dlog_ref, s_r.at[1], q_r.at[1], {"role": 1})
        to0.start()
        to1.start()
        rolled = shift_rows(widen(dlog_ref[...]), off, True)
        acc = None
        for g in range(GAMES):
            lhs = jnp.where(jnp.concatenate([ids == g] * (WIN // 128), axis=1), rolled, 0.0).astype(jnp.bfloat16)
            a = window_of(g)
            p = jnp.dot(lhs, head_ref[a:a + WIN, :], preferred_element_type=jnp.float32)
            acc = p if acc is None else acc + p
        dsend[...] = acc.reshape(n, TB, 128)
        for k, p in enumerate(peers):
            rc(dsend.at[p], drecv.at[me], s_d.at[k], q_d.at[me], {"dp": p}).start()
        drecv[me] = dsend[me]
        for k, p in enumerate(peers):
            rc(dsend.at[p], drecv.at[p], s_d.at[k], q_d.at[p], {"dp": p}).wait_recv()
        for j in range(n):
            dfeat_ref[:, j * 128:(j + 1) * 128] = drecv[j]
        for k, p in enumerate(pps):
            rc(down_s, dlog_ref.at[me], s_l.at[k], q_l.at[me], {"dp": 2 * p + c}).wait_send()
        rc(down_s, dlog_ref.at[me], s_c.at[0], q_c.at[me], {"dp": cp}).wait_send()
        for k, p in enumerate(pps):
            o = 2 * p + c
            rc(dlog_ref.at[o], dlog_ref.at[o], s_c.at[k + 1], q_c.at[o], {"dp": cp}).wait_send()
        for k, p in enumerate(peers):
            rc(dsend.at[p], drecv.at[me], s_d.at[k], q_d.at[me], {"dp": p}).wait_send()
        to0.wait_send()
        to1.wait_send()

    for j in range(n):
        pl.when(me != j)(rc(fsend.at[j], frecv.at[me], s_f.at[j], q_f.at[me], {"dp": j}).wait_send)
    for k, p in enumerate(pps):
        rc(r1.at[p], r2.at[pair], s_2.at[k], q_2.at[pair], {"dp": 2 * p + c}).wait_send()
    tail = dlog_ref[:, :, 384:512].astype(jnp.float32)[:, TB:2 * TB].reshape(n * TB, 128)
    lanes = lax.broadcasted_iota(jnp.int32, (n * TB, 128), 1)
    total = jnp.sum(jnp.where(lanes >= 125, tail, 0.0))
    loss_ref[...] = jnp.full((TB, 128), total, jnp.float32)

    z8 = jnp.zeros((TB, CH), jnp.float32)

    def last_norm():
        for k in range(D // CH):
            lo = k * CH
            mean = st_ref[0:8, 2 * MID + lo:2 * MID + lo + CH]
            rstd = st_ref[8:16, 2 * MID + lo:2 * MID + lo + CH]
            gain = g_ref[:, 4 * MID + lo:4 * MID + lo + CH]
            shift = g_ref[:, 4 * MID + D + lo:4 * MID + D + lo + CH]
            dout = dfeat_ref[:, lo:lo + CH] / float(PIX)
            mr = mean * rstd

            def one(r, acc):
                s1, s2 = acc
                h = h3_ref[row_at(r), lo:lo + CH].reshape(SIDE, TB, CH)
                s = x_ref[rows_full(r), lo:lo + CH].astype(jnp.float32)[0:VR].reshape(SIDE, TB, CH)
                xh = h * rstd[None] - mr[None]
                du = dout[None] * dgelu(s + (xh * gain + shift))
                du_ref[row_at(r), :] = du.reshape(VR, CH)
                return s1 + jnp.sum(du, axis=0), s2 + jnp.sum(du * xh, axis=0)
            s1, s2 = lax.fori_loop(0, SIDE, one, (z8, z8))
            put_gain(gg_ref, 4 * MID + lo, s2)
            put_gain(gg_ref, 4 * MID + D + lo, s1)

            def put3(r, v):
                dh3_ref[rows_full(r), lo:lo + CH] = jnp.concatenate([v, z8], axis=0).astype(jnp.bfloat16)
            norm_back(h3_ref, lo, du_ref, mean, rstd, gain, D // GROUPS, s1, s2, put3)

    @pl.when(role == 0)
    def _():
        last_norm()
        kept[3].start()

        def da2(i, c):
            rs = pl.ds(pl.multiple_of(i * BLK, BLK), BLK)
            d2_ref[rs, :] = lax.dot_general(dh3_ref[rs, :], wout_ref[...], T1, preferred_element_type=jnp.float32)
            return c
        lax.fori_loop(0, ROWS // BLK, da2, 0)
        far_a1(1).wait_send()
        through(h2_ref, d2_ref, st_ref, g_ref, gg_ref, MID, 2 * MID, 3 * MID,
                lambda r, v: put_shifted(e_ref, o_ref, r, v))
        kept[4].start()
        kept[5].start()
        gg_ref[:, 0:2 * MID] = jnp.zeros((1, 2 * MID), jnp.float32)
        for d in kept:
            d.wait()

    @pl.when(role == 1)
    def _():
        far_a1(0).wait_recv()
        for k in range(MID // 128):
            fart_ref[k * 128:(k + 1) * 128, :] = jnp.transpose(far_ref[:, k * 128:(k + 1) * 128])
        d = pltpu.make_async_copy(fart_ref, fart_hbm, k_sem.at[7])
        d.start()
        d.wait()
        gg_ref[...] = jnp.zeros_like(gg_ref)
    gath.end()


def block_step(frames, weights, averages, scal, head, avg_head, n, cid):
    f32, b16 = jnp.float32, jnp.bfloat16
    S = jax.ShapeDtypeStruct
    V, dma = pltpu.VMEM, pltpu.SemaphoreType.DMA
    vs, hs = pl.BlockSpec(memory_space=pltpu.VMEM), pl.BlockSpec(memory_space=pl.ANY)
    h = n // 2
    nz = n // 4
    sends = 4 + 6 * (nz - 1) + 2 * nz
    return pl.pallas_call(
        functools.partial(step_kernel, n),
        out_shape=(S((ROWS, D), b16), S((ROWS, MID), f32), S((ROWS, MID), b16), S((ROWS, D), b16), S((EROWS, MID), b16),
                   S((EROWS, MID), b16), S((9 * MID, MID), b16), S((MID, ROWS), b16), S((16, 2 * MID + D), f32),
                   S((1, 4 * MID + 2 * D), f32), S((1, 4 * MID + 2 * D), f32), S((n, TB, 128), f32), S((n * TB, 128), b16), S((n, 16, 512), b16), S((TB, 128), f32)),
        in_specs=[hs] + [vs] * 8 + [pl.BlockSpec(memory_space=pltpu.SMEM)] * 6 + [hs] * 2,
        out_specs=(hs,) * 8 + (vs,) * 7,
        scratch_shapes=[
            V((6, TB, 128), f32), V((D // n, MID), b16), V((9 * MID // n, MID), b16), V((MID // n, D), b16), V((16, 128), f32),
            V((D, MID), b16), V((9 * MID, MID), b16), V((MID, D), b16), V((n, 16, 128), f32),
            V((ROWS, D), b16), V((ROWS, MID), f32), V((ROWS, MID), f32), V((ROWS, D), f32), V((ROWS, MID), b16),
            V((TB, D), f32), V((EROWS, MID), b16), V((EROWS, MID), b16),
            V((ROWS, MID), f32), V((ROWS, D), b16), V((ROWS, MID), b16), V((MID, ROWS), b16),
            V((2, SIDE, TB, D), b16), V((2, HC, 128), f32), V((PADC, 128), b16),
            V((n, TB, 128), f32), V((n, TB, 128), f32), V((h, 2, TB, LW), f32), V((h, TB, LW), f32),
            V((h, TB, LW), f32), V((TB, 128), f32), V((TB, 128), f32), V((16, 512), b16),
            V((n, TB, 128), f32), V((n, TB, 128), f32),
            dma((4,)), dma((4, sends)), dma((4, n)), dma((2,)), dma((2,)), dma((8,)), dma((1,)), dma((1,)),
            dma((n,)), dma((n,)), dma, dma, dma((h,)), dma((h,)), dma, dma, dma((h,)), dma((n,)),
            dma((h,)), dma((n,)), dma((n,)), dma((n,)), dma((2,)), dma((2,))],
        compiler_params=pltpu.CompilerParams(collective_id=cid, has_side_effects=True,
                                             vmem_limit_bytes=64 * 1024 * 1024),
        name="block_step",
    )(frames, *weights, *averages, *scal, head, avg_head)


KEEP, SEND, BOTH = 0, 1, 2
OUT, MIDDLE, IN, GAINS = 0, 1, 2, 3


def units_of(ri, ro, rm):
    q, h, t = MID // 4, ri // 2, rm // 2
    online = ((0, ri + 2 * ro, 2 * ro, 0, MID, SEND, OUT), (0, ri, 2 * ro, 0, MID, KEEP, OUT),
              (0, 0, ri, MID // 2, MID // 2, SEND, IN), (0, 0, h, 0, MID // 2, KEEP, IN), (0, h, h, 0, MID // 2, KEEP, IN),
              (1, 0, 3, 0, 128, BOTH, GAINS))
    target = ((0, 0, rm, 0, q, SEND, MIDDLE), (0, 0, rm, q, q, SEND, MIDDLE), (0, 0, rm, 2 * q, q, KEEP, MIDDLE),
              (0, 0, t, 3 * q, q, KEEP, MIDDLE), (0, t, 96, 3 * q, q, KEEP, MIDDLE),
              (0, t + 96, t - 96, 3 * q, q, KEEP, MIDDLE))
    return online, target


def sums_kernel(n_dev, rows, x_hbm, h1_hbm, a2_hbm, dh3_hbm, e_hbm, o_hbm, wmid_hbm, fart_hbm, st_ref, g_ref, gpart_ref,
                t_out, t_mid, t_in, t_gains, x_ref, h1_ref, a2_ref, dh3_ref, e_ref, o_ref, wmid_ref, fart_ref, low_ref,
                d2_ref, gg_ref, *refs):
    outs = (t_out, t_mid, t_in, t_gains)
    g, r1, r2, rz = (refs[2 * j:2 * j + 2] for j in range(4))
    fs, fr = refs[8:12], refs[12:16]
    s1, q1, s2, q2, s3, q3, sf, qf, sl, sd, qd = refs[16:]
    nz = n_dev // 4
    ri, ro, rm = rows
    online, target = units_of(*rows)
    me, z, x, c = place()
    role = lax.axis_index("role")
    xp = {"dp": me + 2 - 4 * x}
    cp = {"dp": me + 1 - 2 * c}

    def slot(zz, xx, cc):
        return zz * 4 + xx * 2 + cc

    order = list(range(nz))
    HW = MID // 2

    def load(k):
        src = (x_hbm, h1_hbm, a2_hbm, dh3_hbm, e_hbm, o_hbm, wmid_hbm, fart_hbm)[k]
        dst = (x_ref, h1_ref, a2_ref, dh3_ref, e_ref, o_ref, wmid_ref, fart_ref)[k]
        return pltpu.make_async_copy(src, dst, sl.at[k])

    def far_d2(to, k):
        cs = pl.ds(k * HW, HW)
        return rc(e_hbm.at[pl.ds(PAD, ROWS), cs], low_ref.at[:, cs], sd.at[k], qd.at[k], {"role": to})

    @pl.when(role == 0)
    def _():
        for k in (3, 2, 6, 4, 5, 1, 0):
            load(k).start()
    pl.when(role == 1)(load(7).start)
    zs = [{"dp": lax.rem(me + 4 * k, 4 * nz)} for k in range(1, nz)]
    greet([(None, p) for p in [xp, cp, {"role": 1 - role}] + zs])
    z8 = jnp.zeros((TB, CH), jnp.float32)

    def online_first():
        far_d2(1, 0).start()
        far_d2(1, 1).start()
        gg_ref[...] = gpart_ref[...]
        load(3).wait()
        load(2).wait()
        for k in (2, 3, 0, 1):
            v = lax.dot_general(a2_ref[...], dh3_ref[:, k * CH:(k + 1) * CH], T0, preferred_element_type=jnp.float32)
            g[0][:, ri + k * ro:ri + (k + 1) * ro, :] = v.reshape(n_dev, ro, CH)

    def online_rest():
        for k in (6, 4, 5, 1, 0):
            load(k).wait()

        def da1(i, carry):
            row = i * BLK
            acc = None
            for m, s in enumerate(OFFS):
                p = lax.dot_general(shifted(e_ref, o_ref, -s, row, BLK), wmid_ref[m * MID:(m + 1) * MID, :], T1,
                                    preferred_element_type=jnp.float32)
                acc = p if acc is None else acc + p
            d2_ref[pl.ds(pl.multiple_of(row, BLK), BLK), :] = acc
            return carry
        lax.fori_loop(0, ROWS // BLK, da1, 0)

        def put1(r, v):
            low_ref[rows_full(r), :] = jnp.concatenate([v, z8], axis=0).astype(jnp.bfloat16)
        through(h1_ref, d2_ref, st_ref, g_ref, gg_ref, 0, 0, MID, put1)
        per = CH // ri
        for k in range(D // CH):
            v = lax.dot_general(x_ref[:, k * CH:(k + 1) * CH], low_ref[...], T0, preferred_element_type=jnp.float32)
            g[0][k * per:(k + 1) * per, 0:ri, :] = v.reshape(per, ri, MID)
        for i in range(n_dev):
            for k in range(3):
                at = (i * 3 + k) * 128
                g[1][i, k:k + 1, :] = gg_ref[:, at:at + 128]

    def target_half(k):
        cs = slice(k * HW, (k + 1) * HW)
        far_d2(0, k).wait_recv()
        zh = jnp.zeros((TB, HW), jnp.float32)

        def rebuild(r, carry):
            v = low_ref[rows_full(r), cs].astype(jnp.float32)
            at = pl.ds(pl.multiple_of(PAD + r * RB, 16), RB)
            e_ref[at, cs] = low_ref[rows_full(r), cs]
            o_ref[at, cs] = jnp.concatenate([zh, v[0:VR]], axis=0).astype(jnp.bfloat16)
            return carry
        lax.fori_loop(0, SIDE, rebuild, 0)
        for m, s in enumerate(OFFS):
            ref, base = (e_ref, 16 - s) if s % 2 == 0 else (o_ref, 17 - s)
            v = jnp.dot(fart_ref[...], ref[base * TB:base * TB + ROWS, cs], preferred_element_type=jnp.float32)
            at = m * MID
            while at < (m + 1) * MID:
                i = at // rm
                end = min((i + 1) * rm, (m + 1) * MID)
                g[0][i, at - i * rm:end - i * rm, cs] = v[at - m * MID:end - m * MID]
                at = end

    def target_first():
        clear_margins(e_ref, o_ref)
        load(7).wait()
        target_half(0)

    def cut(ref, i, u):
        return ref.at[i, pl.ds(u[1], u[2]), pl.ds(u[3], u[4])]

    def region(u):
        if u[6] == OUT:
            return slice(0, ro), slice(0, outs[OUT].shape[1])
        at = u[3] % outs[u[6]].shape[1]
        return slice(u[1], u[1] + u[2]), slice(at, at + u[4])

    def place_sum(u, total):
        if u[6] == OUT:
            return jnp.concatenate([total[j * ro:(j + 1) * ro] for j in range(u[2] // ro)], axis=1)
        return total

    def final(u, to, n):
        rs, cs = region(u)
        at = (pl.ds(rs.start, rs.stop - rs.start), pl.ds(cs.start, cs.stop - cs.start))
        return rc(fs[u[6]].at[at], fr[u[6]].at[at], sf.at[n], qf.at[n], {"role": to})

    def run(units, mine, before, rest):
        def add(u, i, ref, j):
            a, rs, cs = u[0], slice(u[1], u[1] + u[2]), slice(u[3], u[3] + u[4])
            g[a][i, rs, cs] = g[a][i, rs, cs] + ref[a][j, rs, cs]

        def c1(n, zz, k):
            u = units[n]
            xx = 1 - x if k == 0 else x
            return rc(cut(g[u[0]], slot(zz, xx, 1 - c), u), cut(r1[u[0]], k * nz + zz, u), s1.at[n, k * nz + zz],
                      q1.at[n, k * nz + zz], cp)

        def c2(n, zz):
            u = units[n]
            return rc(cut(g[u[0]], slot(zz, 1 - x, c), u), cut(r2[u[0]], zz, u), s2.at[n, zz], q2.at[n, zz], xp)

        def c3(n, t, at):
            u = units[n]
            return rc(cut(g[u[0]], slot(t, x, c), u), cut(rz[u[0]], at, u), s3.at[n, t], q3.at[n, at],
                      {"dp": slot(t, x, c)})

        nu = len(units)

        def first(n):
            for k in range(2):
                for zz in order:
                    c1(n, zz, k).start()

        def second(n):
            for zz in order:
                c1(n, zz, 0).wait_recv()
                add(units[n], slot(zz, 1 - x, c), r1, zz)
                c2(n, zz).start()

        def finish(n):
            u = units[n]
            a, rs, cs = u[0], slice(u[1], u[1] + u[2]), slice(u[3], u[3] + u[4])
            for zz in order:
                @pl.when(z != zz)
                def _(zz=zz):
                    c3(n, z, zz).wait_recv()
                    add(u, me, rz, zz)
            total = place_sum(u, g[a][me, rs, cs])
            at = region(u)
            if u[5] != SEND:
                outs[u[6]][at] = total
            if u[5] != KEEP:
                fs[u[6]][at] = total.astype(fs[u[6]].dtype)
                final(u, 1 - mine, n).start()
        before()
        first(0)
        first(1)
        second(0)
        second(1)
        rest()
        for n in range(2, nu):
            first(n)
        for n in range(2, nu):
            second(n)
        for n, u in enumerate(units):
            for zz in order:
                c1(n, zz, 1).wait_recv()
                add(u, slot(zz, x, c), r1, nz + zz)
            for zz in order:
                c2(n, zz).wait_recv()
                add(u, slot(zz, x, c), r2, zz)
                pl.when(z != zz)(c3(n, zz, z).start)
            if n > 0:
                finish(n - 1)
        finish(nu - 1)
        for n, u in enumerate(units):
            for zz in order:
                c1(n, zz, 0).wait_send()
                c1(n, zz, 1).wait_send()
                c2(n, zz).wait_send()
                pl.when(z != zz)(c3(n, zz, z).wait_send)
            if u[5] != KEEP:
                final(u, 1 - mine, n).wait_send()

    def receive(units, other):
        for n, u in enumerate(units):
            if u[5] != KEEP:
                final(u, other, n).wait_recv()
                outs[u[6]][region(u)] = fr[u[6]][region(u)].astype(jnp.float32)

    @pl.when(role == 0)
    def _():
        run(online, 0, online_first, online_rest)
        receive(target, 1)
        far_d2(1, 0).wait_send()
        far_d2(1, 1).wait_send()

    @pl.when(role == 1)
    def _():
        run(target, 1, target_first, lambda: target_half(1))
        receive(online, 0)


def sums(saved, n, cid):
    nz = n // 4
    V, dma = pltpu.VMEM, pltpu.SemaphoreType.DMA
    f32, b16 = jnp.float32, jnp.bfloat16
    S = jax.ShapeDtypeStruct
    rows = ri, ro, rm = D // n, MID // n, 9 * MID // n
    half = [(ro, D // 2), (rm, MID // 2), (ri, MID // 2), (3, 128)]
    low = [b16, b16, b16, f32]
    sh = [(rm, MID), (3, 128)]
    nu = max(len(u) for u in units_of(*rows))
    vs, hs = pl.BlockSpec(memory_space=pltpu.VMEM), pl.BlockSpec(memory_space=pl.ANY)
    return pl.pallas_call(
        functools.partial(sums_kernel, n, rows),
        out_shape=tuple(S(s, f32) for s in half),
        in_specs=[hs] * 8 + [vs] * 3,
        out_specs=(vs,) * 4,
        scratch_shapes=[V(s.shape, s.dtype) for s in saved[:8]] +
        [V((ROWS, MID), b16), V((ROWS, MID), f32), V((1, 4 * MID + 2 * D), f32)] +
        [V((k * nz,) + s, f32) for k in (4, 2, 1, 1) for s in sh] + [V(s, t) for s, t in zip(half, low)] * 2 +
        [dma((nu, 2 * nz))] * 2 + [dma((nu, nz))] * 4 + [dma((nu,))] * 2 + [dma((8,)), dma((2,)), dma((2,))],
        compiler_params=pltpu.CompilerParams(collective_id=cid, has_side_effects=True,
                                             vmem_limit_bytes=63 * 1024 * 1024),
        name="gradient_sums",
    )(*saved)


UB = 1024
NU = -(-HALF // UB)
LASTU = HALF - (NU - 1) * UB


def segments(k):
    lo, hi = k * UB, min((k + 1) * UB, -(-HALF // 16) * 16)
    parts = []
    for i in range(GAMES // 2):
        a, end = window_of(i), window_of(i + 1)
        mixed = i > 0 and WIDE * i != a
        for r0, r1, games in ((a, a + 16, (i - 1, i)), (a + 16, end, (i,))) if mixed else ((a, end, (i,)),):
            if i == GAMES // 2 - 1 and r1 == end:
                r1 = -(-HALF // 16) * 16
            r0, r1 = max(r0, lo), min(r1, hi)
            if r0 < r1:
                parts.append((r0, r1, games))
    return parts


def update_kernel(gall_ref, frow_ref, dlog_ref, loss_ref, *refs):
    grads, olds_hbm = refs[:4], refs[4:16]
    hbm = refs[16:19]
    loss_out, news, hbm_out = refs[19], refs[20:36], refs[36:40]
    olds = refs[40:52]
    dlt, rhs, grow, ibuf, obuf, cbuf, si, so, sw = refs[52:]
    role = lax.axis_index("role")

    def rows_of(k):
        return UB if k < NU - 1 else LASTU

    def fetch(k):
        n = rows_of(k)
        return [pltpu.make_async_copy(hbm[t].at[pl.ds(pl.multiple_of(role * HALF + k * UB, 8), n)],
                                      ibuf.at[k % 3, t, pl.ds(0, n)], si.at[k % 3, t]) for t in range(3)]

    def store(k):
        n = rows_of(k)
        cs = [pltpu.make_async_copy(obuf.at[k % 2, t, pl.ds(0, n)], hbm_out[t].at[pl.ds(k * UB, n)], so.at[k % 2, t])
              for t in range(3)]
        return cs + [pltpu.make_async_copy(cbuf.at[k % 2, pl.ds(0, n)], hbm_out[3].at[pl.ds(k * UB, n)], so.at[k % 2, 3])]

    old_copies = [pltpu.make_async_copy(olds_hbm[i], olds[i], sw.at[i]) for i in range(12)]
    for d in fetch(0) + fetch(1) + old_copies:
        d.start()
    loss_out[...] = loss_ref[0:1, 0:1]
    ids = gall_ref[...].reshape(-1, 128).astype(jnp.int32) - role * (GAMES // 2)
    v = shift_rows(widen(dlog_ref[...]), ids_offset(ids), True)
    for k in range(WIN // 128):
        dlt[k * 128:(k + 1) * 128, :] = jnp.transpose(v[:, k * 128:(k + 1) * 128]).astype(jnp.bfloat16)
    rows = frow_ref[...].astype(jnp.float32)
    for i in range(GAMES // 2):
        rhs[i] = jnp.where(ids == i, rows, 0.0).astype(jnp.bfloat16)

    def small(a, right):
        w, m, v = olds[3 * a:3 * a + 3]
        nw, nm, nv, nc = news[4 * a:4 * a + 4]
        cols = grads[a].shape[1]
        cs = slice(cols if right else 0, (cols if right else 0) + cols)
        gv = grads[a][...]
        rate = learn_rate
        if a == 3:
            gv = jnp.concatenate([gv[k:k + 1, :] for k in range(gv.shape[0])], axis=1)
            cs = slice(0, gv.shape[1])
            rate = gain_rate
        mv = momentum_decay * m[:, cs] + gv
        wv = w[:, cs] - rate * (gv + momentum_decay * mv)
        nw[...] = wv
        nm[...] = gv if a == 0 else mv
        nv[...] = average_decay * v[:, cs] + (1.0 - average_decay) * wv
        nc[...] = wv.astype(jnp.bfloat16)

    for k in range(NU):
        if k + 2 < NU:
            for d in fetch(k + 2):
                d.start()
        lo = k * UB
        for r0, r1, games in segments(k):
            acc = None
            for i in games:
                at = r0 - window_of(i)
                p = jnp.dot(dlt[at:at + r1 - r0, :], rhs[i], preferred_element_type=jnp.float32)
                acc = p if acc is None else acc + p
            grow[r0 - lo:r1 - lo, :] = acc
        for d in fetch(k):
            d.wait()
        if k >= 2:
            for d in store(k - 2):
                d.wait()
        b, s = k % 2, k % 3

        def one(r, carry, b=b, s=s):
            rs = pl.ds(pl.multiple_of(r * 128, 128), 128)
            gv = grow[rs, :]
            m = momentum_decay * ibuf[s, 1, rs, :] + gv
            w = ibuf[s, 0, rs, :] - learn_rate * (gv + momentum_decay * m)
            obuf[b, 0, rs, :] = w
            obuf[b, 1, rs, :] = m
            obuf[b, 2, rs, :] = average_decay * ibuf[s, 2, rs, :] + (1.0 - average_decay) * w
            cbuf[b, rs, :] = w.astype(jnp.bfloat16)
            return carry
        lax.fori_loop(0, UB // 128, one, 0)
        for d in store(k):
            d.start()
        if 4 <= k < 8:
            a = k - 4
            for i in range(3 * a, 3 * a + 3):
                old_copies[i].wait()
            if a == 3:
                small(a, False)
            else:
                pl.when(role == 0)(lambda a=a: small(a, False))
                pl.when(role != 0)(lambda a=a: small(a, True))
    for k in (NU - 2, NU - 1):
        for d in store(k):
            d.wait()


def final_update(games_all, frow, dlog, loss, grads, olds, tables):
    n = games_all.shape[0]
    lanes = tables[0].shape[1]
    f32, b16 = jnp.float32, jnp.bfloat16
    S, V, dma = jax.ShapeDtypeStruct, pltpu.VMEM, pltpu.SemaphoreType.DMA
    vs, hs = pl.BlockSpec(memory_space=pltpu.VMEM), pl.BlockSpec(memory_space=pl.ANY)
    new_shapes = []
    for a in range(4):
        s = olds[3 * a].shape if a == 3 else grads[a].shape
        new_shapes += [S(s, f32)] * 3 + [S(s, b16)]
    return pl.pallas_call(
        update_kernel,
        in_specs=[vs] * 8 + [hs] * 15,
        out_specs=[vs] * 17 + [hs] * 4,
        scratch_shapes=[V(o.shape, f32) for o in olds] +
        [V((WIN, n * TB), b16), V((GAMES // 2, n * TB, lanes), b16), V((UB, lanes), f32), V((3, 3, UB, lanes), f32),
         V((2, 3, UB, lanes), f32), V((2, UB, lanes), b16), dma((3, 3)), dma((2, 4)), dma((12,))],
        out_shape=[S((1, 1), f32)] + new_shapes + [S((HALF, lanes), f32)] * 3 + [S((HALF, lanes), b16)],
        compiler_params=pltpu.CompilerParams(vmem_limit_bytes=63 * 1024 * 1024),
        name="final_update",
    )(games_all, frow, dlog, loss, *grads, *olds, *tables)


def fast_device(
    frames,
    game_ids,
    taken_actions,
    next_actions,
    expert_flags,
    rewards,
    done_flags,
    weight_in,
    weight_mid,
    weight_out,
    norm_gains,
    head_table,
    moment_in,
    moment_mid,
    moment_out,
    moment_gains,
    moment_head,
    average_in,
    average_mid,
    average_out,
    average_gains,
    average_head,
):
    n = lax.axis_size("dp")
    *saved, all_ids, feat_rows, dlog, loss = block_step(
        jnp.transpose(frames[0], (1, 0, 2)),
        (weight_in[0], weight_mid[0], weight_out[0], norm_gains),
        (average_in[0], average_mid[0], average_out[0], average_gains),
        (taken_actions, next_actions, expert_flags, rewards, done_flags, game_ids),
        head_table.T,
        average_head.T,
        n,
        1,
    )
    grad_out, grad_mid, grad_in, grad_gains = sums(saved, n, 2)
    loss, *rest = final_update(
        all_ids,
        feat_rows,
        dlog,
        loss,
        (grad_in, grad_mid, grad_out, grad_gains),
        (
            weight_in[0],
            moment_in[0],
            average_in[0],
            weight_mid[0],
            moment_mid[0],
            average_mid[0],
            weight_out[0],
            moment_out[0],
            average_out[0],
            norm_gains,
            moment_gains,
            average_gains,
        ),
        (head_table.T, moment_head.T, average_head.T),
    )
    return (
        loss.reshape(()),
        *(v[None] for v in rest[:12]),
        *rest[12:16],
        *(v.T for v in rest[16:]),
    )


def solution(mesh):
    return jax.shard_map(
        fast_device if mesh.shape["dp"] == 16 else on_device,
        mesh=mesh,
        in_specs=(
            P("role", "dp", None, None),
            P("dp"),
            P("dp"),
            P("dp"),
            P("dp"),
            P("dp"),
            P("dp"),
            P(None, "dp", None),
            P(None, "dp", None),
            P(None, "dp", None),
            P(None, "dp"),
            P("dp", None),
            P(None, "dp", None),
            P(None, "dp", None),
            P(None, "dp", None),
            P(None, "dp"),
            P("dp", None),
            P(None, "dp", None),
            P(None, "dp", None),
            P(None, "dp", None),
            P(None, "dp"),
            P("dp", None),
        ),
        out_specs=(
            P(),
            P(None, "dp", "role"),
            P(None, "dp", "role"),
            P(None, "dp", "role"),
            P(None, "dp", "role"),
            P(None, "dp", "role"),
            P(None, "dp", "role"),
            P(None, "dp", "role"),
            P(None, "dp", "role"),
            P(None, "dp", "role"),
            P(None, "dp", "role"),
            P(None, "dp", "role"),
            P(None, "dp", "role"),
            P(None, "dp"),
            P(None, "dp"),
            P(None, "dp"),
            P(None, "dp"),
            P("dp", "role"),
            P("dp", "role"),
            P("dp", "role"),
            P("dp", "role"),
        ),
        check_vma=False,
    )
```

```python
import functools

import jax
import jax.numpy as jnp
import numpy as np
from jax import lax
from jax.experimental import pallas as pl
from jax.experimental.pallas import tpu as pltpu
from jax.sharding import PartitionSpec as P

D = 2048
MID = 512
GAMES = 40
ACTIONS = 18
ATOMS = 51
GROUPS = 32
SIDE = 11
LAYERS = 1


support_low = -10.0
support_high = 10.0
discount = 0.99
penalty = 0.05
momentum_decay = 0.5
average_decay = 0.5
learn_rate = 4.0
gain_rate = 40.0
epsilon = 1e-05
HIGHEST = lax.Precision.HIGHEST


def passed_along(block, axis, distance):
    devices = range(lax.axis_size(axis))
    route = [(i - distance, i) for i in devices if i - distance in devices]
    return lax.ppermute(block, axis, route)


def split_gains(gains):
    return (
        gains[:MID],
        gains[MID : 2 * MID],
        gains[2 * MID : 3 * MID],
        gains[3 * MID : 4 * MID],
        gains[4 * MID : 4 * MID + D],
        gains[4 * MID + D :],
    )


def group_norm(values, gain, shift):
    rows, pixels, width = values.shape
    grouped = values.reshape(rows, pixels, GROUPS, width // GROUPS)
    center = grouped - jnp.mean(grouped, axis=(1, 3), keepdims=True)
    spread = jnp.mean(center * center, axis=(1, 3), keepdims=True)
    normed = (center * lax.rsqrt(spread + epsilon)).reshape(values.shape)
    return normed * gain + shift


def patches_of(acts):
    rows, pixels, width = acts.shape
    grid = acts.reshape(rows, SIDE, SIDE, width)
    padded = jnp.pad(grid, ((0, 0), (1, 1), (1, 1), (0, 0)))
    pieces = [
        padded[:, down : down + SIDE, right : right + SIDE, :]
        for down in range(3)
        for right in range(3)
    ]
    return jnp.concatenate(pieces, axis=-1).reshape(rows, pixels, 9 * width)


def transition_loss(logits, target_dist, action_hot, expert, support):
    log_prob = jax.nn.log_softmax(logits, axis=-1)
    values = jnp.sum(jnp.exp(log_prob) * support, axis=-1)
    spread_sum = jax.nn.logsumexp(values, axis=-1)
    chosen_log = jnp.sum(log_prob * action_hot[:, :, None], axis=1)
    cross = -jnp.sum(target_dist * chosen_log, axis=-1)
    regular = spread_sum - jnp.sum(values * action_hot, axis=-1)
    return cross + penalty * expert * regular


def project_target(next_prob, rewards, done_f, support):
    moved = jnp.clip(
        rewards[:, None] + discount * (1.0 - done_f)[:, None] * support[None, :],
        support_low,
        support_high,
    )
    spacing = (support_high - support_low) / (ATOMS - 1)
    weight = jnp.maximum(0.0, 1.0 - jnp.abs(moved[:, :, None] - support[None, None, :]) / spacing)
    return jnp.sum(next_prob[:, :, None] * weight, axis=1)


def renew(weight, grad, moment, average, rate):
    new_moment = momentum_decay * moment + grad
    new_weight = weight - rate * (grad + momentum_decay * new_moment)
    new_average = average_decay * average + (1.0 - average_decay) * new_weight
    return (new_weight, new_moment, new_average, new_weight.astype(jnp.bfloat16))


def lower_half(values):
    return values[..., : values.shape[-1] // 2]


def upper_half(values):
    return values[..., values.shape[-1] // 2 :]


def own_half(values, role_index):
    half = values.shape[-1] // 2
    return lax.dynamic_slice_in_dim(values, role_index * half, half, values.ndim - 1)


def norm_act(hidden, gain, shift):
    return jax.nn.gelu(group_norm(hidden, gain, shift))


def outer_act(hidden, gain, shift, stream):
    return jax.nn.gelu(stream + group_norm(hidden, gain, shift))


def block_forward(stream, weights):
    w_in, w_mid, w_out, gains = weights
    gain_one, shift_one, gain_two, shift_two, gain_three, shift_three = split_gains(gains)
    stream_low = stream.astype(jnp.bfloat16)
    hidden_in = jnp.einsum("bpc,cm->bpm", stream_low, w_in, preferred_element_type=jnp.float32)
    act_in = norm_act(hidden_in, gain_one, shift_one).astype(jnp.bfloat16)
    hidden_mid = jnp.einsum(
        "bpc,cm->bpm", patches_of(act_in), w_mid, preferred_element_type=jnp.float32
    )
    act_mid = norm_act(hidden_mid, gain_two, shift_two).astype(jnp.bfloat16)
    hidden_out = jnp.einsum("bpc,cm->bpm", act_mid, w_out, preferred_element_type=jnp.float32)
    result = outer_act(hidden_out, gain_three, shift_three, stream)
    return (result, (stream, stream_low, hidden_in, act_in, hidden_mid, act_mid, hidden_out))


def block_backward(grad_result, weights, kept, settle):
    w_in, w_mid, w_out, gains = weights
    stream, stream_low, hidden_in, act_in, hidden_mid, act_mid, hidden_out = kept
    gain_one, shift_one, gain_two, shift_two, gain_three, shift_three = split_gains(gains)
    _, back_three = jax.vjp(outer_act, hidden_out, gain_three, shift_three, stream)
    d_three, dg_three, db_three, d_resid = back_three(grad_result)
    d_three = d_three.astype(jnp.bfloat16)
    grad_out = settle(
        jnp.einsum("bpm,bpc->mc", act_mid, d_three, preferred_element_type=jnp.float32)
    )
    d_act_mid = jnp.einsum("bpc,mc->bpm", d_three, w_out, preferred_element_type=jnp.float32)
    _, back_two = jax.vjp(norm_act, hidden_mid, gain_two, shift_two)
    d_two, dg_two, db_two = back_two(d_act_mid)
    d_two = d_two.astype(jnp.bfloat16)
    grad_mid = settle(
        jnp.einsum("bpk,bpm->km", patches_of(act_in), d_two, preferred_element_type=jnp.float32)
    )
    d_cols = jnp.einsum("bpm,km->bpk", d_two, w_mid, preferred_element_type=jnp.float32)
    _, back_cols = jax.vjp(patches_of, act_in.astype(jnp.float32))
    (d_act_in,) = back_cols(d_cols)
    _, back_one = jax.vjp(norm_act, hidden_in, gain_one, shift_one)
    d_one, dg_one, db_one = back_one(d_act_in)
    d_one = d_one.astype(jnp.bfloat16)
    grad_in = jnp.einsum("bpc,bpm->cm", stream_low, d_one, preferred_element_type=jnp.float32)
    d_stream = d_resid + jnp.einsum("bpm,cm->bpc", d_one, w_in, preferred_element_type=jnp.float32)
    grad_gains = jnp.concatenate([dg_one, db_one, dg_two, db_two, dg_three, db_three])
    grad_in, grad_gains = settle((grad_in, grad_gains))
    return (d_stream, (grad_in, grad_mid, grad_out, grad_gains))


def on_device(
    frames,
    game_ids,
    taken_actions,
    next_actions,
    expert_flags,
    rewards,
    done_flags,
    weight_in,
    weight_mid,
    weight_out,
    norm_gains,
    head_table,
    moment_in,
    moment_mid,
    moment_out,
    moment_gains,
    moment_head,
    average_in,
    average_mid,
    average_out,
    average_gains,
    average_head,
):
    role_index = lax.axis_index("role")
    online = role_index == 0
    use_in = jnp.where(online, weight_in, average_in).astype(jnp.bfloat16)
    use_mid = jnp.where(online, weight_mid, average_mid).astype(jnp.bfloat16)
    use_out = jnp.where(online, weight_out, average_out).astype(jnp.bfloat16)
    use_gains = jnp.where(online, norm_gains, average_gains).astype(jnp.bfloat16)
    use_head = jnp.where(online, head_table, average_head).astype(jnp.bfloat16)
    support = support_low + (support_high - support_low) * jnp.arange(ATOMS, dtype=jnp.float32) / (
        ATOMS - 1
    )
    own_hot = (game_ids[:, None] == lax.broadcasted_iota(jnp.int32, (1, GAMES), 1)).astype(
        jnp.float32
    )
    counts = jnp.sum(own_hot, axis=0)
    stream = frames[0].astype(jnp.float32)
    layer = 0
    pieces = (
        lax.all_gather(use_in[layer], "dp", axis=0, tiled=True),
        lax.all_gather(use_mid[layer], "dp", axis=0, tiled=True),
        lax.all_gather(use_out[layer], "dp", axis=0, tiled=True),
        lax.all_gather(use_gains[layer], "dp", axis=0, tiled=True),
    )
    weights = (pieces[0], pieces[1], pieces[2], pieces[3].astype(jnp.float32))
    stream, saved = block_forward(stream, weights)
    gathered = [weights]
    kept = [saved]
    trans = stream.shape[0]
    pixels = stream.shape[1]
    wide_k = ACTIONS * ATOMS
    head_rows = head_table.shape[0]
    feat_low = jnp.mean(stream, axis=1).astype(jnp.bfloat16)
    feat_all, game_all = (
        lax.all_gather(feat_low, "dp", axis=0, tiled=True),
        lax.all_gather(game_ids.astype(jnp.bfloat16)[:, None], "dp", axis=0, tiled=True),
    )
    game_iota = lax.broadcasted_iota(jnp.int32, (1, GAMES), 1).astype(jnp.float32)
    all_hot = (game_all.astype(jnp.float32) == game_iota).astype(jnp.bfloat16)
    feat_rows = lax.dynamic_slice_in_dim(feat_all, lax.axis_index("dp") * head_rows, head_rows, 1)
    head_low = use_head.reshape(head_rows * GAMES, wide_k)

    def widen(count):
        spread_rows = (feat_rows[:, :, None] * all_hot[:, None, :]).reshape(
            count, head_rows * GAMES
        )
        return (spread_rows, all_hot)

    spread_rows, hot_piece = widen(trans * lax.axis_size("dp"))
    flat_logits = lax.psum_scatter(
        jnp.dot(spread_rows, head_low, preferred_element_type=jnp.float32),
        "dp",
        scatter_dimension=0,
        tiled=True,
    )
    logits = flat_logits.reshape(trans, ACTIONS, ATOMS)
    next_hot = (next_actions[:, None] == lax.broadcasted_iota(jnp.int32, (1, ACTIONS), 1)).astype(
        jnp.float32
    )
    next_prob = jax.nn.softmax(jnp.sum(logits * next_hot[:, :, None], axis=1), axis=-1)
    projected = project_target(next_prob, rewards, done_flags.astype(jnp.float32), support)
    target_dist = passed_along(projected, "role", -1)
    action_hot = (
        taken_actions[:, None] == lax.broadcasted_iota(jnp.int32, (1, ACTIONS), 1)
    ).astype(jnp.float32)
    expert = expert_flags.astype(jnp.float32)

    def local_loss(values):
        return transition_loss(values, target_dist, action_hot, expert, support)

    row_loss, loss_back = jax.vjp(local_loss, logits)
    sums = jnp.dot(row_loss, own_hot, precision=HIGHEST)
    total_counts, total_sums = lax.psum((counts, sums), "dp")
    floor_counts = jnp.maximum(total_counts, 1.0)
    loss_total = jnp.sum(total_sums / floor_counts)
    row_weight = jnp.dot(own_hot, 1.0 / (GAMES * floor_counts), precision=HIGHEST)
    (d_logits,) = loss_back(row_weight)
    d_low = d_logits.reshape(trans, wide_k).astype(jnp.bfloat16)
    piece = lax.all_gather(d_low, "dp", axis=0, tiled=True)
    count = piece.shape[0]
    spread_rows, hot_piece = widen(count)
    grad_head = lax.dot_general(
        spread_rows, piece, (((0,), (0,)), ((), ())), preferred_element_type=jnp.float32
    )
    back_wide = jnp.dot(piece, head_low.T, preferred_element_type=jnp.float32)
    back_rows = jnp.sum(
        back_wide.reshape(count, head_rows, GAMES) * hot_piece[:, None, :].astype(jnp.float32),
        axis=2,
    )
    grad_rows = back_rows
    grad_head, grad_rows = (grad_head, grad_rows)
    feat_grad = lax.all_to_all(
        grad_rows.astype(jnp.bfloat16), "dp", split_axis=0, concat_axis=1, tiled=True
    ).astype(grad_rows.dtype)
    d_stream = jnp.broadcast_to(feat_grad[:, None, :] / pixels, stream.shape)

    def settle(values):
        return values

    layer_grads = [None] * LAYERS
    for layer in reversed(range(LAYERS)):
        d_stream, block_grad = block_backward(d_stream, gathered[layer], kept[layer], settle)
        layer_grads[layer] = block_grad
    stacked = tuple((jnp.stack([layer_grads[0][kind]]) for kind in range(4)))
    reduced = lax.psum_scatter(stacked, "dp", scatter_dimension=1, tiled=True)
    head_grad = grad_head.reshape(head_rows, GAMES * wide_k)
    sent = (
        passed_along(upper_half(reduced[0]).astype(jnp.bfloat16), "role", 1).astype(jnp.float32),
        passed_along(upper_half(reduced[1]).astype(jnp.bfloat16), "role", 1).astype(jnp.float32),
        passed_along(upper_half(reduced[2]).astype(jnp.bfloat16), "role", 1).astype(jnp.float32),
        passed_along(reduced[3].astype(jnp.bfloat16), "role", 1).astype(jnp.float32),
        passed_along(upper_half(head_grad).astype(jnp.bfloat16), "role", 1).astype(jnp.float32),
        passed_along(loss_total.astype(jnp.bfloat16), "role", 1).astype(loss_total.dtype),
    )
    grad_in = jnp.where(online, lower_half(reduced[0]), sent[0])
    grad_mid = jnp.where(online, lower_half(reduced[1]), sent[1])
    grad_out = jnp.where(online, lower_half(reduced[2]), sent[2])
    grad_gains = jnp.where(online, reduced[3], sent[3])
    grad_table = jnp.where(online, lower_half(head_grad), sent[4])
    loss_out = jnp.where(online, loss_total, sent[5])
    in_w, in_m, in_a, in_c = renew(
        own_half(weight_in, role_index),
        grad_in,
        own_half(moment_in, role_index),
        own_half(average_in, role_index),
        learn_rate,
    )
    mid_w, mid_m, mid_a, mid_c = renew(
        own_half(weight_mid, role_index),
        grad_mid,
        own_half(moment_mid, role_index),
        own_half(average_mid, role_index),
        learn_rate,
    )
    out_w, out_m, out_a, out_c = renew(
        own_half(weight_out, role_index),
        grad_out,
        own_half(moment_out, role_index),
        own_half(average_out, role_index),
        learn_rate,
    )
    gain_w, gain_m, gain_a, gain_c = renew(
        norm_gains, grad_gains, moment_gains, average_gains, gain_rate
    )
    head_w, head_m, head_a, head_c = renew(
        own_half(head_table, role_index),
        grad_table,
        own_half(moment_head, role_index),
        own_half(average_head, role_index),
        learn_rate,
    )
    return (
        loss_out,
        in_w,
        grad_in,
        in_a,
        in_c,
        mid_w,
        mid_m,
        mid_a,
        mid_c,
        out_w,
        out_m,
        out_a,
        out_c,
        gain_w,
        gain_m,
        gain_a,
        gain_c,
        head_w,
        head_m,
        head_a,
        head_c,
    )


MESH = pl.DeviceIdType.MESH


def any_spec():
    return pl.BlockSpec(memory_space=pl.ANY)


def greet(peers):
    barrier = pltpu.get_barrier_semaphore()
    for cond, dev in peers:
        def go(dev=dev):
            pl.semaphore_signal(barrier, inc=1, device_id=dev, device_id_type=MESH)
        go() if cond is None else pl.when(cond)(go)
    count = sum(1 for cond, _ in peers if cond is None)
    for cond, _ in peers:
        if cond is not None:
            count = count + cond.astype(jnp.int32)
    pl.semaphore_wait(barrier, count)


def place():
    me = lax.axis_index("dp")
    core = lax.rem(me, 2)
    x = lax.rem(me // 2, 2)
    z = me // 4
    return me, z, x, core


D = 2048
MID = 512
GROUPS = 32
SIDE = 11
PIX = 121
TB = 8
PITCH = 12
RB = PITCH * TB
VR = SIDE * TB
ROWS = SIDE * RB
PAD = 16 * TB
EROWS = 164 * TB
BLK = 352
CH = 512
epsilon = 1e-05
GK = 0.7978845608028654
GC = 0.044715
OFFS = [(i - 1) * PITCH + (j - 1) for i in range(3) for j in range(3)]


def group_sum(v, gs):
    width = v.shape[1]
    n = width // 128
    a = lax.broadcasted_iota(jnp.int32, (128, 128), 0) // gs
    b = lax.broadcasted_iota(jnp.int32, (128, 128), 1) // gs
    m = (a == b).astype(jnp.float32)
    st = jnp.concatenate([v[:, k * 128:(k + 1) * 128] for k in range(n)], axis=0)
    r = jnp.dot(st, m, precision=lax.Precision.HIGHEST, preferred_element_type=jnp.float32)
    return jnp.concatenate([r[k * 8:(k + 1) * 8] for k in range(n)], axis=1)


def fold(v):
    rows, w = v.shape
    return jnp.sum(v.reshape(rows // TB, TB, w), axis=0)


def moments(h_ref, lo, gs):
    def one(r, acc):
        return acc + fold(h_ref[pl.ds(pl.multiple_of(r * RB, RB), VR), lo:lo + CH])
    s = lax.fori_loop(0, SIDE, one, jnp.zeros((TB, CH), jnp.float32))
    mean = group_sum(s, gs) / float(PIX * gs)

    def two(r, acc):
        h = h_ref[pl.ds(pl.multiple_of(r * RB, RB), VR), lo:lo + CH].reshape(SIDE, TB, CH) - mean[None]
        return acc + jnp.sum(h * h, axis=0)
    q = lax.fori_loop(0, SIDE, two, jnp.zeros((TB, CH), jnp.float32))
    var = group_sum(q, gs) / float(PIX * gs)
    return mean, lax.rsqrt(var + epsilon)


def gelu(u):
    return 0.5 * u * (1.0 + jnp.tanh(GK * (u + GC * (u * u * u))))


def dgelu(u):
    uu = u * u
    t = jnp.tanh(GK * u * (1.0 + GC * uu))
    return 0.5 * (1.0 + t) + 0.5 * u * (1.0 - t * t) * (GK + (3.0 * GK * GC) * uu)


def shifted(e_ref, o_ref, s, row, n):
    ref, base = (e_ref, 16 + s) if s % 2 == 0 else (o_ref, 17 + s)
    return ref[pl.ds(pl.multiple_of(row + base * TB, 16), n), :]


def put_shifted(e_ref, o_ref, r, v):
    z = jnp.zeros((TB, v.shape[1]), jnp.float32)
    at = pl.ds(pl.multiple_of(PAD + r * RB, 16), RB)
    e_ref[at, :] = jnp.concatenate([v, z], axis=0).astype(jnp.bfloat16)
    o_ref[at, :] = jnp.concatenate([z, v], axis=0).astype(jnp.bfloat16)


def clear_margins(e_ref, o_ref):
    z = jnp.zeros((PAD, MID), jnp.bfloat16)
    for ref in (e_ref, o_ref):
        ref[0:PAD, :] = z
        ref[PAD + ROWS:EROWS, :] = z


def row_at(r):
    return pl.ds(pl.multiple_of(r * RB, RB), VR)


def rows_full(r):
    return pl.ds(pl.multiple_of(r * RB, RB), RB)


def norm_back(h_ref, lo, dy_ref, mean, rstd, gain, gs, s1, s2, emit):
    n = 1.0 / float(PIX * gs)
    m1 = group_sum(gain * s1, gs) * n
    m2 = group_sum(gain * s2, gs) * n
    ca = rstd * gain
    cc = -rstd * rstd * m2
    cb = -rstd * m1 - mean * cc

    def one(r, c):
        h = h_ref[row_at(r), lo:lo + CH].reshape(SIDE, TB, CH)
        dy = dy_ref[row_at(r), :].reshape(SIDE, TB, CH)
        emit(r, (ca[None] * dy + cc[None] * h + cb[None]).reshape(VR, CH))
        return c
    lax.fori_loop(0, SIDE, one, 0)


D = 2048
GAMES = 40
ACTIONS = 18
ATOMS = 51
WIDE = ACTIONS * ATOMS
LW = 1024
WIN = 1024
COLS = GAMES * WIDE
HALF = COLS // 2
PADC = 36864
TB = 8
support_low = -10.0
support_high = 10.0
discount = 0.99
penalty = 0.05


def window_of(g):
    return (WIDE * g) // 16 * 16


def ids_offset(ids):
    return lax.bitwise_and(WIDE * ids, 15)


def shift_rows(v, off, right):
    width = v.shape[1]
    for b in range(1, 4):
        n = 1 << b
        bit = lax.bitwise_and(off, n) != 0
        bit = jnp.concatenate([bit.astype(jnp.float32)] * (width // 128), axis=1) > 0.5
        v = jnp.where(bit, pltpu.roll(v, n if right else width - n, 1), v)
    return v


def widen(dl):
    n = dl.shape[0]
    v = dl.astype(jnp.float32)
    v = jnp.concatenate([v[:, 0:TB], v[:, TB:2 * TB]], axis=2).reshape(n * TB, LW)
    lanes = lax.broadcasted_iota(jnp.int32, (n * TB, 128), 1)
    last = jnp.where(lanes < WIDE - LW + 128, v[:, LW - 128:], 0.0)
    return jnp.concatenate([v[:, :LW - 128], last], axis=1)


W_IN, W_MID, W_OUT, MISC = 0, 1, 2, 3
HC = 2048
NHC = -(-COLS // HC)
T0 = (((0,), (0,)), ((), ()))
T1 = (((1,), (1,)), ((), ()))


def rc(src, dst, ss, rs, dev):
    return pltpu.make_async_remote_copy(src_ref=src, dst_ref=dst, send_sem=ss, recv_sem=rs, device_id=dev,
                                        device_id_type=MESH)


def when(cond, do):
    if cond is None:
        do()
    else:
        pl.when(cond)(do)


class Gather:
    def __init__(self, nz, own, full, rows, own_sem, send, recv):
        self.nz, self.own_refs, self.full, self.rows = nz, own, full, rows
        self.own_sem, self.send, self.recv = own_sem, send, recv
        self.me, self.z, self.x, self.c = place()
        me, x, c = self.me, self.x, self.c
        self.up, self.down = {"dp": me + 4}, {"dp": me - 4}
        self.xp, self.cp = {"dp": me + 2 - 4 * x}, {"dp": me + 1 - 2 * c}
        self.has_up, self.has_down = self.z < nz - 1, self.z > 0
        self.started = []

    def slot(self, a, i):
        n = self.rows[a]
        return self.full[a].at[i] if n is None else self.full[a].at[pl.ds(pl.multiple_of(i * n, 16), n)]

    def put(self, cond, a, src, i, dev, k):
        d = rc(src, self.slot(a, i), self.send.at[a, k], self.recv.at[a, i], dev)
        when(cond, d.start)
        self.started.append((cond, d))

    def take(self, cond, a, i):
        d = rc(self.slot(a, i), self.slot(a, i), self.send.at[a, 0], self.recv.at[a, i], self.cp)
        when(cond, d.wait_recv)

    def begin(self, a):
        src = self.own_refs[a]
        self.put(self.has_up, a, src, self.me, self.up, 0)
        self.put(self.has_down, a, src, self.me, self.down, 1)
        self.put(None, a, src, self.me, self.xp, 2)
        self.put(None, a, src, self.me, self.cp, 3)
        pltpu.make_async_copy(src, self.slot(a, self.me), self.own_sem.at[a]).start()

    def along_z(self, a, d):
        k = 4 + (d - 1) * 6
        for up in (True, False):
            s = self.me - 4 * d if up else self.me + 4 * d
            ok = self.z - d >= 0 if up else self.z + d < self.nz
            more = jnp.logical_and(ok, self.has_up if up else self.has_down)
            m = k if up else k + 3
            self.take(ok, a, s)
            self.put(more, a, self.slot(a, s), s, self.up if up else self.down, m)
            self.put(ok, a, self.slot(a, s), s, self.xp, m + 1)
            self.put(ok, a, self.slot(a, s), s, self.cp, m + 2)

    def at_distance(self, d):
        for up in ((True,) if d == 0 else (False, True)):
            zz = self.z + d if up else self.z - d
            yield zz, (None if d == 0 else zz < self.nz if up else zz >= 0), up

    def along_x(self, a, d):
        k = 4 + (self.nz - 1) * 6
        for zz, ok, up in self.at_distance(d):
            s = zz * 4 + (1 - self.x) * 2 + self.c
            self.take(ok, a, s)
            self.put(ok, a, self.slot(a, s), s, self.cp, k + 2 * d + (1 if up else 0))

    def arrived(self, a):
        for d in range(self.nz):
            for zz, ok, _ in self.at_distance(d):
                for xx in (self.x, 1 - self.x):
                    self.take(ok, a, zz * 4 + xx * 2 + 1 - self.c)
        pltpu.make_async_copy(self.own_refs[a], self.slot(a, self.me), self.own_sem.at[a]).wait()

    def end(self):
        for cond, d in self.started:
            when(cond, d.wait_send)


def put_gain(gg_ref, at, s):
    gg_ref[:, at:at + CH] = jnp.sum(s, axis=0, keepdims=True)


def through(h_ref, d2_ref, st_ref, g_ref, gg_ref, at, goff, boff, emit):
    z8 = jnp.zeros((TB, CH), jnp.float32)
    mean = st_ref[0:8, at:at + MID]
    rstd = st_ref[8:16, at:at + MID]
    gain = g_ref[:, goff:goff + MID]
    shift = g_ref[:, boff:boff + MID]
    mr = mean * rstd

    def one(r, acc):
        s1, s2 = acc
        h = h_ref[row_at(r), :].reshape(SIDE, TB, MID)
        da = d2_ref[row_at(r), :].reshape(SIDE, TB, MID)
        xh = h * rstd[None] - mr[None]
        dy = da * dgelu(xh * gain + shift)
        d2_ref[row_at(r), :] = dy.reshape(VR, MID)
        return s1 + jnp.sum(dy, axis=0), s2 + jnp.sum(dy * xh, axis=0)
    s1, s2 = lax.fori_loop(0, SIDE, one, (z8, z8))
    put_gain(gg_ref, goff, s2)
    put_gain(gg_ref, boff, s1)
    norm_back(h_ref, 0, d2_ref, mean, rstd, gain, MID // GROUPS, s1, s2, emit)


def step_kernel(n, fr_hbm, wi, wm, wo, wg, ai, am, ao, ag, k0, k1, k2, k3, k4, k5, ht_hbm, ha_hbm,
                x_hbm, h1_hbm, a2_hbm, dh3_hbm, e_hbm, o_hbm, wmid_hbm, fart_hbm,
                st_ref, g_ref, gg_ref, gall_ref, frow_ref, dlog_ref, loss_ref,
                scal_ref, own_in, own_mid, own_out, own_misc, win_ref, wmid_ref, wout_ref, misc_ref,
                x_ref, h1_ref, h2_ref, h3_ref, a2_ref, dfeat_ref, sl_ref, e_ref, o_ref,
                d2_ref, dh3_ref, far_ref, fart_ref, fbuf, hbuf, head_ref,
                fsend, frecv, part, r1, r2, tgt_s, tgt_r, down_s, dsend, drecv,
                own_sem, g_send, g_recv, f_sem, h_sem, k_sem, ss, rs_,
                s_f, q_f, s_1, q_1, s_2, q_2, s_t, q_t, s_l, q_l, s_c, q_c, s_d, q_d, s_r, q_r):
    me, z, x, c = place()
    role = lax.axis_index("role")
    half = n // 2
    peers = [lax.rem(me + k, n) for k in range(1, n)]
    cp = me + 1 - 2 * c
    du_ref = d2_ref

    def pick(w, a, dst):
        def fill(src):
            dst[...] = src[...].astype(jnp.bfloat16)
        pl.when(role == 0)(lambda: fill(w))
        pl.when(role != 0)(lambda: fill(a))

    def fetch_frames(r):
        return pltpu.make_async_copy(fr_hbm.at[pl.ds(r * SIDE, SIDE)], fbuf.at[r % 2], f_sem.at[r % 2])

    def fetch_head(k, go):
        m = HC if k < NHC - 1 else COLS - (NHC - 1) * HC

        def one(src):
            d = pltpu.make_async_copy(src.at[pl.ds(k * HC, m)], hbuf.at[k % 2, pl.ds(0, m)], h_sem.at[k % 2])
            d.start() if go else d.wait()
        if go:
            pl.when(role == 0)(lambda: one(ht_hbm))
            pl.when(role != 0)(lambda: one(ha_hbm))
        else:
            one(ht_hbm)
    fetch_frames(0).start()
    fetch_head(0, True)
    pick(wi, ai, own_in)
    pick(wm, am, own_mid)
    pick(wo, ao, own_out)

    def pick_gains(src):
        v = src[...].astype(jnp.bfloat16).astype(jnp.float32)
        for k in range(3):
            own_misc[k:k + 1, :] = v[:, k * 128:(k + 1) * 128]
    own_misc[0:TB, :] = jnp.zeros((TB, 128), jnp.float32)
    pl.when(role == 0)(lambda: pick_gains(wg))
    pl.when(role != 0)(lambda: pick_gains(ag))
    for k, ref in enumerate((k0, k1, k2, k3, k4, k5)):
        for t in range(TB):
            scal_ref[k, t:t + 1, :] = jnp.full((1, 128), ref[t].astype(jnp.float32), jnp.float32)
    own_misc[TB:2 * TB, :] = scal_ref[5]
    greet([(None, {"dp": p}) for p in peers] + [(None, {"role": 1 - role})])

    gath = Gather(n // 4, (own_in, own_mid, own_out, own_misc), (win_ref, wmid_ref, wout_ref, misc_ref),
               (D // n, 9 * MID // n, MID // n, None), own_sem, g_send, g_recv)
    casts = iter(range(NHC))

    def cast_head(times):
        for _ in range(times):
            k = next(casts, None)
            if k is None:
                return
            if k + 1 < NHC:
                fetch_head(k + 1, True)
            fetch_head(k, False)
            m = HC if k < NHC - 1 else COLS - (NHC - 1) * HC
            u = 128 if m % 128 == 0 else 112

            def one(i, carry, k=k, u=u):
                rs = pl.ds(pl.multiple_of(i * u, 16), u)
                head_ref[pl.ds(pl.multiple_of(k * HC + i * u, 16), u), :] = hbuf[k % 2, rs, :].astype(jnp.bfloat16)
                return carry
            lax.fori_loop(0, m // u, one, 0)

    for a in (MISC, W_IN, W_MID):
        gath.begin(a)
    for r in range(SIDE):
        if r + 1 < SIDE:
            fetch_frames(r + 1).start()
        fetch_frames(r).wait()
        v = fbuf[r % 2].astype(jnp.float32).reshape(VR, D)
        x_ref[r * RB:(r + 1) * RB, :] = jnp.concatenate([v, jnp.zeros((TB, D), jnp.float32)], axis=0).astype(jnp.bfloat16)
    clear_margins(e_ref, o_ref)
    head_ref[COLS:PADC, :] = jnp.zeros((PADC - COLS, 128), jnp.bfloat16)
    far = n // 4 - 1
    kept = [pltpu.make_async_copy(src, dst, k_sem.at[k]) for k, (src, dst) in enumerate((
        (x_ref, x_hbm), (h1_ref, h1_hbm), (a2_ref, a2_hbm), (dh3_ref, dh3_hbm), (e_ref, e_hbm), (o_ref, o_hbm),
        (wmid_ref, wmid_hbm)))]

    def keep(k):
        pl.when(role == 0)(kept[k].start)
    keep(0)

    def z_step(a, d):
        if d <= far:
            gath.along_z(a, d)

    def x_step(a, d):
        if d <= far:
            gath.along_x(a, d)
    for d in range(1, far + 1):
        z_step(W_IN, d)
        z_step(MISC, d)
        cast_head(2)
        x_step(W_IN, d - 1)
        x_step(MISC, d - 1)
        z_step(W_MID, d)
        cast_head(2)
        if d == max(far - 1, 1):
            gath.begin(W_OUT)
    x_step(W_IN, far)
    x_step(MISC, far)
    x_step(W_MID, 0)
    x_step(W_MID, 1)
    cast_head(1)
    z_step(W_OUT, 1)
    gath.arrived(MISC)
    gath.arrived(W_IN)
    for i in range(n):
        gall_ref[i] = misc_ref[i, TB:2 * TB, :]
        for k in range(3):
            at = (i * 3 + k) * 128
            g_ref[:, at:at + 128] = misc_ref[i, k:k + 1, :]

    def mm1(i, carry):
        rs = pl.ds(pl.multiple_of(i * BLK, BLK), BLK)
        h1_ref[rs, :] = jnp.dot(x_ref[rs, :], win_ref[...], preferred_element_type=jnp.float32)
        return carry
    lax.fori_loop(0, ROWS // BLK, mm1, 0)
    z_step(W_OUT, 2)
    x_step(W_MID, 2)
    keep(1)
    mean, rstd = moments(h1_ref, 0, MID // GROUPS)
    st_ref[0:8, 0:MID] = mean
    st_ref[8:16, 0:MID] = rstd
    sc = rstd * g_ref[:, 0:MID]
    sh = g_ref[:, MID:2 * MID] - mean * sc

    def act1(r, carry):
        h = h1_ref[row_at(r), :].reshape(SIDE, TB, MID)
        a = gelu(h * sc[None] + sh[None]).reshape(VR, MID)
        put_shifted(e_ref, o_ref, r, a)
        return carry
    lax.fori_loop(0, SIDE, act1, 0)
    inner = pl.ds(PAD, ROWS)

    def far_a1(to):
        return rc(e_ref.at[inner], far_ref, ss.at[0], rs_.at[0], {"role": to})

    pl.when(role == 0)(lambda: far_a1(1).start())
    cast_head(NHC)
    z_step(W_OUT, 3)
    for d in range(3, far + 1):
        x_step(W_MID, d)
    gath.arrived(W_MID)
    keep(6)

    def mm2(i, carry):
        row = i * BLK
        acc = None
        for m, s in enumerate(OFFS):
            p = jnp.dot(shifted(e_ref, o_ref, s, row, BLK), wmid_ref[m * MID:(m + 1) * MID, :],
                        preferred_element_type=jnp.float32)
            acc = p if acc is None else acc + p
        h2_ref[pl.ds(pl.multiple_of(row, BLK), BLK), :] = acc
        return carry
    lax.fori_loop(0, ROWS // BLK, mm2, 0)
    for d in range(far + 1):
        x_step(W_OUT, d)
    mean, rstd = moments(h2_ref, 0, MID // GROUPS)
    st_ref[0:8, MID:2 * MID] = mean
    st_ref[8:16, MID:2 * MID] = rstd
    sc2 = rstd * g_ref[:, 2 * MID:3 * MID]
    sh2 = g_ref[:, 3 * MID:4 * MID] - mean * sc2

    def act2(r, carry):
        h = h2_ref[rows_full(r), :].reshape(PITCH, TB, MID)
        a2_ref[rows_full(r), :] = gelu(h * sc2[None] + sh2[None]).reshape(RB, MID).astype(jnp.bfloat16)
        return carry
    lax.fori_loop(0, SIDE, act2, 0)
    keep(2)
    gath.arrived(W_OUT)

    def mm3(i, carry):
        rs = pl.ds(pl.multiple_of(i * BLK, BLK), BLK)
        h3_ref[rs, :] = jnp.dot(a2_ref[rs, :], wout_ref[...], preferred_element_type=jnp.float32)
        return carry
    lax.fori_loop(0, ROWS // BLK, mm3, 0)
    for k in range(D // CH):
        lo = k * CH
        mean, rstd = moments(h3_ref, lo, D // GROUPS)
        st_ref[0:8, 2 * MID + lo:2 * MID + lo + CH] = mean
        st_ref[8:16, 2 * MID + lo:2 * MID + lo + CH] = rstd
        sc3 = rstd * g_ref[:, 4 * MID + lo:4 * MID + lo + CH]
        sh3 = g_ref[:, 4 * MID + D + lo:4 * MID + D + lo + CH] - mean * sc3

        def act3(r, acc):
            h = h3_ref[row_at(r), lo:lo + CH].reshape(SIDE, TB, CH)
            s = x_ref[rows_full(r), lo:lo + CH].astype(jnp.float32)[0:VR].reshape(SIDE, TB, CH)
            return acc + jnp.sum(gelu(s + (h * sc3[None] + sh3[None])), axis=0)
        acc = lax.fori_loop(0, SIDE, act3, jnp.zeros((TB, CH), jnp.float32))
        feat = (acc / float(PIX)).astype(jnp.bfloat16).astype(jnp.float32)
        for j in range(lo // 128, (lo + CH) // 128):
            fsend[j] = feat[:, j * 128 - lo:(j + 1) * 128 - lo]

            @pl.when(me != j)
            def _(j=j):
                rc(fsend.at[j], frecv.at[me], s_f.at[j], q_f.at[me], {"dp": j}).start()

            @pl.when(me == j)
            def _(j=j):
                frecv[j] = fsend[j]

    z8 = jnp.zeros((TB, CH), jnp.float32)

    def slopes(k):
        lo = k * CH
        cs = slice(lo, lo + CH)
        mean = st_ref[0:8, 2 * MID + lo:2 * MID + lo + CH]
        rstd = st_ref[8:16, 2 * MID + lo:2 * MID + lo + CH]
        gain = g_ref[:, 4 * MID + lo:4 * MID + lo + CH]
        shift = g_ref[:, 4 * MID + D + lo:4 * MID + D + lo + CH]
        mr = mean * rstd

        def one(r, acc):
            s1, s2 = acc
            h = h3_ref[row_at(r), cs].reshape(SIDE, TB, CH)
            v = x_ref[rows_full(r), cs].astype(jnp.float32)[0:VR].reshape(SIDE, TB, CH)
            xh = h * rstd[None] - mr[None]
            t = dgelu(v + (xh * gain + shift))
            dh3_ref[rows_full(r), cs] = jnp.concatenate([t.reshape(VR, CH), z8], axis=0).astype(jnp.bfloat16)
            return s1 + jnp.sum(t, axis=0), s2 + jnp.sum(t * xh, axis=0)
        s1, s2 = lax.fori_loop(0, SIDE, one, (z8, z8))
        sl_ref[0:8, cs] = s1
        sl_ref[8:16, cs] = s2

    @pl.when(role == 0)
    def _():
        slopes(0)
        slopes(1)
    for p in peers:
        rc(fsend.at[p], frecv.at[p], s_f.at[0], q_f.at[p], {"dp": p}).wait_recv()
    feats = frecv[...].reshape(n * TB, 128)
    ids = gall_ref[...].reshape(n * TB, 128).astype(jnp.int32)

    acc = None
    def two_windows(i):
        a, b = window_of(i), window_of(i + 1)
        return jnp.concatenate([head_ref[a:a + WIN, :], head_ref[b:b + WIN, :]], axis=1)
    for i in range(0, GAMES, 2):
        lhs = jnp.concatenate([jnp.where(ids == i, feats, 0.0), jnp.where(ids == i + 1, feats, 0.0)], axis=1)
        p = lax.dot_general(lhs.astype(jnp.bfloat16), two_windows(i), T1, preferred_element_type=jnp.float32)
        acc = p if acc is None else acc + p
    off = ids_offset(ids)
    part[...] = shift_rows(acc, off, False).reshape(half, 2, TB, LW)

    d1 = rc(part.at[:, 1 - c], r1, s_1, q_1, {"dp": cp})
    d1.start()
    d1.wait()
    pair = me // 2
    r1[...] = r1[...] + part[:, c]
    pps = [lax.rem(pair + k, half) for k in range(1, half)]
    for k, p in enumerate(pps):
        rc(r1.at[p], r2.at[pair], s_2.at[k], q_2.at[pair], {"dp": 2 * p + c}).start()
    r2[pair] = r1[pair]

    @pl.when(role == 0)
    def _():
        slopes(2)
        slopes(3)
    for k, p in enumerate(pps):
        rc(r1.at[p], r2.at[p], s_2.at[k], q_2.at[p], {"dp": 2 * p + c}).wait_recv()
    logits = jnp.sum(r2[...], axis=0)

    lane = lax.broadcasted_iota(jnp.int32, (TB, 128), 1)
    live = lane < ATOMS
    zi = support_low + (support_high - support_low) * lane.astype(jnp.float32) / (ATOMS - 1)
    zi = jnp.where(live, zi, 0.0)
    taken, nxt, expert, reward, done, gid = (scal_ref[k] for k in range(6))
    pieces = []
    for a in range(ACTIONS):
        v = logits if a == 0 else pltpu.roll(logits, LW - ATOMS * a, 1)
        pieces.append(v[:, :128])

    @pl.when(role == 1)
    def _():
        sel = jnp.zeros((TB, 128), jnp.float32)
        for a in range(ACTIONS):
            sel = sel + jnp.where(nxt == float(a), pieces[a], 0.0)
        sel = jnp.where(live, sel, -1e30)
        e = jnp.exp(sel - jnp.max(sel, axis=1, keepdims=True))
        e = jnp.where(live, e, 0.0)
        prob = e / jnp.sum(e, axis=1, keepdims=True)
        spacing = (support_high - support_low) / (ATOMS - 1)
        m = jnp.zeros((TB, 128), jnp.float32)
        for j in range(ATOMS):
            zj = float(np.float32(support_low) + np.float32(support_high - support_low) * np.float32(j) /
                       np.float32(ATOMS - 1))
            tz = jnp.clip(reward + discount * (1.0 - done) * zj, support_low, support_high)
            wt = jnp.maximum(0.0, 1.0 - jnp.abs(tz - zi) / spacing)
            m = m + prob[:, j:j + 1] * wt
        tgt_s[...] = jnp.where(live, m, 0.0)
        d = rc(tgt_s, tgt_r, s_t, q_t, {"role": 0})
        d.start()
        d.wait_send()
        rc(frow_ref, frow_ref, s_r.at[0], q_r.at[0], {"role": 0}).wait_recv()
        rc(dlog_ref, dlog_ref, s_r.at[1], q_r.at[1], {"role": 0}).wait_recv()
        dfeat_ref[...] = jnp.zeros_like(dfeat_ref)

    @pl.when(role == 0)
    def _():
        frow_ref[...] = feats.astype(jnp.bfloat16)
        gt = jnp.transpose(gall_ref[...].reshape(n * TB, 128))[0:TB]
        count = jnp.sum((gt == gid).astype(jnp.float32), axis=1, keepdims=True)
        weight = 1.0 / jnp.maximum(count, 1.0)
        x3 = jnp.where(live[None], jnp.stack(pieces), -1e30)
        act = lax.broadcasted_iota(jnp.int32, (ACTIONS, TB, 128), 0).astype(jnp.float32)
        hot = (act == taken[None]).astype(jnp.float32)
        mx = jnp.max(x3, axis=2, keepdims=True)
        e = jnp.where(live[None], jnp.exp(x3 - mx), 0.0)
        s = jnp.sum(e, axis=2, keepdims=True)
        logp = jnp.where(live[None], x3 - mx - jnp.log(s), 0.0)
        prob = e / s
        q = jnp.sum(prob * zi[None], axis=2, keepdims=True)
        qb = jnp.broadcast_to(q, (ACTIONS, TB, 128))
        qm = jnp.max(qb, axis=0)
        qe = jnp.exp(qb - qm[None])
        qs = jnp.sum(qe, axis=0)
        lse = qm + jnp.log(qs)
        pol = qe / qs[None]
        chosen = jnp.sum(logp * hot, axis=0)
        qt = jnp.sum(qb * hot, axis=0)
        rc(tgt_s, tgt_r, s_t, q_t, {"role": 1}).wait_recv()
        m = tgt_r[...]
        cross = -jnp.sum(m * chosen, axis=1, keepdims=True)
        row_loss = cross + penalty * expert * (lse - qt)
        msum = jnp.sum(m, axis=1, keepdims=True)
        dl = hot * (prob * msum[None] - m[None]) + (penalty * expert)[None] * (pol - hot) * prob * (zi[None] - qb)
        dl = jnp.where(live[None], dl * (weight * (1.0 / GAMES))[None], 0.0)
        flat = jnp.zeros((TB, LW), jnp.float32)
        pad = jnp.zeros((TB, LW - 128), jnp.float32)
        for a in range(ACTIONS):
            v = jnp.concatenate([dl[a], pad], axis=1)
            flat = flat + (v if a == 0 else pltpu.roll(v, ATOMS * a, 1))
        l0 = row_loss * weight
        p0 = l0.astype(jnp.bfloat16).astype(jnp.float32)
        p1 = (l0 - p0).astype(jnp.bfloat16).astype(jnp.float32)
        p2 = l0 - p0 - p1
        last = flat[:, LW - 128:]
        last = jnp.where(lane == 125, p0, jnp.where(lane == 126, p1, jnp.where(lane == 127, p2, last)))
        flat = jnp.concatenate([flat[:, :LW - 128], last], axis=1)
        down_s[...] = jnp.concatenate([flat[:, :LW // 2], flat[:, LW // 2:]], axis=0).astype(jnp.bfloat16)
        for k, p in enumerate(pps):
            rc(down_s, dlog_ref.at[me], s_l.at[k], q_l.at[me], {"dp": 2 * p + c}).start()
        rc(down_s, dlog_ref.at[me], s_c.at[0], q_c.at[me], {"dp": cp}).start()
        dlog_ref[me] = down_s[...]
        for k, p in enumerate(pps):
            o = 2 * p + c
            rc(down_s, dlog_ref.at[o], s_l.at[k], q_l.at[o], {"dp": cp}).wait_recv()
            rc(dlog_ref.at[o], dlog_ref.at[o], s_c.at[k + 1], q_c.at[o], {"dp": cp}).start()
        for p in [pair] + pps:
            o = 2 * p + 1 - c
            rc(dlog_ref.at[o], dlog_ref.at[o], s_c.at[0], q_c.at[o], {"dp": cp}).wait_recv()
        to0 = rc(frow_ref, frow_ref, s_r.at[0], q_r.at[0], {"role": 1})
        to1 = rc(dlog_ref, dlog_ref, s_r.at[1], q_r.at[1], {"role": 1})
        to0.start()
        to1.start()
        rolled = shift_rows(widen(dlog_ref[...]), off, True).astype(jnp.bfloat16)
        acc = None
        for i in range(0, GAMES, 2):
            p = jnp.dot(rolled, two_windows(i), preferred_element_type=jnp.float32)
            p = jnp.where(ids == i, p[:, :128], jnp.where(ids == i + 1, p[:, 128:], 0.0))
            acc = p if acc is None else acc + p
        dsend[...] = acc.reshape(n, TB, 128)
        for k, p in enumerate(peers):
            rc(dsend.at[p], drecv.at[me], s_d.at[k], q_d.at[me], {"dp": p}).start()
        drecv[me] = dsend[me]
        for k, p in enumerate(peers):
            rc(dsend.at[p], drecv.at[p], s_d.at[k], q_d.at[p], {"dp": p}).wait_recv()
        for j in range(n):
            dfeat_ref[:, j * 128:(j + 1) * 128] = drecv[j]
        for k, p in enumerate(pps):
            rc(down_s, dlog_ref.at[me], s_l.at[k], q_l.at[me], {"dp": 2 * p + c}).wait_send()
        rc(down_s, dlog_ref.at[me], s_c.at[0], q_c.at[me], {"dp": cp}).wait_send()
        for k, p in enumerate(pps):
            o = 2 * p + c
            rc(dlog_ref.at[o], dlog_ref.at[o], s_c.at[k + 1], q_c.at[o], {"dp": cp}).wait_send()
        for k, p in enumerate(peers):
            rc(dsend.at[p], drecv.at[me], s_d.at[k], q_d.at[me], {"dp": p}).wait_send()
        to0.wait_send()
        to1.wait_send()

    for j in range(n):
        pl.when(me != j)(rc(fsend.at[j], frecv.at[me], s_f.at[j], q_f.at[me], {"dp": j}).wait_send)
    for k, p in enumerate(pps):
        rc(r1.at[p], r2.at[pair], s_2.at[k], q_2.at[pair], {"dp": 2 * p + c}).wait_send()
    tail = dlog_ref[:, :, 384:512].astype(jnp.float32)[:, TB:2 * TB].reshape(n * TB, 128)
    lanes = lax.broadcasted_iota(jnp.int32, (n * TB, 128), 1)
    total = jnp.sum(jnp.where(lanes >= 125, tail, 0.0))
    loss_ref[...] = jnp.full((TB, 128), total, jnp.float32)

    def last_norm():
        for k in range(D // CH):
            lo = k * CH
            cs = slice(lo, lo + CH)
            mean = st_ref[0:8, 2 * MID + lo:2 * MID + lo + CH]
            rstd = st_ref[8:16, 2 * MID + lo:2 * MID + lo + CH]
            gain = g_ref[:, 4 * MID + lo:4 * MID + lo + CH]
            dout = dfeat_ref[:, cs] / float(PIX)
            s1 = dout * sl_ref[0:8, cs]
            s2 = dout * sl_ref[8:16, cs]
            put_gain(gg_ref, 4 * MID + lo, s2)
            put_gain(gg_ref, 4 * MID + D + lo, s1)
            count = 1.0 / float(PIX * D // GROUPS)
            m1 = group_sum(gain * s1, D // GROUPS) * count
            m2 = group_sum(gain * s2, D // GROUPS) * count
            cc = -rstd * rstd * m2
            cb = -rstd * m1 - mean * cc
            ca = rstd * gain * dout

            def one(r, carry):
                h = h3_ref[row_at(r), cs].reshape(SIDE, TB, CH)
                t = dh3_ref[rows_full(r), cs].astype(jnp.float32)[0:VR].reshape(SIDE, TB, CH)
                v = (ca[None] * t + cc[None] * h + cb[None]).reshape(VR, CH)
                dh3_ref[rows_full(r), cs] = jnp.concatenate([v, z8], axis=0).astype(jnp.bfloat16)
                return carry
            lax.fori_loop(0, SIDE, one, 0)

    @pl.when(role == 0)
    def _():
        last_norm()
        kept[3].start()

        def da2(i, c):
            rs = pl.ds(pl.multiple_of(i * BLK, BLK), BLK)
            d2_ref[rs, :] = lax.dot_general(dh3_ref[rs, :], wout_ref[...], T1, preferred_element_type=jnp.float32)
            return c
        lax.fori_loop(0, ROWS // BLK, da2, 0)
        far_a1(1).wait_send()
        through(h2_ref, d2_ref, st_ref, g_ref, gg_ref, MID, 2 * MID, 3 * MID,
                lambda r, v: put_shifted(e_ref, o_ref, r, v))
        kept[4].start()
        kept[5].start()
        gg_ref[:, 0:2 * MID] = jnp.zeros((1, 2 * MID), jnp.float32)
        for d in kept:
            d.wait()

    @pl.when(role == 1)
    def _():
        far_a1(0).wait_recv()
        for k in range(MID // 128):
            fart_ref[k * 128:(k + 1) * 128, :] = jnp.transpose(far_ref[:, k * 128:(k + 1) * 128])
        d = pltpu.make_async_copy(fart_ref, fart_hbm, k_sem.at[7])
        d.start()
        d.wait()
        gg_ref[...] = jnp.zeros_like(gg_ref)
    gath.end()


def block_step(frames, weights, averages, scal, head, avg_head, n, cid):
    f32, b16 = jnp.float32, jnp.bfloat16
    S = jax.ShapeDtypeStruct
    V, dma = pltpu.VMEM, pltpu.SemaphoreType.DMA
    vs, hs = pl.BlockSpec(memory_space=pltpu.VMEM), pl.BlockSpec(memory_space=pl.ANY)
    h = n // 2
    nz = n // 4
    sends = 4 + 6 * (nz - 1) + 2 * nz
    return pl.pallas_call(
        functools.partial(step_kernel, n),
        out_shape=(S((ROWS, D), b16), S((ROWS, MID), f32), S((ROWS, MID), b16), S((ROWS, D), b16), S((EROWS, MID), b16),
                   S((EROWS, MID), b16), S((9 * MID, MID), b16), S((MID, ROWS), b16), S((16, 2 * MID + D), f32),
                   S((1, 4 * MID + 2 * D), f32), S((1, 4 * MID + 2 * D), f32), S((n, TB, 128), f32), S((n * TB, 128), b16), S((n, 16, 512), b16), S((TB, 128), f32)),
        in_specs=[hs] + [vs] * 8 + [pl.BlockSpec(memory_space=pltpu.SMEM)] * 6 + [hs] * 2,
        out_specs=(hs,) * 8 + (vs,) * 7,
        scratch_shapes=[
            V((6, TB, 128), f32), V((D // n, MID), b16), V((9 * MID // n, MID), b16), V((MID // n, D), b16), V((16, 128), f32),
            V((D, MID), b16), V((9 * MID, MID), b16), V((MID, D), b16), V((n, 16, 128), f32),
            V((ROWS, D), b16), V((ROWS, MID), f32), V((ROWS, MID), f32), V((ROWS, D), f32), V((ROWS, MID), b16),
            V((TB, D), f32), V((16, D), f32), V((EROWS, MID), b16), V((EROWS, MID), b16),
            V((ROWS, MID), f32), V((ROWS, D), b16), V((ROWS, MID), b16), V((MID, ROWS), b16),
            V((2, SIDE, TB, D), b16), V((2, HC, 128), f32), V((PADC, 128), b16),
            V((n, TB, 128), f32), V((n, TB, 128), f32), V((h, 2, TB, LW), f32), V((h, TB, LW), f32),
            V((h, TB, LW), f32), V((TB, 128), f32), V((TB, 128), f32), V((16, 512), b16),
            V((n, TB, 128), f32), V((n, TB, 128), f32),
            dma((4,)), dma((4, sends)), dma((4, n)), dma((2,)), dma((2,)), dma((8,)), dma((1,)), dma((1,)),
            dma((n,)), dma((n,)), dma, dma, dma((h,)), dma((h,)), dma, dma, dma((h,)), dma((n,)),
            dma((h,)), dma((n,)), dma((n,)), dma((n,)), dma((2,)), dma((2,))],
        compiler_params=pltpu.CompilerParams(collective_id=cid, has_side_effects=True,
                                             vmem_limit_bytes=64 * 1024 * 1024),
        name="block_step",
    )(frames, *weights, *averages, *scal, head, avg_head)


KEEP, SEND, BOTH = 0, 1, 2
OUT, MIDDLE, IN, GAINS = 0, 1, 2, 3


def units_of(ri, ro, rm):
    q, h, t = MID // 4, ri // 2, rm // 2
    online = ((0, ri + 2 * ro, 2 * ro, 0, MID, SEND, OUT), (0, ri, 2 * ro, 0, MID, KEEP, OUT),
              (0, 0, ri, MID // 2, MID // 2, SEND, IN), (0, 0, h, 0, MID // 2, KEEP, IN), (0, h, h, 0, MID // 2, KEEP, IN),
              (1, 0, 3, 0, 128, BOTH, GAINS))
    target = ((0, 0, rm, 0, q, SEND, MIDDLE), (0, 0, rm, q, q, SEND, MIDDLE), (0, 0, rm, 2 * q, q, KEEP, MIDDLE),
              (0, 0, t, 3 * q, q, KEEP, MIDDLE), (0, t, 96, 3 * q, q, KEEP, MIDDLE),
              (0, t + 96, t - 96, 3 * q, q, KEEP, MIDDLE))
    return online, target


def sums_kernel(n_dev, rows, x_hbm, h1_hbm, a2_hbm, dh3_hbm, e_hbm, o_hbm, wmid_hbm, fart_hbm, st_ref, g_ref, gpart_ref,
                gall_ref, frow_ref, dlog_ref, t_out, t_mid, t_in, t_gains, dlt, rhs, x_ref, h1_ref, a2_ref, dh3_ref, e_ref, o_ref, wmid_ref, fart_ref, low_ref,
                d2_ref, gg_ref, *refs):
    outs = (t_out, t_mid, t_in, t_gains)
    g, r1, r2, rz, rh = (refs[2 * j:2 * j + 2] for j in range(5))
    fs, fr = refs[10:14], refs[14:18]
    s1, q1, s2, q2, s3, q3, sh, qh, sf, qf, sl, sd, qd = refs[18:]
    nz = n_dev // 4
    ri, ro, rm = rows
    online, target = units_of(*rows)
    me, z, x, c = place()
    role = lax.axis_index("role")
    xp = {"dp": me + 2 - 4 * x}
    cp = {"dp": me + 1 - 2 * c}

    def slot(zz, xx, cc):
        return zz * 4 + xx * 2 + cc

    order = list(range(nz))
    parts = ((0, 128), (128, 128), (256, MID - 256))

    def load(k):
        src = (x_hbm, h1_hbm, a2_hbm, dh3_hbm, e_hbm, o_hbm, wmid_hbm, fart_hbm)[k]
        dst = (x_ref, h1_ref, a2_ref, dh3_ref, e_ref, o_ref, wmid_ref, fart_ref)[k]
        return pltpu.make_async_copy(src, dst, sl.at[k])

    def far_d2(to, k):
        cs = pl.ds(*parts[k])
        return rc(e_hbm.at[pl.ds(PAD, ROWS), cs], low_ref.at[:, cs], sd.at[k], qd.at[k], {"role": to})

    @pl.when(role == 0)
    def _():
        for k in (3, 2, 6, 4, 5, 1, 0):
            load(k).start()
    pl.when(role == 1)(load(7).start)
    zs = [{"dp": lax.rem(me + 4 * k, 4 * nz)} for k in range(1, nz)]
    greet([(None, p) for p in [xp, cp, {"role": 1 - role}] + zs])
    z8 = jnp.zeros((TB, CH), jnp.float32)

    def online_first():
        for k in range(len(parts)):
            far_d2(1, k).start()
        gg_ref[...] = gpart_ref[...]
        load(3).wait()
        load(2).wait()
        for k in (2, 3, 0, 1):
            v = lax.dot_general(a2_ref[...], dh3_ref[:, k * CH:(k + 1) * CH], T0, preferred_element_type=jnp.float32)
            g[0][:, ri + k * ro:ri + (k + 1) * ro, :] = v.reshape(n_dev, ro, CH)

    def online_rest():
        for k in (6, 4, 5, 1, 0):
            load(k).wait()

        def da1(i, carry):
            row = i * BLK
            acc = None
            for m, s in enumerate(OFFS):
                p = lax.dot_general(shifted(e_ref, o_ref, -s, row, BLK), wmid_ref[m * MID:(m + 1) * MID, :], T1,
                                    preferred_element_type=jnp.float32)
                acc = p if acc is None else acc + p
            d2_ref[pl.ds(pl.multiple_of(row, BLK), BLK), :] = acc
            return carry
        lax.fori_loop(0, ROWS // BLK, da1, 0)

        def put1(r, v):
            low_ref[rows_full(r), :] = jnp.concatenate([v, z8], axis=0).astype(jnp.bfloat16)
        through(h1_ref, d2_ref, st_ref, g_ref, gg_ref, 0, 0, MID, put1)
        per = CH // ri
        for k in range(D // CH):
            v = lax.dot_general(x_ref[:, k * CH:(k + 1) * CH], low_ref[...], T0, preferred_element_type=jnp.float32)
            g[0][k * per:(k + 1) * per, 0:ri, :] = v.reshape(per, ri, MID)
        for i in range(n_dev):
            for k in range(3):
                at = (i * 3 + k) * 128
                g[1][i, k:k + 1, :] = gg_ref[:, at:at + 128]

    def target_part(k):
        if k == 0:
            clear_margins(e_ref, o_ref)
            load(7).wait()
        cs = slice(parts[k][0], parts[k][0] + parts[k][1])
        far_d2(0, k).wait_recv()
        zh = jnp.zeros((TB, parts[k][1]), jnp.float32)

        def rebuild(r, carry):
            v = low_ref[rows_full(r), cs].astype(jnp.float32)
            at = pl.ds(pl.multiple_of(PAD + r * RB, 16), RB)
            e_ref[at, cs] = low_ref[rows_full(r), cs]
            o_ref[at, cs] = jnp.concatenate([zh, v[0:VR]], axis=0).astype(jnp.bfloat16)
            return carry
        lax.fori_loop(0, SIDE, rebuild, 0)
        for m, s in enumerate(OFFS):
            ref, base = (e_ref, 16 - s) if s % 2 == 0 else (o_ref, 17 - s)
            v = jnp.dot(fart_ref[...], ref[base * TB:base * TB + ROWS, cs], preferred_element_type=jnp.float32)
            at = m * MID
            while at < (m + 1) * MID:
                i = at // rm
                end = min((i + 1) * rm, (m + 1) * MID)
                g[0][i, at - i * rm:end - i * rm, cs] = v[at - m * MID:end - m * MID]
                at = end

    def cut(ref, i, u):
        return ref.at[i, pl.ds(u[1], u[2]), pl.ds(u[3], u[4])]

    def region(u):
        if u[6] == OUT:
            return slice(0, ro), slice(0, outs[OUT].shape[1])
        at = u[3] % outs[u[6]].shape[1]
        return slice(u[1], u[1] + u[2]), slice(at, at + u[4])

    def place_sum(u, total):
        if u[6] == OUT:
            return jnp.concatenate([total[j * ro:(j + 1) * ro] for j in range(u[2] // ro)], axis=1)
        return total

    def final(u, to, n):
        rs, cs = region(u)
        at = (pl.ds(rs.start, rs.stop - rs.start), pl.ds(cs.start, cs.stop - cs.start))
        return rc(fs[u[6]].at[at], fr[u[6]].at[at], sf.at[n], qf.at[n], {"role": to})

    def run(units, mine, plan):
        def add(u, i, ref, j):
            a, rs, cs = u[0], slice(u[1], u[1] + u[2]), slice(u[3], u[3] + u[4])
            g[a][i, rs, cs] = g[a][i, rs, cs] + ref[a][j, rs, cs]

        def c1(n, zz, k):
            u = units[n]
            xx = 1 - x if k == 0 else x
            return rc(cut(g[u[0]], slot(zz, xx, 1 - c), u), cut(r1[u[0]], k * nz + zz, u), s1.at[n, k * nz + zz],
                      q1.at[n, k * nz + zz], cp)

        def c2(n, zz):
            u = units[n]
            return rc(cut(g[u[0]], slot(zz, 1 - x, c), u), cut(r2[u[0]], zz, u), s2.at[n, zz], q2.at[n, zz], xp)

        def c3(n, t, at):
            u = units[n]
            return rc(cut(g[u[0]], slot(t, x, c), u), cut(rz[u[0]], at, u), s3.at[n, t], q3.at[n, at],
                      {"dp": slot(t, x, c)})

        def hop(n, t, via, side):
            u = units[n]
            return rc(cut(g[u[0]], slot(t, x, c), u), cut(rh[u[0]], side, u), sh.at[n, side], qh.at[n, side],
                      {"dp": slot(via, x, c)})

        def gather_x(n):
            u = units[n]
            for zz in order:
                c1(n, zz, 1).wait_recv()
                add(u, slot(zz, x, c), r1, nz + zz)
            for zz in order:
                c2(n, zz).wait_recv()
                add(u, slot(zz, x, c), r2, zz)
                pl.when(jnp.logical_or(z == zz + 3, zz == z + 3))(c3(n, zz, z).start)
                pl.when(zz == z + 2)(hop(n, zz, z + 1, 0).start)
                pl.when(zz == z - 2)(hop(n, zz, z - 1, 1).start)

        def pass_on(n):
            u = units[n]

            @pl.when(z < nz - 1)
            def _():
                @pl.when(z > 0)
                def _():
                    hop(n, z, z, 0).wait_recv()
                    add(u, slot(z + 1, x, c), rh, 0)
                c3(n, z + 1, z).start()

            @pl.when(z > 0)
            def _():
                @pl.when(z < nz - 1)
                def _():
                    hop(n, z, z, 1).wait_recv()
                    add(u, slot(z - 1, x, c), rh, 1)
                c3(n, z - 1, z).start()

        def near(zz):
            d = z - zz
            return jnp.logical_or(jnp.logical_or(d == 1, d == -1), jnp.logical_or(d == 3, d == -3))

        def first(n):
            for k in range(2):
                for zz in order:
                    c1(n, zz, k).start()

        def second(n):
            for zz in order:
                c1(n, zz, 0).wait_recv()
                add(units[n], slot(zz, 1 - x, c), r1, zz)
                c2(n, zz).start()

        def finish(n):
            u = units[n]
            a, rs, cs = u[0], slice(u[1], u[1] + u[2]), slice(u[3], u[3] + u[4])
            for zz in order:
                @pl.when(near(zz))
                def _(zz=zz):
                    c3(n, z, zz).wait_recv()
                    add(u, me, rz, zz)
            total = place_sum(u, g[a][me, rs, cs])
            at = region(u)
            if u[5] != SEND:
                outs[u[6]][at] = total
            if u[5] != KEEP:
                fs[u[6]][at] = total.astype(fs[u[6]].dtype)
                final(u, 1 - mine, n).start()
        def operands():
            ids = gall_ref[...].reshape(-1, 128).astype(jnp.int32) - mine * (GAMES // 2)
            v = shift_rows(widen(dlog_ref[...]), ids_offset(ids), True)
            for k in range(WIN // 128):
                dlt[k * 128:(k + 1) * 128, :] = jnp.transpose(v[:, k * 128:(k + 1) * 128]).astype(jnp.bfloat16)
            feats = frow_ref[...].astype(jnp.float32)
            for i in range(GAMES // 2):
                rhs[i] = jnp.where(ids == i, feats, 0.0).astype(jnp.bfloat16)

        def terms(ns):
            for n in ns:
                first(n)
            for n in ns:
                second(n)
        for do, what in plan:
            if do == "make":
                what()
            elif do == "head":
                operands()
            else:
                {"start": terms, "x": gather_x, "z": pass_on, "end": finish}[do](what)
        for n, u in enumerate(units):
            for zz in order:
                c1(n, zz, 0).wait_send()
                c1(n, zz, 1).wait_send()
                c2(n, zz).wait_send()
                pl.when(near(zz))(c3(n, zz, z).wait_send)
                pl.when(zz == z + 2)(hop(n, zz, z + 1, 0).wait_send)
                pl.when(zz == z - 2)(hop(n, zz, z - 1, 1).wait_send)
            if u[5] != KEEP:
                final(u, 1 - mine, n).wait_send()

    def receive(units, other):
        for n, u in enumerate(units):
            if u[5] != KEEP:
                final(u, other, n).wait_recv()
                outs[u[6]][region(u)] = fr[u[6]][region(u)].astype(jnp.float32)

    rest = [("x", 0), ("z", 0), ("x", 1), ("x", 2), ("z", 1), ("end", 0), ("x", 3), ("z", 2), ("end", 1), ("x", 4), ("z", 3),
            ("end", 2), ("x", 5), ("z", 4), ("end", 3), ("z", 5), ("end", 4), ("end", 5)]

    @pl.when(role == 0)
    def _():
        run(online, 0, [("make", online_first), ("start", (0, 1)), ("make", online_rest), ("start", (2, 3, 4, 5)), ("head", 0)] + rest)
        receive(target, 1)
        for k in range(len(parts)):
            far_d2(1, k).wait_send()

    @pl.when(role == 1)
    def _():
        run(target, 1, [("make", lambda: target_part(0)), ("start", (0,)), ("make", lambda: target_part(1)), ("start", (1,)),
                        ("x", 0), ("make", lambda: target_part(2)), ("start", (2, 3, 4, 5)), ("head", 0)] + rest[1:])
        receive(online, 0)


def sums(saved, games_all, frow, dlog, n, cid):
    nz = n // 4
    V, dma = pltpu.VMEM, pltpu.SemaphoreType.DMA
    f32, b16 = jnp.float32, jnp.bfloat16
    S = jax.ShapeDtypeStruct
    rows = ri, ro, rm = D // n, MID // n, 9 * MID // n
    half = [(ro, D // 2), (rm, MID // 2), (ri, MID // 2), (3, 128)]
    low = [b16, b16, b16, f32]
    sh = [(rm, MID), (3, 128)]
    nu = max(len(u) for u in units_of(*rows))
    vs, hs = pl.BlockSpec(memory_space=pltpu.VMEM), pl.BlockSpec(memory_space=pl.ANY)
    return pl.pallas_call(
        functools.partial(sums_kernel, n, rows),
        out_shape=tuple(S(s, f32) for s in half) + (S((WIN, n * TB), b16), S((GAMES // 2, n * TB, 128), b16)),
        in_specs=[hs] * 8 + [vs] * 6,
        out_specs=(vs,) * 6,
        scratch_shapes=[V(s.shape, s.dtype) for s in saved[:8]] +
        [V((ROWS, MID), b16), V((ROWS, MID), f32), V((1, 4 * MID + 2 * D), f32)] +
        [V((k,) + s, f32) for k in (4 * nz, 2 * nz, nz, nz, 2) for s in sh] + [V(s, t) for s, t in zip(half, low)] * 2 +
        [dma((nu, 2 * nz))] * 2 + [dma((nu, nz))] * 4 + [dma((nu, 2))] * 2 + [dma((nu,))] * 2 + [dma((8,)), dma((3,)), dma((3,))],
        compiler_params=pltpu.CompilerParams(collective_id=cid, has_side_effects=True,
                                             vmem_limit_bytes=63 * 1024 * 1024),
        name="gradient_sums",
    )(*saved, games_all, frow, dlog)


UB = 2048
NU = -(-HALF // UB)
LASTU = HALF - (NU - 1) * UB


def segments(k):
    lo, hi = k * UB, min((k + 1) * UB, -(-HALF // 16) * 16)
    parts = []
    for i in range(GAMES // 2):
        a, end = window_of(i), window_of(i + 1)
        mixed = i > 0 and WIDE * i != a
        for r0, r1, games in ((a, a + 16, (i - 1, i)), (a + 16, end, (i,))) if mixed else ((a, end, (i,)),):
            if i == GAMES // 2 - 1 and r1 == end:
                r1 = -(-HALF // 16) * 16
            r0, r1 = max(r0, lo), min(r1, hi)
            if r0 < r1:
                parts.append((r0, r1, games))
    return parts


def update_kernel(dlt, rhs, loss_ref, *refs):
    grads, olds_hbm = refs[:4], refs[4:16]
    hbm = refs[16:19]
    loss_out, news, hbm_out = refs[19], refs[20:36], refs[36:40]
    olds = refs[40:52]
    grow, ibuf, obuf, cbuf, si, so, sw = refs[52:]
    role = lax.axis_index("role")

    def rows_of(k):
        return UB if k < NU - 1 else LASTU

    def fetch(k):
        n = rows_of(k)
        return [pltpu.make_async_copy(hbm[t].at[pl.ds(pl.multiple_of(role * HALF + k * UB, 8), n)],
                                      ibuf.at[k % 3, t, pl.ds(0, n)], si.at[k % 3, t]) for t in range(3)]

    def store(k):
        n = rows_of(k)
        cs = [pltpu.make_async_copy(obuf.at[k % 2, t, pl.ds(0, n)], hbm_out[t].at[pl.ds(k * UB, n)], so.at[k % 2, t])
              for t in range(3)]
        return cs + [pltpu.make_async_copy(cbuf.at[k % 2, pl.ds(0, n)], hbm_out[3].at[pl.ds(k * UB, n)], so.at[k % 2, 3])]

    old_copies = [pltpu.make_async_copy(olds_hbm[i], olds[i], sw.at[i]) for i in range(12)]
    for d in fetch(0) + fetch(1) + old_copies:
        d.start()
    loss_out[...] = loss_ref[0:1, 0:1]

    def small(a, right):
        w, m, v = olds[3 * a:3 * a + 3]
        nw, nm, nv, nc = news[4 * a:4 * a + 4]
        cols = grads[a].shape[1]
        cs = slice(cols if right else 0, (cols if right else 0) + cols)
        gv = grads[a][...]
        rate = learn_rate
        if a == 3:
            gv = jnp.concatenate([gv[k:k + 1, :] for k in range(gv.shape[0])], axis=1)
            cs = slice(0, gv.shape[1])
            rate = gain_rate
        mv = momentum_decay * m[:, cs] + gv
        wv = w[:, cs] - rate * (gv + momentum_decay * mv)
        nw[...] = wv
        nm[...] = gv if a == 0 else mv
        nv[...] = average_decay * v[:, cs] + (1.0 - average_decay) * wv
        nc[...] = wv.astype(jnp.bfloat16)

    for k in range(NU):
        if k + 2 < NU:
            for d in fetch(k + 2):
                d.start()
        lo = k * UB
        for r0, r1, games in segments(k):
            acc = None
            for i in games:
                at = r0 - window_of(i)
                p = jnp.dot(dlt[at:at + r1 - r0, :], rhs[i], preferred_element_type=jnp.float32)
                acc = p if acc is None else acc + p
            grow[r0 - lo:r1 - lo, :] = acc
        for d in fetch(k):
            d.wait()
        if k >= 2:
            for d in store(k - 2):
                d.wait()
        b, s = k % 2, k % 3

        def one(r, carry, b=b, s=s):
            rs = pl.ds(pl.multiple_of(r * 128, 128), 128)
            gv = grow[rs, :]
            m = momentum_decay * ibuf[s, 1, rs, :] + gv
            w = ibuf[s, 0, rs, :] - learn_rate * (gv + momentum_decay * m)
            obuf[b, 0, rs, :] = w
            obuf[b, 1, rs, :] = m
            obuf[b, 2, rs, :] = average_decay * ibuf[s, 2, rs, :] + (1.0 - average_decay) * w
            cbuf[b, rs, :] = w.astype(jnp.bfloat16)
            return carry
        lax.fori_loop(0, UB // 128, one, 0)
        for d in store(k):
            d.start()
        if 4 <= k < 8:
            a = k - 4
            for i in range(3 * a, 3 * a + 3):
                old_copies[i].wait()
            if a == 3:
                small(a, False)
            else:
                pl.when(role == 0)(lambda a=a: small(a, False))
                pl.when(role != 0)(lambda a=a: small(a, True))
    for k in (NU - 2, NU - 1):
        for d in store(k):
            d.wait()


def final_update(dlt, rhs, loss, grads, olds, tables):
    lanes = tables[0].shape[1]
    f32, b16 = jnp.float32, jnp.bfloat16
    S, V, dma = jax.ShapeDtypeStruct, pltpu.VMEM, pltpu.SemaphoreType.DMA
    vs, hs = pl.BlockSpec(memory_space=pltpu.VMEM), pl.BlockSpec(memory_space=pl.ANY)
    new_shapes = []
    for a in range(4):
        s = olds[3 * a].shape if a == 3 else grads[a].shape
        new_shapes += [S(s, f32)] * 3 + [S(s, b16)]
    return pl.pallas_call(
        update_kernel,
        in_specs=[vs] * 7 + [hs] * 15,
        out_specs=[vs] * 17 + [hs] * 4,
        scratch_shapes=[V(o.shape, f32) for o in olds] +
        [V((UB, lanes), f32), V((3, 3, UB, lanes), f32),
         V((2, 3, UB, lanes), f32), V((2, UB, lanes), b16), dma((3, 3)), dma((2, 4)), dma((12,))],
        out_shape=[S((1, 1), f32)] + new_shapes + [S((HALF, lanes), f32)] * 3 + [S((HALF, lanes), b16)],
        compiler_params=pltpu.CompilerParams(vmem_limit_bytes=63 * 1024 * 1024),
        name="final_update",
    )(dlt, rhs, loss, *grads, *olds, *tables)


def fast_device(
    frames,
    game_ids,
    taken_actions,
    next_actions,
    expert_flags,
    rewards,
    done_flags,
    weight_in,
    weight_mid,
    weight_out,
    norm_gains,
    head_table,
    moment_in,
    moment_mid,
    moment_out,
    moment_gains,
    moment_head,
    average_in,
    average_mid,
    average_out,
    average_gains,
    average_head,
):
    n = lax.axis_size("dp")
    *saved, all_ids, feat_rows, dlog, loss = block_step(
        jnp.transpose(frames[0], (1, 0, 2)),
        (weight_in[0], weight_mid[0], weight_out[0], norm_gains),
        (average_in[0], average_mid[0], average_out[0], average_gains),
        (taken_actions, next_actions, expert_flags, rewards, done_flags, game_ids),
        head_table.T,
        average_head.T,
        n,
        1,
    )
    grad_out, grad_mid, grad_in, grad_gains, dlt, rhs = sums(saved, all_ids, feat_rows, dlog, n, 2)
    loss, *rest = final_update(
        dlt,
        rhs,
        loss,
        (grad_in, grad_mid, grad_out, grad_gains),
        (
            weight_in[0],
            moment_in[0],
            average_in[0],
            weight_mid[0],
            moment_mid[0],
            average_mid[0],
            weight_out[0],
            moment_out[0],
            average_out[0],
            norm_gains,
            moment_gains,
            average_gains,
        ),
        (head_table.T, moment_head.T, average_head.T),
    )
    return (
        loss.reshape(()),
        *(v[None] for v in rest[:12]),
        *rest[12:16],
        *(v.T for v in rest[16:]),
    )


def solution(mesh):
    return jax.shard_map(
        fast_device if mesh.shape["dp"] == 16 else on_device,
        mesh=mesh,
        in_specs=(
            P("role", "dp", None, None),
            P("dp"),
            P("dp"),
            P("dp"),
            P("dp"),
            P("dp"),
            P("dp"),
            P(None, "dp", None),
            P(None, "dp", None),
            P(None, "dp", None),
            P(None, "dp"),
            P("dp", None),
            P(None, "dp", None),
            P(None, "dp", None),
            P(None, "dp", None),
            P(None, "dp"),
            P("dp", None),
            P(None, "dp", None),
            P(None, "dp", None),
            P(None, "dp", None),
            P(None, "dp"),
            P("dp", None),
        ),
        out_specs=(
            P(),
            P(None, "dp", "role"),
            P(None, "dp", "role"),
            P(None, "dp", "role"),
            P(None, "dp", "role"),
            P(None, "dp", "role"),
            P(None, "dp", "role"),
            P(None, "dp", "role"),
            P(None, "dp", "role"),
            P(None, "dp", "role"),
            P(None, "dp", "role"),
            P(None, "dp", "role"),
            P(None, "dp", "role"),
            P(None, "dp"),
            P(None, "dp"),
            P(None, "dp"),
            P(None, "dp"),
            P("dp", "role"),
            P("dp", "role"),
            P("dp", "role"),
            P("dp", "role"),
        ),
        check_vma=False,
    )
```

```python
import functools

import jax
import jax.numpy as jnp
import numpy as np
from jax import lax
from jax.experimental import pallas as pl
from jax.experimental.pallas import tpu as pltpu
from jax.sharding import PartitionSpec as P

D = 2048
MID = 512
GAMES = 40
ACTIONS = 18
ATOMS = 51
GROUPS = 32
SIDE = 11
LAYERS = 1


support_low = -10.0
support_high = 10.0
discount = 0.99
penalty = 0.05
momentum_decay = 0.5
average_decay = 0.5
learn_rate = 4.0
gain_rate = 40.0
epsilon = 1e-05
HIGHEST = lax.Precision.HIGHEST


def passed_along(block, axis, distance):
    devices = range(lax.axis_size(axis))
    route = [(i - distance, i) for i in devices if i - distance in devices]
    return lax.ppermute(block, axis, route)


def split_gains(gains):
    return (
        gains[:MID],
        gains[MID : 2 * MID],
        gains[2 * MID : 3 * MID],
        gains[3 * MID : 4 * MID],
        gains[4 * MID : 4 * MID + D],
        gains[4 * MID + D :],
    )


def group_norm(values, gain, shift):
    rows, pixels, width = values.shape
    grouped = values.reshape(rows, pixels, GROUPS, width // GROUPS)
    center = grouped - jnp.mean(grouped, axis=(1, 3), keepdims=True)
    spread = jnp.mean(center * center, axis=(1, 3), keepdims=True)
    normed = (center * lax.rsqrt(spread + epsilon)).reshape(values.shape)
    return normed * gain + shift


def patches_of(acts):
    rows, pixels, width = acts.shape
    grid = acts.reshape(rows, SIDE, SIDE, width)
    padded = jnp.pad(grid, ((0, 0), (1, 1), (1, 1), (0, 0)))
    pieces = [
        padded[:, down : down + SIDE, right : right + SIDE, :]
        for down in range(3)
        for right in range(3)
    ]
    return jnp.concatenate(pieces, axis=-1).reshape(rows, pixels, 9 * width)


def transition_loss(logits, target_dist, action_hot, expert, support):
    log_prob = jax.nn.log_softmax(logits, axis=-1)
    values = jnp.sum(jnp.exp(log_prob) * support, axis=-1)
    spread_sum = jax.nn.logsumexp(values, axis=-1)
    chosen_log = jnp.sum(log_prob * action_hot[:, :, None], axis=1)
    cross = -jnp.sum(target_dist * chosen_log, axis=-1)
    regular = spread_sum - jnp.sum(values * action_hot, axis=-1)
    return cross + penalty * expert * regular


def project_target(next_prob, rewards, done_f, support):
    moved = jnp.clip(
        rewards[:, None] + discount * (1.0 - done_f)[:, None] * support[None, :],
        support_low,
        support_high,
    )
    spacing = (support_high - support_low) / (ATOMS - 1)
    weight = jnp.maximum(0.0, 1.0 - jnp.abs(moved[:, :, None] - support[None, None, :]) / spacing)
    return jnp.sum(next_prob[:, :, None] * weight, axis=1)


def renew(weight, grad, moment, average, rate):
    new_moment = momentum_decay * moment + grad
    new_weight = weight - rate * (grad + momentum_decay * new_moment)
    new_average = average_decay * average + (1.0 - average_decay) * new_weight
    return (new_weight, new_moment, new_average, new_weight.astype(jnp.bfloat16))


def lower_half(values):
    return values[..., : values.shape[-1] // 2]


def upper_half(values):
    return values[..., values.shape[-1] // 2 :]


def own_half(values, role_index):
    half = values.shape[-1] // 2
    return lax.dynamic_slice_in_dim(values, role_index * half, half, values.ndim - 1)


def norm_act(hidden, gain, shift):
    return jax.nn.gelu(group_norm(hidden, gain, shift))


def outer_act(hidden, gain, shift, stream):
    return jax.nn.gelu(stream + group_norm(hidden, gain, shift))


def block_forward(stream, weights):
    w_in, w_mid, w_out, gains = weights
    gain_one, shift_one, gain_two, shift_two, gain_three, shift_three = split_gains(gains)
    stream_low = stream.astype(jnp.bfloat16)
    hidden_in = jnp.einsum("bpc,cm->bpm", stream_low, w_in, preferred_element_type=jnp.float32)
    act_in = norm_act(hidden_in, gain_one, shift_one).astype(jnp.bfloat16)
    hidden_mid = jnp.einsum(
        "bpc,cm->bpm", patches_of(act_in), w_mid, preferred_element_type=jnp.float32
    )
    act_mid = norm_act(hidden_mid, gain_two, shift_two).astype(jnp.bfloat16)
    hidden_out = jnp.einsum("bpc,cm->bpm", act_mid, w_out, preferred_element_type=jnp.float32)
    result = outer_act(hidden_out, gain_three, shift_three, stream)
    return (result, (stream, stream_low, hidden_in, act_in, hidden_mid, act_mid, hidden_out))


def block_backward(grad_result, weights, kept, settle):
    w_in, w_mid, w_out, gains = weights
    stream, stream_low, hidden_in, act_in, hidden_mid, act_mid, hidden_out = kept
    gain_one, shift_one, gain_two, shift_two, gain_three, shift_three = split_gains(gains)
    _, back_three = jax.vjp(outer_act, hidden_out, gain_three, shift_three, stream)
    d_three, dg_three, db_three, d_resid = back_three(grad_result)
    d_three = d_three.astype(jnp.bfloat16)
    grad_out = settle(
        jnp.einsum("bpm,bpc->mc", act_mid, d_three, preferred_element_type=jnp.float32)
    )
    d_act_mid = jnp.einsum("bpc,mc->bpm", d_three, w_out, preferred_element_type=jnp.float32)
    _, back_two = jax.vjp(norm_act, hidden_mid, gain_two, shift_two)
    d_two, dg_two, db_two = back_two(d_act_mid)
    d_two = d_two.astype(jnp.bfloat16)
    grad_mid = settle(
        jnp.einsum("bpk,bpm->km", patches_of(act_in), d_two, preferred_element_type=jnp.float32)
    )
    d_cols = jnp.einsum("bpm,km->bpk", d_two, w_mid, preferred_element_type=jnp.float32)
    _, back_cols = jax.vjp(patches_of, act_in.astype(jnp.float32))
    (d_act_in,) = back_cols(d_cols)
    _, back_one = jax.vjp(norm_act, hidden_in, gain_one, shift_one)
    d_one, dg_one, db_one = back_one(d_act_in)
    d_one = d_one.astype(jnp.bfloat16)
    grad_in = jnp.einsum("bpc,bpm->cm", stream_low, d_one, preferred_element_type=jnp.float32)
    d_stream = d_resid + jnp.einsum("bpm,cm->bpc", d_one, w_in, preferred_element_type=jnp.float32)
    grad_gains = jnp.concatenate([dg_one, db_one, dg_two, db_two, dg_three, db_three])
    grad_in, grad_gains = settle((grad_in, grad_gains))
    return (d_stream, (grad_in, grad_mid, grad_out, grad_gains))


def on_device(
    frames,
    game_ids,
    taken_actions,
    next_actions,
    expert_flags,
    rewards,
    done_flags,
    weight_in,
    weight_mid,
    weight_out,
    norm_gains,
    head_table,
    moment_in,
    moment_mid,
    moment_out,
    moment_gains,
    moment_head,
    average_in,
    average_mid,
    average_out,
    average_gains,
    average_head,
):
    role_index = lax.axis_index("role")
    online = role_index == 0
    use_in = jnp.where(online, weight_in, average_in).astype(jnp.bfloat16)
    use_mid = jnp.where(online, weight_mid, average_mid).astype(jnp.bfloat16)
    use_out = jnp.where(online, weight_out, average_out).astype(jnp.bfloat16)
    use_gains = jnp.where(online, norm_gains, average_gains).astype(jnp.bfloat16)
    use_head = jnp.where(online, head_table, average_head).astype(jnp.bfloat16)
    support = support_low + (support_high - support_low) * jnp.arange(ATOMS, dtype=jnp.float32) / (
        ATOMS - 1
    )
    own_hot = (game_ids[:, None] == lax.broadcasted_iota(jnp.int32, (1, GAMES), 1)).astype(
        jnp.float32
    )
    counts = jnp.sum(own_hot, axis=0)
    stream = frames[0].astype(jnp.float32)
    layer = 0
    pieces = (
        lax.all_gather(use_in[layer], "dp", axis=0, tiled=True),
        lax.all_gather(use_mid[layer], "dp", axis=0, tiled=True),
        lax.all_gather(use_out[layer], "dp", axis=0, tiled=True),
        lax.all_gather(use_gains[layer], "dp", axis=0, tiled=True),
    )
    weights = (pieces[0], pieces[1], pieces[2], pieces[3].astype(jnp.float32))
    stream, saved = block_forward(stream, weights)
    gathered = [weights]
    kept = [saved]
    trans = stream.shape[0]
    pixels = stream.shape[1]
    wide_k = ACTIONS * ATOMS
    head_rows = head_table.shape[0]
    feat_low = jnp.mean(stream, axis=1).astype(jnp.bfloat16)
    feat_all, game_all = (
        lax.all_gather(feat_low, "dp", axis=0, tiled=True),
        lax.all_gather(game_ids.astype(jnp.bfloat16)[:, None], "dp", axis=0, tiled=True),
    )
    game_iota = lax.broadcasted_iota(jnp.int32, (1, GAMES), 1).astype(jnp.float32)
    all_hot = (game_all.astype(jnp.float32) == game_iota).astype(jnp.bfloat16)
    feat_rows = lax.dynamic_slice_in_dim(feat_all, lax.axis_index("dp") * head_rows, head_rows, 1)
    head_low = use_head.reshape(head_rows * GAMES, wide_k)

    def widen(count):
        spread_rows = (feat_rows[:, :, None] * all_hot[:, None, :]).reshape(
            count, head_rows * GAMES
        )
        return (spread_rows, all_hot)

    spread_rows, hot_piece = widen(trans * lax.axis_size("dp"))
    flat_logits = lax.psum_scatter(
        jnp.dot(spread_rows, head_low, preferred_element_type=jnp.float32),
        "dp",
        scatter_dimension=0,
        tiled=True,
    )
    logits = flat_logits.reshape(trans, ACTIONS, ATOMS)
    next_hot = (next_actions[:, None] == lax.broadcasted_iota(jnp.int32, (1, ACTIONS), 1)).astype(
        jnp.float32
    )
    next_prob = jax.nn.softmax(jnp.sum(logits * next_hot[:, :, None], axis=1), axis=-1)
    projected = project_target(next_prob, rewards, done_flags.astype(jnp.float32), support)
    target_dist = passed_along(projected, "role", -1)
    action_hot = (
        taken_actions[:, None] == lax.broadcasted_iota(jnp.int32, (1, ACTIONS), 1)
    ).astype(jnp.float32)
    expert = expert_flags.astype(jnp.float32)

    def local_loss(values):
        return transition_loss(values, target_dist, action_hot, expert, support)

    row_loss, loss_back = jax.vjp(local_loss, logits)
    sums = jnp.dot(row_loss, own_hot, precision=HIGHEST)
    total_counts, total_sums = lax.psum((counts, sums), "dp")
    floor_counts = jnp.maximum(total_counts, 1.0)
    loss_total = jnp.sum(total_sums / floor_counts)
    row_weight = jnp.dot(own_hot, 1.0 / (GAMES * floor_counts), precision=HIGHEST)
    (d_logits,) = loss_back(row_weight)
    d_low = d_logits.reshape(trans, wide_k).astype(jnp.bfloat16)
    piece = lax.all_gather(d_low, "dp", axis=0, tiled=True)
    count = piece.shape[0]
    spread_rows, hot_piece = widen(count)
    grad_head = lax.dot_general(
        spread_rows, piece, (((0,), (0,)), ((), ())), preferred_element_type=jnp.float32
    )
    back_wide = jnp.dot(piece, head_low.T, preferred_element_type=jnp.float32)
    back_rows = jnp.sum(
        back_wide.reshape(count, head_rows, GAMES) * hot_piece[:, None, :].astype(jnp.float32),
        axis=2,
    )
    grad_rows = back_rows
    grad_head, grad_rows = (grad_head, grad_rows)
    feat_grad = lax.all_to_all(
        grad_rows.astype(jnp.bfloat16), "dp", split_axis=0, concat_axis=1, tiled=True
    ).astype(grad_rows.dtype)
    d_stream = jnp.broadcast_to(feat_grad[:, None, :] / pixels, stream.shape)

    def settle(values):
        return values

    layer_grads = [None] * LAYERS
    for layer in reversed(range(LAYERS)):
        d_stream, block_grad = block_backward(d_stream, gathered[layer], kept[layer], settle)
        layer_grads[layer] = block_grad
    stacked = tuple((jnp.stack([layer_grads[0][kind]]) for kind in range(4)))
    reduced = lax.psum_scatter(stacked, "dp", scatter_dimension=1, tiled=True)
    head_grad = grad_head.reshape(head_rows, GAMES * wide_k)
    sent = (
        passed_along(upper_half(reduced[0]).astype(jnp.bfloat16), "role", 1).astype(jnp.float32),
        passed_along(upper_half(reduced[1]).astype(jnp.bfloat16), "role", 1).astype(jnp.float32),
        passed_along(upper_half(reduced[2]).astype(jnp.bfloat16), "role", 1).astype(jnp.float32),
        passed_along(reduced[3].astype(jnp.bfloat16), "role", 1).astype(jnp.float32),
        passed_along(upper_half(head_grad).astype(jnp.bfloat16), "role", 1).astype(jnp.float32),
        passed_along(loss_total.astype(jnp.bfloat16), "role", 1).astype(loss_total.dtype),
    )
    grad_in = jnp.where(online, lower_half(reduced[0]), sent[0])
    grad_mid = jnp.where(online, lower_half(reduced[1]), sent[1])
    grad_out = jnp.where(online, lower_half(reduced[2]), sent[2])
    grad_gains = jnp.where(online, reduced[3], sent[3])
    grad_table = jnp.where(online, lower_half(head_grad), sent[4])
    loss_out = jnp.where(online, loss_total, sent[5])
    in_w, in_m, in_a, in_c = renew(
        own_half(weight_in, role_index),
        grad_in,
        own_half(moment_in, role_index),
        own_half(average_in, role_index),
        learn_rate,
    )
    mid_w, mid_m, mid_a, mid_c = renew(
        own_half(weight_mid, role_index),
        grad_mid,
        own_half(moment_mid, role_index),
        own_half(average_mid, role_index),
        learn_rate,
    )
    out_w, out_m, out_a, out_c = renew(
        own_half(weight_out, role_index),
        grad_out,
        own_half(moment_out, role_index),
        own_half(average_out, role_index),
        learn_rate,
    )
    gain_w, gain_m, gain_a, gain_c = renew(
        norm_gains, grad_gains, moment_gains, average_gains, gain_rate
    )
    head_w, head_m, head_a, head_c = renew(
        own_half(head_table, role_index),
        grad_table,
        own_half(moment_head, role_index),
        own_half(average_head, role_index),
        learn_rate,
    )
    return (
        loss_out,
        in_w,
        grad_in,
        in_a,
        in_c,
        mid_w,
        mid_m,
        mid_a,
        mid_c,
        out_w,
        out_m,
        out_a,
        out_c,
        gain_w,
        gain_m,
        gain_a,
        gain_c,
        head_w,
        head_m,
        head_a,
        head_c,
    )


MESH = pl.DeviceIdType.MESH


def any_spec():
    return pl.BlockSpec(memory_space=pl.ANY)


def greet(peers):
    barrier = pltpu.get_barrier_semaphore()
    for cond, dev in peers:
        def go(dev=dev):
            pl.semaphore_signal(barrier, inc=1, device_id=dev, device_id_type=MESH)
        go() if cond is None else pl.when(cond)(go)
    count = sum(1 for cond, _ in peers if cond is None)
    for cond, _ in peers:
        if cond is not None:
            count = count + cond.astype(jnp.int32)
    pl.semaphore_wait(barrier, count)


def place():
    me = lax.axis_index("dp")
    core = lax.rem(me, 2)
    x = lax.rem(me // 2, 2)
    z = me // 4
    return me, z, x, core


D = 2048
MID = 512
GROUPS = 32
SIDE = 11
PIX = 121
TB = 8
PITCH = 12
RB = PITCH * TB
VR = SIDE * TB
ROWS = SIDE * RB
PAD = 16 * TB
EROWS = 164 * TB
BLK = 352
CH = 512
epsilon = 1e-05
GK = 0.7978845608028654
GC = 0.044715
OFFS = [(i - 1) * PITCH + (j - 1) for i in range(3) for j in range(3)]


def group_sum(v, gs):
    width = v.shape[1]
    n = width // 128
    a = lax.broadcasted_iota(jnp.int32, (128, 128), 0) // gs
    b = lax.broadcasted_iota(jnp.int32, (128, 128), 1) // gs
    m = (a == b).astype(jnp.float32)
    st = jnp.concatenate([v[:, k * 128:(k + 1) * 128] for k in range(n)], axis=0)
    r = jnp.dot(st, m, precision=lax.Precision.HIGHEST, preferred_element_type=jnp.float32)
    return jnp.concatenate([r[k * 8:(k + 1) * 8] for k in range(n)], axis=1)


def fold(v):
    rows, w = v.shape
    return jnp.sum(v.reshape(rows // TB, TB, w), axis=0)


def moments(h_ref, lo, gs):
    def one(r, acc):
        return acc + fold(h_ref[pl.ds(pl.multiple_of(r * RB, RB), VR), lo:lo + CH])
    s = lax.fori_loop(0, SIDE, one, jnp.zeros((TB, CH), jnp.float32))
    mean = group_sum(s, gs) / float(PIX * gs)

    def two(r, acc):
        h = h_ref[pl.ds(pl.multiple_of(r * RB, RB), VR), lo:lo + CH].reshape(SIDE, TB, CH) - mean[None]
        return acc + jnp.sum(h * h, axis=0)
    q = lax.fori_loop(0, SIDE, two, jnp.zeros((TB, CH), jnp.float32))
    var = group_sum(q, gs) / float(PIX * gs)
    return mean, lax.rsqrt(var + epsilon)


def gelu(u):
    return 0.5 * u * (1.0 + jnp.tanh(GK * (u + GC * (u * u * u))))


def dgelu(u):
    uu = u * u
    t = jnp.tanh(GK * u * (1.0 + GC * uu))
    return 0.5 * (1.0 + t) + 0.5 * u * (1.0 - t * t) * (GK + (3.0 * GK * GC) * uu)


def shifted(e_ref, o_ref, s, row, n):
    ref, base = (e_ref, 16 + s) if s % 2 == 0 else (o_ref, 17 + s)
    return ref[pl.ds(pl.multiple_of(row + base * TB, 16), n), :]


def put_shifted(e_ref, o_ref, r, v):
    z = jnp.zeros((TB, v.shape[1]), jnp.float32)
    at = pl.ds(pl.multiple_of(PAD + r * RB, 16), RB)
    e_ref[at, :] = jnp.concatenate([v, z], axis=0).astype(jnp.bfloat16)
    o_ref[at, :] = jnp.concatenate([z, v], axis=0).astype(jnp.bfloat16)


def clear_margins(e_ref, o_ref):
    z = jnp.zeros((PAD, MID), jnp.bfloat16)
    for ref in (e_ref, o_ref):
        ref[0:PAD, :] = z
        ref[PAD + ROWS:EROWS, :] = z


def row_at(r):
    return pl.ds(pl.multiple_of(r * RB, RB), VR)


def rows_full(r):
    return pl.ds(pl.multiple_of(r * RB, RB), RB)


def norm_back(h_ref, lo, dy_ref, mean, rstd, gain, gs, s1, s2, emit):
    n = 1.0 / float(PIX * gs)
    m1 = group_sum(gain * s1, gs) * n
    m2 = group_sum(gain * s2, gs) * n
    ca = rstd * gain
    cc = -rstd * rstd * m2
    cb = -rstd * m1 - mean * cc

    def one(r, c):
        h = h_ref[row_at(r), lo:lo + CH].reshape(SIDE, TB, CH)
        dy = dy_ref[row_at(r), :].reshape(SIDE, TB, CH)
        emit(r, (ca[None] * dy + cc[None] * h + cb[None]).reshape(VR, CH))
        return c
    lax.fori_loop(0, SIDE, one, 0)


D = 2048
GAMES = 40
ACTIONS = 18
ATOMS = 51
WIDE = ACTIONS * ATOMS
LW = 1024
WIN = 1024
COLS = GAMES * WIDE
HALF = COLS // 2
PADC = 36864
TB = 8
support_low = -10.0
support_high = 10.0
discount = 0.99
penalty = 0.05


def window_of(g):
    return (WIDE * g) // 16 * 16


def ids_offset(ids):
    return lax.bitwise_and(WIDE * ids, 15)


def shift_rows(v, off, right):
    width = v.shape[1]
    for b in range(1, 4):
        n = 1 << b
        bit = lax.bitwise_and(off, n) != 0
        bit = jnp.concatenate([bit.astype(jnp.float32)] * (width // 128), axis=1) > 0.5
        v = jnp.where(bit, pltpu.roll(v, n if right else width - n, 1), v)
    return v


def widen(dl):
    n = dl.shape[0]
    v = dl.astype(jnp.float32)
    v = jnp.concatenate([v[:, 0:TB], v[:, TB:2 * TB]], axis=2).reshape(n * TB, LW)
    lanes = lax.broadcasted_iota(jnp.int32, (n * TB, 128), 1)
    last = jnp.where(lanes < WIDE - LW + 128, v[:, LW - 128:], 0.0)
    return jnp.concatenate([v[:, :LW - 128], last], axis=1)


W_IN, W_MID, W_OUT, MISC = 0, 1, 2, 3
HC = 2048
NHC = -(-COLS // HC)
T0 = (((0,), (0,)), ((), ()))
T1 = (((1,), (1,)), ((), ()))


def rc(src, dst, ss, rs, dev):
    return pltpu.make_async_remote_copy(src_ref=src, dst_ref=dst, send_sem=ss, recv_sem=rs, device_id=dev,
                                        device_id_type=MESH)


def when(cond, do):
    if cond is None:
        do()
    else:
        pl.when(cond)(do)


class Gather:
    def __init__(self, nz, own, full, rows, own_sem, send, recv):
        self.nz, self.own_refs, self.full, self.rows = nz, own, full, rows
        self.own_sem, self.send, self.recv = own_sem, send, recv
        self.me, self.z, self.x, self.c = place()
        me, x, c = self.me, self.x, self.c
        self.up, self.down = {"dp": me + 4}, {"dp": me - 4}
        self.xp, self.cp = {"dp": me + 2 - 4 * x}, {"dp": me + 1 - 2 * c}
        self.has_up, self.has_down = self.z < nz - 1, self.z > 0
        self.started = []

    def slot(self, a, i):
        n = self.rows[a]
        return self.full[a].at[i] if n is None else self.full[a].at[pl.ds(pl.multiple_of(i * n, 16), n)]

    def put(self, cond, a, src, i, dev, k):
        d = rc(src, self.slot(a, i), self.send.at[a, k], self.recv.at[a, i], dev)
        when(cond, d.start)
        self.started.append((cond, d))

    def take(self, cond, a, i):
        d = rc(self.slot(a, i), self.slot(a, i), self.send.at[a, 0], self.recv.at[a, i], self.cp)
        when(cond, d.wait_recv)

    def begin(self, a):
        src = self.own_refs[a]
        self.put(self.has_up, a, src, self.me, self.up, 0)
        self.put(self.has_down, a, src, self.me, self.down, 1)
        self.put(None, a, src, self.me, self.xp, 2)
        self.put(None, a, src, self.me, self.cp, 3)
        pltpu.make_async_copy(src, self.slot(a, self.me), self.own_sem.at[a]).start()

    def along_z(self, a, d):
        k = 4 + (d - 1) * 6
        for up in (True, False):
            s = self.me - 4 * d if up else self.me + 4 * d
            ok = self.z - d >= 0 if up else self.z + d < self.nz
            more = jnp.logical_and(ok, self.has_up if up else self.has_down)
            m = k if up else k + 3
            self.take(ok, a, s)
            self.put(more, a, self.slot(a, s), s, self.up if up else self.down, m)
            self.put(ok, a, self.slot(a, s), s, self.xp, m + 1)
            self.put(ok, a, self.slot(a, s), s, self.cp, m + 2)

    def at_distance(self, d):
        for up in ((True,) if d == 0 else (False, True)):
            zz = self.z + d if up else self.z - d
            yield zz, (None if d == 0 else zz < self.nz if up else zz >= 0), up

    def along_x(self, a, d):
        k = 4 + (self.nz - 1) * 6
        for zz, ok, up in self.at_distance(d):
            s = zz * 4 + (1 - self.x) * 2 + self.c
            self.take(ok, a, s)
            self.put(ok, a, self.slot(a, s), s, self.cp, k + 2 * d + (1 if up else 0))

    def arrived(self, a):
        for d in range(self.nz):
            for zz, ok, _ in self.at_distance(d):
                for xx in (self.x, 1 - self.x):
                    self.take(ok, a, zz * 4 + xx * 2 + 1 - self.c)
        pltpu.make_async_copy(self.own_refs[a], self.slot(a, self.me), self.own_sem.at[a]).wait()

    def end(self):
        for cond, d in self.started:
            when(cond, d.wait_send)


def put_gain(gg_ref, at, s):
    gg_ref[:, at:at + CH] = jnp.sum(s, axis=0, keepdims=True)


def through(h_ref, d2_ref, st_ref, g_ref, gg_ref, at, goff, boff, emit):
    z8 = jnp.zeros((TB, CH), jnp.float32)
    mean = st_ref[0:8, at:at + MID]
    rstd = st_ref[8:16, at:at + MID]
    gain = g_ref[:, goff:goff + MID]
    shift = g_ref[:, boff:boff + MID]
    mr = mean * rstd

    def one(r, acc):
        s1, s2 = acc
        h = h_ref[row_at(r), :].reshape(SIDE, TB, MID)
        da = d2_ref[row_at(r), :].reshape(SIDE, TB, MID)
        xh = h * rstd[None] - mr[None]
        dy = da * dgelu(xh * gain + shift)
        d2_ref[row_at(r), :] = dy.reshape(VR, MID)
        return s1 + jnp.sum(dy, axis=0), s2 + jnp.sum(dy * xh, axis=0)
    s1, s2 = lax.fori_loop(0, SIDE, one, (z8, z8))
    put_gain(gg_ref, goff, s2)
    put_gain(gg_ref, boff, s1)
    norm_back(h_ref, 0, d2_ref, mean, rstd, gain, MID // GROUPS, s1, s2, emit)


def step_kernel(n, fr_hbm, wi, wm, wo, wg, ai, am, ao, ag, k0, k1, k2, k3, k4, k5, ht_hbm, ha_hbm,
                x_hbm, h1_hbm, a2_hbm, dh3_hbm, e_hbm, o_hbm, wmid_hbm, fart_hbm,
                st_ref, g_ref, gg_ref, gall_ref, frow_ref, dlog_ref, loss_ref,
                scal_ref, own_in, own_mid, own_out, own_misc, win_ref, wmid_ref, wout_ref, misc_ref,
                x_ref, h1_ref, h2_ref, h3_ref, a2_ref, dfeat_ref, sl_ref, e_ref, o_ref,
                d2_ref, dh3_ref, far_ref, fart_ref, fbuf, hbuf, head_ref,
                fsend, frecv, part, r1, r2, tgt_s, tgt_r, down_s, dsend, drecv,
                own_sem, g_send, g_recv, f_sem, h_sem, k_sem, ss, rs_,
                s_f, q_f, s_1, q_1, s_2, q_2, s_t, q_t, s_l, q_l, s_c, q_c, s_d, q_d, s_r, q_r):
    me, z, x, c = place()
    role = lax.axis_index("role")
    half = n // 2
    peers = [lax.rem(me + k, n) for k in range(1, n)]
    cp = me + 1 - 2 * c
    du_ref = d2_ref

    def pick(w, a, dst):
        def fill(src):
            dst[...] = src[...].astype(jnp.bfloat16)
        pl.when(role == 0)(lambda: fill(w))
        pl.when(role != 0)(lambda: fill(a))

    def fetch_frames(r):
        return pltpu.make_async_copy(fr_hbm.at[pl.ds(r * SIDE, SIDE)], fbuf.at[r % 2], f_sem.at[r % 2])

    def fetch_head(k, go):
        m = HC if k < NHC - 1 else COLS - (NHC - 1) * HC

        def one(src):
            d = pltpu.make_async_copy(src.at[pl.ds(k * HC, m)], hbuf.at[k % 2, pl.ds(0, m)], h_sem.at[k % 2])
            d.start() if go else d.wait()
        if go:
            pl.when(role == 0)(lambda: one(ht_hbm))
            pl.when(role != 0)(lambda: one(ha_hbm))
        else:
            one(ht_hbm)
    fetch_frames(0).start()
    fetch_head(0, True)
    pick(wi, ai, own_in)
    pick(wm, am, own_mid)
    pick(wo, ao, own_out)

    def pick_gains(src):
        v = src[...].astype(jnp.bfloat16).astype(jnp.float32)
        for k in range(3):
            own_misc[k:k + 1, :] = v[:, k * 128:(k + 1) * 128]
    own_misc[0:TB, :] = jnp.zeros((TB, 128), jnp.float32)
    pl.when(role == 0)(lambda: pick_gains(wg))
    pl.when(role != 0)(lambda: pick_gains(ag))
    for k, ref in enumerate((k0, k1, k2, k3, k4, k5)):
        for t in range(TB):
            scal_ref[k, t:t + 1, :] = jnp.full((1, 128), ref[t].astype(jnp.float32), jnp.float32)
    own_misc[TB:2 * TB, :] = scal_ref[5]
    greet([(None, {"dp": p}) for p in peers] + [(None, {"role": 1 - role})])

    gath = Gather(n // 4, (own_in, own_mid, own_out, own_misc), (win_ref, wmid_ref, wout_ref, misc_ref),
               (D // n, 9 * MID // n, MID // n, None), own_sem, g_send, g_recv)
    casts = iter(range(NHC))

    def cast_head(times):
        for _ in range(times):
            k = next(casts, None)
            if k is None:
                return
            if k + 1 < NHC:
                fetch_head(k + 1, True)
            fetch_head(k, False)
            m = HC if k < NHC - 1 else COLS - (NHC - 1) * HC
            u = 128 if m % 128 == 0 else 112

            def one(i, carry, k=k, u=u):
                rs = pl.ds(pl.multiple_of(i * u, 16), u)
                head_ref[pl.ds(pl.multiple_of(k * HC + i * u, 16), u), :] = hbuf[k % 2, rs, :].astype(jnp.bfloat16)
                return carry
            lax.fori_loop(0, m // u, one, 0)

    for a in (MISC, W_IN, W_MID):
        gath.begin(a)
    for r in range(SIDE):
        if r + 1 < SIDE:
            fetch_frames(r + 1).start()
        fetch_frames(r).wait()
        v = fbuf[r % 2].astype(jnp.float32).reshape(VR, D)
        x_ref[r * RB:(r + 1) * RB, :] = jnp.concatenate([v, jnp.zeros((TB, D), jnp.float32)], axis=0).astype(jnp.bfloat16)
    clear_margins(e_ref, o_ref)
    head_ref[COLS:PADC, :] = jnp.zeros((PADC - COLS, 128), jnp.bfloat16)
    far = n // 4 - 1
    kept = [pltpu.make_async_copy(src, dst, k_sem.at[k]) for k, (src, dst) in enumerate((
        (x_ref, x_hbm), (h1_ref, h1_hbm), (a2_ref, a2_hbm), (dh3_ref, dh3_hbm), (e_ref, e_hbm), (o_ref, o_hbm),
        (wmid_ref, wmid_hbm)))]

    def keep(k):
        pl.when(role == 0)(kept[k].start)
    keep(0)

    def z_step(a, d):
        if d <= far:
            gath.along_z(a, d)

    def x_step(a, d):
        if d <= far:
            gath.along_x(a, d)
    for d in range(1, far + 1):
        z_step(W_IN, d)
        z_step(MISC, d)
        cast_head(2)
        x_step(W_IN, d - 1)
        x_step(MISC, d - 1)
        z_step(W_MID, d)
        cast_head(2)
        if d == max(far - 1, 1):
            gath.begin(W_OUT)
    x_step(W_IN, far)
    x_step(MISC, far)
    x_step(W_MID, 0)
    x_step(W_MID, 1)
    cast_head(1)
    z_step(W_OUT, 1)
    gath.arrived(MISC)
    gath.arrived(W_IN)
    for i in range(n):
        gall_ref[i] = misc_ref[i, TB:2 * TB, :]
        for k in range(3):
            at = (i * 3 + k) * 128
            g_ref[:, at:at + 128] = misc_ref[i, k:k + 1, :]

    def mm1(i, carry):
        rs = pl.ds(pl.multiple_of(i * BLK, BLK), BLK)
        h1_ref[rs, :] = jnp.dot(x_ref[rs, :], win_ref[...], preferred_element_type=jnp.float32)
        return carry
    lax.fori_loop(0, ROWS // BLK, mm1, 0)
    z_step(W_OUT, 2)
    x_step(W_MID, 2)
    keep(1)
    mean, rstd = moments(h1_ref, 0, MID // GROUPS)
    st_ref[0:8, 0:MID] = mean
    st_ref[8:16, 0:MID] = rstd
    sc = rstd * g_ref[:, 0:MID]
    sh = g_ref[:, MID:2 * MID] - mean * sc

    def act1(r, carry):
        h = h1_ref[row_at(r), :].reshape(SIDE, TB, MID)
        a = gelu(h * sc[None] + sh[None]).reshape(VR, MID)
        put_shifted(e_ref, o_ref, r, a)
        return carry
    lax.fori_loop(0, SIDE, act1, 0)
    inner = pl.ds(PAD, ROWS)

    def far_a1(to):
        return rc(e_ref.at[inner], far_ref, ss.at[0], rs_.at[0], {"role": to})

    pl.when(role == 0)(lambda: far_a1(1).start())
    cast_head(NHC)
    z_step(W_OUT, 3)
    for d in range(3, far + 1):
        x_step(W_MID, d)
    gath.arrived(W_MID)
    keep(6)

    def mm2(i, carry):
        row = i * BLK
        acc = None
        for m, s in enumerate(OFFS):
            p = jnp.dot(shifted(e_ref, o_ref, s, row, BLK), wmid_ref[m * MID:(m + 1) * MID, :],
                        preferred_element_type=jnp.float32)
            acc = p if acc is None else acc + p
        h2_ref[pl.ds(pl.multiple_of(row, BLK), BLK), :] = acc
        return carry
    lax.fori_loop(0, ROWS // BLK, mm2, 0)
    for d in range(far + 1):
        x_step(W_OUT, d)
    mean, rstd = moments(h2_ref, 0, MID // GROUPS)
    st_ref[0:8, MID:2 * MID] = mean
    st_ref[8:16, MID:2 * MID] = rstd
    sc2 = rstd * g_ref[:, 2 * MID:3 * MID]
    sh2 = g_ref[:, 3 * MID:4 * MID] - mean * sc2

    def act2(r, carry):
        h = h2_ref[rows_full(r), :].reshape(PITCH, TB, MID)
        a2_ref[rows_full(r), :] = gelu(h * sc2[None] + sh2[None]).reshape(RB, MID).astype(jnp.bfloat16)
        return carry
    lax.fori_loop(0, SIDE, act2, 0)
    keep(2)
    gath.arrived(W_OUT)

    def mm3(i, carry):
        rs = pl.ds(pl.multiple_of(i * BLK, BLK), BLK)
        h3_ref[rs, :] = jnp.dot(a2_ref[rs, :], wout_ref[...], preferred_element_type=jnp.float32)
        return carry
    lax.fori_loop(0, ROWS // BLK, mm3, 0)
    for k in range(D // CH):
        lo = k * CH
        mean, rstd = moments(h3_ref, lo, D // GROUPS)
        st_ref[0:8, 2 * MID + lo:2 * MID + lo + CH] = mean
        st_ref[8:16, 2 * MID + lo:2 * MID + lo + CH] = rstd
        sc3 = rstd * g_ref[:, 4 * MID + lo:4 * MID + lo + CH]
        sh3 = g_ref[:, 4 * MID + D + lo:4 * MID + D + lo + CH] - mean * sc3

        def act3(r, acc):
            h = h3_ref[row_at(r), lo:lo + CH].reshape(SIDE, TB, CH)
            s = x_ref[rows_full(r), lo:lo + CH].astype(jnp.float32)[0:VR].reshape(SIDE, TB, CH)
            return acc + jnp.sum(gelu(s + (h * sc3[None] + sh3[None])), axis=0)
        acc = lax.fori_loop(0, SIDE, act3, jnp.zeros((TB, CH), jnp.float32))
        feat = (acc / float(PIX)).astype(jnp.bfloat16).astype(jnp.float32)
        for j in range(lo // 128, (lo + CH) // 128):
            fsend[j] = feat[:, j * 128 - lo:(j + 1) * 128 - lo]

            @pl.when(me != j)
            def _(j=j):
                rc(fsend.at[j], frecv.at[me], s_f.at[j], q_f.at[me], {"dp": j}).start()

            @pl.when(me == j)
            def _(j=j):
                frecv[j] = fsend[j]

    z8 = jnp.zeros((TB, CH), jnp.float32)

    def slopes(k):
        lo = k * CH
        cs = slice(lo, lo + CH)
        mean = st_ref[0:8, 2 * MID + lo:2 * MID + lo + CH]
        rstd = st_ref[8:16, 2 * MID + lo:2 * MID + lo + CH]
        gain = g_ref[:, 4 * MID + lo:4 * MID + lo + CH]
        shift = g_ref[:, 4 * MID + D + lo:4 * MID + D + lo + CH]
        mr = mean * rstd

        def one(r, acc):
            s1, s2 = acc
            h = h3_ref[row_at(r), cs].reshape(SIDE, TB, CH)
            v = x_ref[rows_full(r), cs].astype(jnp.float32)[0:VR].reshape(SIDE, TB, CH)
            xh = h * rstd[None] - mr[None]
            t = dgelu(v + (xh * gain + shift))
            dh3_ref[rows_full(r), cs] = jnp.concatenate([t.reshape(VR, CH), z8], axis=0).astype(jnp.bfloat16)
            return s1 + jnp.sum(t, axis=0), s2 + jnp.sum(t * xh, axis=0)
        s1, s2 = lax.fori_loop(0, SIDE, one, (z8, z8))
        sl_ref[0:8, cs] = s1
        sl_ref[8:16, cs] = s2

    @pl.when(role == 0)
    def _():
        slopes(0)
        slopes(1)
    for p in peers:
        rc(fsend.at[p], frecv.at[p], s_f.at[0], q_f.at[p], {"dp": p}).wait_recv()
    feats = frecv[...].reshape(n * TB, 128)
    ids = gall_ref[...].reshape(n * TB, 128).astype(jnp.int32)

    acc = None
    def two_windows(i):
        a, b = window_of(i), window_of(i + 1)
        return jnp.concatenate([head_ref[a:a + WIN, :], head_ref[b:b + WIN, :]], axis=1)
    for i in range(0, GAMES, 2):
        lhs = jnp.concatenate([jnp.where(ids == i, feats, 0.0), jnp.where(ids == i + 1, feats, 0.0)], axis=1)
        p = lax.dot_general(lhs.astype(jnp.bfloat16), two_windows(i), T1, preferred_element_type=jnp.float32)
        acc = p if acc is None else acc + p
    off = ids_offset(ids)
    part[...] = shift_rows(acc, off, False).reshape(half, 2, TB, LW)

    d1 = rc(part.at[:, 1 - c], r1, s_1, q_1, {"dp": cp})
    d1.start()
    d1.wait()
    pair = me // 2
    r1[...] = r1[...] + part[:, c]
    pps = [lax.rem(pair + k, half) for k in range(1, half)]
    for k, p in enumerate(pps):
        rc(r1.at[p], r2.at[pair], s_2.at[k], q_2.at[pair], {"dp": 2 * p + c}).start()
    r2[pair] = r1[pair]

    @pl.when(role == 0)
    def _():
        slopes(2)
        slopes(3)
    for k, p in enumerate(pps):
        rc(r1.at[p], r2.at[p], s_2.at[k], q_2.at[p], {"dp": 2 * p + c}).wait_recv()
    logits = jnp.sum(r2[...], axis=0)

    lane = lax.broadcasted_iota(jnp.int32, (TB, 128), 1)
    live = lane < ATOMS
    zi = support_low + (support_high - support_low) * lane.astype(jnp.float32) / (ATOMS - 1)
    zi = jnp.where(live, zi, 0.0)
    taken, nxt, expert, reward, done, gid = (scal_ref[k] for k in range(6))
    pieces = []
    for a in range(ACTIONS):
        v = logits if a == 0 else pltpu.roll(logits, LW - ATOMS * a, 1)
        pieces.append(v[:, :128])

    @pl.when(role == 1)
    def _():
        sel = jnp.zeros((TB, 128), jnp.float32)
        for a in range(ACTIONS):
            sel = sel + jnp.where(nxt == float(a), pieces[a], 0.0)
        sel = jnp.where(live, sel, -1e30)
        e = jnp.exp(sel - jnp.max(sel, axis=1, keepdims=True))
        e = jnp.where(live, e, 0.0)
        prob = e / jnp.sum(e, axis=1, keepdims=True)
        spacing = (support_high - support_low) / (ATOMS - 1)
        m = jnp.zeros((TB, 128), jnp.float32)
        for j in range(ATOMS):
            zj = float(np.float32(support_low) + np.float32(support_high - support_low) * np.float32(j) /
                       np.float32(ATOMS - 1))
            tz = jnp.clip(reward + discount * (1.0 - done) * zj, support_low, support_high)
            wt = jnp.maximum(0.0, 1.0 - jnp.abs(tz - zi) / spacing)
            m = m + prob[:, j:j + 1] * wt
        tgt_s[...] = jnp.where(live, m, 0.0)
        d = rc(tgt_s, tgt_r, s_t, q_t, {"role": 0})
        d.start()
        d.wait_send()
        rc(frow_ref, frow_ref, s_r.at[0], q_r.at[0], {"role": 0}).wait_recv()
        rc(dlog_ref, dlog_ref, s_r.at[1], q_r.at[1], {"role": 0}).wait_recv()
        dfeat_ref[...] = jnp.zeros_like(dfeat_ref)

    @pl.when(role == 0)
    def _():
        frow_ref[...] = feats.astype(jnp.bfloat16)
        gt = jnp.transpose(gall_ref[...].reshape(n * TB, 128))[0:TB]
        count = jnp.sum((gt == gid).astype(jnp.float32), axis=1, keepdims=True)
        weight = 1.0 / jnp.maximum(count, 1.0)
        x3 = jnp.where(live[None], jnp.stack(pieces), -1e30)
        act = lax.broadcasted_iota(jnp.int32, (ACTIONS, TB, 128), 0).astype(jnp.float32)
        hot = (act == taken[None]).astype(jnp.float32)
        mx = jnp.max(x3, axis=2, keepdims=True)
        e = jnp.where(live[None], jnp.exp(x3 - mx), 0.0)
        s = jnp.sum(e, axis=2, keepdims=True)
        logp = jnp.where(live[None], x3 - mx - jnp.log(s), 0.0)
        prob = e / s
        q = jnp.sum(prob * zi[None], axis=2, keepdims=True)
        qb = jnp.broadcast_to(q, (ACTIONS, TB, 128))
        qm = jnp.max(qb, axis=0)
        qe = jnp.exp(qb - qm[None])
        qs = jnp.sum(qe, axis=0)
        lse = qm + jnp.log(qs)
        pol = qe / qs[None]
        chosen = jnp.sum(logp * hot, axis=0)
        qt = jnp.sum(qb * hot, axis=0)
        rc(tgt_s, tgt_r, s_t, q_t, {"role": 1}).wait_recv()
        m = tgt_r[...]
        cross = -jnp.sum(m * chosen, axis=1, keepdims=True)
        row_loss = cross + penalty * expert * (lse - qt)
        msum = jnp.sum(m, axis=1, keepdims=True)
        dl = hot * (prob * msum[None] - m[None]) + (penalty * expert)[None] * (pol - hot) * prob * (zi[None] - qb)
        dl = jnp.where(live[None], dl * (weight * (1.0 / GAMES))[None], 0.0)
        flat = jnp.zeros((TB, LW), jnp.float32)
        pad = jnp.zeros((TB, LW - 128), jnp.float32)
        for a in range(ACTIONS):
            v = jnp.concatenate([dl[a], pad], axis=1)
            flat = flat + (v if a == 0 else pltpu.roll(v, ATOMS * a, 1))
        l0 = row_loss * weight
        p0 = l0.astype(jnp.bfloat16).astype(jnp.float32)
        p1 = (l0 - p0).astype(jnp.bfloat16).astype(jnp.float32)
        p2 = l0 - p0 - p1
        last = flat[:, LW - 128:]
        last = jnp.where(lane == 125, p0, jnp.where(lane == 126, p1, jnp.where(lane == 127, p2, last)))
        flat = jnp.concatenate([flat[:, :LW - 128], last], axis=1)
        down_s[...] = jnp.concatenate([flat[:, :LW // 2], flat[:, LW // 2:]], axis=0).astype(jnp.bfloat16)
        for k, p in enumerate(pps):
            rc(down_s, dlog_ref.at[me], s_l.at[k], q_l.at[me], {"dp": 2 * p + c}).start()
        rc(down_s, dlog_ref.at[me], s_c.at[0], q_c.at[me], {"dp": cp}).start()
        dlog_ref[me] = down_s[...]
        for k, p in enumerate(pps):
            o = 2 * p + c
            rc(down_s, dlog_ref.at[o], s_l.at[k], q_l.at[o], {"dp": cp}).wait_recv()
            rc(dlog_ref.at[o], dlog_ref.at[o], s_c.at[k + 1], q_c.at[o], {"dp": cp}).start()
        for p in [pair] + pps:
            o = 2 * p + 1 - c
            rc(dlog_ref.at[o], dlog_ref.at[o], s_c.at[0], q_c.at[o], {"dp": cp}).wait_recv()
        to0 = rc(frow_ref, frow_ref, s_r.at[0], q_r.at[0], {"role": 1})
        to1 = rc(dlog_ref, dlog_ref, s_r.at[1], q_r.at[1], {"role": 1})
        to0.start()
        to1.start()
        rolled = shift_rows(widen(dlog_ref[...]), off, True).astype(jnp.bfloat16)
        acc = None
        for i in range(0, GAMES, 2):
            p = jnp.dot(rolled, two_windows(i), preferred_element_type=jnp.float32)
            p = jnp.where(ids == i, p[:, :128], jnp.where(ids == i + 1, p[:, 128:], 0.0))
            acc = p if acc is None else acc + p
        dsend[...] = acc.reshape(n, TB, 128)
        for k, p in enumerate(peers):
            rc(dsend.at[p], drecv.at[me], s_d.at[k], q_d.at[me], {"dp": p}).start()
        drecv[me] = dsend[me]
        for k, p in enumerate(peers):
            rc(dsend.at[p], drecv.at[p], s_d.at[k], q_d.at[p], {"dp": p}).wait_recv()
        for j in range(n):
            dfeat_ref[:, j * 128:(j + 1) * 128] = drecv[j]
        for k, p in enumerate(pps):
            rc(down_s, dlog_ref.at[me], s_l.at[k], q_l.at[me], {"dp": 2 * p + c}).wait_send()
        rc(down_s, dlog_ref.at[me], s_c.at[0], q_c.at[me], {"dp": cp}).wait_send()
        for k, p in enumerate(pps):
            o = 2 * p + c
            rc(dlog_ref.at[o], dlog_ref.at[o], s_c.at[k + 1], q_c.at[o], {"dp": cp}).wait_send()
        for k, p in enumerate(peers):
            rc(dsend.at[p], drecv.at[me], s_d.at[k], q_d.at[me], {"dp": p}).wait_send()
        to0.wait_send()
        to1.wait_send()

    for j in range(n):
        pl.when(me != j)(rc(fsend.at[j], frecv.at[me], s_f.at[j], q_f.at[me], {"dp": j}).wait_send)
    for k, p in enumerate(pps):
        rc(r1.at[p], r2.at[pair], s_2.at[k], q_2.at[pair], {"dp": 2 * p + c}).wait_send()
    tail = dlog_ref[:, :, 384:512].astype(jnp.float32)[:, TB:2 * TB].reshape(n * TB, 128)
    lanes = lax.broadcasted_iota(jnp.int32, (n * TB, 128), 1)
    total = jnp.sum(jnp.where(lanes >= 125, tail, 0.0))
    loss_ref[...] = jnp.full((TB, 128), total, jnp.float32)

    def last_norm():
        for k in range(D // CH):
            lo = k * CH
            cs = slice(lo, lo + CH)
            mean = st_ref[0:8, 2 * MID + lo:2 * MID + lo + CH]
            rstd = st_ref[8:16, 2 * MID + lo:2 * MID + lo + CH]
            gain = g_ref[:, 4 * MID + lo:4 * MID + lo + CH]
            dout = dfeat_ref[:, cs] / float(PIX)
            s1 = dout * sl_ref[0:8, cs]
            s2 = dout * sl_ref[8:16, cs]
            put_gain(gg_ref, 4 * MID + lo, s2)
            put_gain(gg_ref, 4 * MID + D + lo, s1)
            count = 1.0 / float(PIX * D // GROUPS)
            m1 = group_sum(gain * s1, D // GROUPS) * count
            m2 = group_sum(gain * s2, D // GROUPS) * count
            cc = -rstd * rstd * m2
            cb = -rstd * m1 - mean * cc
            ca = rstd * gain * dout

            def one(r, carry):
                h = h3_ref[row_at(r), cs].reshape(SIDE, TB, CH)
                t = dh3_ref[rows_full(r), cs].astype(jnp.float32)[0:VR].reshape(SIDE, TB, CH)
                v = (ca[None] * t + cc[None] * h + cb[None]).reshape(VR, CH)
                dh3_ref[rows_full(r), cs] = jnp.concatenate([v, z8], axis=0).astype(jnp.bfloat16)
                return carry
            lax.fori_loop(0, SIDE, one, 0)

    @pl.when(role == 0)
    def _():
        last_norm()
        kept[3].start()

        def da2(i, c):
            rs = pl.ds(pl.multiple_of(i * BLK, BLK), BLK)
            d2_ref[rs, :] = lax.dot_general(dh3_ref[rs, :], wout_ref[...], T1, preferred_element_type=jnp.float32)
            return c
        lax.fori_loop(0, ROWS // BLK, da2, 0)
        far_a1(1).wait_send()
        through(h2_ref, d2_ref, st_ref, g_ref, gg_ref, MID, 2 * MID, 3 * MID,
                lambda r, v: put_shifted(e_ref, o_ref, r, v))
        kept[4].start()
        kept[5].start()
        gg_ref[:, 0:2 * MID] = jnp.zeros((1, 2 * MID), jnp.float32)
        for d in kept:
            d.wait()

    @pl.when(role == 1)
    def _():
        far_a1(0).wait_recv()
        for k in range(MID // 128):
            fart_ref[k * 128:(k + 1) * 128, :] = jnp.transpose(far_ref[:, k * 128:(k + 1) * 128])
        d = pltpu.make_async_copy(fart_ref, fart_hbm, k_sem.at[7])
        d.start()
        d.wait()
        gg_ref[...] = jnp.zeros_like(gg_ref)
    gath.end()


def block_step(frames, weights, averages, scal, head, avg_head, n, cid):
    f32, b16 = jnp.float32, jnp.bfloat16
    S = jax.ShapeDtypeStruct
    V, dma = pltpu.VMEM, pltpu.SemaphoreType.DMA
    vs, hs = pl.BlockSpec(memory_space=pltpu.VMEM), pl.BlockSpec(memory_space=pl.ANY)
    h = n // 2
    nz = n // 4
    sends = 4 + 6 * (nz - 1) + 2 * nz
    return pl.pallas_call(
        functools.partial(step_kernel, n),
        out_shape=(S((ROWS, D), b16), S((ROWS, MID), f32), S((ROWS, MID), b16), S((ROWS, D), b16), S((EROWS, MID), b16),
                   S((EROWS, MID), b16), S((9 * MID, MID), b16), S((MID, ROWS), b16), S((16, 2 * MID + D), f32),
                   S((1, 4 * MID + 2 * D), f32), S((1, 4 * MID + 2 * D), f32), S((n, TB, 128), f32), S((n * TB, 128), b16), S((n, 16, 512), b16), S((TB, 128), f32)),
        in_specs=[hs] + [vs] * 8 + [pl.BlockSpec(memory_space=pltpu.SMEM)] * 6 + [hs] * 2,
        out_specs=(hs,) * 8 + (vs,) * 7,
        scratch_shapes=[
            V((6, TB, 128), f32), V((D // n, MID), b16), V((9 * MID // n, MID), b16), V((MID // n, D), b16), V((16, 128), f32),
            V((D, MID), b16), V((9 * MID, MID), b16), V((MID, D), b16), V((n, 16, 128), f32),
            V((ROWS, D), b16), V((ROWS, MID), f32), V((ROWS, MID), f32), V((ROWS, D), f32), V((ROWS, MID), b16),
            V((TB, D), f32), V((16, D), f32), V((EROWS, MID), b16), V((EROWS, MID), b16),
            V((ROWS, MID), f32), V((ROWS, D), b16), V((ROWS, MID), b16), V((MID, ROWS), b16),
            V((2, SIDE, TB, D), b16), V((2, HC, 128), f32), V((PADC, 128), b16),
            V((n, TB, 128), f32), V((n, TB, 128), f32), V((h, 2, TB, LW), f32), V((h, TB, LW), f32),
            V((h, TB, LW), f32), V((TB, 128), f32), V((TB, 128), f32), V((16, 512), b16),
            V((n, TB, 128), f32), V((n, TB, 128), f32),
            dma((4,)), dma((4, sends)), dma((4, n)), dma((2,)), dma((2,)), dma((8,)), dma((1,)), dma((1,)),
            dma((n,)), dma((n,)), dma, dma, dma((h,)), dma((h,)), dma, dma, dma((h,)), dma((n,)),
            dma((h,)), dma((n,)), dma((n,)), dma((n,)), dma((2,)), dma((2,))],
        compiler_params=pltpu.CompilerParams(collective_id=cid, has_side_effects=True,
                                             vmem_limit_bytes=64 * 1024 * 1024),
        name="block_step",
    )(frames, *weights, *averages, *scal, head, avg_head)


KEEP, SEND, BOTH = 0, 1, 2
OUT, MIDDLE, IN, GAINS = 0, 1, 2, 3


def units_of(ri, ro, rm):
    q, h, t = MID // 4, ri // 2, rm // 2
    online = ((0, ri + 2 * ro, 2 * ro, 0, MID, SEND, OUT), (0, ri, 2 * ro, 0, MID, KEEP, OUT),
              (0, 0, ri, MID // 2, MID // 2, SEND, IN), (0, 0, h, 0, MID // 2, KEEP, IN), (0, h, h, 0, MID // 2, KEEP, IN),
              (1, 0, 3, 0, 128, BOTH, GAINS))
    target = ((0, 0, rm, 0, q, SEND, MIDDLE), (0, 0, rm, q, q, SEND, MIDDLE), (0, 0, rm, 2 * q, q, KEEP, MIDDLE),
              (0, 0, t, 3 * q, q, KEEP, MIDDLE), (0, t, 96, 3 * q, q, KEEP, MIDDLE),
              (0, t + 96, t - 96, 3 * q, q, KEEP, MIDDLE))
    return online, target


def sums_kernel(n_dev, rows, x_hbm, h1_hbm, a2_hbm, dh3_hbm, e_hbm, o_hbm, wmid_hbm, fart_hbm, st_ref, g_ref, gpart_ref,
                gall_ref, frow_ref, dlog_ref, t_out, t_mid, t_in, t_gains, dlt, rhs, x_ref, h1_ref, a2_ref, dh3_ref, e_ref, o_ref, wmid_ref, fart_ref, low_ref,
                d2_ref, gg_ref, *refs):
    outs = (t_out, t_mid, t_in, t_gains)
    g, r1, r2, rz = (refs[2 * j:2 * j + 2] for j in range(4))
    fs, fr = refs[8:12], refs[12:16]
    s1, q1, s2, q2, s3, q3, sf, qf, sl, sd, qd = refs[16:]
    nz = n_dev // 4
    ri, ro, rm = rows
    online, target = units_of(*rows)
    me, z, x, c = place()
    role = lax.axis_index("role")
    xp = {"dp": me + 2 - 4 * x}
    cp = {"dp": me + 1 - 2 * c}

    def slot(zz, xx, cc):
        return zz * 4 + xx * 2 + cc

    order = list(range(nz))
    parts = ((0, 128), (128, 128), (256, 128), (384, MID - 384))

    def load(k):
        src = (x_hbm, h1_hbm, a2_hbm, dh3_hbm, e_hbm, o_hbm, wmid_hbm, fart_hbm)[k]
        dst = (x_ref, h1_ref, a2_ref, dh3_ref, e_ref, o_ref, wmid_ref, fart_ref)[k]
        return pltpu.make_async_copy(src, dst, sl.at[k])

    def far_d2(to, k):
        cs = pl.ds(*parts[k])
        return rc(e_hbm.at[pl.ds(PAD, ROWS), cs], low_ref.at[:, cs], sd.at[k], qd.at[k], {"role": to})

    @pl.when(role == 0)
    def _():
        for k in (3, 2, 6, 4, 5, 1, 0):
            load(k).start()
    pl.when(role == 1)(load(7).start)
    zs = [{"dp": lax.rem(me + 4 * k, 4 * nz)} for k in range(1, nz)]
    greet([(None, p) for p in [xp, cp, {"role": 1 - role}] + zs])
    z8 = jnp.zeros((TB, CH), jnp.float32)

    def online_first():
        for k in range(len(parts)):
            far_d2(1, k).start()
        gg_ref[...] = gpart_ref[...]
        load(3).wait()
        load(2).wait()
        for k in (2, 3, 0, 1):
            v = lax.dot_general(a2_ref[...], dh3_ref[:, k * CH:(k + 1) * CH], T0, preferred_element_type=jnp.float32)
            g[0][:, ri + k * ro:ri + (k + 1) * ro, :] = v.reshape(n_dev, ro, CH)

    def online_rest():
        for k in (6, 4, 5, 1, 0):
            load(k).wait()

        def da1(i, carry):
            row = i * BLK
            acc = None
            for m, s in enumerate(OFFS):
                p = lax.dot_general(shifted(e_ref, o_ref, -s, row, BLK), wmid_ref[m * MID:(m + 1) * MID, :], T1,
                                    preferred_element_type=jnp.float32)
                acc = p if acc is None else acc + p
            d2_ref[pl.ds(pl.multiple_of(row, BLK), BLK), :] = acc
            return carry
        lax.fori_loop(0, ROWS // BLK, da1, 0)

        def put1(r, v):
            low_ref[rows_full(r), :] = jnp.concatenate([v, z8], axis=0).astype(jnp.bfloat16)
        through(h1_ref, d2_ref, st_ref, g_ref, gg_ref, 0, 0, MID, put1)
        per = CH // ri
        for k in range(D // CH):
            v = lax.dot_general(x_ref[:, k * CH:(k + 1) * CH], low_ref[...], T0, preferred_element_type=jnp.float32)
            g[0][k * per:(k + 1) * per, 0:ri, :] = v.reshape(per, ri, MID)
        for i in range(n_dev):
            for k in range(3):
                at = (i * 3 + k) * 128
                g[1][i, k:k + 1, :] = gg_ref[:, at:at + 128]

    def target_part(k):
        if k == 0:
            clear_margins(e_ref, o_ref)
            load(7).wait()
        cs = slice(parts[k][0], parts[k][0] + parts[k][1] if k < 2 else MID)
        far_d2(0, k).wait_recv()
        if k == 2:
            far_d2(0, 3).wait_recv()
        zh = jnp.zeros((TB, cs.stop - cs.start), jnp.float32)

        def rebuild(r, carry):
            v = low_ref[rows_full(r), cs].astype(jnp.float32)
            at = pl.ds(pl.multiple_of(PAD + r * RB, 16), RB)
            e_ref[at, cs] = low_ref[rows_full(r), cs]
            o_ref[at, cs] = jnp.concatenate([zh, v[0:VR]], axis=0).astype(jnp.bfloat16)
            return carry
        lax.fori_loop(0, SIDE, rebuild, 0)
        for m, s in enumerate(OFFS):
            ref, base = (e_ref, 16 - s) if s % 2 == 0 else (o_ref, 17 - s)
            v = jnp.dot(fart_ref[...], ref[base * TB:base * TB + ROWS, cs], preferred_element_type=jnp.float32)
            at = m * MID
            while at < (m + 1) * MID:
                i = at // rm
                end = min((i + 1) * rm, (m + 1) * MID)
                g[0][i, at - i * rm:end - i * rm, cs] = v[at - m * MID:end - m * MID]
                at = end

    def cut(ref, i, u):
        return ref.at[i, pl.ds(u[1], u[2]), pl.ds(u[3], u[4])]

    def region(u):
        if u[6] == OUT:
            return slice(0, ro), slice(0, outs[OUT].shape[1])
        at = u[3] % outs[u[6]].shape[1]
        return slice(u[1], u[1] + u[2]), slice(at, at + u[4])

    def place_sum(u, total):
        if u[6] == OUT:
            return jnp.concatenate([total[j * ro:(j + 1) * ro] for j in range(u[2] // ro)], axis=1)
        return total

    def final(u, to, n):
        rs, cs = region(u)
        at = (pl.ds(rs.start, rs.stop - rs.start), pl.ds(cs.start, cs.stop - cs.start))
        return rc(fs[u[6]].at[at], fr[u[6]].at[at], sf.at[n], qf.at[n], {"role": to})

    def run(units, mine, plan):
        def add(u, i, ref, j):
            a, rs, cs = u[0], slice(u[1], u[1] + u[2]), slice(u[3], u[3] + u[4])
            g[a][i, rs, cs] = g[a][i, rs, cs] + ref[a][j, rs, cs]

        def c1(n, zz, k):
            u = units[n]
            xx = 1 - x if k == 0 else x
            return rc(cut(g[u[0]], slot(zz, xx, 1 - c), u), cut(r1[u[0]], k * nz + zz, u), s1.at[n, k * nz + zz],
                      q1.at[n, k * nz + zz], cp)

        def c2(n, zz):
            u = units[n]
            return rc(cut(g[u[0]], slot(zz, 1 - x, c), u), cut(r2[u[0]], zz, u), s2.at[n, zz], q2.at[n, zz], xp)

        def c3(n, t, at):
            u = units[n]
            return rc(cut(g[u[0]], slot(t, x, c), u), cut(rz[u[0]], at, u), s3.at[n, t], q3.at[n, at],
                      {"dp": slot(t, x, c)})

        def gather_x(n):
            u = units[n]
            for zz in order:
                c1(n, zz, 1).wait_recv()
                add(u, slot(zz, x, c), r1, nz + zz)
            for zz in order:
                c2(n, zz).wait_recv()
                add(u, slot(zz, x, c), r2, zz)
                pl.when(z != zz)(c3(n, zz, z).start)

        def first(n):
            for k in range(2):
                for zz in order:
                    c1(n, zz, k).start()

        def second(n):
            for zz in order:
                c1(n, zz, 0).wait_recv()
                add(units[n], slot(zz, 1 - x, c), r1, zz)
                c2(n, zz).start()

        def finish(n):
            u = units[n]
            a, rs, cs = u[0], slice(u[1], u[1] + u[2]), slice(u[3], u[3] + u[4])
            for zz in order:
                @pl.when(z != zz)
                def _(zz=zz):
                    c3(n, z, zz).wait_recv()
                    add(u, me, rz, zz)
            total = place_sum(u, g[a][me, rs, cs])
            at = region(u)
            if u[5] != SEND:
                outs[u[6]][at] = total
            if u[5] != KEEP:
                fs[u[6]][at] = total.astype(fs[u[6]].dtype)
                final(u, 1 - mine, n).start()
        def operands():
            ids = gall_ref[...].reshape(-1, 128).astype(jnp.int32) - mine * (GAMES // 2)
            v = shift_rows(widen(dlog_ref[...]), ids_offset(ids), True)
            for k in range(WIN // 128):
                dlt[k * 128:(k + 1) * 128, :] = jnp.transpose(v[:, k * 128:(k + 1) * 128]).astype(jnp.bfloat16)
            feats = frow_ref[...].astype(jnp.float32)
            for i in range(GAMES // 2):
                rhs[i] = jnp.where(ids == i, feats, 0.0).astype(jnp.bfloat16)

        def terms(ns):
            for n in ns:
                first(n)
            for n in ns:
                second(n)
        for do, what in plan:
            if do == "make":
                what()
            elif do == "head":
                operands()
            else:
                {"start": terms, "x": gather_x, "end": finish}[do](what)
        for n, u in enumerate(units):
            for zz in order:
                c1(n, zz, 0).wait_send()
                c1(n, zz, 1).wait_send()
                c2(n, zz).wait_send()
                pl.when(z != zz)(c3(n, zz, z).wait_send)
            if u[5] != KEEP:
                final(u, 1 - mine, n).wait_send()

    def receive(units, other):
        for n, u in enumerate(units):
            if u[5] != KEEP:
                final(u, other, n).wait_recv()
                outs[u[6]][region(u)] = fr[u[6]][region(u)].astype(jnp.float32)

    rest = [("x", 0), ("x", 1), ("x", 2), ("end", 0), ("x", 3), ("end", 1), ("x", 4), ("end", 2), ("x", 5), ("end", 3),
            ("end", 4), ("end", 5)]

    @pl.when(role == 0)
    def _():
        run(online, 0, [("make", online_first), ("start", (0, 1)), ("make", online_rest), ("start", (2, 3, 4, 5)), ("head", 0)] + rest)
        receive(target, 1)
        for k in range(len(parts)):
            far_d2(1, k).wait_send()

    @pl.when(role == 1)
    def _():
        run(target, 1, [("make", lambda: target_part(0)), ("start", (0,)), ("make", lambda: target_part(1)), ("start", (1,)),
                        ("x", 0), ("make", lambda: target_part(2)), ("start", (2, 3, 4, 5)), ("head", 0)] + rest[1:])
        receive(online, 0)


def sums(saved, games_all, frow, dlog, n, cid):
    nz = n // 4
    V, dma = pltpu.VMEM, pltpu.SemaphoreType.DMA
    f32, b16 = jnp.float32, jnp.bfloat16
    S = jax.ShapeDtypeStruct
    rows = ri, ro, rm = D // n, MID // n, 9 * MID // n
    half = [(ro, D // 2), (rm, MID // 2), (ri, MID // 2), (3, 128)]
    low = [b16, b16, b16, f32]
    sh = [(rm, MID), (3, 128)]
    nu = max(len(u) for u in units_of(*rows))
    vs, hs = pl.BlockSpec(memory_space=pltpu.VMEM), pl.BlockSpec(memory_space=pl.ANY)
    return pl.pallas_call(
        functools.partial(sums_kernel, n, rows),
        out_shape=tuple(S(s, f32) for s in half) + (S((WIN, n * TB), b16), S((GAMES // 2, n * TB, 128), b16)),
        in_specs=[hs] * 8 + [vs] * 6,
        out_specs=(vs,) * 6,
        scratch_shapes=[V(s.shape, s.dtype) for s in saved[:8]] +
        [V((ROWS, MID), b16), V((ROWS, MID), f32), V((1, 4 * MID + 2 * D), f32)] +
        [V((k,) + s, f32) for k in (4 * nz, 2 * nz, nz, nz) for s in sh] + [V(s, t) for s, t in zip(half, low)] * 2 +
        [dma((nu, 2 * nz))] * 2 + [dma((nu, nz))] * 4 + [dma((nu,))] * 2 + [dma((8,)), dma((4,)), dma((4,))],
        compiler_params=pltpu.CompilerParams(collective_id=cid, has_side_effects=True,
                                             vmem_limit_bytes=63 * 1024 * 1024),
        name="gradient_sums",
    )(*saved, games_all, frow, dlog)


UB = 2048
NU = -(-HALF // UB)
LASTU = HALF - (NU - 1) * UB


def segments(k):
    lo, hi = k * UB, min((k + 1) * UB, -(-HALF // 16) * 16)
    parts = []
    for i in range(GAMES // 2):
        a, end = window_of(i), window_of(i + 1)
        mixed = i > 0 and WIDE * i != a
        for r0, r1, games in ((a, a + 16, (i - 1, i)), (a + 16, end, (i,))) if mixed else ((a, end, (i,)),):
            if i == GAMES // 2 - 1 and r1 == end:
                r1 = -(-HALF // 16) * 16
            r0, r1 = max(r0, lo), min(r1, hi)
            if r0 < r1:
                parts.append((r0, r1, games))
    return parts


def update_kernel(dlt, rhs, loss_ref, *refs):
    grads, olds_hbm = refs[:4], refs[4:16]
    hbm = refs[16:19]
    loss_out, news, hbm_out = refs[19], refs[20:36], refs[36:40]
    olds = refs[40:52]
    grow, ibuf, obuf, cbuf, si, so, sw = refs[52:]
    role = lax.axis_index("role")

    def rows_of(k):
        return UB if k < NU - 1 else LASTU

    def fetch(k):
        n = rows_of(k)
        return [pltpu.make_async_copy(hbm[t].at[pl.ds(pl.multiple_of(role * HALF + k * UB, 8), n)],
                                      ibuf.at[k % 3, t, pl.ds(0, n)], si.at[k % 3, t]) for t in range(3)]

    def store(k):
        n = rows_of(k)
        cs = [pltpu.make_async_copy(obuf.at[k % 2, t, pl.ds(0, n)], hbm_out[t].at[pl.ds(k * UB, n)], so.at[k % 2, t])
              for t in range(3)]
        return cs + [pltpu.make_async_copy(cbuf.at[k % 2, pl.ds(0, n)], hbm_out[3].at[pl.ds(k * UB, n)], so.at[k % 2, 3])]

    old_copies = [pltpu.make_async_copy(olds_hbm[i], olds[i], sw.at[i]) for i in range(12)]
    for d in fetch(0) + fetch(1) + old_copies:
        d.start()
    loss_out[...] = loss_ref[0:1, 0:1]

    def small(a, right):
        w, m, v = olds[3 * a:3 * a + 3]
        nw, nm, nv, nc = news[4 * a:4 * a + 4]
        cols = grads[a].shape[1]
        cs = slice(cols if right else 0, (cols if right else 0) + cols)
        gv = grads[a][...]
        rate = learn_rate
        if a == 3:
            gv = jnp.concatenate([gv[k:k + 1, :] for k in range(gv.shape[0])], axis=1)
            cs = slice(0, gv.shape[1])
            rate = gain_rate
        mv = momentum_decay * m[:, cs] + gv
        wv = w[:, cs] - rate * (gv + momentum_decay * mv)
        nw[...] = wv
        nm[...] = gv if a == 0 else mv
        nv[...] = average_decay * v[:, cs] + (1.0 - average_decay) * wv
        nc[...] = wv.astype(jnp.bfloat16)

    for k in range(NU):
        if k + 2 < NU:
            for d in fetch(k + 2):
                d.start()
        lo = k * UB
        for r0, r1, games in segments(k):
            acc = None
            for i in games:
                at = r0 - window_of(i)
                p = jnp.dot(dlt[at:at + r1 - r0, :], rhs[i], preferred_element_type=jnp.float32)
                acc = p if acc is None else acc + p
            grow[r0 - lo:r1 - lo, :] = acc
        for d in fetch(k):
            d.wait()
        if k >= 2:
            for d in store(k - 2):
                d.wait()
        b, s = k % 2, k % 3

        def one(r, carry, b=b, s=s):
            rs = pl.ds(pl.multiple_of(r * 128, 128), 128)
            gv = grow[rs, :]
            m = momentum_decay * ibuf[s, 1, rs, :] + gv
            w = ibuf[s, 0, rs, :] - learn_rate * (gv + momentum_decay * m)
            obuf[b, 0, rs, :] = w
            obuf[b, 1, rs, :] = m
            obuf[b, 2, rs, :] = average_decay * ibuf[s, 2, rs, :] + (1.0 - average_decay) * w
            cbuf[b, rs, :] = w.astype(jnp.bfloat16)
            return carry
        lax.fori_loop(0, UB // 128, one, 0)
        for d in store(k):
            d.start()
        if 4 <= k < 8:
            a = k - 4
            for i in range(3 * a, 3 * a + 3):
                old_copies[i].wait()
            if a == 3:
                small(a, False)
            else:
                pl.when(role == 0)(lambda a=a: small(a, False))
                pl.when(role != 0)(lambda a=a: small(a, True))
    for k in (NU - 2, NU - 1):
        for d in store(k):
            d.wait()


def final_update(dlt, rhs, loss, grads, olds, tables):
    lanes = tables[0].shape[1]
    f32, b16 = jnp.float32, jnp.bfloat16
    S, V, dma = jax.ShapeDtypeStruct, pltpu.VMEM, pltpu.SemaphoreType.DMA
    vs, hs = pl.BlockSpec(memory_space=pltpu.VMEM), pl.BlockSpec(memory_space=pl.ANY)
    new_shapes = []
    for a in range(4):
        s = olds[3 * a].shape if a == 3 else grads[a].shape
        new_shapes += [S(s, f32)] * 3 + [S(s, b16)]
    return pl.pallas_call(
        update_kernel,
        in_specs=[vs] * 7 + [hs] * 15,
        out_specs=[vs] * 17 + [hs] * 4,
        scratch_shapes=[V(o.shape, f32) for o in olds] +
        [V((UB, lanes), f32), V((3, 3, UB, lanes), f32),
         V((2, 3, UB, lanes), f32), V((2, UB, lanes), b16), dma((3, 3)), dma((2, 4)), dma((12,))],
        out_shape=[S((1, 1), f32)] + new_shapes + [S((HALF, lanes), f32)] * 3 + [S((HALF, lanes), b16)],
        compiler_params=pltpu.CompilerParams(vmem_limit_bytes=63 * 1024 * 1024),
        name="final_update",
    )(dlt, rhs, loss, *grads, *olds, *tables)


def fast_device(
    frames,
    game_ids,
    taken_actions,
    next_actions,
    expert_flags,
    rewards,
    done_flags,
    weight_in,
    weight_mid,
    weight_out,
    norm_gains,
    head_table,
    moment_in,
    moment_mid,
    moment_out,
    moment_gains,
    moment_head,
    average_in,
    average_mid,
    average_out,
    average_gains,
    average_head,
):
    n = lax.axis_size("dp")
    *saved, all_ids, feat_rows, dlog, loss = block_step(
        jnp.transpose(frames[0], (1, 0, 2)),
        (weight_in[0], weight_mid[0], weight_out[0], norm_gains),
        (average_in[0], average_mid[0], average_out[0], average_gains),
        (taken_actions, next_actions, expert_flags, rewards, done_flags, game_ids),
        head_table.T,
        average_head.T,
        n,
        1,
    )
    grad_out, grad_mid, grad_in, grad_gains, dlt, rhs = sums(saved, all_ids, feat_rows, dlog, n, 2)
    loss, *rest = final_update(
        dlt,
        rhs,
        loss,
        (grad_in, grad_mid, grad_out, grad_gains),
        (
            weight_in[0],
            moment_in[0],
            average_in[0],
            weight_mid[0],
            moment_mid[0],
            average_mid[0],
            weight_out[0],
            moment_out[0],
            average_out[0],
            norm_gains,
            moment_gains,
            average_gains,
        ),
        (head_table.T, moment_head.T, average_head.T),
    )
    return (
        loss.reshape(()),
        *(v[None] for v in rest[:12]),
        *rest[12:16],
        *(v.T for v in rest[16:]),
    )


def solution(mesh):
    return jax.shard_map(
        fast_device if mesh.shape["dp"] == 16 else on_device,
        mesh=mesh,
        in_specs=(
            P("role", "dp", None, None),
            P("dp"),
            P("dp"),
            P("dp"),
            P("dp"),
            P("dp"),
            P("dp"),
            P(None, "dp", None),
            P(None, "dp", None),
            P(None, "dp", None),
            P(None, "dp"),
            P("dp", None),
            P(None, "dp", None),
            P(None, "dp", None),
            P(None, "dp", None),
            P(None, "dp"),
            P("dp", None),
            P(None, "dp", None),
            P(None, "dp", None),
            P(None, "dp", None),
            P(None, "dp"),
            P("dp", None),
        ),
        out_specs=(
            P(),
            P(None, "dp", "role"),
            P(None, "dp", "role"),
            P(None, "dp", "role"),
            P(None, "dp", "role"),
            P(None, "dp", "role"),
            P(None, "dp", "role"),
            P(None, "dp", "role"),
            P(None, "dp", "role"),
            P(None, "dp", "role"),
            P(None, "dp", "role"),
            P(None, "dp", "role"),
            P(None, "dp", "role"),
            P(None, "dp"),
            P(None, "dp"),
            P(None, "dp"),
            P(None, "dp"),
            P("dp", "role"),
            P("dp", "role"),
            P("dp", "role"),
            P("dp", "role"),
        ),
        check_vma=False,
    )
```

```python
import functools

import jax
import jax.numpy as jnp
import numpy as np
from jax import lax
from jax.experimental import pallas as pl
from jax.experimental.pallas import tpu as pltpu
from jax.sharding import PartitionSpec as P

D = 2048
MID = 512
GAMES = 40
ACTIONS = 18
ATOMS = 51
GROUPS = 32
SIDE = 11
LAYERS = 1


support_low = -10.0
support_high = 10.0
discount = 0.99
penalty = 0.05
momentum_decay = 0.5
average_decay = 0.5
learn_rate = 4.0
gain_rate = 40.0
epsilon = 1e-05
HIGHEST = lax.Precision.HIGHEST


def passed_along(block, axis, distance):
    devices = range(lax.axis_size(axis))
    route = [(i - distance, i) for i in devices if i - distance in devices]
    return lax.ppermute(block, axis, route)


def split_gains(gains):
    return (
        gains[:MID],
        gains[MID : 2 * MID],
        gains[2 * MID : 3 * MID],
        gains[3 * MID : 4 * MID],
        gains[4 * MID : 4 * MID + D],
        gains[4 * MID + D :],
    )


def group_norm(values, gain, shift):
    rows, pixels, width = values.shape
    grouped = values.reshape(rows, pixels, GROUPS, width // GROUPS)
    center = grouped - jnp.mean(grouped, axis=(1, 3), keepdims=True)
    spread = jnp.mean(center * center, axis=(1, 3), keepdims=True)
    normed = (center * lax.rsqrt(spread + epsilon)).reshape(values.shape)
    return normed * gain + shift


def patches_of(acts):
    rows, pixels, width = acts.shape
    grid = acts.reshape(rows, SIDE, SIDE, width)
    padded = jnp.pad(grid, ((0, 0), (1, 1), (1, 1), (0, 0)))
    pieces = [
        padded[:, down : down + SIDE, right : right + SIDE, :]
        for down in range(3)
        for right in range(3)
    ]
    return jnp.concatenate(pieces, axis=-1).reshape(rows, pixels, 9 * width)


def transition_loss(logits, target_dist, action_hot, expert, support):
    log_prob = jax.nn.log_softmax(logits, axis=-1)
    values = jnp.sum(jnp.exp(log_prob) * support, axis=-1)
    spread_sum = jax.nn.logsumexp(values, axis=-1)
    chosen_log = jnp.sum(log_prob * action_hot[:, :, None], axis=1)
    cross = -jnp.sum(target_dist * chosen_log, axis=-1)
    regular = spread_sum - jnp.sum(values * action_hot, axis=-1)
    return cross + penalty * expert * regular


def project_target(next_prob, rewards, done_f, support):
    moved = jnp.clip(
        rewards[:, None] + discount * (1.0 - done_f)[:, None] * support[None, :],
        support_low,
        support_high,
    )
    spacing = (support_high - support_low) / (ATOMS - 1)
    weight = jnp.maximum(0.0, 1.0 - jnp.abs(moved[:, :, None] - support[None, None, :]) / spacing)
    return jnp.sum(next_prob[:, :, None] * weight, axis=1)


def renew(weight, grad, moment, average, rate):
    new_moment = momentum_decay * moment + grad
    new_weight = weight - rate * (grad + momentum_decay * new_moment)
    new_average = average_decay * average + (1.0 - average_decay) * new_weight
    return (new_weight, new_moment, new_average, new_weight.astype(jnp.bfloat16))


def lower_half(values):
    return values[..., : values.shape[-1] // 2]


def upper_half(values):
    return values[..., values.shape[-1] // 2 :]


def own_half(values, role_index):
    half = values.shape[-1] // 2
    return lax.dynamic_slice_in_dim(values, role_index * half, half, values.ndim - 1)


def norm_act(hidden, gain, shift):
    return jax.nn.gelu(group_norm(hidden, gain, shift))


def outer_act(hidden, gain, shift, stream):
    return jax.nn.gelu(stream + group_norm(hidden, gain, shift))


def block_forward(stream, weights):
    w_in, w_mid, w_out, gains = weights
    gain_one, shift_one, gain_two, shift_two, gain_three, shift_three = split_gains(gains)
    stream_low = stream.astype(jnp.bfloat16)
    hidden_in = jnp.einsum("bpc,cm->bpm", stream_low, w_in, preferred_element_type=jnp.float32)
    act_in = norm_act(hidden_in, gain_one, shift_one).astype(jnp.bfloat16)
    hidden_mid = jnp.einsum(
        "bpc,cm->bpm", patches_of(act_in), w_mid, preferred_element_type=jnp.float32
    )
    act_mid = norm_act(hidden_mid, gain_two, shift_two).astype(jnp.bfloat16)
    hidden_out = jnp.einsum("bpc,cm->bpm", act_mid, w_out, preferred_element_type=jnp.float32)
    result = outer_act(hidden_out, gain_three, shift_three, stream)
    return (result, (stream, stream_low, hidden_in, act_in, hidden_mid, act_mid, hidden_out))


def block_backward(grad_result, weights, kept, settle):
    w_in, w_mid, w_out, gains = weights
    stream, stream_low, hidden_in, act_in, hidden_mid, act_mid, hidden_out = kept
    gain_one, shift_one, gain_two, shift_two, gain_three, shift_three = split_gains(gains)
    _, back_three = jax.vjp(outer_act, hidden_out, gain_three, shift_three, stream)
    d_three, dg_three, db_three, d_resid = back_three(grad_result)
    d_three = d_three.astype(jnp.bfloat16)
    grad_out = settle(
        jnp.einsum("bpm,bpc->mc", act_mid, d_three, preferred_element_type=jnp.float32)
    )
    d_act_mid = jnp.einsum("bpc,mc->bpm", d_three, w_out, preferred_element_type=jnp.float32)
    _, back_two = jax.vjp(norm_act, hidden_mid, gain_two, shift_two)
    d_two, dg_two, db_two = back_two(d_act_mid)
    d_two = d_two.astype(jnp.bfloat16)
    grad_mid = settle(
        jnp.einsum("bpk,bpm->km", patches_of(act_in), d_two, preferred_element_type=jnp.float32)
    )
    d_cols = jnp.einsum("bpm,km->bpk", d_two, w_mid, preferred_element_type=jnp.float32)
    _, back_cols = jax.vjp(patches_of, act_in.astype(jnp.float32))
    (d_act_in,) = back_cols(d_cols)
    _, back_one = jax.vjp(norm_act, hidden_in, gain_one, shift_one)
    d_one, dg_one, db_one = back_one(d_act_in)
    d_one = d_one.astype(jnp.bfloat16)
    grad_in = jnp.einsum("bpc,bpm->cm", stream_low, d_one, preferred_element_type=jnp.float32)
    d_stream = d_resid + jnp.einsum("bpm,cm->bpc", d_one, w_in, preferred_element_type=jnp.float32)
    grad_gains = jnp.concatenate([dg_one, db_one, dg_two, db_two, dg_three, db_three])
    grad_in, grad_gains = settle((grad_in, grad_gains))
    return (d_stream, (grad_in, grad_mid, grad_out, grad_gains))


def on_device(
    frames,
    game_ids,
    taken_actions,
    next_actions,
    expert_flags,
    rewards,
    done_flags,
    weight_in,
    weight_mid,
    weight_out,
    norm_gains,
    head_table,
    moment_in,
    moment_mid,
    moment_out,
    moment_gains,
    moment_head,
    average_in,
    average_mid,
    average_out,
    average_gains,
    average_head,
):
    role_index = lax.axis_index("role")
    online = role_index == 0
    use_in = jnp.where(online, weight_in, average_in).astype(jnp.bfloat16)
    use_mid = jnp.where(online, weight_mid, average_mid).astype(jnp.bfloat16)
    use_out = jnp.where(online, weight_out, average_out).astype(jnp.bfloat16)
    use_gains = jnp.where(online, norm_gains, average_gains).astype(jnp.bfloat16)
    use_head = jnp.where(online, head_table, average_head).astype(jnp.bfloat16)
    support = support_low + (support_high - support_low) * jnp.arange(ATOMS, dtype=jnp.float32) / (
        ATOMS - 1
    )
    own_hot = (game_ids[:, None] == lax.broadcasted_iota(jnp.int32, (1, GAMES), 1)).astype(
        jnp.float32
    )
    counts = jnp.sum(own_hot, axis=0)
    stream = frames[0].astype(jnp.float32)
    layer = 0
    pieces = (
        lax.all_gather(use_in[layer], "dp", axis=0, tiled=True),
        lax.all_gather(use_mid[layer], "dp", axis=0, tiled=True),
        lax.all_gather(use_out[layer], "dp", axis=0, tiled=True),
        lax.all_gather(use_gains[layer], "dp", axis=0, tiled=True),
    )
    weights = (pieces[0], pieces[1], pieces[2], pieces[3].astype(jnp.float32))
    stream, saved = block_forward(stream, weights)
    gathered = [weights]
    kept = [saved]
    trans = stream.shape[0]
    pixels = stream.shape[1]
    wide_k = ACTIONS * ATOMS
    head_rows = head_table.shape[0]
    feat_low = jnp.mean(stream, axis=1).astype(jnp.bfloat16)
    feat_all, game_all = (
        lax.all_gather(feat_low, "dp", axis=0, tiled=True),
        lax.all_gather(game_ids.astype(jnp.bfloat16)[:, None], "dp", axis=0, tiled=True),
    )
    game_iota = lax.broadcasted_iota(jnp.int32, (1, GAMES), 1).astype(jnp.float32)
    all_hot = (game_all.astype(jnp.float32) == game_iota).astype(jnp.bfloat16)
    feat_rows = lax.dynamic_slice_in_dim(feat_all, lax.axis_index("dp") * head_rows, head_rows, 1)
    head_low = use_head.reshape(head_rows * GAMES, wide_k)

    def widen(count):
        spread_rows = (feat_rows[:, :, None] * all_hot[:, None, :]).reshape(
            count, head_rows * GAMES
        )
        return (spread_rows, all_hot)

    spread_rows, hot_piece = widen(trans * lax.axis_size("dp"))
    flat_logits = lax.psum_scatter(
        jnp.dot(spread_rows, head_low, preferred_element_type=jnp.float32),
        "dp",
        scatter_dimension=0,
        tiled=True,
    )
    logits = flat_logits.reshape(trans, ACTIONS, ATOMS)
    next_hot = (next_actions[:, None] == lax.broadcasted_iota(jnp.int32, (1, ACTIONS), 1)).astype(
        jnp.float32
    )
    next_prob = jax.nn.softmax(jnp.sum(logits * next_hot[:, :, None], axis=1), axis=-1)
    projected = project_target(next_prob, rewards, done_flags.astype(jnp.float32), support)
    target_dist = passed_along(projected, "role", -1)
    action_hot = (
        taken_actions[:, None] == lax.broadcasted_iota(jnp.int32, (1, ACTIONS), 1)
    ).astype(jnp.float32)
    expert = expert_flags.astype(jnp.float32)

    def local_loss(values):
        return transition_loss(values, target_dist, action_hot, expert, support)

    row_loss, loss_back = jax.vjp(local_loss, logits)
    sums = jnp.dot(row_loss, own_hot, precision=HIGHEST)
    total_counts, total_sums = lax.psum((counts, sums), "dp")
    floor_counts = jnp.maximum(total_counts, 1.0)
    loss_total = jnp.sum(total_sums / floor_counts)
    row_weight = jnp.dot(own_hot, 1.0 / (GAMES * floor_counts), precision=HIGHEST)
    (d_logits,) = loss_back(row_weight)
    d_low = d_logits.reshape(trans, wide_k).astype(jnp.bfloat16)
    piece = lax.all_gather(d_low, "dp", axis=0, tiled=True)
    count = piece.shape[0]
    spread_rows, hot_piece = widen(count)
    grad_head = lax.dot_general(
        spread_rows, piece, (((0,), (0,)), ((), ())), preferred_element_type=jnp.float32
    )
    back_wide = jnp.dot(piece, head_low.T, preferred_element_type=jnp.float32)
    back_rows = jnp.sum(
        back_wide.reshape(count, head_rows, GAMES) * hot_piece[:, None, :].astype(jnp.float32),
        axis=2,
    )
    grad_rows = back_rows
    grad_head, grad_rows = (grad_head, grad_rows)
    feat_grad = lax.all_to_all(
        grad_rows.astype(jnp.bfloat16), "dp", split_axis=0, concat_axis=1, tiled=True
    ).astype(grad_rows.dtype)
    d_stream = jnp.broadcast_to(feat_grad[:, None, :] / pixels, stream.shape)

    def settle(values):
        return values

    layer_grads = [None] * LAYERS
    for layer in reversed(range(LAYERS)):
        d_stream, block_grad = block_backward(d_stream, gathered[layer], kept[layer], settle)
        layer_grads[layer] = block_grad
    stacked = tuple((jnp.stack([layer_grads[0][kind]]) for kind in range(4)))
    reduced = lax.psum_scatter(stacked, "dp", scatter_dimension=1, tiled=True)
    head_grad = grad_head.reshape(head_rows, GAMES * wide_k)
    sent = (
        passed_along(upper_half(reduced[0]).astype(jnp.bfloat16), "role", 1).astype(jnp.float32),
        passed_along(upper_half(reduced[1]).astype(jnp.bfloat16), "role", 1).astype(jnp.float32),
        passed_along(upper_half(reduced[2]).astype(jnp.bfloat16), "role", 1).astype(jnp.float32),
        passed_along(reduced[3].astype(jnp.bfloat16), "role", 1).astype(jnp.float32),
        passed_along(upper_half(head_grad).astype(jnp.bfloat16), "role", 1).astype(jnp.float32),
        passed_along(loss_total.astype(jnp.bfloat16), "role", 1).astype(loss_total.dtype),
    )
    grad_in = jnp.where(online, lower_half(reduced[0]), sent[0])
    grad_mid = jnp.where(online, lower_half(reduced[1]), sent[1])
    grad_out = jnp.where(online, lower_half(reduced[2]), sent[2])
    grad_gains = jnp.where(online, reduced[3], sent[3])
    grad_table = jnp.where(online, lower_half(head_grad), sent[4])
    loss_out = jnp.where(online, loss_total, sent[5])
    in_w, in_m, in_a, in_c = renew(
        own_half(weight_in, role_index),
        grad_in,
        own_half(moment_in, role_index),
        own_half(average_in, role_index),
        learn_rate,
    )
    mid_w, mid_m, mid_a, mid_c = renew(
        own_half(weight_mid, role_index),
        grad_mid,
        own_half(moment_mid, role_index),
        own_half(average_mid, role_index),
        learn_rate,
    )
    out_w, out_m, out_a, out_c = renew(
        own_half(weight_out, role_index),
        grad_out,
        own_half(moment_out, role_index),
        own_half(average_out, role_index),
        learn_rate,
    )
    gain_w, gain_m, gain_a, gain_c = renew(
        norm_gains, grad_gains, moment_gains, average_gains, gain_rate
    )
    head_w, head_m, head_a, head_c = renew(
        own_half(head_table, role_index),
        grad_table,
        own_half(moment_head, role_index),
        own_half(average_head, role_index),
        learn_rate,
    )
    return (
        loss_out,
        in_w,
        grad_in,
        in_a,
        in_c,
        mid_w,
        mid_m,
        mid_a,
        mid_c,
        out_w,
        out_m,
        out_a,
        out_c,
        gain_w,
        gain_m,
        gain_a,
        gain_c,
        head_w,
        head_m,
        head_a,
        head_c,
    )


MESH = pl.DeviceIdType.MESH


def any_spec():
    return pl.BlockSpec(memory_space=pl.ANY)


def greet(peers):
    barrier = pltpu.get_barrier_semaphore()
    for cond, dev in peers:
        def go(dev=dev):
            pl.semaphore_signal(barrier, inc=1, device_id=dev, device_id_type=MESH)
        go() if cond is None else pl.when(cond)(go)
    count = sum(1 for cond, _ in peers if cond is None)
    for cond, _ in peers:
        if cond is not None:
            count = count + cond.astype(jnp.int32)
    pl.semaphore_wait(barrier, count)


def place():
    me = lax.axis_index("dp")
    core = lax.rem(me, 2)
    x = lax.rem(me // 2, 2)
    z = me // 4
    return me, z, x, core


D = 2048
MID = 512
GROUPS = 32
SIDE = 11
PIX = 121
TB = 8
PITCH = 12
RB = PITCH * TB
VR = SIDE * TB
ROWS = SIDE * RB
PAD = 16 * TB
EROWS = 164 * TB
BLK = 352
CH = 512
epsilon = 1e-05
GK = 0.7978845608028654
GC = 0.044715
OFFS = [(i - 1) * PITCH + (j - 1) for i in range(3) for j in range(3)]


def group_sum(v, gs):
    width = v.shape[1]
    n = width // 128
    a = lax.broadcasted_iota(jnp.int32, (128, 128), 0) // gs
    b = lax.broadcasted_iota(jnp.int32, (128, 128), 1) // gs
    m = (a == b).astype(jnp.float32)
    st = jnp.concatenate([v[:, k * 128:(k + 1) * 128] for k in range(n)], axis=0)
    r = jnp.dot(st, m, precision=lax.Precision.HIGHEST, preferred_element_type=jnp.float32)
    return jnp.concatenate([r[k * 8:(k + 1) * 8] for k in range(n)], axis=1)


def fold(v):
    rows, w = v.shape
    return jnp.sum(v.reshape(rows // TB, TB, w), axis=0)


def moments(h_ref, lo, gs):
    def one(r, acc):
        return acc + fold(h_ref[pl.ds(pl.multiple_of(r * RB, RB), VR), lo:lo + CH])
    s = lax.fori_loop(0, SIDE, one, jnp.zeros((TB, CH), jnp.float32))
    mean = group_sum(s, gs) / float(PIX * gs)

    def two(r, acc):
        h = h_ref[pl.ds(pl.multiple_of(r * RB, RB), VR), lo:lo + CH].reshape(SIDE, TB, CH) - mean[None]
        return acc + jnp.sum(h * h, axis=0)
    q = lax.fori_loop(0, SIDE, two, jnp.zeros((TB, CH), jnp.float32))
    var = group_sum(q, gs) / float(PIX * gs)
    return mean, lax.rsqrt(var + epsilon)


def gelu(u):
    return 0.5 * u * (1.0 + jnp.tanh(GK * (u + GC * (u * u * u))))


def dgelu(u):
    uu = u * u
    t = jnp.tanh(GK * u * (1.0 + GC * uu))
    return 0.5 * (1.0 + t) + 0.5 * u * (1.0 - t * t) * (GK + (3.0 * GK * GC) * uu)


def shifted(e_ref, o_ref, s, row, n):
    ref, base = (e_ref, 16 + s) if s % 2 == 0 else (o_ref, 17 + s)
    return ref[pl.ds(pl.multiple_of(row + base * TB, 16), n), :]


def put_shifted(e_ref, o_ref, r, v):
    z = jnp.zeros((TB, v.shape[1]), jnp.float32)
    at = pl.ds(pl.multiple_of(PAD + r * RB, 16), RB)
    e_ref[at, :] = jnp.concatenate([v, z], axis=0).astype(jnp.bfloat16)
    o_ref[at, :] = jnp.concatenate([z, v], axis=0).astype(jnp.bfloat16)


def clear_margins(e_ref, o_ref):
    z = jnp.zeros((PAD, MID), jnp.bfloat16)
    for ref in (e_ref, o_ref):
        ref[0:PAD, :] = z
        ref[PAD + ROWS:EROWS, :] = z


def row_at(r):
    return pl.ds(pl.multiple_of(r * RB, RB), VR)


def rows_full(r):
    return pl.ds(pl.multiple_of(r * RB, RB), RB)


def norm_back(h_ref, lo, dy_ref, mean, rstd, gain, gs, s1, s2, emit):
    n = 1.0 / float(PIX * gs)
    m1 = group_sum(gain * s1, gs) * n
    m2 = group_sum(gain * s2, gs) * n
    ca = rstd * gain
    cc = -rstd * rstd * m2
    cb = -rstd * m1 - mean * cc

    def one(r, c):
        h = h_ref[row_at(r), lo:lo + CH].reshape(SIDE, TB, CH)
        dy = dy_ref[row_at(r), :].reshape(SIDE, TB, CH)
        emit(r, (ca[None] * dy + cc[None] * h + cb[None]).reshape(VR, CH))
        return c
    lax.fori_loop(0, SIDE, one, 0)


D = 2048
GAMES = 40
ACTIONS = 18
ATOMS = 51
WIDE = ACTIONS * ATOMS
LW = 1024
WIN = 1024
COLS = GAMES * WIDE
HALF = COLS // 2
PADC = 36864
TB = 8
support_low = -10.0
support_high = 10.0
discount = 0.99
penalty = 0.05


def window_of(g):
    return (WIDE * g) // 16 * 16


def ids_offset(ids):
    return lax.bitwise_and(WIDE * ids, 15)


def shift_rows(v, off, right):
    width = v.shape[1]
    for b in range(1, 4):
        n = 1 << b
        bit = lax.bitwise_and(off, n) != 0
        bit = jnp.concatenate([bit.astype(jnp.float32)] * (width // 128), axis=1) > 0.5
        v = jnp.where(bit, pltpu.roll(v, n if right else width - n, 1), v)
    return v


def widen(dl):
    n = dl.shape[0]
    v = dl.astype(jnp.float32)
    v = jnp.concatenate([v[:, 0:TB], v[:, TB:2 * TB]], axis=2).reshape(n * TB, LW)
    lanes = lax.broadcasted_iota(jnp.int32, (n * TB, 128), 1)
    last = jnp.where(lanes < WIDE - LW + 128, v[:, LW - 128:], 0.0)
    return jnp.concatenate([v[:, :LW - 128], last], axis=1)


W_IN, W_MID, W_OUT, MISC = 0, 1, 2, 3
HC = 2048
NHC = -(-COLS // HC)
T0 = (((0,), (0,)), ((), ()))
T1 = (((1,), (1,)), ((), ()))


def rc(src, dst, ss, rs, dev):
    return pltpu.make_async_remote_copy(src_ref=src, dst_ref=dst, send_sem=ss, recv_sem=rs, device_id=dev,
                                        device_id_type=MESH)


def when(cond, do):
    if cond is None:
        do()
    else:
        pl.when(cond)(do)


class Gather:
    def __init__(self, nz, own, full, rows, own_sem, send, recv):
        self.nz, self.own_refs, self.full, self.rows = nz, own, full, rows
        self.own_sem, self.send, self.recv = own_sem, send, recv
        self.me, self.z, self.x, self.c = place()
        me, x, c = self.me, self.x, self.c
        self.up, self.down = {"dp": me + 4}, {"dp": me - 4}
        self.xp, self.cp = {"dp": me + 2 - 4 * x}, {"dp": me + 1 - 2 * c}
        self.has_up, self.has_down = self.z < nz - 1, self.z > 0
        self.started = []

    def slot(self, a, i):
        n = self.rows[a]
        return self.full[a].at[i] if n is None else self.full[a].at[pl.ds(pl.multiple_of(i * n, 16), n)]

    def put(self, cond, a, src, i, dev, k):
        d = rc(src, self.slot(a, i), self.send.at[a, k], self.recv.at[a, i], dev)
        when(cond, d.start)
        self.started.append((cond, d))

    def take(self, cond, a, i):
        d = rc(self.slot(a, i), self.slot(a, i), self.send.at[a, 0], self.recv.at[a, i], self.cp)
        when(cond, d.wait_recv)

    def begin(self, a):
        src = self.own_refs[a]
        self.put(self.has_up, a, src, self.me, self.up, 0)
        self.put(self.has_down, a, src, self.me, self.down, 1)
        self.put(None, a, src, self.me, self.xp, 2)
        self.put(None, a, src, self.me, self.cp, 3)
        pltpu.make_async_copy(src, self.slot(a, self.me), self.own_sem.at[a]).start()

    def along_z(self, a, d):
        k = 4 + (d - 1) * 6
        for up in (True, False):
            s = self.me - 4 * d if up else self.me + 4 * d
            ok = self.z - d >= 0 if up else self.z + d < self.nz
            more = jnp.logical_and(ok, self.has_up if up else self.has_down)
            m = k if up else k + 3
            self.take(ok, a, s)
            self.put(more, a, self.slot(a, s), s, self.up if up else self.down, m)
            self.put(ok, a, self.slot(a, s), s, self.xp, m + 1)
            self.put(ok, a, self.slot(a, s), s, self.cp, m + 2)

    def at_distance(self, d):
        for up in ((True,) if d == 0 else (False, True)):
            zz = self.z + d if up else self.z - d
            yield zz, (None if d == 0 else zz < self.nz if up else zz >= 0), up

    def along_x(self, a, d):
        k = 4 + (self.nz - 1) * 6
        for zz, ok, up in self.at_distance(d):
            s = zz * 4 + (1 - self.x) * 2 + self.c
            self.take(ok, a, s)
            self.put(ok, a, self.slot(a, s), s, self.cp, k + 2 * d + (1 if up else 0))

    def arrived(self, a):
        for d in range(self.nz):
            for zz, ok, _ in self.at_distance(d):
                for xx in (self.x, 1 - self.x):
                    self.take(ok, a, zz * 4 + xx * 2 + 1 - self.c)
        pltpu.make_async_copy(self.own_refs[a], self.slot(a, self.me), self.own_sem.at[a]).wait()

    def end(self):
        for cond, d in self.started:
            when(cond, d.wait_send)


def put_gain(gg_ref, at, s):
    gg_ref[:, at:at + CH] = jnp.sum(s, axis=0, keepdims=True)


def through(h_ref, d2_ref, st_ref, g_ref, gg_ref, at, goff, boff, emit):
    z8 = jnp.zeros((TB, CH), jnp.float32)
    mean = st_ref[0:8, at:at + MID]
    rstd = st_ref[8:16, at:at + MID]
    gain = g_ref[:, goff:goff + MID]
    shift = g_ref[:, boff:boff + MID]
    mr = mean * rstd

    def one(r, acc):
        s1, s2 = acc
        h = h_ref[row_at(r), :].reshape(SIDE, TB, MID)
        da = d2_ref[row_at(r), :].reshape(SIDE, TB, MID)
        xh = h * rstd[None] - mr[None]
        dy = da * dgelu(xh * gain + shift)
        d2_ref[row_at(r), :] = dy.reshape(VR, MID)
        return s1 + jnp.sum(dy, axis=0), s2 + jnp.sum(dy * xh, axis=0)
    s1, s2 = lax.fori_loop(0, SIDE, one, (z8, z8))
    put_gain(gg_ref, goff, s2)
    put_gain(gg_ref, boff, s1)
    norm_back(h_ref, 0, d2_ref, mean, rstd, gain, MID // GROUPS, s1, s2, emit)


def step_kernel(n, fr_hbm, wi, wm, wo, wg, ai, am, ao, ag, k0, k1, k2, k3, k4, k5, ht_hbm, ha_hbm,
                x_hbm, h1_hbm, a2_hbm, dh3_hbm, e_hbm, o_hbm, wmid_hbm, fart_hbm,
                st_ref, g_ref, gg_ref, gall_ref, frow_ref, dlog_ref, loss_ref,
                scal_ref, own_in, own_mid, own_out, own_misc, win_ref, wmid_ref, wout_ref, misc_ref,
                x_ref, h1_ref, h2_ref, h3_ref, a2_ref, dfeat_ref, sl_ref, e_ref, o_ref,
                d2_ref, dh3_ref, far_ref, fart_ref, fbuf, hbuf, head_ref,
                fsend, frecv, part, r1, r2, tgt_s, tgt_r, down_s, dsend, drecv,
                own_sem, g_send, g_recv, f_sem, h_sem, k_sem, ss, rs_,
                s_f, q_f, s_1, q_1, s_2, q_2, s_t, q_t, s_l, q_l, s_c, q_c, s_d, q_d, s_r, q_r):
    me, z, x, c = place()
    role = lax.axis_index("role")
    half = n // 2
    peers = [lax.rem(me + k, n) for k in range(1, n)]
    cp = me + 1 - 2 * c
    du_ref = d2_ref

    def pick(w, a, dst):
        def fill(src):
            dst[...] = src[...].astype(jnp.bfloat16)
        pl.when(role == 0)(lambda: fill(w))
        pl.when(role != 0)(lambda: fill(a))

    def fetch_frames(r):
        return pltpu.make_async_copy(fr_hbm.at[pl.ds(r * SIDE, SIDE)], fbuf.at[r % 2], f_sem.at[r % 2])

    def fetch_head(k, go):
        m = HC if k < NHC - 1 else COLS - (NHC - 1) * HC

        def one(src):
            d = pltpu.make_async_copy(src.at[pl.ds(k * HC, m)], hbuf.at[k % 2, pl.ds(0, m)], h_sem.at[k % 2])
            d.start() if go else d.wait()
        if go:
            pl.when(role == 0)(lambda: one(ht_hbm))
            pl.when(role != 0)(lambda: one(ha_hbm))
        else:
            one(ht_hbm)
    fetch_frames(0).start()
    fetch_head(0, True)
    pick(wi, ai, own_in)
    pick(wm, am, own_mid)
    pick(wo, ao, own_out)

    def pick_gains(src):
        v = src[...].astype(jnp.bfloat16).astype(jnp.float32)
        for k in range(3):
            own_misc[k:k + 1, :] = v[:, k * 128:(k + 1) * 128]
    own_misc[0:TB, :] = jnp.zeros((TB, 128), jnp.float32)
    pl.when(role == 0)(lambda: pick_gains(wg))
    pl.when(role != 0)(lambda: pick_gains(ag))
    for k, ref in enumerate((k0, k1, k2, k3, k4, k5)):
        for t in range(TB):
            scal_ref[k, t:t + 1, :] = jnp.full((1, 128), ref[t].astype(jnp.float32), jnp.float32)
    own_misc[TB:2 * TB, :] = scal_ref[5]
    greet([(None, {"dp": p}) for p in peers] + [(None, {"role": 1 - role})])

    gath = Gather(n // 4, (own_in, own_mid, own_out, own_misc), (win_ref, wmid_ref, wout_ref, misc_ref),
               (D // n, 9 * MID // n, MID // n, None), own_sem, g_send, g_recv)
    casts = iter(range(NHC))

    def cast_head(times):
        for _ in range(times):
            k = next(casts, None)
            if k is None:
                return
            if k + 1 < NHC:
                fetch_head(k + 1, True)
            fetch_head(k, False)
            m = HC if k < NHC - 1 else COLS - (NHC - 1) * HC
            u = 128 if m % 128 == 0 else 112

            def one(i, carry, k=k, u=u):
                rs = pl.ds(pl.multiple_of(i * u, 16), u)
                head_ref[pl.ds(pl.multiple_of(k * HC + i * u, 16), u), :] = hbuf[k % 2, rs, :].astype(jnp.bfloat16)
                return carry
            lax.fori_loop(0, m // u, one, 0)

    for a in (MISC, W_IN, W_MID):
        gath.begin(a)
    for r in range(SIDE):
        if r + 1 < SIDE:
            fetch_frames(r + 1).start()
        fetch_frames(r).wait()
        v = fbuf[r % 2].astype(jnp.float32).reshape(VR, D)
        x_ref[r * RB:(r + 1) * RB, :] = jnp.concatenate([v, jnp.zeros((TB, D), jnp.float32)], axis=0).astype(jnp.bfloat16)
    clear_margins(e_ref, o_ref)
    head_ref[COLS:PADC, :] = jnp.zeros((PADC - COLS, 128), jnp.bfloat16)
    far = n // 4 - 1
    kept = [pltpu.make_async_copy(src, dst, k_sem.at[k]) for k, (src, dst) in enumerate((
        (x_ref, x_hbm), (h1_ref, h1_hbm), (a2_ref, a2_hbm), (dh3_ref, dh3_hbm), (e_ref, e_hbm), (o_ref, o_hbm),
        (wmid_ref, wmid_hbm)))]

    def keep(k):
        pl.when(role == 0)(kept[k].start)
    keep(0)

    def z_step(a, d):
        if d <= far:
            gath.along_z(a, d)

    def x_step(a, d):
        if d <= far:
            gath.along_x(a, d)
    for d in range(1, far + 1):
        z_step(W_IN, d)
        z_step(MISC, d)
        cast_head(2)
        x_step(W_IN, d - 1)
        x_step(MISC, d - 1)
        z_step(W_MID, d)
        cast_head(2)
        if d == max(far - 1, 1):
            gath.begin(W_OUT)
    x_step(W_IN, far)
    x_step(MISC, far)
    x_step(W_MID, 0)
    x_step(W_MID, 1)
    cast_head(1)
    z_step(W_OUT, 1)
    gath.arrived(MISC)
    gath.arrived(W_IN)
    for i in range(n):
        gall_ref[i] = misc_ref[i, TB:2 * TB, :]
        for k in range(3):
            at = (i * 3 + k) * 128
            g_ref[:, at:at + 128] = misc_ref[i, k:k + 1, :]

    def mm1(i, carry):
        rs = pl.ds(pl.multiple_of(i * BLK, BLK), BLK)
        h1_ref[rs, :] = jnp.dot(x_ref[rs, :], win_ref[...], preferred_element_type=jnp.float32)
        return carry
    lax.fori_loop(0, ROWS // BLK, mm1, 0)
    z_step(W_OUT, 2)
    x_step(W_MID, 2)
    keep(1)
    mean, rstd = moments(h1_ref, 0, MID // GROUPS)
    st_ref[0:8, 0:MID] = mean
    st_ref[8:16, 0:MID] = rstd
    sc = rstd * g_ref[:, 0:MID]
    sh = g_ref[:, MID:2 * MID] - mean * sc

    def act1(r, carry):
        h = h1_ref[row_at(r), :].reshape(SIDE, TB, MID)
        a = gelu(h * sc[None] + sh[None]).reshape(VR, MID)
        put_shifted(e_ref, o_ref, r, a)
        return carry
    lax.fori_loop(0, SIDE, act1, 0)
    inner = pl.ds(PAD, ROWS)

    def far_a1(to):
        return rc(e_ref.at[inner], far_ref, ss.at[0], rs_.at[0], {"role": to})

    pl.when(role == 0)(lambda: far_a1(1).start())
    cast_head(NHC)
    z_step(W_OUT, 3)
    for d in range(3, far + 1):
        x_step(W_MID, d)
    gath.arrived(W_MID)
    keep(6)

    def mm2(i, carry):
        row = i * BLK
        acc = None
        for m, s in enumerate(OFFS):
            p = jnp.dot(shifted(e_ref, o_ref, s, row, BLK), wmid_ref[m * MID:(m + 1) * MID, :],
                        preferred_element_type=jnp.float32)
            acc = p if acc is None else acc + p
        h2_ref[pl.ds(pl.multiple_of(row, BLK), BLK), :] = acc
        return carry
    lax.fori_loop(0, ROWS // BLK, mm2, 0)
    for d in range(far + 1):
        x_step(W_OUT, d)
    mean, rstd = moments(h2_ref, 0, MID // GROUPS)
    st_ref[0:8, MID:2 * MID] = mean
    st_ref[8:16, MID:2 * MID] = rstd
    sc2 = rstd * g_ref[:, 2 * MID:3 * MID]
    sh2 = g_ref[:, 3 * MID:4 * MID] - mean * sc2

    def act2(r, carry):
        h = h2_ref[rows_full(r), :].reshape(PITCH, TB, MID)
        a2_ref[rows_full(r), :] = gelu(h * sc2[None] + sh2[None]).reshape(RB, MID).astype(jnp.bfloat16)
        return carry
    lax.fori_loop(0, SIDE, act2, 0)
    keep(2)
    gath.arrived(W_OUT)

    def mm3(i, carry):
        rs = pl.ds(pl.multiple_of(i * BLK, BLK), BLK)
        h3_ref[rs, :] = jnp.dot(a2_ref[rs, :], wout_ref[...], preferred_element_type=jnp.float32)
        return carry
    lax.fori_loop(0, ROWS // BLK, mm3, 0)
    for k in range(D // CH):
        lo = k * CH
        mean, rstd = moments(h3_ref, lo, D // GROUPS)
        st_ref[0:8, 2 * MID + lo:2 * MID + lo + CH] = mean
        st_ref[8:16, 2 * MID + lo:2 * MID + lo + CH] = rstd
        sc3 = rstd * g_ref[:, 4 * MID + lo:4 * MID + lo + CH]
        sh3 = g_ref[:, 4 * MID + D + lo:4 * MID + D + lo + CH] - mean * sc3

        def act3(r, acc):
            h = h3_ref[row_at(r), lo:lo + CH].reshape(SIDE, TB, CH)
            s = x_ref[rows_full(r), lo:lo + CH].astype(jnp.float32)[0:VR].reshape(SIDE, TB, CH)
            return acc + jnp.sum(gelu(s + (h * sc3[None] + sh3[None])), axis=0)
        acc = lax.fori_loop(0, SIDE, act3, jnp.zeros((TB, CH), jnp.float32))
        feat = (acc / float(PIX)).astype(jnp.bfloat16).astype(jnp.float32)
        for j in range(lo // 128, (lo + CH) // 128):
            fsend[j] = feat[:, j * 128 - lo:(j + 1) * 128 - lo]

            @pl.when(me != j)
            def _(j=j):
                rc(fsend.at[j], frecv.at[me], s_f.at[j], q_f.at[me], {"dp": j}).start()

            @pl.when(me == j)
            def _(j=j):
                frecv[j] = fsend[j]

    z8 = jnp.zeros((TB, CH), jnp.float32)

    def slopes(k):
        lo = k * CH
        cs = slice(lo, lo + CH)
        mean = st_ref[0:8, 2 * MID + lo:2 * MID + lo + CH]
        rstd = st_ref[8:16, 2 * MID + lo:2 * MID + lo + CH]
        gain = g_ref[:, 4 * MID + lo:4 * MID + lo + CH]
        shift = g_ref[:, 4 * MID + D + lo:4 * MID + D + lo + CH]
        mr = mean * rstd

        def one(r, acc):
            s1, s2 = acc
            h = h3_ref[row_at(r), cs].reshape(SIDE, TB, CH)
            v = x_ref[rows_full(r), cs].astype(jnp.float32)[0:VR].reshape(SIDE, TB, CH)
            xh = h * rstd[None] - mr[None]
            t = dgelu(v + (xh * gain + shift))
            dh3_ref[rows_full(r), cs] = jnp.concatenate([t.reshape(VR, CH), z8], axis=0).astype(jnp.bfloat16)
            return s1 + jnp.sum(t, axis=0), s2 + jnp.sum(t * xh, axis=0)
        s1, s2 = lax.fori_loop(0, SIDE, one, (z8, z8))
        sl_ref[0:8, cs] = s1
        sl_ref[8:16, cs] = s2

    @pl.when(role == 0)
    def _():
        slopes(0)
        slopes(1)
    for p in peers:
        rc(fsend.at[p], frecv.at[p], s_f.at[0], q_f.at[p], {"dp": p}).wait_recv()
    feats = frecv[...].reshape(n * TB, 128)
    ids = gall_ref[...].reshape(n * TB, 128).astype(jnp.int32)

    acc = None
    def two_windows(i):
        a, b = window_of(i), window_of(i + 1)
        return jnp.concatenate([head_ref[a:a + WIN, :], head_ref[b:b + WIN, :]], axis=1)
    for i in range(0, GAMES, 2):
        lhs = jnp.concatenate([jnp.where(ids == i, feats, 0.0), jnp.where(ids == i + 1, feats, 0.0)], axis=1)
        p = lax.dot_general(lhs.astype(jnp.bfloat16), two_windows(i), T1, preferred_element_type=jnp.float32)
        acc = p if acc is None else acc + p
    off = ids_offset(ids)
    part[...] = shift_rows(acc, off, False).reshape(half, 2, TB, LW)

    d1 = rc(part.at[:, 1 - c], r1, s_1, q_1, {"dp": cp})
    d1.start()
    d1.wait()
    pair = me // 2
    r1[...] = r1[...] + part[:, c]
    pps = [lax.rem(pair + k, half) for k in range(1, half)]
    for k, p in enumerate(pps):
        rc(r1.at[p], r2.at[pair], s_2.at[k], q_2.at[pair], {"dp": 2 * p + c}).start()
    r2[pair] = r1[pair]

    @pl.when(role == 0)
    def _():
        slopes(2)
        slopes(3)
    for k, p in enumerate(pps):
        rc(r1.at[p], r2.at[p], s_2.at[k], q_2.at[p], {"dp": 2 * p + c}).wait_recv()
    logits = jnp.sum(r2[...], axis=0)

    lane = lax.broadcasted_iota(jnp.int32, (TB, 128), 1)
    live = lane < ATOMS
    zi = support_low + (support_high - support_low) * lane.astype(jnp.float32) / (ATOMS - 1)
    zi = jnp.where(live, zi, 0.0)
    taken, nxt, expert, reward, done, gid = (scal_ref[k] for k in range(6))
    pieces = []
    for a in range(ACTIONS):
        v = logits if a == 0 else pltpu.roll(logits, LW - ATOMS * a, 1)
        pieces.append(v[:, :128])

    @pl.when(role == 1)
    def _():
        sel = jnp.zeros((TB, 128), jnp.float32)
        for a in range(ACTIONS):
            sel = sel + jnp.where(nxt == float(a), pieces[a], 0.0)
        sel = jnp.where(live, sel, -1e30)
        e = jnp.exp(sel - jnp.max(sel, axis=1, keepdims=True))
        e = jnp.where(live, e, 0.0)
        prob = e / jnp.sum(e, axis=1, keepdims=True)
        spacing = (support_high - support_low) / (ATOMS - 1)
        m = jnp.zeros((TB, 128), jnp.float32)
        for j in range(ATOMS):
            zj = float(np.float32(support_low) + np.float32(support_high - support_low) * np.float32(j) /
                       np.float32(ATOMS - 1))
            tz = jnp.clip(reward + discount * (1.0 - done) * zj, support_low, support_high)
            wt = jnp.maximum(0.0, 1.0 - jnp.abs(tz - zi) / spacing)
            m = m + prob[:, j:j + 1] * wt
        tgt_s[...] = jnp.where(live, m, 0.0)
        d = rc(tgt_s, tgt_r, s_t, q_t, {"role": 0})
        d.start()
        d.wait_send()
        rc(frow_ref, frow_ref, s_r.at[0], q_r.at[0], {"role": 0}).wait_recv()
        rc(dlog_ref, dlog_ref, s_r.at[1], q_r.at[1], {"role": 0}).wait_recv()
        dfeat_ref[...] = jnp.zeros_like(dfeat_ref)

    @pl.when(role == 0)
    def _():
        frow_ref[...] = feats.astype(jnp.bfloat16)
        gt = jnp.transpose(gall_ref[...].reshape(n * TB, 128))[0:TB]
        count = jnp.sum((gt == gid).astype(jnp.float32), axis=1, keepdims=True)
        weight = 1.0 / jnp.maximum(count, 1.0)
        x3 = jnp.where(live[None], jnp.stack(pieces), -1e30)
        act = lax.broadcasted_iota(jnp.int32, (ACTIONS, TB, 128), 0).astype(jnp.float32)
        hot = (act == taken[None]).astype(jnp.float32)
        mx = jnp.max(x3, axis=2, keepdims=True)
        e = jnp.where(live[None], jnp.exp(x3 - mx), 0.0)
        s = jnp.sum(e, axis=2, keepdims=True)
        logp = jnp.where(live[None], x3 - mx - jnp.log(s), 0.0)
        prob = e / s
        q = jnp.sum(prob * zi[None], axis=2, keepdims=True)
        qb = jnp.broadcast_to(q, (ACTIONS, TB, 128))
        qm = jnp.max(qb, axis=0)
        qe = jnp.exp(qb - qm[None])
        qs = jnp.sum(qe, axis=0)
        lse = qm + jnp.log(qs)
        pol = qe / qs[None]
        chosen = jnp.sum(logp * hot, axis=0)
        qt = jnp.sum(qb * hot, axis=0)
        rc(tgt_s, tgt_r, s_t, q_t, {"role": 1}).wait_recv()
        m = tgt_r[...]
        cross = -jnp.sum(m * chosen, axis=1, keepdims=True)
        row_loss = cross + penalty * expert * (lse - qt)
        msum = jnp.sum(m, axis=1, keepdims=True)
        dl = hot * (prob * msum[None] - m[None]) + (penalty * expert)[None] * (pol - hot) * prob * (zi[None] - qb)
        dl = jnp.where(live[None], dl * (weight * (1.0 / GAMES))[None], 0.0)
        flat = jnp.zeros((TB, LW), jnp.float32)
        pad = jnp.zeros((TB, LW - 128), jnp.float32)
        for a in range(ACTIONS):
            v = jnp.concatenate([dl[a], pad], axis=1)
            flat = flat + (v if a == 0 else pltpu.roll(v, ATOMS * a, 1))
        l0 = row_loss * weight
        p0 = l0.astype(jnp.bfloat16).astype(jnp.float32)
        p1 = (l0 - p0).astype(jnp.bfloat16).astype(jnp.float32)
        p2 = l0 - p0 - p1
        last = flat[:, LW - 128:]
        last = jnp.where(lane == 125, p0, jnp.where(lane == 126, p1, jnp.where(lane == 127, p2, last)))
        flat = jnp.concatenate([flat[:, :LW - 128], last], axis=1)
        down_s[...] = jnp.concatenate([flat[:, :LW // 2], flat[:, LW // 2:]], axis=0).astype(jnp.bfloat16)
        for k, p in enumerate(pps):
            rc(down_s, dlog_ref.at[me], s_l.at[k], q_l.at[me], {"dp": 2 * p + c}).start()
        rc(down_s, dlog_ref.at[me], s_c.at[0], q_c.at[me], {"dp": cp}).start()
        dlog_ref[me] = down_s[...]
        for k, p in enumerate(pps):
            o = 2 * p + c
            rc(down_s, dlog_ref.at[o], s_l.at[k], q_l.at[o], {"dp": cp}).wait_recv()
            rc(dlog_ref.at[o], dlog_ref.at[o], s_c.at[k + 1], q_c.at[o], {"dp": cp}).start()
        for p in [pair] + pps:
            o = 2 * p + 1 - c
            rc(dlog_ref.at[o], dlog_ref.at[o], s_c.at[0], q_c.at[o], {"dp": cp}).wait_recv()
        to0 = rc(frow_ref, frow_ref, s_r.at[0], q_r.at[0], {"role": 1})
        to1 = rc(dlog_ref, dlog_ref, s_r.at[1], q_r.at[1], {"role": 1})
        to0.start()
        to1.start()
        rolled = shift_rows(widen(dlog_ref[...]), off, True).astype(jnp.bfloat16)
        acc = None
        for i in range(0, GAMES, 2):
            p = jnp.dot(rolled, two_windows(i), preferred_element_type=jnp.float32)
            p = jnp.where(ids == i, p[:, :128], jnp.where(ids == i + 1, p[:, 128:], 0.0))
            acc = p if acc is None else acc + p
        dsend[...] = acc.reshape(n, TB, 128)
        for k, p in enumerate(peers):
            rc(dsend.at[p], drecv.at[me], s_d.at[k], q_d.at[me], {"dp": p}).start()
        drecv[me] = dsend[me]
        for k, p in enumerate(peers):
            rc(dsend.at[p], drecv.at[p], s_d.at[k], q_d.at[p], {"dp": p}).wait_recv()
        for j in range(n):
            dfeat_ref[:, j * 128:(j + 1) * 128] = drecv[j]
        for k, p in enumerate(pps):
            rc(down_s, dlog_ref.at[me], s_l.at[k], q_l.at[me], {"dp": 2 * p + c}).wait_send()
        rc(down_s, dlog_ref.at[me], s_c.at[0], q_c.at[me], {"dp": cp}).wait_send()
        for k, p in enumerate(pps):
            o = 2 * p + c
            rc(dlog_ref.at[o], dlog_ref.at[o], s_c.at[k + 1], q_c.at[o], {"dp": cp}).wait_send()
        for k, p in enumerate(peers):
            rc(dsend.at[p], drecv.at[me], s_d.at[k], q_d.at[me], {"dp": p}).wait_send()
        to0.wait_send()
        to1.wait_send()

    for j in range(n):
        pl.when(me != j)(rc(fsend.at[j], frecv.at[me], s_f.at[j], q_f.at[me], {"dp": j}).wait_send)
    for k, p in enumerate(pps):
        rc(r1.at[p], r2.at[pair], s_2.at[k], q_2.at[pair], {"dp": 2 * p + c}).wait_send()
    tail = dlog_ref[:, :, 384:512].astype(jnp.float32)[:, TB:2 * TB].reshape(n * TB, 128)
    lanes = lax.broadcasted_iota(jnp.int32, (n * TB, 128), 1)
    total = jnp.sum(jnp.where(lanes >= 125, tail, 0.0))
    loss_ref[...] = jnp.full((TB, 128), total, jnp.float32)

    def last_norm():
        for k in range(D // CH):
            lo = k * CH
            cs = slice(lo, lo + CH)
            mean = st_ref[0:8, 2 * MID + lo:2 * MID + lo + CH]
            rstd = st_ref[8:16, 2 * MID + lo:2 * MID + lo + CH]
            gain = g_ref[:, 4 * MID + lo:4 * MID + lo + CH]
            dout = dfeat_ref[:, cs] / float(PIX)
            s1 = dout * sl_ref[0:8, cs]
            s2 = dout * sl_ref[8:16, cs]
            put_gain(gg_ref, 4 * MID + lo, s2)
            put_gain(gg_ref, 4 * MID + D + lo, s1)
            count = 1.0 / float(PIX * D // GROUPS)
            m1 = group_sum(gain * s1, D // GROUPS) * count
            m2 = group_sum(gain * s2, D // GROUPS) * count
            cc = -rstd * rstd * m2
            cb = -rstd * m1 - mean * cc
            ca = rstd * gain * dout

            def one(r, carry):
                h = h3_ref[row_at(r), cs].reshape(SIDE, TB, CH)
                t = dh3_ref[rows_full(r), cs].astype(jnp.float32)[0:VR].reshape(SIDE, TB, CH)
                v = (ca[None] * t + cc[None] * h + cb[None]).reshape(VR, CH)
                dh3_ref[rows_full(r), cs] = jnp.concatenate([v, z8], axis=0).astype(jnp.bfloat16)
                return carry
            lax.fori_loop(0, SIDE, one, 0)

    @pl.when(role == 0)
    def _():
        last_norm()
        kept[3].start()

        def da2(i, c):
            rs = pl.ds(pl.multiple_of(i * BLK, BLK), BLK)
            d2_ref[rs, :] = lax.dot_general(dh3_ref[rs, :], wout_ref[...], T1, preferred_element_type=jnp.float32)
            return c
        lax.fori_loop(0, ROWS // BLK, da2, 0)
        far_a1(1).wait_send()
        through(h2_ref, d2_ref, st_ref, g_ref, gg_ref, MID, 2 * MID, 3 * MID,
                lambda r, v: put_shifted(e_ref, o_ref, r, v))
        kept[4].start()
        kept[5].start()
        gg_ref[:, 0:2 * MID] = jnp.zeros((1, 2 * MID), jnp.float32)
        for d in kept:
            d.wait()

    @pl.when(role == 1)
    def _():
        far_a1(0).wait_recv()
        for k in range(MID // 128):
            fart_ref[k * 128:(k + 1) * 128, :] = jnp.transpose(far_ref[:, k * 128:(k + 1) * 128])
        d = pltpu.make_async_copy(fart_ref, fart_hbm, k_sem.at[7])
        d.start()
        d.wait()
        gg_ref[...] = jnp.zeros_like(gg_ref)
    gath.end()


def block_step(frames, weights, averages, scal, head, avg_head, n, cid):
    f32, b16 = jnp.float32, jnp.bfloat16
    S = jax.ShapeDtypeStruct
    V, dma = pltpu.VMEM, pltpu.SemaphoreType.DMA
    vs, hs = pl.BlockSpec(memory_space=pltpu.VMEM), pl.BlockSpec(memory_space=pl.ANY)
    h = n // 2
    nz = n // 4
    sends = 4 + 6 * (nz - 1) + 2 * nz
    return pl.pallas_call(
        functools.partial(step_kernel, n),
        out_shape=(S((ROWS, D), b16), S((ROWS, MID), f32), S((ROWS, MID), b16), S((ROWS, D), b16), S((EROWS, MID), b16),
                   S((EROWS, MID), b16), S((9 * MID, MID), b16), S((MID, ROWS), b16), S((16, 2 * MID + D), f32),
                   S((1, 4 * MID + 2 * D), f32), S((1, 4 * MID + 2 * D), f32), S((n, TB, 128), f32), S((n * TB, 128), b16), S((n, 16, 512), b16), S((TB, 128), f32)),
        in_specs=[hs] + [vs] * 8 + [pl.BlockSpec(memory_space=pltpu.SMEM)] * 6 + [hs] * 2,
        out_specs=(hs,) * 8 + (vs,) * 7,
        scratch_shapes=[
            V((6, TB, 128), f32), V((D // n, MID), b16), V((9 * MID // n, MID), b16), V((MID // n, D), b16), V((16, 128), f32),
            V((D, MID), b16), V((9 * MID, MID), b16), V((MID, D), b16), V((n, 16, 128), f32),
            V((ROWS, D), b16), V((ROWS, MID), f32), V((ROWS, MID), f32), V((ROWS, D), f32), V((ROWS, MID), b16),
            V((TB, D), f32), V((16, D), f32), V((EROWS, MID), b16), V((EROWS, MID), b16),
            V((ROWS, MID), f32), V((ROWS, D), b16), V((ROWS, MID), b16), V((MID, ROWS), b16),
            V((2, SIDE, TB, D), b16), V((2, HC, 128), f32), V((PADC, 128), b16),
            V((n, TB, 128), f32), V((n, TB, 128), f32), V((h, 2, TB, LW), f32), V((h, TB, LW), f32),
            V((h, TB, LW), f32), V((TB, 128), f32), V((TB, 128), f32), V((16, 512), b16),
            V((n, TB, 128), f32), V((n, TB, 128), f32),
            dma((4,)), dma((4, sends)), dma((4, n)), dma((2,)), dma((2,)), dma((8,)), dma((1,)), dma((1,)),
            dma((n,)), dma((n,)), dma, dma, dma((h,)), dma((h,)), dma, dma, dma((h,)), dma((n,)),
            dma((h,)), dma((n,)), dma((n,)), dma((n,)), dma((2,)), dma((2,))],
        compiler_params=pltpu.CompilerParams(collective_id=cid, has_side_effects=True,
                                             vmem_limit_bytes=64 * 1024 * 1024),
        name="block_step",
    )(frames, *weights, *averages, *scal, head, avg_head)


KEEP, SEND, BOTH = 0, 1, 2
OUT, MIDDLE, IN, GAINS = 0, 1, 2, 3


def units_of(ri, ro, rm):
    q, h, t = MID // 4, ri // 2, rm // 2
    online = ((0, ri + 2 * ro, 2 * ro, 0, MID, SEND, OUT), (0, ri, 2 * ro, 0, MID, KEEP, OUT),
              (0, 0, ri, MID // 2, MID // 2, SEND, IN), (0, 0, h, 0, MID // 2, KEEP, IN), (0, h, h, 0, MID // 2, KEEP, IN),
              (1, 0, 3, 0, 128, BOTH, GAINS))
    target = ((0, 0, t, 0, q, SEND, MIDDLE), (0, t, t, 0, q, SEND, MIDDLE), (0, 0, rm, q, q, SEND, MIDDLE), (0, 0, rm, 2 * q, q, KEEP, MIDDLE),
              (0, 0, rm, 3 * q, q, KEEP, MIDDLE))
    return online, target


def sums_kernel(n_dev, rows, x_hbm, h1_hbm, a2_hbm, dh3_hbm, e_hbm, o_hbm, wmid_hbm, fart_hbm, st_ref, g_ref, gpart_ref,
                gall_ref, frow_ref, dlog_ref, t_out, t_mid, t_in, t_gains, dlt, rhs, x_ref, h1_ref, a2_ref, dh3_ref, e_ref, o_ref, wmid_ref, fart_ref, low_ref,
                d2_ref, gg_ref, *refs):
    outs = (t_out, t_mid, t_in, t_gains)
    g, r1, r2, rz = (refs[2 * j:2 * j + 2] for j in range(4))
    fs, fr = refs[8:12], refs[12:16]
    s1, q1, s2, q2, s3, q3, sf, qf, sl, sd, qd = refs[16:]
    nz = n_dev // 4
    ri, ro, rm = rows
    online, target = units_of(*rows)
    me, z, x, c = place()
    role = lax.axis_index("role")
    xp = {"dp": me + 2 - 4 * x}
    cp = {"dp": me + 1 - 2 * c}

    def slot(zz, xx, cc):
        return zz * 4 + xx * 2 + cc

    order = list(range(nz))
    parts = ((0, 128), (128, 128), (256, 128), (384, MID - 384))

    def load(k):
        src = (x_hbm, h1_hbm, a2_hbm, dh3_hbm, e_hbm, o_hbm, wmid_hbm, fart_hbm)[k]
        dst = (x_ref, h1_ref, a2_ref, dh3_ref, e_ref, o_ref, wmid_ref, fart_ref)[k]
        return pltpu.make_async_copy(src, dst, sl.at[k])

    def far_d2(to, k):
        cs = pl.ds(*parts[k])
        return rc(e_hbm.at[pl.ds(PAD, ROWS), cs], low_ref.at[:, cs], sd.at[k], qd.at[k], {"role": to})

    @pl.when(role == 0)
    def _():
        for k in (3, 2, 6, 4, 5, 1, 0):
            load(k).start()
    pl.when(role == 1)(load(7).start)
    zs = [{"dp": lax.rem(me + 4 * k, 4 * nz)} for k in range(1, nz)]
    greet([(None, p) for p in [xp, cp, {"role": 1 - role}] + zs])
    z8 = jnp.zeros((TB, CH), jnp.float32)

    def online_first():
        for k in range(len(parts)):
            far_d2(1, k).start()
        gg_ref[...] = gpart_ref[...]
        load(3).wait()
        load(2).wait()
        for k in (2, 3, 0, 1):
            v = lax.dot_general(a2_ref[...], dh3_ref[:, k * CH:(k + 1) * CH], T0, preferred_element_type=jnp.float32)
            g[0][:, ri + k * ro:ri + (k + 1) * ro, :] = v.reshape(n_dev, ro, CH)

    def online_rest():
        for k in (6, 4, 5, 1, 0):
            load(k).wait()

        def da1(i, carry):
            row = i * BLK
            acc = None
            for m, s in enumerate(OFFS):
                p = lax.dot_general(shifted(e_ref, o_ref, -s, row, BLK), wmid_ref[m * MID:(m + 1) * MID, :], T1,
                                    preferred_element_type=jnp.float32)
                acc = p if acc is None else acc + p
            d2_ref[pl.ds(pl.multiple_of(row, BLK), BLK), :] = acc
            return carry
        lax.fori_loop(0, ROWS // BLK, da1, 0)

        def put1(r, v):
            low_ref[rows_full(r), :] = jnp.concatenate([v, z8], axis=0).astype(jnp.bfloat16)
        through(h1_ref, d2_ref, st_ref, g_ref, gg_ref, 0, 0, MID, put1)
        per = CH // ri
        for k in range(D // CH):
            v = lax.dot_general(x_ref[:, k * CH:(k + 1) * CH], low_ref[...], T0, preferred_element_type=jnp.float32)
            g[0][k * per:(k + 1) * per, 0:ri, :] = v.reshape(per, ri, MID)
        for i in range(n_dev):
            for k in range(3):
                at = (i * 3 + k) * 128
                g[1][i, k:k + 1, :] = gg_ref[:, at:at + 128]

    def target_part(k):
        if k == 0:
            clear_margins(e_ref, o_ref)
            load(7).wait()
        cs = slice(parts[k][0], parts[k][0] + parts[k][1] if k < 2 else MID)
        far_d2(0, k).wait_recv()
        if k == 2:
            far_d2(0, 3).wait_recv()
        zh = jnp.zeros((TB, cs.stop - cs.start), jnp.float32)

        def rebuild(r, carry):
            v = low_ref[rows_full(r), cs].astype(jnp.float32)
            at = pl.ds(pl.multiple_of(PAD + r * RB, 16), RB)
            e_ref[at, cs] = low_ref[rows_full(r), cs]
            o_ref[at, cs] = jnp.concatenate([zh, v[0:VR]], axis=0).astype(jnp.bfloat16)
            return carry
        lax.fori_loop(0, SIDE, rebuild, 0)
        for m, s in enumerate(OFFS):
            ref, base = (e_ref, 16 - s) if s % 2 == 0 else (o_ref, 17 - s)
            v = jnp.dot(fart_ref[...], ref[base * TB:base * TB + ROWS, cs], preferred_element_type=jnp.float32)
            at = m * MID
            while at < (m + 1) * MID:
                i = at // rm
                end = min((i + 1) * rm, (m + 1) * MID)
                g[0][i, at - i * rm:end - i * rm, cs] = v[at - m * MID:end - m * MID]
                at = end

    def cut(ref, i, u):
        return ref.at[i, pl.ds(u[1], u[2]), pl.ds(u[3], u[4])]

    def region(u):
        if u[6] == OUT:
            return slice(0, ro), slice(0, outs[OUT].shape[1])
        at = u[3] % outs[u[6]].shape[1]
        return slice(u[1], u[1] + u[2]), slice(at, at + u[4])

    def place_sum(u, total):
        if u[6] == OUT:
            return jnp.concatenate([total[j * ro:(j + 1) * ro] for j in range(u[2] // ro)], axis=1)
        return total

    def final(u, to, n):
        rs, cs = region(u)
        at = (pl.ds(rs.start, rs.stop - rs.start), pl.ds(cs.start, cs.stop - cs.start))
        return rc(fs[u[6]].at[at], fr[u[6]].at[at], sf.at[n], qf.at[n], {"role": to})

    def run(units, mine, plan):
        def add(u, i, ref, j):
            a, rs, cs = u[0], slice(u[1], u[1] + u[2]), slice(u[3], u[3] + u[4])
            g[a][i, rs, cs] = g[a][i, rs, cs] + ref[a][j, rs, cs]

        def c1(n, zz, k):
            u = units[n]
            xx = 1 - x if k == 0 else x
            return rc(cut(g[u[0]], slot(zz, xx, 1 - c), u), cut(r1[u[0]], k * nz + zz, u), s1.at[n, k * nz + zz],
                      q1.at[n, k * nz + zz], cp)

        def c2(n, zz):
            u = units[n]
            return rc(cut(g[u[0]], slot(zz, 1 - x, c), u), cut(r2[u[0]], zz, u), s2.at[n, zz], q2.at[n, zz], xp)

        def c3(n, t, at):
            u = units[n]
            return rc(cut(g[u[0]], slot(t, x, c), u), cut(rz[u[0]], at, u), s3.at[n, t], q3.at[n, at],
                      {"dp": slot(t, x, c)})

        def gather_x(n):
            u = units[n]
            for zz in order:
                c1(n, zz, 1).wait_recv()
                add(u, slot(zz, x, c), r1, nz + zz)
            for zz in order:
                c2(n, zz).wait_recv()
                add(u, slot(zz, x, c), r2, zz)
                pl.when(z != zz)(c3(n, zz, z).start)

        def first(n):
            for k in range(2):
                for zz in order:
                    c1(n, zz, k).start()

        def second(n):
            for zz in order:
                c1(n, zz, 0).wait_recv()
                add(units[n], slot(zz, 1 - x, c), r1, zz)
                c2(n, zz).start()

        def finish(n):
            u = units[n]
            a, rs, cs = u[0], slice(u[1], u[1] + u[2]), slice(u[3], u[3] + u[4])
            for zz in order:
                @pl.when(z != zz)
                def _(zz=zz):
                    c3(n, z, zz).wait_recv()
                    add(u, me, rz, zz)
            total = place_sum(u, g[a][me, rs, cs])
            at = region(u)
            if u[5] != SEND:
                outs[u[6]][at] = total
            if u[5] != KEEP:
                fs[u[6]][at] = total.astype(fs[u[6]].dtype)
                final(u, 1 - mine, n).start()
        def operands():
            ids = gall_ref[...].reshape(-1, 128).astype(jnp.int32) - mine * (GAMES // 2)
            v = shift_rows(widen(dlog_ref[...]), ids_offset(ids), True)
            for k in range(WIN // 128):
                dlt[k * 128:(k + 1) * 128, :] = jnp.transpose(v[:, k * 128:(k + 1) * 128]).astype(jnp.bfloat16)
            feats = frow_ref[...].astype(jnp.float32)
            for i in range(GAMES // 2):
                rhs[i] = jnp.where(ids == i, feats, 0.0).astype(jnp.bfloat16)

        def terms(ns):
            for n in ns:
                first(n)
            for n in ns:
                second(n)
        for do, what in plan:
            if do == "make":
                what()
            elif do == "head":
                operands()
            else:
                {"start": terms, "x": gather_x, "end": finish}[do](what)
        for n, u in enumerate(units):
            for zz in order:
                c1(n, zz, 0).wait_send()
                c1(n, zz, 1).wait_send()
                c2(n, zz).wait_send()
                pl.when(z != zz)(c3(n, zz, z).wait_send)
            if u[5] != KEEP:
                final(u, 1 - mine, n).wait_send()

    def receive(units, other):
        for n, u in enumerate(units):
            if u[5] != KEEP:
                final(u, other, n).wait_recv()
                outs[u[6]][region(u)] = fr[u[6]][region(u)].astype(jnp.float32)

    def rest(nu):
        steps = [("x", 0), ("x", 1)]
        for k in range(2, nu):
            steps += [("x", k), ("end", k - 2)]
        return steps + [("end", nu - 2), ("end", nu - 1)]

    @pl.when(role == 0)
    def _():
        run(online, 0, [("make", online_first), ("start", (0, 1)), ("make", online_rest), ("start", (2, 3, 4, 5)), ("head", 0)] + rest(6))
        receive(target, 1)
        for k in range(len(parts)):
            far_d2(1, k).wait_send()

    @pl.when(role == 1)
    def _():
        run(target, 1, [("make", lambda: target_part(0)), ("start", (0, 1)), ("make", lambda: target_part(1)), ("x", 0),
                        ("start", (2,)), ("x", 1), ("make", lambda: target_part(2)), ("start", (3, 4)),
                        ("head", 0)] + rest(5)[2:])
        receive(online, 0)


def sums(saved, games_all, frow, dlog, n, cid):
    nz = n // 4
    V, dma = pltpu.VMEM, pltpu.SemaphoreType.DMA
    f32, b16 = jnp.float32, jnp.bfloat16
    S = jax.ShapeDtypeStruct
    rows = ri, ro, rm = D // n, MID // n, 9 * MID // n
    half = [(ro, D // 2), (rm, MID // 2), (ri, MID // 2), (3, 128)]
    low = [b16, b16, b16, f32]
    sh = [(rm, MID), (3, 128)]
    nu = max(len(u) for u in units_of(*rows))
    vs, hs = pl.BlockSpec(memory_space=pltpu.VMEM), pl.BlockSpec(memory_space=pl.ANY)
    return pl.pallas_call(
        functools.partial(sums_kernel, n, rows),
        out_shape=tuple(S(s, f32) for s in half) + (S((WIN, n * TB), b16), S((GAMES // 2, n * TB, 128), b16)),
        in_specs=[hs] * 8 + [vs] * 6,
        out_specs=(vs,) * 6,
        scratch_shapes=[V(s.shape, s.dtype) for s in saved[:8]] +
        [V((ROWS, MID), b16), V((ROWS, MID), f32), V((1, 4 * MID + 2 * D), f32)] +
        [V((k,) + s, f32) for k in (4 * nz, 2 * nz, nz, nz) for s in sh] + [V(s, t) for s, t in zip(half, low)] * 2 +
        [dma((nu, 2 * nz))] * 2 + [dma((nu, nz))] * 4 + [dma((nu,))] * 2 + [dma((8,)), dma((4,)), dma((4,))],
        compiler_params=pltpu.CompilerParams(collective_id=cid, has_side_effects=True,
                                             vmem_limit_bytes=63 * 1024 * 1024),
        name="gradient_sums",
    )(*saved, games_all, frow, dlog)


UB = 2048
NU = -(-HALF // UB)
LASTU = HALF - (NU - 1) * UB


def segments(k):
    lo, hi = k * UB, min((k + 1) * UB, -(-HALF // 16) * 16)
    parts = []
    for i in range(GAMES // 2):
        a, end = window_of(i), window_of(i + 1)
        mixed = i > 0 and WIDE * i != a
        for r0, r1, games in ((a, a + 16, (i - 1, i)), (a + 16, end, (i,))) if mixed else ((a, end, (i,)),):
            if i == GAMES // 2 - 1 and r1 == end:
                r1 = -(-HALF // 16) * 16
            r0, r1 = max(r0, lo), min(r1, hi)
            if r0 < r1:
                parts.append((r0, r1, games))
    return parts


def update_kernel(dlt, rhs, loss_ref, *refs):
    grads, olds_hbm = refs[:4], refs[4:16]
    hbm = refs[16:19]
    loss_out, news, hbm_out = refs[19], refs[20:36], refs[36:40]
    olds = refs[40:52]
    grow, ibuf, obuf, cbuf, si, so, sw = refs[52:]
    role = lax.axis_index("role")

    def rows_of(k):
        return UB if k < NU - 1 else LASTU

    def fetch(k):
        n = rows_of(k)
        return [pltpu.make_async_copy(hbm[t].at[pl.ds(pl.multiple_of(role * HALF + k * UB, 8), n)],
                                      ibuf.at[k % 3, t, pl.ds(0, n)], si.at[k % 3, t]) for t in range(3)]

    def store(k):
        n = rows_of(k)
        cs = [pltpu.make_async_copy(obuf.at[k % 2, t, pl.ds(0, n)], hbm_out[t].at[pl.ds(k * UB, n)], so.at[k % 2, t])
              for t in range(3)]
        return cs + [pltpu.make_async_copy(cbuf.at[k % 2, pl.ds(0, n)], hbm_out[3].at[pl.ds(k * UB, n)], so.at[k % 2, 3])]

    old_copies = [pltpu.make_async_copy(olds_hbm[i], olds[i], sw.at[i]) for i in range(12)]
    for d in fetch(0) + fetch(1) + old_copies:
        d.start()
    loss_out[...] = loss_ref[0:1, 0:1]

    def small(a, right):
        w, m, v = olds[3 * a:3 * a + 3]
        nw, nm, nv, nc = news[4 * a:4 * a + 4]
        cols = grads[a].shape[1]
        cs = slice(cols if right else 0, (cols if right else 0) + cols)
        gv = grads[a][...]
        rate = learn_rate
        if a == 3:
            gv = jnp.concatenate([gv[k:k + 1, :] for k in range(gv.shape[0])], axis=1)
            cs = slice(0, gv.shape[1])
            rate = gain_rate
        mv = momentum_decay * m[:, cs] + gv
        wv = w[:, cs] - rate * (gv + momentum_decay * mv)
        nw[...] = wv
        nm[...] = gv if a == 0 else mv
        nv[...] = average_decay * v[:, cs] + (1.0 - average_decay) * wv
        nc[...] = wv.astype(jnp.bfloat16)

    for k in range(NU):
        if k + 2 < NU:
            for d in fetch(k + 2):
                d.start()
        lo = k * UB
        for r0, r1, games in segments(k):
            acc = None
            for i in games:
                at = r0 - window_of(i)
                p = jnp.dot(dlt[at:at + r1 - r0, :], rhs[i], preferred_element_type=jnp.float32)
                acc = p if acc is None else acc + p
            grow[r0 - lo:r1 - lo, :] = acc
        for d in fetch(k):
            d.wait()
        if k >= 2:
            for d in store(k - 2):
                d.wait()
        b, s = k % 2, k % 3

        def one(r, carry, b=b, s=s):
            rs = pl.ds(pl.multiple_of(r * 128, 128), 128)
            gv = grow[rs, :]
            m = momentum_decay * ibuf[s, 1, rs, :] + gv
            w = ibuf[s, 0, rs, :] - learn_rate * (gv + momentum_decay * m)
            obuf[b, 0, rs, :] = w
            obuf[b, 1, rs, :] = m
            obuf[b, 2, rs, :] = average_decay * ibuf[s, 2, rs, :] + (1.0 - average_decay) * w
            cbuf[b, rs, :] = w.astype(jnp.bfloat16)
            return carry
        lax.fori_loop(0, UB // 128, one, 0)
        for d in store(k):
            d.start()
        if 4 <= k < 8:
            a = k - 4
            for i in range(3 * a, 3 * a + 3):
                old_copies[i].wait()
            if a == 3:
                small(a, False)
            else:
                pl.when(role == 0)(lambda a=a: small(a, False))
                pl.when(role != 0)(lambda a=a: small(a, True))
    for k in (NU - 2, NU - 1):
        for d in store(k):
            d.wait()


def final_update(dlt, rhs, loss, grads, olds, tables):
    lanes = tables[0].shape[1]
    f32, b16 = jnp.float32, jnp.bfloat16
    S, V, dma = jax.ShapeDtypeStruct, pltpu.VMEM, pltpu.SemaphoreType.DMA
    vs, hs = pl.BlockSpec(memory_space=pltpu.VMEM), pl.BlockSpec(memory_space=pl.ANY)
    new_shapes = []
    for a in range(4):
        s = olds[3 * a].shape if a == 3 else grads[a].shape
        new_shapes += [S(s, f32)] * 3 + [S(s, b16)]
    return pl.pallas_call(
        update_kernel,
        in_specs=[vs] * 7 + [hs] * 15,
        out_specs=[vs] * 17 + [hs] * 4,
        scratch_shapes=[V(o.shape, f32) for o in olds] +
        [V((UB, lanes), f32), V((3, 3, UB, lanes), f32),
         V((2, 3, UB, lanes), f32), V((2, UB, lanes), b16), dma((3, 3)), dma((2, 4)), dma((12,))],
        out_shape=[S((1, 1), f32)] + new_shapes + [S((HALF, lanes), f32)] * 3 + [S((HALF, lanes), b16)],
        compiler_params=pltpu.CompilerParams(vmem_limit_bytes=63 * 1024 * 1024),
        name="final_update",
    )(dlt, rhs, loss, *grads, *olds, *tables)


def fast_device(
    frames,
    game_ids,
    taken_actions,
    next_actions,
    expert_flags,
    rewards,
    done_flags,
    weight_in,
    weight_mid,
    weight_out,
    norm_gains,
    head_table,
    moment_in,
    moment_mid,
    moment_out,
    moment_gains,
    moment_head,
    average_in,
    average_mid,
    average_out,
    average_gains,
    average_head,
):
    n = lax.axis_size("dp")
    *saved, all_ids, feat_rows, dlog, loss = block_step(
        jnp.transpose(frames[0], (1, 0, 2)),
        (weight_in[0], weight_mid[0], weight_out[0], norm_gains),
        (average_in[0], average_mid[0], average_out[0], average_gains),
        (taken_actions, next_actions, expert_flags, rewards, done_flags, game_ids),
        head_table.T,
        average_head.T,
        n,
        1,
    )
    grad_out, grad_mid, grad_in, grad_gains, dlt, rhs = sums(saved, all_ids, feat_rows, dlog, n, 2)
    loss, *rest = final_update(
        dlt,
        rhs,
        loss,
        (grad_in, grad_mid, grad_out, grad_gains),
        (
            weight_in[0],
            moment_in[0],
            average_in[0],
            weight_mid[0],
            moment_mid[0],
            average_mid[0],
            weight_out[0],
            moment_out[0],
            average_out[0],
            norm_gains,
            moment_gains,
            average_gains,
        ),
        (head_table.T, moment_head.T, average_head.T),
    )
    return (
        loss.reshape(()),
        *(v[None] for v in rest[:12]),
        *rest[12:16],
        *(v.T for v in rest[16:]),
    )


def solution(mesh):
    return jax.shard_map(
        fast_device if mesh.shape["dp"] == 16 else on_device,
        mesh=mesh,
        in_specs=(
            P("role", "dp", None, None),
            P("dp"),
            P("dp"),
            P("dp"),
            P("dp"),
            P("dp"),
            P("dp"),
            P(None, "dp", None),
            P(None, "dp", None),
            P(None, "dp", None),
            P(None, "dp"),
            P("dp", None),
            P(None, "dp", None),
            P(None, "dp", None),
            P(None, "dp", None),
            P(None, "dp"),
            P("dp", None),
            P(None, "dp", None),
            P(None, "dp", None),
            P(None, "dp", None),
            P(None, "dp"),
            P("dp", None),
        ),
        out_specs=(
            P(),
            P(None, "dp", "role"),
            P(None, "dp", "role"),
            P(None, "dp", "role"),
            P(None, "dp", "role"),
            P(None, "dp", "role"),
            P(None, "dp", "role"),
            P(None, "dp", "role"),
            P(None, "dp", "role"),
            P(None, "dp", "role"),
            P(None, "dp", "role"),
            P(None, "dp", "role"),
            P(None, "dp", "role"),
            P(None, "dp"),
            P(None, "dp"),
            P(None, "dp"),
            P(None, "dp"),
            P("dp", "role"),
            P("dp", "role"),
            P("dp", "role"),
            P("dp", "role"),
        ),
        check_vma=False,
    )
```
